128 devices in a mesh: tp: 16 (over x, z_hi, core), grp: 8 (over y, z_lo).
Axes of the slice: x: 4, y: 4, z: 4 (z_hi: 2, z_lo: 2; z = z_hi * 2 + z_lo), core: 2. Of those that a mesh axis runs over, the one named last changes fastest.
Arguments:
- hidden_rows: bfloat16 [64, 256, 16384], P('grp', None, 'tp'), may hold values from -6 to 6
- key_value_weight: bfloat16 [16384, 2048], P('tp'), may hold values from -0.046875 to 0.046875
- prefill_query: bfloat16 [64, 256, 16384], P('grp', None, 'tp'), may hold values from -20 to 20
- earlier_cache: bfloat16 [64, 16, 512, 256], P('grp', 'tp'), may hold values from -5 to 5
- stretch_offset: int32 [64], replicated, may hold values from 256 to 1024, as said below
- prompt_length: int32 [64], replicated, may hold values from 257 to 1280, as said below
- decode_owner: int32 [64], replicated, may hold values from 0 to 7, as said below
- decode_query: bfloat16 [64, 4, 16384], P('grp', None, 'tp'), may hold values from -20 to 20
- decode_kv: bfloat16 [64, 4, 2048], P('grp'), may hold values from -5 to 5
Outputs:
- prefill_out: bfloat16 [64, 256, 16384], P('grp', None, 'tp')
- decode_out: bfloat16 [64, 4, 16384], P('grp', None, 'tp')
The draws below stay inside these ranges and needn't reach their ends.
Inputs may be any that keep to these rules, and one draw needn't show every extreme that they name: `stretch_offset`: a multiple of 256; some prompt has offset 1024 in every draw. `prompt_length`: between stretch_offset + 1 and stretch_offset + 256; positions of the final block from the length on are padding; some prompt reaches 1280 in every draw. `decode_owner`: among the 8 prompts of each replica r (prompts r * 8 to r * 8 + 7) every owner occurs exactly once.
All inputs are finite; a program needn't handle non-finite values.
Results may differ from the reference program's by a relative error of at most 0.04.
Values may be sent and summed in bfloat16 or wider, within the bound.
No kernel may reach another device: no remote copies, remote signals or barrier semaphores. Data moves between devices by JAX's collectives and lax.ppermute only.
A program may use at most 128 MiB of HBM per device.

```python
import jax
import jax.numpy as jnp
from jax import lax

MODEL_WIDTH = 16384
QUERY_HEADS = 128
VALUE_HEADS = 8
HEAD_SIZE = 128
FINAL_LENGTH = 256
CONTEXT_LENGTH = 1024
DECODE_STEPS = 4
CACHE_BLOCKS = 2
BLOCK_POSITIONS = 512
PR_DEV = 8
PROMPT_COUNT = 64
N_TP = 16


def offsets_lengths(key):
    key = jax.random.fold_in(key, 303)
    first, second, third = jax.random.split(key, 3)
    blocks = jax.random.randint(first, (PROMPT_COUNT,), 1, CONTEXT_LENGTH // FINAL_LENGTH + 1)
    longest = jax.random.randint(third, (), 0, PROMPT_COUNT)
    marked = jnp.arange(PROMPT_COUNT) == longest
    offsets = jnp.where(marked, CONTEXT_LENGTH // FINAL_LENGTH, blocks) * FINAL_LENGTH
    extra = jax.random.randint(second, (PROMPT_COUNT,), 1, FINAL_LENGTH + 1)
    extra = jnp.where(marked, FINAL_LENGTH, extra)
    return (offsets.astype(jnp.int32), (offsets + extra).astype(jnp.int32))


def draw_stretch_offset(key, part):
    offsets, lengths = offsets_lengths(key)
    return offsets


def draw_prompt_length(key, part):
    offsets, lengths = offsets_lengths(key)
    return lengths


def draw_decode_owner(key, part):
    key = jax.random.fold_in(key, 404)
    key_rows = jax.random.split(key, PROMPT_COUNT // PR_DEV)
    orders = jax.vmap(lambda one: jax.random.permutation(one, PR_DEV))(key_rows)
    return orders.reshape(-1).astype(jnp.int32)


def draw_earlier_cache(key, part):
    key = jax.random.fold_in(key, 1)
    array_shape = (PROMPT_COUNT, VALUE_HEADS, CONTEXT_LENGTH, 2 * HEAD_SIZE)
    value_rows = jax.random.truncated_normal(key, -5.0, 5.0, array_shape, jnp.float32)
    return value_rows.reshape(PROMPT_COUNT, VALUE_HEADS * CACHE_BLOCKS, BLOCK_POSITIONS, 2 * HEAD_SIZE).astype(jnp.bfloat16)


def draw_prefill_query(key, part):
    key = jax.random.fold_in(key, 2)
    array_shape = (PROMPT_COUNT, FINAL_LENGTH, QUERY_HEADS, HEAD_SIZE)
    value_rows = jax.random.truncated_normal(key, -5.0, 5.0, array_shape, jnp.float32)
    return value_rows.reshape(PROMPT_COUNT, FINAL_LENGTH, QUERY_HEADS * HEAD_SIZE).astype(jnp.bfloat16)


def draw_decode_kv(key, part):
    key = jax.random.fold_in(key, 3)
    array_shape = (PROMPT_COUNT, DECODE_STEPS, VALUE_HEADS, 2 * HEAD_SIZE)
    value_rows = jax.random.truncated_normal(key, -5.0, 5.0, array_shape, jnp.float32)
    return value_rows.reshape(PROMPT_COUNT, DECODE_STEPS, VALUE_HEADS * 2 * HEAD_SIZE).astype(jnp.bfloat16)


def draw_decode_query(key, part):
    key = jax.random.fold_in(key, 4)
    array_shape = (PROMPT_COUNT, DECODE_STEPS, QUERY_HEADS, HEAD_SIZE)
    value_rows = jax.random.truncated_normal(key, -5.0, 5.0, array_shape, jnp.float32)
    return value_rows.reshape(PROMPT_COUNT, DECODE_STEPS, QUERY_HEADS * HEAD_SIZE).astype(jnp.bfloat16)


def level_of(stream_key, shape, shards, least, high):
    def one(axis_at, parts):
        draws = jax.random.uniform(jax.random.fold_in(jax.random.fold_in(stream_key, 6), axis_at), (parts,), jnp.float32, least / len(shards), high / len(shards))
        return jnp.repeat(jnp.exp(draws), shape[axis_at] // parts).reshape((-1,) + (1,) * (len(shape) - axis_at - 1))

    loudness = one(*shards[0])
    for cut in shards[1:]:
        loudness = loudness * one(*cut)
    return loudness


def gaussian(own_key, shape, spread, reach, cuts=(), held_as=jnp.bfloat16):
    loudness = level_of(own_key, shape, cuts, -0.22, 0.18) if cuts else 1.0
    entries = jax.random.normal(own_key, shape, jnp.float32) * spread * loudness
    return jnp.minimum(jnp.maximum(entries, -reach), reach).astype(held_as)


def setup_inputs(seed: int = 0) -> dict:
    key_list = jax.random.split(jax.random.key(seed), 10)
    return {
        "hidden_rows": gaussian(key_list[0], (PROMPT_COUNT, FINAL_LENGTH, MODEL_WIDTH), 1.0, 6.0, ((0, 8), (2, 16))),
        "key_value_weight": gaussian(key_list[1], (MODEL_WIDTH, 2 * VALUE_HEADS * HEAD_SIZE), MODEL_WIDTH ** -0.5, 0.046875, ((0, 16),)),
        "prefill_query": draw_prefill_query(jax.random.fold_in(key_list[9], 71), 0),
        "earlier_cache": draw_earlier_cache(jax.random.fold_in(key_list[9], 71), 0),
        "stretch_offset": draw_stretch_offset(jax.random.fold_in(key_list[9], 71), 0),
        "prompt_length": draw_prompt_length(jax.random.fold_in(key_list[9], 71), 0),
        "decode_owner": draw_decode_owner(jax.random.fold_in(key_list[9], 71), 0),
        "decode_query": draw_decode_query(jax.random.fold_in(key_list[9], 71), 0),
        "decode_kv": draw_decode_kv(jax.random.fold_in(key_list[9], 71), 0),
    }


NEG = -1.0e30
ROPE_BASE = 500000.0


def rotate(key_rows, positions):
    half = key_rows.shape[-1] // 2
    freq = ROPE_BASE ** (jnp.arange(half, dtype=jnp.float32) * (-2.0 / key_rows.shape[-1]))
    angle = positions.astype(jnp.float32)[..., None] * freq
    cosine = jnp.cos(angle)
    sine = jnp.sin(angle)
    first = key_rows[..., :half]
    second = key_rows[..., half:]
    return jnp.concatenate([first * cosine - second * sine, second * cosine + first * sine], axis=-1)


def attend_heads(query_rows, key_rows, visible_mask):
    scores = jnp.einsum("qhgd,hkd->hgqk", query_rows.astype(jnp.float32), key_rows[..., :HEAD_SIZE].astype(jnp.float32)) * (HEAD_SIZE ** -0.5)
    masked = jnp.where(visible_mask[None, None], scores, NEG)
    top = jnp.max(masked, axis=-1, keepdims=True)
    weights = jnp.exp(masked - top)
    total = jnp.sum(weights, axis=-1)
    rounded = lax.optimization_barrier(weights.astype(jnp.bfloat16)).astype(jnp.float32)
    mixed_output = jnp.einsum("hgqk,hkd->qhgd", rounded, key_rows[..., HEAD_SIZE:].astype(jnp.float32))
    return mixed_output / jnp.transpose(total, (2, 0, 1))[..., None]


def reference(hidden_rows, key_value_weight, prefill_query, earlier_cache, stretch_offset, prompt_length, decode_owner, decode_query, decode_kv):
    prompt_batch = hidden_rows.shape[0]
    groups = prompt_batch // PR_DEV
    rows = hidden_rows.reshape(prompt_batch * FINAL_LENGTH, MODEL_WIDTH)
    feature_width = MODEL_WIDTH // N_TP

    def append_block(index, total):
        start = (index * feature_width).astype(jnp.int32)
        left = lax.dynamic_slice_in_dim(rows, start, feature_width, 1)
        right = lax.dynamic_slice_in_dim(key_value_weight, start, feature_width, 0)
        term = jnp.dot(left, right, preferred_element_type=jnp.float32).astype(jnp.bfloat16)
        return total + lax.optimization_barrier(term).astype(jnp.float32)

    summed_scores = lax.fori_loop(0, N_TP, append_block, jnp.zeros((prompt_batch * FINAL_LENGTH, 2 * VALUE_HEADS * HEAD_SIZE), jnp.float32))
    summed_scores = summed_scores.reshape(prompt_batch, FINAL_LENGTH, VALUE_HEADS, 2 * HEAD_SIZE)
    stretch_index = jnp.arange(FINAL_LENGTH, dtype=jnp.int32)
    positions = stretch_offset[:, None] + stretch_index[None, :]
    turned = rotate(summed_scores[..., :HEAD_SIZE], positions[:, :, None])
    fresh = jnp.concatenate([turned, summed_scores[..., HEAD_SIZE:]], axis=-1).astype(jnp.bfloat16)
    fresh = jnp.transpose(fresh, (0, 2, 1, 3))
    cache_table = earlier_cache.reshape(prompt_batch, VALUE_HEADS, CONTEXT_LENGTH, 2 * HEAD_SIZE)
    queries_per_group = QUERY_HEADS // VALUE_HEADS
    cache_index = jnp.arange(CONTEXT_LENGTH, dtype=jnp.int32)
    step_index = jnp.arange(DECODE_STEPS, dtype=jnp.int32)

    def prefill_one(items):
        query_rows, stored, newest_positions, offset, length = items
        key_rows = jnp.concatenate([stored, newest_positions], axis=1)
        key_pos = jnp.concatenate([cache_index, offset + stretch_index])
        key_ok = jnp.concatenate([cache_index < offset, jnp.ones((FINAL_LENGTH,), dtype=bool)])
        query_pos = offset + stretch_index
        visible_mask = key_ok[None, :] & (key_pos[None, :] <= query_pos[:, None])
        mixed_output = attend_heads(query_rows.reshape(FINAL_LENGTH, VALUE_HEADS, queries_per_group, HEAD_SIZE), key_rows, visible_mask)
        mixed_output = jnp.where((query_pos < length)[:, None, None, None], mixed_output, 0.0)
        return mixed_output.reshape(FINAL_LENGTH, QUERY_HEADS * HEAD_SIZE).astype(jnp.bfloat16)

    prefill_out = lax.map(prefill_one, (prefill_query, cache_table, fresh, stretch_offset, prompt_length))

    owners = decode_owner.reshape(groups, PR_DEV)
    match = owners[None, :, :] == jnp.arange(groups, dtype=jnp.int32)[:, None, None]
    picked = jnp.sum(jnp.where(match, jnp.arange(PR_DEV, dtype=jnp.int32)[None, None, :], 0), axis=2)
    slot_prompt = (jnp.arange(groups, dtype=jnp.int32)[None, :] * PR_DEV + picked).reshape(-1).astype(jnp.int32)

    def decode_one(items):
        query_rows, recent_block, prompt = items
        offset = stretch_offset[prompt]
        length = prompt_length[prompt]
        newest_positions = jnp.transpose(recent_block.reshape(DECODE_STEPS, VALUE_HEADS, 2 * HEAD_SIZE), (1, 0, 2))
        key_rows = jnp.concatenate([cache_table[prompt], fresh[prompt], newest_positions], axis=1)
        key_pos = jnp.concatenate([cache_index, offset + stretch_index, length + step_index])
        key_ok = jnp.concatenate([cache_index < offset, offset + stretch_index < length, jnp.ones((DECODE_STEPS,), dtype=bool)])
        query_pos = length + step_index
        visible_mask = key_ok[None, :] & (key_pos[None, :] <= query_pos[:, None])
        mixed_output = attend_heads(query_rows.reshape(DECODE_STEPS, VALUE_HEADS, queries_per_group, HEAD_SIZE), key_rows, visible_mask)
        return mixed_output.reshape(DECODE_STEPS, QUERY_HEADS * HEAD_SIZE).astype(jnp.bfloat16)

    decode_out = lax.map(decode_one, (decode_query, decode_kv, slot_prompt))
    return prefill_out, decode_out
```

```python
import functools
import math

import jax
import jax.numpy as jnp
import numpy as np
from jax import lax
from jax.experimental import pallas as pl
from jax.experimental.pallas import tpu as pltpu
from jax.sharding import PartitionSpec as P

HEAD_SIZE = 128
PAIR = 2 * HEAD_SIZE
LOCAL = 8
FINAL_LENGTH = 256
CONTEXT_LENGTH = 1024
PART = 512
STEPS = 4
HEADS = 8
ROPE_BASE = 500000.0
G = 16
DROWS = 16
TILE = 32
SCALE2 = HEAD_SIZE**-0.5 * math.log2(math.e)
NEG = -1e30
F32 = jnp.float32
BF16 = jnp.bfloat16
ANY = pl.BlockSpec(memory_space=pl.ANY)
VMEM = pl.BlockSpec(memory_space=pltpu.VMEM)
PARAMS = pltpu.CompilerParams(vmem_limit_bytes=48 * 2**20)


def pairs(move):
    out = []
    for x in range(4):
        for z in range(2):
            for core in range(2):
                nx, nz, nc = move(x, z, core)
                out.append((x * 4 + z * 2 + core, (nx % 4) * 4 + (nz % 2) * 2 + nc % 2))
    return out


SIBLING = pairs(lambda x, z, c: (x, z, c + 1))
ACROSS_Z = pairs(lambda x, z, c: (x, z + 1, c))
ALONG_X = [pairs(lambda x, z, c, d=d: (x + d, z, c)) for d in range(4)]


def rope_table():
    half = HEAD_SIZE // 2
    freq = ROPE_BASE ** (np.arange(half, dtype=np.float64) * (-2.0 / HEAD_SIZE))
    angle = np.arange(CONTEXT_LENGTH + FINAL_LENGTH, dtype=np.float64)[:, None] * freq
    cosine, sine = np.cos(angle), np.sin(angle)
    return np.concatenate([cosine, cosine, -sine, sine], axis=1).astype(np.float32)


def plan(ids, offs, lens):
    starts, counts, at = [], [], jnp.int32(0)
    for p in range(LOCAL):
        i = ids[3] * LOCAL + p
        count = lax.shift_right_logical(lens[i] - offs[i] + (G - 1), 4)
        starts.append(at)
        counts.append(count)
        at = at + count
    return starts, counts, at


def ready_in_first(ids, offs, lens, limit):
    starts, counts, _ = plan(ids, offs, lens)
    ready = jnp.int32(0)
    for p in range(LOCAL - 1):
        ready = ready + (starts[p] + counts[p] <= limit).astype(jnp.int32)
    return ready


def ragged(starts, counts, first_block, blocks, copy):
    for p in range(LOCAL):
        low = jnp.maximum(starts[p], first_block)
        high = jnp.minimum(starts[p] + counts[p], first_block + blocks)
        n = jnp.maximum(high - low, 0)
        for bit in range(4, -1, -1):
            done = lax.shift_left(lax.shift_right_logical(n, bit + 1), bit + 1)

            @pl.when(lax.bitwise_and(n, 1 << bit) != 0)
            def _(p=p, bit=bit, low=low, done=done):
                copy(p, bit, low + done - starts[p], low + done - first_block, 1 << bit)


def rows(block, count):
    return pl.ds(pl.multiple_of(block * G, G), count * G)


def project(ids, offs, lens, hid, w, hbuf, wbuf, hsem, wsem, first_block, blocks):
    x, z = ids[0], ids[1]

    def weight_copy(j):
        head = lax.rem(x + j // 2, 4) * 2 + lax.rem(z + j % 2, 2)
        return pltpu.make_async_copy(
            w.at[:, pl.ds(pl.multiple_of(head * PAIR, PAIR), PAIR)], wbuf.at[j], wsem.at[j]
        )

    starts, counts, total = plan(ids, offs, lens)

    def hidden_copy(p, bit, source, target, count):
        return pltpu.make_async_copy(
            hid.at[rows(p * (FINAL_LENGTH // G) + source, count)],
            hbuf.at[rows(target, count)],
            hsem.at[p, bit],
        )

    ragged(starts, counts, first_block, blocks, lambda *a: hidden_copy(*a).start())
    for j in range(8):
        weight_copy(j).start()

    @pl.loop(jnp.clip(total - first_block, 0, blocks), blocks)
    def _(b):
        hbuf[rows(b, 1), :] = jnp.zeros((G, hbuf.shape[1]), BF16)

    ragged(starts, counts, first_block, blocks, lambda *a: hidden_copy(*a).wait())
    return weight_copy


def send_kernel(ids, offs, lens, hid, w, out, hbuf, wbuf, obuf, hsem, wsem, osem, *, chunk, q):
    first_block = (chunk * 2 + 1 - ids[2]) * (q // G)
    weight_copy = project(ids, offs, lens, hid, w, hbuf, wbuf, hsem, wsem, first_block, q // G)
    for j in range(8):
        weight_copy(j).wait()
        obuf[j] = jnp.dot(hbuf[...], wbuf[j], preferred_element_type=F32).astype(BF16)
        pltpu.make_async_copy(obuf.at[j], out.at[j], osem.at[j]).start()
    for j in range(8):
        pltpu.make_async_copy(obuf.at[j], out.at[j], osem.at[j]).wait()


def keep_kernel(ids, offs, lens, hid, w, other, *refs, chunk, q, qx):
    outs = refs[:6]
    hbuf, wbuf, rbuf, hsem, wsem, rsem = refs[6:12]
    obufs = refs[12:18]
    osem = refs[18]
    first_block = (chunk * 2 + ids[2]) * (q // G)
    for j in range(8):
        pltpu.make_async_copy(other.at[j], rbuf.at[j], rsem.at[j]).start()
    weight_copy = project(ids, offs, lens, hid, w, hbuf, wbuf, hsem, wsem, first_block, q // G)

    for j in range(8):
        weight_copy(j).wait()
        pltpu.make_async_copy(other.at[j], rbuf.at[j], rsem.at[j]).wait()
        d, e = j // 2, j % 2
        value = jnp.dot(hbuf[...], wbuf[j], preferred_element_type=F32) + rbuf[j].astype(F32)
        value = value.astype(BF16)
        obufs[d][e] = value[:qx]
        obufs[4 + e][d] = value[qx:]
        if e == 1:
            pltpu.make_async_copy(obufs[d], outs[d], osem.at[d]).start()
    for e in range(2):
        pltpu.make_async_copy(obufs[4 + e], outs[4 + e], osem.at[4 + e]).start()
    for i in range(6):
        pltpu.make_async_copy(obufs[i], outs[i], osem.at[i]).wait()


def project_scratch(q):
    return [
        pltpu.VMEM((q, 1024), BF16),
        pltpu.VMEM((8, 1024, PAIR), BF16),
    ]


def call(kernel, prefetched, operands, out_shape, scratch=(), specs=None, out_specs=None, grid=(), flops=0, moved=0, aliases=None):
    n = len(prefetched)
    return pl.pallas_call(
        kernel,
        out_shape=out_shape,
        grid_spec=pltpu.PrefetchScalarGridSpec(
            num_scalar_prefetch=n,
            grid=grid,
            in_specs=specs if specs is not None else [ANY] * len(operands),
            out_specs=out_specs if out_specs is not None else jax.tree.map(lambda _: ANY, out_shape),
            scratch_shapes=list(scratch),
        ),
        compiler_params=PARAMS,
        input_output_aliases=aliases or {},
        cost_estimate=pl.CostEstimate(flops=flops, bytes_accessed=moved, transcendentals=0),
    )(*prefetched, *operands)


def send_half(meta, hid, w, chunk, q):
    return call(
        functools.partial(send_kernel, chunk=chunk, q=q),
        meta,
        (hid, w),
        jax.ShapeDtypeStruct((8, q, PAIR), BF16),
        project_scratch(q)
        + [
            pltpu.VMEM((8, q, PAIR), BF16),
            pltpu.SemaphoreType.DMA((LOCAL, 5)),
            pltpu.SemaphoreType.DMA((8,)),
            pltpu.SemaphoreType.DMA((8,)),
        ],
        flops=2 * q * 1024 * 2048,
        moved=2 * (q * 1024 + 1024 * 2048 + q * 2048),
    )


def keep_half(meta, hid, w, other, chunk, q, qx):
    shapes = [(2, qx, PAIR)] * 4 + [(4, q - qx, PAIR)] * 2
    return call(
        functools.partial(keep_kernel, chunk=chunk, q=q, qx=qx),
        meta,
        (hid, w, other),
        [jax.ShapeDtypeStruct(s, BF16) for s in shapes],
        project_scratch(q)
        + [
            pltpu.VMEM((8, q, PAIR), BF16),
            pltpu.SemaphoreType.DMA((LOCAL, 5)),
            pltpu.SemaphoreType.DMA((8,)),
            pltpu.SemaphoreType.DMA((8,)),
        ]
        + [pltpu.VMEM(s, BF16) for s in shapes]
        + [pltpu.SemaphoreType.DMA((6,))],
        flops=2 * q * 1024 * 2048,
        moved=2 * (q * 1024 + 1024 * 2048 + 2 * q * 2048),
    )


def middle_kernel(x0, x1, x2, x3, z0, z1, xk, xs, zk, zs1, zs2, zs3):
    for e, out in ((0, xk), (1, xs)):
        total = (x0[e].astype(F32) + x1[e].astype(F32)) + (x2[e].astype(F32) + x3[e].astype(F32))
        out[...] = total.astype(out.dtype)
    for d, out in enumerate((zk, zs1, zs2, zs3)):
        out[...] = (z0[d].astype(F32) + z1[d].astype(F32)).astype(out.dtype)


def middle(xs, zs, qx, qz):
    outs = [((qx, PAIR), F32), ((qx, PAIR), BF16), ((qz, PAIR), F32)] + [((qz, PAIR), BF16)] * 3
    n = 2 if qx % 32 == 0 and qz % 32 == 0 else 1
    return call(
        middle_kernel,
        (),
        (*xs, *zs),
        [jax.ShapeDtypeStruct(*s) for s in outs],
        grid=(n,),
        specs=[pl.BlockSpec((2, qx // n, PAIR), lambda i: (0, i, 0))] * 4
        + [pl.BlockSpec((4, qz // n, PAIR), lambda i: (0, i, 0))] * 2,
        out_specs=[pl.BlockSpec((s[0] // n, PAIR), lambda i: (i, 0)) for s, _ in outs],
        moved=2 * PAIR * (8 * qx + 8 * qz + 3 * qx + 5 * qz),
        flops=PAIR * (8 * qx + 4 * qz),
    )


def rope_rows_kernel(ids, offs, lens, table, out, sem, *, q):
    starts, counts, _ = plan(ids, offs, lens)
    for verb in ("start", "wait"):
        for chunk in range(2):
            first_block = (chunk * 2 + ids[2]) * (q // G)

            def copy(p, bit, source, target, count, chunk=chunk, verb=verb):
                base = lax.shift_right_logical(offs[ids[3] * LOCAL + p], 4)
                c = pltpu.make_async_copy(
                    table.at[rows(base + source, count)],
                    out.at[chunk, rows(target, count)],
                    sem.at[chunk, p, bit],
                )
                c.start() if verb == "start" else c.wait()

            ragged(starts, counts, first_block, q // G, copy)


def rope_rows(meta, table, q):
    return call(
        functools.partial(rope_rows_kernel, q=q),
        meta,
        (table,),
        jax.ShapeDtypeStruct((2, q, PAIR), F32),
        [pltpu.SemaphoreType.DMA((2, LOCAL, 5))],
        moved=2 * q * PAIR * 8,
    )


def finish_kernel(ids, offs, lens, xk, xr, zk, z1, z2, z3, turn, out, *, chunk, q, qx):
    _, _, total = plan(ids, offs, lens)
    valid = (total - (chunk * 2 + ids[2]) * (q // G)) * G

    def put(first, value):
        n = value.shape[0]
        row = lax.broadcasted_iota(jnp.int32, (n, HEAD_SIZE), 0) + first
        key = value[:, :HEAD_SIZE]
        cosine = turn[0, first : first + n, :HEAD_SIZE]
        sine = turn[0, first : first + n, HEAD_SIZE:]
        key = key * cosine + pltpu.roll(key, HEAD_SIZE // 2, 1) * sine
        out[first : first + n, :HEAD_SIZE] = jnp.where(row < valid, key, 0.0).astype(BF16)
        out[first : first + n, HEAD_SIZE:] = value[:, HEAD_SIZE:].astype(BF16)

    put(0, xk[...] + xr[...].astype(F32))
    put(qx, (zk[...] + z1[...].astype(F32)) + (z2[...].astype(F32) + z3[...].astype(F32)))


def finish(meta, xk, xr, zk, zr, turn, chunk, q, qx):
    return call(
        functools.partial(finish_kernel, chunk=chunk, q=q, qx=qx),
        meta,
        (xk, xr, zk, *zr, turn),
        jax.ShapeDtypeStruct((q, PAIR), BF16),
        grid=(1,),
        specs=[pl.BlockSpec(a.shape, lambda i, *_: (0, 0)) for a in (xk, xr, zk, *zr)]
        + [pl.BlockSpec((1, q, PAIR), lambda i, *_, chunk=chunk: (chunk, 0, 0))],
        out_specs=pl.BlockSpec((q, PAIR), lambda i, *_: (0, 0)),
        moved=q * PAIR * 12,
        flops=q * PAIR * 4,
    )


def stack_heads(tile):
    return jnp.concatenate([tile[:, h * HEAD_SIZE : (h + 1) * HEAD_SIZE] for h in range(HEADS)], axis=0)


def scores_of(query, keys):
    return lax.dot_general(query, keys, (((1,), (1,)), ((), ())), preferred_element_type=F32)


def spread(column, n):
    lane = lax.broadcasted_iota(jnp.int32, (n, HEAD_SIZE), 1)
    out = jnp.zeros((n, HEAD_SIZE), F32)
    for h in range(HEADS):
        out = jnp.where(lane == h, column[h * n : (h + 1) * n], out)
    return out


def gather_column(stats):
    return jnp.concatenate([stats[:, h : h + 1] for h in range(HEADS)], axis=0)


def prior_kernel(ids, offs, lens, owner, query, dquery, mine, theirs, out, stat, dout, dstat, kbuf, sem, *, first):
    step = pl.program_id(0)
    steps = pl.num_programs(0)

    def copies(i):
        slot = lax.rem(i, 2)
        core = ids[2]
        return (
            pltpu.make_async_copy(
                mine.at[first + i],
                kbuf.at[slot, pl.ds(pl.multiple_of(core * PART, PART), PART)],
                sem.at[slot, 0],
            ),
            pltpu.make_async_copy(
                theirs.at[first + i],
                kbuf.at[slot, pl.ds(pl.multiple_of((1 - core) * PART, PART), PART)],
                sem.at[slot, 1],
            ),
        )

    @pl.when(step == 0)
    def _():
        for c in copies(step):
            c.start()

    @pl.when(step + 1 < steps)
    def _():
        for c in copies(step + 1):
            c.start()

    for c in copies(step):
        c.wait()

    slot = lax.rem(step, 2)
    at = ids[3] * LOCAL + first + step
    offset, length = offs[at], lens[at]
    tiles = lax.div(length - offset + (TILE - 1), TILE)

    def part(tile, keys):
        n = tile.shape[0]
        scores = scores_of(stack_heads(tile), kbuf[slot, :keys, :HEAD_SIZE])
        top = jnp.max(scores, axis=1, keepdims=True) * SCALE2
        weights = jnp.exp2(scores * SCALE2 - top)
        total = jnp.sum(weights, axis=1, keepdims=True)
        mixed = jnp.dot(weights.astype(BF16), kbuf[slot, :keys, HEAD_SIZE:], preferred_element_type=F32)
        return (mixed / total).astype(BF16), spread(top + jnp.log2(total), n)

    for blocks in range(1, 5):

        @pl.when(offset == blocks * 256)
        def _(keys=blocks * 256):
            @pl.loop(0, tiles)
            def _(t):
                where = pl.ds(pl.multiple_of(t * TILE, TILE), TILE)
                mixed, stats = part(query[0, where, :], keys)
                for h in range(HEADS):
                    out[0, where, h * HEAD_SIZE : (h + 1) * HEAD_SIZE] = mixed[h * TILE : (h + 1) * TILE]
                stat[0, where, :] = stats

            mixed, stats = part(dquery[0], keys)
            for h in range(HEADS):
                dout[0, :, h * HEAD_SIZE : (h + 1) * HEAD_SIZE] = mixed[h * DROWS : (h + 1) * DROWS]
            dstat[0] = stats


def prior(meta, owner, query, dquery, mine, theirs, first, n):
    def at(i, ids, offs, lens, owner):
        return (first + i, 0, 0)

    def decode_at(i, ids, offs, lens, owner):
        return (owner[ids[3] * LOCAL + first + i], 0, 0)

    def here(i, *_):
        return (i, 0, 0)

    shapes = [
        ((n, FINAL_LENGTH, HEADS * HEAD_SIZE), BF16),
        ((n, FINAL_LENGTH, HEAD_SIZE), F32),
        ((n, DROWS, HEADS * HEAD_SIZE), BF16),
        ((n, DROWS, HEAD_SIZE), F32),
    ]
    return call(
        functools.partial(prior_kernel, first=first),
        (*meta, owner),
        (query, dquery, mine, theirs),
        [jax.ShapeDtypeStruct(*s) for s in shapes],
        [pltpu.VMEM((2, CONTEXT_LENGTH, PAIR), BF16), pltpu.SemaphoreType.DMA((2, 2))],
        grid=(n,),
        specs=[
            pl.BlockSpec((1, FINAL_LENGTH, HEADS * HEAD_SIZE), at),
            pl.BlockSpec((1, DROWS, HEADS * HEAD_SIZE), decode_at),
            ANY,
            ANY,
        ],
        out_specs=[pl.BlockSpec((1,) + s[1:], here) for s, _ in shapes],
        flops=n * 3 * 10**9,
        moved=n * 2 * 10**6,
    )


def assemble(ids, pieces, fbuf, sem, q, act):
    for chunk, (own, other) in enumerate(pieces):
        for i, (ref, core) in enumerate(((own, ids[2]), (other, 1 - ids[2]))):
            target = fbuf.at[pl.ds(pl.multiple_of((chunk * 2 + core) * q, G), q)]
            c = pltpu.make_async_copy(ref, target, sem.at[chunk, i])
            c.start() if act == "start" else c.wait()


def fresh_kernel(ids, offs, lens, *refs, chunks, q):
    pieces = [(refs[2 * c], refs[2 * c + 1]) for c in range(chunks)]
    refs = refs[2 * chunks :]
    if chunks == 2:
        refs = refs[1:]
    query, prior_out, prior_stat, out, fbuf, sem = refs
    p = pl.program_id(0)

    @pl.when(p == 0)
    def _():
        assemble(ids, pieces, fbuf, sem, q, "start")
        fbuf[chunks * 2 * q :, :] = jnp.zeros((FINAL_LENGTH, PAIR), BF16)
        assemble(ids, pieces, fbuf, sem, q, "wait")

    ready = ready_in_first(ids, offs, lens, 2 * q // G)
    starts, _, _ = plan(ids, offs, lens)
    start = jnp.int32(0)
    for i in range(1, LOCAL):
        start = jnp.where(p == i, starts[i], start)
    at = ids[3] * LOCAL + p
    count = lens[at] - offs[at]
    tiles = lax.div(count + (TILE - 1), TILE)
    mine = (p < ready) if chunks == 1 else (p >= ready)

    @pl.when(mine)
    def _():
        where_keys = pl.ds(pl.multiple_of(start * G, G), FINAL_LENGTH)
        n = HEADS * TILE
        position = lax.bitwise_and(lax.broadcasted_iota(jnp.int32, (n, FINAL_LENGTH), 0), TILE - 1)
        ahead = lax.broadcasted_iota(jnp.int32, (n, FINAL_LENGTH), 1) - position
        row = lax.broadcasted_iota(jnp.int32, (TILE, HEAD_SIZE), 0)

        @pl.loop(tiles, FINAL_LENGTH // TILE)
        def _(t):
            where = pl.ds(pl.multiple_of(t * TILE, TILE), TILE)
            out[0, where, :] = jnp.zeros((TILE, HEADS * HEAD_SIZE), BF16)

        @pl.loop(0, tiles)
        def _(t):
            where = pl.ds(pl.multiple_of(t * TILE, TILE), TILE)
            scores = scores_of(stack_heads(query[0, where, :]), fbuf[where_keys, :HEAD_SIZE])
            scores = jnp.where(ahead <= t * TILE, scores * SCALE2, NEG)
            before = gather_column(prior_stat[0, where, :])
            top = jnp.maximum(jnp.max(scores, axis=1, keepdims=True), before)
            weights = jnp.exp2(scores - top)
            share = jnp.exp2(before - top)
            total = jnp.sum(weights, axis=1, keepdims=True) + share
            mixed = jnp.dot(weights.astype(BF16), fbuf[where_keys, HEAD_SIZE:], preferred_element_type=F32)
            share, scale = share / total, 1.0 / total
            keep = row + t * TILE < count
            for h in range(HEADS):
                lanes = slice(h * HEAD_SIZE, (h + 1) * HEAD_SIZE)
                stack = slice(h * TILE, (h + 1) * TILE)
                old = prior_out[0, where, lanes].astype(F32)
                value = mixed[stack] * scale[stack] + old * share[stack]
                out[0, where, lanes] = jnp.where(keep, value, 0.0).astype(BF16)


def fresh(meta, pieces, query, prior_out, prior_stat, earlier, q):
    chunks = len(pieces)

    def at(p, ids, offs, lens):
        ready = ready_in_first(ids, offs, lens, 2 * q // G)
        if chunks == 1:
            return (jnp.minimum(p, jnp.maximum(ready - 1, 0)), 0, 0)
        return (jnp.maximum(p, ready), 0, 0)

    wide = pl.BlockSpec((1, FINAL_LENGTH, HEADS * HEAD_SIZE), at)
    flat = [a for piece in pieces for a in piece]
    extra = [] if earlier is None else [earlier]
    return call(
        functools.partial(fresh_kernel, chunks=chunks, q=q),
        meta,
        (*flat, *extra, query, prior_out, prior_stat),
        jax.ShapeDtypeStruct((LOCAL, FINAL_LENGTH, HEADS * HEAD_SIZE), BF16),
        [pltpu.VMEM((chunks * 2 * q + FINAL_LENGTH, PAIR), BF16), pltpu.SemaphoreType.DMA((2, 2))],
        grid=(LOCAL,),
        specs=[ANY] * (len(flat) + len(extra))
        + [wide, wide, pl.BlockSpec((1, FINAL_LENGTH, HEAD_SIZE), at)],
        out_specs=wide,
        aliases={3 + len(flat): 0} if extra else None,
        flops=4 * 10**9,
        moved=10**7,
    )


def decode_kernel(ids, offs, lens, owner, *refs, q):
    pieces = [(refs[0], refs[1]), (refs[2], refs[3])]
    query, recent, prior_out, prior_stat, out, fbuf, sem = refs[4:]
    assemble(ids, pieces, fbuf, sem, q, "start")
    fbuf[4 * q :, :] = jnp.zeros((FINAL_LENGTH, PAIR), BF16)
    assemble(ids, pieces, fbuf, sem, q, "wait")
    starts, _, _ = plan(ids, offs, lens)
    n = HEADS * DROWS
    step = lax.bitwise_and(lax.broadcasted_iota(jnp.int32, (n, DROWS), 0), DROWS - 1)
    later = lax.broadcasted_iota(jnp.int32, (n, DROWS), 1) > step
    column = lax.broadcasted_iota(jnp.int32, (n, FINAL_LENGTH), 1)
    for p in range(LOCAL):
        i = ids[3] * LOCAL + p
        slot = owner[i]
        keys = pl.ds(pl.multiple_of(starts[p] * G, G), FINAL_LENGTH)
        tile = stack_heads(query[slot])
        block = scores_of(tile, fbuf[keys, :HEAD_SIZE])
        block = jnp.where(column < lens[i] - offs[i], block * SCALE2, NEG)
        near = scores_of(tile, recent[slot, :, :HEAD_SIZE])
        near = jnp.where(later, NEG, near * SCALE2)
        before = gather_column(prior_stat[p])
        top = jnp.maximum(jnp.max(block, axis=1, keepdims=True), jnp.max(near, axis=1, keepdims=True))
        top = jnp.maximum(top, before)
        block_weights = jnp.exp2(block - top)
        near_weights = jnp.exp2(near - top)
        share = jnp.exp2(before - top)
        total = (
            jnp.sum(block_weights, axis=1, keepdims=True)
            + jnp.sum(near_weights, axis=1, keepdims=True)
            + share
        )
        mixed = jnp.dot(block_weights.astype(BF16), fbuf[keys, HEAD_SIZE:], preferred_element_type=F32)
        mixed = mixed + jnp.dot(
            near_weights.astype(BF16), recent[slot, :, HEAD_SIZE:], preferred_element_type=F32
        )
        for h in range(HEADS):
            lanes = slice(h * HEAD_SIZE, (h + 1) * HEAD_SIZE)
            stack = slice(h * DROWS, (h + 1) * DROWS)
            value = (mixed[stack] + prior_out[p, :, lanes].astype(F32) * share[stack]) / total[stack]
            out[slot, :, lanes] = value.astype(BF16)


def decode(meta, owner, pieces, query, recent, prior_out, prior_stat, q):
    flat = [a for piece in pieces for a in piece]
    return call(
        functools.partial(decode_kernel, q=q),
        (*meta, owner),
        (*flat, query, recent, prior_out, prior_stat),
        jax.ShapeDtypeStruct((LOCAL, DROWS, HEADS * HEAD_SIZE), BF16),
        [pltpu.VMEM((4 * q + FINAL_LENGTH, PAIR), BF16), pltpu.SemaphoreType.DMA((2, 2))],
        specs=[ANY] * 4 + [VMEM] * 4,
        out_specs=VMEM,
        flops=10**8,
        moved=2 * 10**6,
    )


def per_device(
    hidden_rows,
    key_value_weight,
    prefill_query,
    earlier_cache,
    stretch_offset,
    prompt_length,
    decode_owner,
    decode_query,
    decode_kv,
):
    lane = lax.axis_index("tp")
    group = lax.axis_index("grp")
    ids = jnp.stack([lane // 4, lane // 2 % 2, lane % 2, group]).astype(jnp.int32)
    meta = (ids, stretch_offset, prompt_length)
    cap = LOCAL * FINAL_LENGTH
    q = cap // 4
    qx = q // 2
    qz = q - qx
    hid = hidden_rows.reshape(LOCAL * FINAL_LENGTH, -1)
    cache = earlier_cache.reshape(LOCAL, PART, PAIR)

    other_cache = lax.ppermute(cache, "tp", SIBLING)
    recent = lax.dynamic_slice_in_dim(decode_kv, (lane // 2) * PAIR, PAIR, 2)
    asked = lax.all_to_all(
        jnp.concatenate([decode_query, recent], axis=2), "grp", split_axis=0, concat_axis=0, tiled=True
    )
    asked = jnp.pad(asked, ((0, 0), (0, DROWS - STEPS), (0, 0)))
    dquery = asked[..., : HEADS * HEAD_SIZE]
    recent = asked[..., HEADS * HEAD_SIZE :]

    turn = rope_rows(meta, jnp.asarray(rope_table()), q)

    other_half = [
        lax.ppermute(send_half(meta, hid, key_value_weight, c, q), "tp", SIBLING) for c in range(2)
    ]
    pieces = []
    for c in range(2):
        x0, x1, x2, x3, z0, z1 = keep_half(meta, hid, key_value_weight, other_half[c], c, q, qx)
        arrived = [lax.ppermute(v, "tp", ALONG_X[d]) for d, v in ((1, x1), (2, x2), (3, x3))]
        z1 = lax.ppermute(z1, "tp", ACROSS_Z)
        xk, xs, zk, *zs = middle((x0, *arrived), (z0, z1), qx, qz)
        xr = lax.ppermute(xs, "tp", ACROSS_Z)
        zr = [lax.ppermute(v, "tp", ALONG_X[d]) for d, v in zip((1, 2, 3), zs)]
        new = finish(meta, xk, xr, zk, zr, turn, c, q, qx)
        pieces.append((new, lax.ppermute(new, "tp", SIBLING)))

    parts = [prior(meta, decode_owner, prefill_query, dquery, cache, other_cache, i, 2) for i in (0, 2, 4, 6)]
    prior_out, prior_stat, prior_dout, prior_dstat = (
        jnp.concatenate([p[i] for p in parts], axis=0) for i in range(4)
    )
    answer = decode(meta, decode_owner, pieces, dquery, recent, prior_dout, prior_dstat, q)
    decode_out = lax.all_to_all(answer[:, :STEPS], "grp", split_axis=0, concat_axis=0, tiled=True)
    early = fresh(meta, pieces[:1], prefill_query, prior_out, prior_stat, None, q)
    prefill_out = fresh(meta, pieces, prefill_query, prior_out, prior_stat, early, q)
    return (prefill_out, decode_out)


def solution(mesh):
    in_specs = (
        P("grp", None, "tp"),
        P("tp", None),
        P("grp", None, "tp"),
        P("grp", "tp", None, None),
        P(),
        P(),
        P(),
        P("grp", None, "tp"),
        P("grp", None, None),
    )
    out_specs = (P("grp", None, "tp"), P("grp", None, "tp"))
    return jax.shard_map(
        per_device, mesh=mesh, in_specs=in_specs, out_specs=out_specs, check_vma=False
    )
```

```python
import functools
import math

import jax
import jax.numpy as jnp
import numpy as np
from jax import lax
from jax.experimental import pallas as pl
from jax.experimental.pallas import tpu as pltpu
from jax.sharding import PartitionSpec as P

HEAD_SIZE = 128
PAIR = 2 * HEAD_SIZE
LOCAL = 8
FINAL_LENGTH = 256
CONTEXT_LENGTH = 1024
PART = 512
STEPS = 4
HEADS = 8
ROPE_BASE = 500000.0
G = 16
DROWS = 16
TILE = 128
SCALE2 = HEAD_SIZE**-0.5 * math.log2(math.e)
NEG = -1e30
F32 = jnp.float32
BF16 = jnp.bfloat16
ANY = pl.BlockSpec(memory_space=pl.ANY)
VMEM = pl.BlockSpec(memory_space=pltpu.VMEM)
PARAMS = pltpu.CompilerParams(vmem_limit_bytes=24 * 2**20)


def pairs(*moves):
    out = []
    for x in range(4):
        for z in range(2):
            for core in range(2):
                if moves[core] is None:
                    continue
                dx, dz, dc = moves[core]
                out.append((x * 4 + z * 2 + core, (x + dx) % 4 * 4 + (z + dz) % 2 * 2 + (core + dc) % 2))
    return out


SIBLING = pairs((0, 0, 1), (0, 0, 1))
FIRST = [pairs((1, 0, 0), (0, 1, 0)), pairs((2, 0, 0), None), pairs((3, 0, 0), (0, 1, 0))]
SECOND = [pairs((0, 1, 0), (1, 0, 0)), pairs(None, (2, 0, 0)), pairs(None, (3, 0, 0))]


def rope_table():
    half = HEAD_SIZE // 2
    freq = ROPE_BASE ** (np.arange(half, dtype=np.float64) * (-2.0 / HEAD_SIZE))
    angle = np.arange(CONTEXT_LENGTH + FINAL_LENGTH, dtype=np.float64)[:, None] * freq
    cosine, sine = np.cos(angle), np.sin(angle)
    return np.concatenate([cosine, cosine, -sine, sine], axis=1).astype(np.float32)


def plan(ids, offs, lens):
    starts, counts, at = [], [], jnp.int32(0)
    for p in range(LOCAL):
        i = ids[3] * LOCAL + p
        count = lax.shift_right_logical(lens[i] - offs[i] + (G - 1), 4)
        starts.append(at)
        counts.append(count)
        at = at + count
    return starts, counts, at


def ragged(starts, counts, first_block, blocks, copy):
    for p in range(LOCAL):
        low = jnp.maximum(starts[p], first_block)
        high = jnp.minimum(starts[p] + counts[p], first_block + blocks)
        n = jnp.maximum(high - low, 0)
        for bit in range(4, -1, -1):
            done = lax.shift_left(lax.shift_right_logical(n, bit + 1), bit + 1)

            @pl.when(lax.bitwise_and(n, 1 << bit) != 0)
            def _(p=p, bit=bit, low=low, done=done):
                copy(p, bit, low + done - starts[p], low + done - first_block, 1 << bit)


def rows(block, count):
    return pl.ds(pl.multiple_of(block * G, G), count * G)


def project(ids, offs, lens, hid, w, hbuf, wbuf, hsem, wsem, first_block, blocks):
    weight_copy = pltpu.make_async_copy(w, wbuf, wsem)
    weight_copy.start()
    starts, counts, total = plan(ids, offs, lens)

    def hidden_copy(p, bit, source, target, count):
        return pltpu.make_async_copy(
            hid.at[rows(p * (FINAL_LENGTH // G) + source, count)],
            hbuf.at[rows(target, count)],
            hsem.at[p, bit],
        )

    ragged(starts, counts, first_block, blocks, lambda *a: hidden_copy(*a).start())

    @pl.loop(jnp.clip(total - first_block, 0, blocks), blocks)
    def _(b):
        hbuf[rows(b, 1), :] = jnp.zeros((G, hbuf.shape[1]), BF16)

    ragged(starts, counts, first_block, blocks, lambda *a: hidden_copy(*a).wait())
    weight_copy.wait()

    def product(d, e):
        head = lax.rem(ids[0] + d, 4) * 2 + lax.rem(ids[1] + e, 2)
        columns = pl.ds(pl.multiple_of(head * PAIR, PAIR), PAIR)
        return jnp.dot(hbuf[...], wbuf[:, columns], preferred_element_type=F32)

    return product


def send_kernel(ids, offs, lens, hid, w, out, hbuf, wbuf, obuf, hsem, wsem, osem, *, q):
    product = project(ids, offs, lens, hid, w, hbuf, wbuf, hsem, wsem, (1 - ids[2]) * (q // G), q // G)
    for j in range(8):
        obuf[j] = product(j // 2, j % 2).astype(BF16)
        pltpu.make_async_copy(obuf.at[j], out.at[j], osem.at[j]).start()
    for j in range(8):
        pltpu.make_async_copy(obuf.at[j], out.at[j], osem.at[j]).wait()


def keep_kernel(ids, offs, lens, hid, w, other, local, s1, s2, s3, hbuf, wbuf, rbuf, obuf, hsem, wsem, rsem, osem, *, q):
    core = ids[2]
    for j in range(8):
        pltpu.make_async_copy(other.at[j], rbuf.at[j], rsem.at[j]).start()
    product = project(ids, offs, lens, hid, w, hbuf, wbuf, hsem, wsem, core * (q // G), q // G)

    def leave(j, verb):
        d, e = j // 2, j % 2
        along = (local, s1, s2, s3)[d].at[e]
        across = local.at[d] if e == 0 else (s1 if d < 2 else s3).at[d % 2]
        for c, target in enumerate((along, across)):

            @pl.when(core == c)
            def _(target=target):
                copy = pltpu.make_async_copy(obuf.at[j], target, osem.at[j])
                copy.start() if verb == "start" else copy.wait()

    for j in range(8):
        value = product(j // 2, j % 2)
        pltpu.make_async_copy(other.at[j], rbuf.at[j], rsem.at[j]).wait()
        obuf[j] = (value + rbuf[j].astype(F32)).astype(BF16)
        leave(j, "start")
    for j in range(8):
        leave(j, "wait")


def call(kernel, prefetched, operands, out_shape, scratch=(), specs=None, out_specs=None, grid=(), flops=0, moved=0, aliases=None):
    n = len(prefetched)
    return pl.pallas_call(
        kernel,
        out_shape=out_shape,
        grid_spec=pltpu.PrefetchScalarGridSpec(
            num_scalar_prefetch=n,
            grid=grid,
            in_specs=specs if specs is not None else [ANY] * len(operands),
            out_specs=out_specs if out_specs is not None else jax.tree.map(lambda _: ANY, out_shape),
            scratch_shapes=list(scratch),
        ),
        compiler_params=PARAMS,
        input_output_aliases=aliases or {},
        cost_estimate=pl.CostEstimate(flops=flops, bytes_accessed=moved, transcendentals=0),
    )(*prefetched, *operands)


def half_scratch(q):
    return [pltpu.VMEM((q, 1024), BF16), pltpu.VMEM((1024, 2048), BF16)]


def half_semaphores():
    return [pltpu.SemaphoreType.DMA((LOCAL, 5)), pltpu.SemaphoreType.DMA]


def send_half(meta, hid, w, q):
    return call(
        functools.partial(send_kernel, q=q),
        meta,
        (hid, w),
        jax.ShapeDtypeStruct((8, q, PAIR), BF16),
        half_scratch(q)
        + [pltpu.VMEM((8, q, PAIR), BF16)]
        + half_semaphores()
        + [pltpu.SemaphoreType.DMA((8,))],
        flops=2 * q * 1024 * 2048,
        moved=2 * (q * 1024 + 1024 * 2048 + q * 2048),
    )


def keep_half(meta, hid, w, other, q):
    return call(
        functools.partial(keep_kernel, q=q),
        meta,
        (hid, w, other),
        [jax.ShapeDtypeStruct((n, q, PAIR), BF16) for n in (4, 2, 2, 2)],
        half_scratch(q)
        + [pltpu.VMEM((8, q, PAIR), BF16)] * 2
        + half_semaphores()
        + [pltpu.SemaphoreType.DMA((8,))] * 2,
        flops=2 * q * 1024 * 2048,
        moved=2 * (q * 1024 + 1024 * 2048 + 2 * q * 2048),
    )


def middle_kernel(ids, local, r1, r2, r3, kept, s1, s2, s3):
    @pl.when(ids[2] == 0)
    def _():
        for e, out in ((0, kept), (1, s1)):
            total = (local[e].astype(F32) + r1[e].astype(F32)) + (r2[e].astype(F32) + r3[e].astype(F32))
            out[...] = total.astype(out.dtype)

    @pl.when(ids[2] == 1)
    def _():
        for d, out in enumerate((kept, s1, s2, s3)):
            arrived = (r1 if d < 2 else r3)[d % 2]
            out[...] = (local[d].astype(F32) + arrived.astype(F32)).astype(out.dtype)


def middle(ids, local, arrived, q):
    n = 2

    def three(i, ids):
        return (0, i, 0)

    def two(i, ids):
        return (i, 0)

    return call(
        middle_kernel,
        (ids,),
        (local, *arrived),
        [jax.ShapeDtypeStruct((q, PAIR), t) for t in (F32, BF16, BF16, BF16)],
        grid=(n,),
        specs=[pl.BlockSpec((a.shape[0], q // n, PAIR), three) for a in (local, *arrived)],
        out_specs=[pl.BlockSpec((q // n, PAIR), two)] * 4,
        moved=2 * PAIR * q * 15,
        flops=PAIR * q * 8,
    )


def rope_rows_kernel(ids, offs, lens, table, out, sem, *, q):
    starts, counts, _ = plan(ids, offs, lens)
    for verb in ("start", "wait"):

        def copy(p, bit, source, target, count, verb=verb):
            base = lax.shift_right_logical(offs[ids[3] * LOCAL + p], 4)
            c = pltpu.make_async_copy(
                table.at[rows(base + source, count)], out.at[rows(target, count)], sem.at[p, bit]
            )
            c.start() if verb == "start" else c.wait()

        ragged(starts, counts, ids[2] * (q // G), q // G, copy)


def rope_rows(meta, table, q):
    return call(
        functools.partial(rope_rows_kernel, q=q),
        meta,
        (table,),
        jax.ShapeDtypeStruct((q, PAIR), F32),
        [pltpu.SemaphoreType.DMA((LOCAL, 5))],
        moved=q * PAIR * 8,
    )


def finish_kernel(ids, offs, lens, kept, r1, r2, r3, turn, out, *, q):
    _, _, total = plan(ids, offs, lens)
    valid = (total - ids[2] * (q // G)) * G

    def put(value):
        row = lax.broadcasted_iota(jnp.int32, (q, HEAD_SIZE), 0)
        key = value[:, :HEAD_SIZE]
        key = key * turn[:, :HEAD_SIZE] + pltpu.roll(key, HEAD_SIZE // 2, 1) * turn[:, HEAD_SIZE:]
        out[:, :HEAD_SIZE] = jnp.where(row < valid, key, 0.0).astype(BF16)
        out[:, HEAD_SIZE:] = value[:, HEAD_SIZE:].astype(BF16)

    @pl.when(ids[2] == 0)
    def _():
        put(kept[...] + r1[...].astype(F32))

    @pl.when(ids[2] == 1)
    def _():
        put((kept[...] + r1[...].astype(F32)) + (r2[...].astype(F32) + r3[...].astype(F32)))


def finish(meta, kept, arrived, turn, q):
    return call(
        functools.partial(finish_kernel, q=q),
        meta,
        (kept, *arrived, turn),
        jax.ShapeDtypeStruct((q, PAIR), BF16),
        specs=[VMEM] * 5,
        out_specs=VMEM,
        moved=q * PAIR * 16,
        flops=q * PAIR * 4,
    )


def stack_heads(tile):
    return [tile[:, h * HEAD_SIZE : (h + 1) * HEAD_SIZE] for h in range(HEADS)]


def scores_of(query, keys):
    return lax.dot_general(query, keys, (((1,), (1,)), ((), ())), preferred_element_type=F32) * SCALE2


def spread(column, n):
    lane = lax.broadcasted_iota(jnp.int32, (n, HEAD_SIZE), 1)
    out = jnp.zeros((n, HEAD_SIZE), F32)
    for h in range(HEADS):
        out = jnp.where(lane == h, column[h * n : (h + 1) * n], out)
    return out


def gather_column(stats):
    return jnp.concatenate([stats[:, h : h + 1] for h in range(HEADS)], axis=0)


def prior_kernel(ids, offs, lens, owner, query, dquery, mine, theirs, *refs, first):
    out, stat, dout, dstat, kbuf, vbuf, sem = refs[-7:]
    step = pl.program_id(0)
    steps = pl.num_programs(0)

    def copies(i):
        slot = lax.rem(i, 2)
        core = ids[2]
        return (
            pltpu.make_async_copy(
                mine.at[first + i],
                kbuf.at[slot, pl.ds(pl.multiple_of(core * PART, PART), PART)],
                sem.at[slot, 0],
            ),
            pltpu.make_async_copy(
                theirs.at[first + i],
                kbuf.at[slot, pl.ds(pl.multiple_of((1 - core) * PART, PART), PART)],
                sem.at[slot, 1],
            ),
        )

    @pl.when(step == 0)
    def _():
        for c in copies(step):
            c.start()
        vbuf[:, HEAD_SIZE:] = jnp.ones((CONTEXT_LENGTH, HEAD_SIZE), BF16)

    @pl.when(step + 1 < steps)
    def _():
        for c in copies(step + 1):
            c.start()

    for c in copies(step):
        c.wait()

    slot = lax.rem(step, 2)
    at = ids[3] * LOCAL + first + step
    offset, length = offs[at], lens[at]
    tiles = lax.div(length - offset + (TILE - 1), TILE)
    vbuf[:, :HEAD_SIZE] = kbuf[slot, :, HEAD_SIZE:]

    for blocks in range(1, 5):

        @pl.when(offset == blocks * 256)
        def _(blocks=blocks):
            @pl.loop(0, tiles)
            def _(t):
                where = pl.ds(pl.multiple_of(t * TILE, TILE), TILE)
                tile = jnp.concatenate(stack_heads(query[0, where, :]) + stack_heads(dquery[0]), axis=0)
                top = mixed = None
                for b in range(blocks):
                    keys = slice(b * 256, (b + 1) * 256)
                    scores = scores_of(tile, kbuf[slot, keys, :HEAD_SIZE])
                    now = jnp.max(scores, axis=1, keepdims=True)
                    now = now if b == 0 else jnp.maximum(now, top)
                    weights = jnp.exp2(scores - now).astype(BF16)
                    more = jnp.dot(weights, vbuf[keys, :], preferred_element_type=F32)
                    mixed = more if b == 0 else mixed * jnp.exp2(top - now) + more
                    top = now
                total = mixed[:, HEAD_SIZE:]
                value = (mixed[:, :HEAD_SIZE] / total).astype(BF16)
                stats = top + jnp.log2(total)
                n = HEADS * TILE
                for h in range(HEADS):
                    lanes = slice(h * HEAD_SIZE, (h + 1) * HEAD_SIZE)
                    out[0, where, lanes] = value[h * TILE : (h + 1) * TILE]
                    dout[0, :, lanes] = value[n + h * DROWS : n + (h + 1) * DROWS]
                stat[0, where, :] = spread(stats[:n], TILE)
                dstat[0] = spread(stats[n:], DROWS)


def prior(meta, owner, query, dquery, mine, theirs, before, first, n):
    def at(i, ids, offs, lens, owner):
        return (first + i, 0, 0)

    def decode_at(i, ids, offs, lens, owner):
        return (owner[ids[3] * LOCAL + first + i], 0, 0)

    shapes = [
        ((LOCAL, FINAL_LENGTH, HEADS * HEAD_SIZE), BF16),
        ((LOCAL, FINAL_LENGTH, HEAD_SIZE), F32),
        ((LOCAL, DROWS, HEADS * HEAD_SIZE), BF16),
        ((LOCAL, DROWS, HEAD_SIZE), F32),
    ]
    return call(
        functools.partial(prior_kernel, first=first),
        (*meta, owner),
        (query, dquery, mine, theirs, *before),
        [jax.ShapeDtypeStruct(*s) for s in shapes],
        [
            pltpu.VMEM((2, CONTEXT_LENGTH, PAIR), BF16),
            pltpu.VMEM((CONTEXT_LENGTH, PAIR), BF16),
            pltpu.SemaphoreType.DMA((2, 2)),
        ],
        grid=(n,),
        specs=[
            pl.BlockSpec((1, FINAL_LENGTH, HEADS * HEAD_SIZE), at),
            pl.BlockSpec((1, DROWS, HEADS * HEAD_SIZE), decode_at),
            ANY,
            ANY,
        ]
        + [ANY] * len(before),
        out_specs=[pl.BlockSpec((1,) + s[1:], at) for s, _ in shapes],
        aliases={8 + i: i for i in range(len(before))},
        flops=n * 3 * 10**9,
        moved=n * 2 * 10**6,
    )


def assemble(ids, pieces, fbuf, sem, q, act):
    for i, core in enumerate((ids[2], 1 - ids[2])):
        target = fbuf.at[pl.ds(pl.multiple_of(core * q, G), q)]
        c = pltpu.make_async_copy(pieces[i], target, sem.at[i])
        c.start() if act == "start" else c.wait()


def load_fresh(ids, pieces, fbuf, sem, q):
    assemble(ids, pieces, fbuf, sem, q, "start")
    fbuf[2 * q :, :] = jnp.zeros((FINAL_LENGTH, PAIR), BF16)
    assemble(ids, pieces, fbuf, sem, q, "wait")


def fresh_kernel(ids, offs, lens, own, other, query, prior_out, prior_stat, out, fbuf, vbuf, sem, *, q):
    p = pl.program_id(0)

    @pl.when(p == 0)
    def _():
        load_fresh(ids, (own, other), fbuf, sem, q)
        vbuf[:, HEAD_SIZE:] = jnp.ones((FINAL_LENGTH, HEAD_SIZE), BF16)

    starts, _, _ = plan(ids, offs, lens)
    start = jnp.int32(0)
    for i in range(1, LOCAL):
        start = jnp.where(p == i, starts[i], start)
    at = ids[3] * LOCAL + p
    count = lens[at] - offs[at]
    where_keys = pl.ds(pl.multiple_of(start * G, G), FINAL_LENGTH)
    vbuf[:, :HEAD_SIZE] = fbuf[where_keys, HEAD_SIZE:]
    n = HEADS * TILE
    for t in range(FINAL_LENGTH // TILE):
        where = slice(t * TILE, (t + 1) * TILE)

        @pl.when(count <= t * TILE)
        def _(where=where):
            out[0, where, :] = jnp.zeros((TILE, HEADS * HEAD_SIZE), BF16)

        @pl.when(count > t * TILE)
        def _(where=where, t=t):
            seen = (t + 1) * TILE
            keys = pl.ds(pl.multiple_of(start * G, G), seen)
            position = lax.bitwise_and(lax.broadcasted_iota(jnp.int32, (n, seen), 0), TILE - 1)
            ahead = lax.broadcasted_iota(jnp.int32, (n, seen), 1) - position
            scores = scores_of(jnp.concatenate(stack_heads(query[0, where, :]), axis=0), fbuf[keys, :HEAD_SIZE])
            scores = jnp.where(ahead <= t * TILE, scores, NEG)
            before = gather_column(prior_stat[0, where, :])
            top = jnp.maximum(jnp.max(scores, axis=1, keepdims=True), before)
            weights = jnp.exp2(scores - top)
            share = jnp.exp2(before - top)
            mixed = jnp.dot(weights.astype(BF16), vbuf[:seen, :], preferred_element_type=F32)
            total = mixed[:, HEAD_SIZE:] + share
            row = lax.broadcasted_iota(jnp.int32, (TILE, HEAD_SIZE), 0)
            keep = row + t * TILE < count
            for h in range(HEADS):
                lanes = slice(h * HEAD_SIZE, (h + 1) * HEAD_SIZE)
                stack = slice(h * TILE, (h + 1) * TILE)
                old = prior_out[0, where, lanes].astype(F32)
                value = (mixed[stack, :HEAD_SIZE] + old * share[stack]) / total[stack]
                out[0, where, lanes] = jnp.where(keep, value, 0.0).astype(BF16)


def fresh(meta, pieces, query, prior_out, prior_stat, q):
    def at(p, ids, offs, lens):
        return (p, 0, 0)

    wide = pl.BlockSpec((1, FINAL_LENGTH, HEADS * HEAD_SIZE), at)
    return call(
        functools.partial(fresh_kernel, q=q),
        meta,
        (*pieces, query, prior_out, prior_stat),
        jax.ShapeDtypeStruct((LOCAL, FINAL_LENGTH, HEADS * HEAD_SIZE), BF16),
        [
            pltpu.VMEM((2 * q + FINAL_LENGTH, PAIR), BF16),
            pltpu.VMEM((FINAL_LENGTH, PAIR), BF16),
            pltpu.SemaphoreType.DMA((2,)),
        ],
        grid=(LOCAL,),
        specs=[ANY, ANY, wide, wide, pl.BlockSpec((1, FINAL_LENGTH, HEAD_SIZE), at)],
        out_specs=wide,
        flops=4 * 10**9,
        moved=10**7,
    )


def decode_kernel(ids, offs, lens, owner, own, other, query, recent, prior_out, prior_stat, out, fbuf, sem, *, q):
    load_fresh(ids, (own, other), fbuf, sem, q)
    starts, _, _ = plan(ids, offs, lens)
    n = HEADS * DROWS
    step = lax.bitwise_and(lax.broadcasted_iota(jnp.int32, (n, DROWS), 0), DROWS - 1)
    later = lax.broadcasted_iota(jnp.int32, (n, DROWS), 1) > step
    column = lax.broadcasted_iota(jnp.int32, (n, FINAL_LENGTH), 1)
    for p in range(LOCAL):
        i = ids[3] * LOCAL + p
        slot = owner[i]
        keys = pl.ds(pl.multiple_of(starts[p] * G, G), FINAL_LENGTH)
        tile = jnp.concatenate(stack_heads(query[slot]), axis=0)
        block = scores_of(tile, fbuf[keys, :HEAD_SIZE])
        block = jnp.where(column < lens[i] - offs[i], block, NEG)
        near = scores_of(tile, recent[slot, :, :HEAD_SIZE])
        near = jnp.where(later, NEG, near)
        before = gather_column(prior_stat[p])
        top = jnp.maximum(jnp.max(block, axis=1, keepdims=True), jnp.max(near, axis=1, keepdims=True))
        top = jnp.maximum(top, before)
        block_weights = jnp.exp2(block - top)
        near_weights = jnp.exp2(near - top)
        share = jnp.exp2(before - top)
        total = (
            jnp.sum(block_weights, axis=1, keepdims=True)
            + jnp.sum(near_weights, axis=1, keepdims=True)
            + share
        )
        mixed = jnp.dot(block_weights.astype(BF16), fbuf[keys, HEAD_SIZE:], preferred_element_type=F32)
        mixed = mixed + jnp.dot(
            near_weights.astype(BF16), recent[slot, :, HEAD_SIZE:], preferred_element_type=F32
        )
        for h in range(HEADS):
            lanes = slice(h * HEAD_SIZE, (h + 1) * HEAD_SIZE)
            stack = slice(h * DROWS, (h + 1) * DROWS)
            value = (mixed[stack] + prior_out[p, :, lanes].astype(F32) * share[stack]) / total[stack]
            out[slot, :, lanes] = value[:STEPS].astype(BF16)


def decode(meta, owner, pieces, query, recent, prior_out, prior_stat, q):
    return call(
        functools.partial(decode_kernel, q=q),
        (*meta, owner),
        (*pieces, query, recent, prior_out, prior_stat),
        jax.ShapeDtypeStruct((LOCAL, STEPS, HEADS * HEAD_SIZE), BF16),
        [pltpu.VMEM((2 * q + FINAL_LENGTH, PAIR), BF16), pltpu.SemaphoreType.DMA((2,))],
        specs=[ANY] * 2 + [VMEM] * 4,
        out_specs=VMEM,
        flops=10**8,
        moved=2 * 10**6,
    )


def take_of_group(value, group):
    return lax.dynamic_index_in_dim(value, group, 1, keepdims=False)


def per_device(
    hidden_rows,
    key_value_weight,
    prefill_query,
    earlier_cache,
    stretch_offset,
    prompt_length,
    decode_owner,
    decode_query,
    decode_kv,
):
    lane = lax.axis_index("tp")
    group = lax.axis_index("grp")
    ids = jnp.stack([lane // 4, lane // 2 % 2, lane % 2, group]).astype(jnp.int32)
    meta = (ids, stretch_offset, prompt_length)
    cap = LOCAL * FINAL_LENGTH
    q = cap // 2
    hid = hidden_rows.reshape(LOCAL * FINAL_LENGTH, -1)
    cache = earlier_cache.reshape(LOCAL, PART, PAIR)

    other_half = lax.ppermute(send_half(meta, hid, key_value_weight, q), "tp", SIBLING)
    other_cache = lax.ppermute(cache, "tp", SIBLING)
    recent = lax.dynamic_slice_in_dim(decode_kv, (lane // 2) * PAIR, PAIR, 2)
    asked = lax.all_gather(jnp.concatenate([decode_query, recent], axis=2), "grp")
    asked = jnp.pad(take_of_group(asked, group), ((0, 0), (0, DROWS - STEPS), (0, 0)))
    dquery = asked[..., : HEADS * HEAD_SIZE]
    recent = asked[..., HEADS * HEAD_SIZE :]
    turn = rope_rows(meta, jnp.asarray(rope_table()), q)

    local, *sent = keep_half(meta, hid, key_value_weight, other_half, q)
    arrived = [lax.ppermute(v, "tp", way) for v, way in zip(sent, FIRST)]
    kept, *sent = middle(ids, local, arrived, q)
    arrived = [lax.ppermute(v, "tp", way) for v, way in zip(sent, SECOND)]
    new = finish(meta, kept, arrived, turn, q)
    pieces = (new, lax.ppermute(new, "tp", SIBLING))

    before = ()
    for i in range(0, LOCAL, 2):
        before = prior(meta, decode_owner, prefill_query, dquery, cache, other_cache, before, i, 2)
    prior_out, prior_stat, prior_dout, prior_dstat = before
    answer = decode(meta, decode_owner, pieces, dquery, recent, prior_dout, prior_dstat, q)
    decode_out = take_of_group(lax.all_gather(answer, "grp"), group)
    prefill_out = fresh(meta, pieces, prefill_query, prior_out, prior_stat, q)
    return (prefill_out, decode_out)


def solution(mesh):
    in_specs = (
        P("grp", None, "tp"),
        P("tp", None),
        P("grp", None, "tp"),
        P("grp", "tp", None, None),
        P(),
        P(),
        P(),
        P("grp", None, "tp"),
        P("grp", None, None),
    )
    out_specs = (P("grp", None, "tp"), P("grp", None, "tp"))
    return jax.shard_map(
        per_device, mesh=mesh, in_specs=in_specs, out_specs=out_specs, check_vma=False
    )
```

```python
import functools
import math

import jax
import jax.numpy as jnp
import numpy as np
from jax import lax
from jax.experimental import pallas as pl
from jax.experimental.pallas import tpu as pltpu
from jax.sharding import PartitionSpec as P

HEAD_SIZE = 128
PAIR = 2 * HEAD_SIZE
LOCAL = 8
FINAL_LENGTH = 256
CONTEXT_LENGTH = 1024
PART = 512
STEPS = 4
HEADS = 8
ROPE_BASE = 500000.0
G = 16
DROWS = 16
TILE = 128
SCALE2 = HEAD_SIZE**-0.5 * math.log2(math.e)
NEG = -1e30
F32 = jnp.float32
BF16 = jnp.bfloat16
ANY = pl.BlockSpec(memory_space=pl.ANY)
VMEM = pl.BlockSpec(memory_space=pltpu.VMEM)
SMALL, LARGE = 20, 60
LOW, HIGH = 2.0**-100, 2.0**100


def pairs(*moves):
    out = []
    for x in range(4):
        for z in range(2):
            for core in range(2):
                if moves[core] is None:
                    continue
                dx, dz, dc = moves[core]
                out.append((x * 4 + z * 2 + core, (x + dx) % 4 * 4 + (z + dz) % 2 * 2 + (core + dc) % 2))
    return out


SIBLING = pairs((0, 0, 1), (0, 0, 1))
FIRST = [pairs((1, 0, 0), (0, 1, 0)), pairs((2, 0, 0), None), pairs((3, 0, 0), (0, 1, 0))]
SECOND = [pairs((0, 1, 0), (1, 0, 0)), pairs(None, (2, 0, 0)), pairs(None, (3, 0, 0))]


def rope_table():
    half = HEAD_SIZE // 2
    freq = ROPE_BASE ** (np.arange(half, dtype=np.float64) * (-2.0 / HEAD_SIZE))
    angle = np.arange(CONTEXT_LENGTH + FINAL_LENGTH, dtype=np.float64)[:, None] * freq
    cosine, sine = np.cos(angle), np.sin(angle)
    return np.concatenate([cosine, cosine, -sine, sine], axis=1).astype(np.float32)


def plan(ids, offs, lens):
    starts, counts, at = [], [], jnp.int32(0)
    for p in range(LOCAL):
        i = ids[3] * LOCAL + p
        count = lax.shift_right_logical(lens[i] - offs[i] + (G - 1), 4)
        starts.append(at)
        counts.append(count)
        at = at + count
    return starts, counts, at


def ragged(starts, counts, first_block, blocks, copy):
    for p in range(LOCAL):
        low = jnp.maximum(starts[p], first_block)
        high = jnp.minimum(starts[p] + counts[p], first_block + blocks)
        n = jnp.maximum(high - low, 0)
        for bit in range(4, -1, -1):
            done = lax.shift_left(lax.shift_right_logical(n, bit + 1), bit + 1)

            @pl.when(lax.bitwise_and(n, 1 << bit) != 0)
            def _(p=p, bit=bit, low=low, done=done):
                copy(p, bit, low + done - starts[p], low + done - first_block, 1 << bit)


def rows(block, count):
    return pl.ds(pl.multiple_of(block * G, G), count * G)


def project(ids, offs, lens, hid, w, hbuf, wbuf, hsem, wsem, first_block, blocks):
    starts, counts, total = plan(ids, offs, lens)

    def hidden_copy(p, bit, source, target, count):
        return pltpu.make_async_copy(
            hid.at[rows(p * (FINAL_LENGTH // G) + source, count)],
            hbuf.at[rows(target, count)],
            hsem.at[p, bit],
        )

    def weight_copy(d):
        first = lax.rem(ids[0] + d, 4) * (2 * PAIR)
        return pltpu.make_async_copy(
            w.at[:, pl.ds(pl.multiple_of(first, 2 * PAIR), 2 * PAIR)], wbuf.at[d], wsem.at[d]
        )

    weight_copy(0).start()
    ragged(starts, counts, first_block, blocks, lambda *a: hidden_copy(*a).start())
    for d in range(1, 4):
        weight_copy(d).start()

    @pl.loop(jnp.clip(total - first_block, 0, blocks), blocks)
    def _(b):
        hbuf[rows(b, 1), :] = jnp.zeros((G, hbuf.shape[1]), BF16)

    ragged(starts, counts, first_block, blocks, lambda *a: hidden_copy(*a).wait())

    def product(d, e, where):
        if e == 0 and where.start == 0:
            weight_copy(d).wait()
        columns = pl.ds(pl.multiple_of(lax.rem(ids[1] + e, 2) * PAIR, PAIR), PAIR)
        return jnp.dot(hbuf[where, :], wbuf[d, :, columns], preferred_element_type=F32)

    return product


def row_tiles(q):
    n = next(n for n in (256, 192, 160, 128, 64) if q % n == 0)
    return [slice(r, r + n) for r in range(0, q, n)]


def send_kernel(ids, offs, lens, hid, w, out, hbuf, wbuf, obuf, hsem, wsem, osem, *, q):
    product = project(ids, offs, lens, hid, w, hbuf, wbuf, hsem, wsem, (1 - ids[2]) * (q // G), q // G)
    for j in range(8):
        for where in row_tiles(q):
            obuf[j, where, :] = product(j // 2, j % 2, where).astype(BF16)
        pltpu.make_async_copy(obuf.at[j], out.at[j], osem.at[j]).start()
    for j in range(8):
        pltpu.make_async_copy(obuf.at[j], out.at[j], osem.at[j]).wait()


def keep_kernel(ids, offs, lens, hid, w, other, local, s1, s2, s3, hbuf, wbuf, rbuf, obuf, hsem, wsem, rsem, osem, *, q):
    core = ids[2]
    product = project(ids, offs, lens, hid, w, hbuf, wbuf, hsem, wsem, core * (q // G), q // G)
    for j in range(8):
        pltpu.make_async_copy(other.at[j], rbuf.at[j], rsem.at[j]).start()

    def leave(j, verb):
        d, e = j // 2, j % 2
        along = (local, s1, s2, s3)[d].at[e]
        across = local.at[d] if e == 0 else (s1 if d < 2 else s3).at[d % 2]
        for c, target in enumerate((along, across)):

            @pl.when(core == c)
            def _(target=target):
                copy = pltpu.make_async_copy(obuf.at[j], target, osem.at[j])
                copy.start() if verb == "start" else copy.wait()

    for j in range(8):
        for where in row_tiles(q):
            value = product(j // 2, j % 2, where)
            if where.start == 0:
                pltpu.make_async_copy(other.at[j], rbuf.at[j], rsem.at[j]).wait()
            obuf[j, where, :] = (value + rbuf[j, where, :].astype(F32)).astype(BF16)
        leave(j, "start")
    for j in range(8):
        leave(j, "wait")


def call(kernel, prefetched, operands, out_shape, scratch=(), specs=None, out_specs=None, grid=(), flops=0, moved=0, aliases=None, room=None):
    n = len(prefetched)
    return pl.pallas_call(
        kernel,
        out_shape=out_shape,
        grid_spec=pltpu.PrefetchScalarGridSpec(
            num_scalar_prefetch=n,
            grid=grid,
            in_specs=specs if specs is not None else [ANY] * len(operands),
            out_specs=out_specs if out_specs is not None else jax.tree.map(lambda _: ANY, out_shape),
            scratch_shapes=list(scratch),
        ),
        compiler_params=pltpu.CompilerParams(vmem_limit_bytes=(room or SMALL) * 2**20),
        input_output_aliases=aliases or {},
        cost_estimate=pl.CostEstimate(flops=flops, bytes_accessed=moved, transcendentals=0),
    )(*prefetched, *operands)


def half_scratch(q):
    return [pltpu.VMEM((q, 1024), BF16), pltpu.VMEM((4, 1024, 2 * PAIR), BF16)]


def half_semaphores():
    return [pltpu.SemaphoreType.DMA((LOCAL, 5)), pltpu.SemaphoreType.DMA((4,))]


def send_half(meta, hid, w, q):
    return call(
        functools.partial(send_kernel, q=q),
        meta,
        (hid, w),
        jax.ShapeDtypeStruct((8, q, PAIR), BF16),
        half_scratch(q)
        + [pltpu.VMEM((8, q, PAIR), BF16)]
        + half_semaphores()
        + [pltpu.SemaphoreType.DMA((8,))],
        flops=2 * q * 1024 * 2048,
        moved=2 * (q * 1024 + 1024 * 2048 + q * 2048),
        room=LARGE,
    )


def keep_half(meta, hid, w, other, q):
    return call(
        functools.partial(keep_kernel, q=q),
        meta,
        (hid, w, other),
        [jax.ShapeDtypeStruct((n, q, PAIR), BF16) for n in (4, 2, 2, 2)],
        half_scratch(q)
        + [pltpu.VMEM((8, q, PAIR), BF16)] * 2
        + half_semaphores()
        + [pltpu.SemaphoreType.DMA((8,))] * 2,
        flops=2 * q * 1024 * 2048,
        moved=2 * (q * 1024 + 1024 * 2048 + 2 * q * 2048),
        room=LARGE,
    )


def middle_kernel(ids, local, r1, r2, r3, kept, s1, s2, s3):
    @pl.when(ids[2] == 0)
    def _():
        for e, out in ((0, kept), (1, s1)):
            total = (local[e].astype(F32) + r1[e].astype(F32)) + (r2[e].astype(F32) + r3[e].astype(F32))
            out[...] = total.astype(out.dtype)

    @pl.when(ids[2] == 1)
    def _():
        for d, out in enumerate((kept, s1, s2, s3)):
            arrived = (r1 if d < 2 else r3)[d % 2]
            out[...] = (local[d].astype(F32) + arrived.astype(F32)).astype(out.dtype)


def middle(ids, local, arrived, q):
    n = 2

    def three(i, ids):
        return (0, i, 0)

    def two(i, ids):
        return (i, 0)

    return call(
        middle_kernel,
        (ids,),
        (local, *arrived),
        [jax.ShapeDtypeStruct((q, PAIR), t) for t in (F32, BF16, BF16, BF16)],
        grid=(n,),
        specs=[pl.BlockSpec((a.shape[0], q // n, PAIR), three) for a in (local, *arrived)],
        out_specs=[pl.BlockSpec((q // n, PAIR), two)] * 4,
        moved=2 * PAIR * q * 15,
        flops=PAIR * q * 8,
    )


def rope_rows_kernel(ids, offs, lens, table, out, sem, *, q):
    starts, counts, _ = plan(ids, offs, lens)
    for verb in ("start", "wait"):

        def copy(p, bit, source, target, count, verb=verb):
            base = lax.shift_right_logical(offs[ids[3] * LOCAL + p], 4)
            c = pltpu.make_async_copy(
                table.at[rows(base + source, count)], out.at[rows(target, count)], sem.at[p, bit]
            )
            c.start() if verb == "start" else c.wait()

        ragged(starts, counts, ids[2] * (q // G), q // G, copy)


def rope_rows(meta, table, q):
    return call(
        functools.partial(rope_rows_kernel, q=q),
        meta,
        (table,),
        jax.ShapeDtypeStruct((q, PAIR), F32),
        [pltpu.SemaphoreType.DMA((LOCAL, 5))],
        moved=q * PAIR * 8,
    )


def finish_kernel(ids, offs, lens, kept, r1, r2, r3, turn, out, *, q):
    _, _, total = plan(ids, offs, lens)
    valid = (total - ids[2] * (q // G)) * G

    def put(value):
        row = lax.broadcasted_iota(jnp.int32, (q, HEAD_SIZE), 0)
        key = value[:, :HEAD_SIZE]
        key = key * turn[:, :HEAD_SIZE] + pltpu.roll(key, HEAD_SIZE // 2, 1) * turn[:, HEAD_SIZE:]
        out[:, :HEAD_SIZE] = jnp.where(row < valid, key, 0.0).astype(BF16)
        out[:, HEAD_SIZE:] = value[:, HEAD_SIZE:].astype(BF16)

    @pl.when(ids[2] == 0)
    def _():
        put(kept[...] + r1[...].astype(F32))

    @pl.when(ids[2] == 1)
    def _():
        put((kept[...] + r1[...].astype(F32)) + (r2[...].astype(F32) + r3[...].astype(F32)))


def finish(meta, kept, arrived, turn, q):
    return call(
        functools.partial(finish_kernel, q=q),
        meta,
        (kept, *arrived, turn),
        jax.ShapeDtypeStruct((q, PAIR), BF16),
        specs=[VMEM] * 5,
        out_specs=VMEM,
        moved=q * PAIR * 16,
        flops=q * PAIR * 4,
    )


def stack_heads(tile):
    return [tile[:, h * HEAD_SIZE : (h + 1) * HEAD_SIZE] for h in range(HEADS)]


def scores_of(query, keys):
    return lax.dot_general(query, keys, (((1,), (1,)), ((), ())), preferred_element_type=F32) * SCALE2


def spread(column, n):
    lane = lax.broadcasted_iota(jnp.int32, (n, HEAD_SIZE), 1)
    out = jnp.zeros((n, HEAD_SIZE), F32)
    for h in range(HEADS):
        out = jnp.where(lane == h, column[h * n : (h + 1) * n], out)
    return out


def smallest(value):
    return jnp.min(value.reshape(-1, 8, HEAD_SIZE), axis=0)


def largest(value):
    return jnp.max(value.reshape(-1, 8, HEAD_SIZE), axis=0)


def gather_column(stats):
    return jnp.concatenate([stats[:, h : h + 1] for h in range(HEADS)], axis=0)


def prior_kernel(ids, offs, lens, owner, query, dquery, mine, theirs, *refs, first):
    out, stat, dout, dstat, kbuf, vbuf, *bounds, sem = refs[-9:]
    step = pl.program_id(0)
    steps = pl.num_programs(0)

    def copies(i):
        slot = lax.rem(i, 2)
        core = ids[2]
        return (
            pltpu.make_async_copy(
                mine.at[first + i],
                kbuf.at[slot, pl.ds(pl.multiple_of(core * PART, PART), PART)],
                sem.at[slot, 0],
            ),
            pltpu.make_async_copy(
                theirs.at[first + i],
                kbuf.at[slot, pl.ds(pl.multiple_of((1 - core) * PART, PART), PART)],
                sem.at[slot, 1],
            ),
        )

    @pl.when(step == 0)
    def _():
        for c in copies(step):
            c.start()
        vbuf[:, HEAD_SIZE:] = jnp.ones((CONTEXT_LENGTH, HEAD_SIZE), BF16)

    @pl.when(step + 1 < steps)
    def _():
        for c in copies(step + 1):
            c.start()

    for c in copies(step):
        c.wait()

    slot = lax.rem(step, 2)
    at = ids[3] * LOCAL + first + step
    offset, length = offs[at], lens[at]
    tiles = lax.div(length - offset + (TILE - 1), TILE)
    vbuf[:, :HEAD_SIZE] = kbuf[slot, :, HEAD_SIZE:]

    least, most = bounds
    least[...] = jnp.full(least.shape, 1.0, F32)
    most[...] = jnp.full(most.shape, 1.0, F32)

    def put(where, value, stats, n):
        for h in range(HEADS):
            out[0, where, h * HEAD_SIZE : (h + 1) * HEAD_SIZE] = value[h * n : (h + 1) * n]
        stat[0, where, :] = spread(stats, n)

    def put_decode(value, stats):
        for h in range(HEADS):
            dout[0, :, h * HEAD_SIZE : (h + 1) * HEAD_SIZE] = value[h * DROWS : (h + 1) * DROWS]
        dstat[0] = spread(stats, DROWS)

    for blocks in range(1, 5):

        @pl.when(offset == blocks * 256)
        def _(keys=blocks * 256):
            @pl.loop(0, tiles)
            def _(t):
                where = pl.ds(pl.multiple_of(t * TILE, TILE), TILE)
                tile = jnp.concatenate(stack_heads(query[0, where, :]) + stack_heads(dquery[0]), axis=0)
                weights = jnp.exp2(scores_of(tile, kbuf[slot, :keys, :HEAD_SIZE])).astype(BF16)
                mixed = jnp.dot(weights, vbuf[:keys, :], preferred_element_type=F32)
                total = mixed[:, HEAD_SIZE:]
                least[...] = jnp.minimum(least[...], smallest(total))
                most[...] = jnp.maximum(most[...], largest(total))
                value = (mixed[:, :HEAD_SIZE] * (1.0 / total)).astype(BF16)
                stats = jnp.log2(total)
                n = HEADS * TILE
                put(where, value[:n], stats[:n], TILE)
                put_decode(value[n:], stats[n:])

    fine = jnp.logical_and(jnp.min(least[...]) >= LOW, jnp.max(most[...]) <= HIGH)

    @pl.when(jnp.logical_not(fine))
    def _():
        def exact(tile):
            def block(b, carry):
                top, mixed = carry
                keys = pl.ds(pl.multiple_of(b * 256, 256), 256)
                scores = scores_of(tile, kbuf[slot, keys, :HEAD_SIZE])
                now = jnp.maximum(jnp.max(scores, axis=1, keepdims=True), top)
                weights = jnp.exp2(scores - now).astype(BF16)
                more = jnp.dot(weights, vbuf[keys, :], preferred_element_type=F32)
                return now, mixed * jnp.exp2(top - now) + more

            n = tile.shape[0]
            first = (jnp.full((n, 1), NEG, F32), jnp.zeros((n, PAIR), F32))
            top, mixed = lax.fori_loop(0, lax.shift_right_logical(offset, 8), block, first)
            total = mixed[:, HEAD_SIZE:]
            return (mixed[:, :HEAD_SIZE] / total).astype(BF16), top + jnp.log2(total)

        @pl.loop(0, FINAL_LENGTH // 32)
        def _(t):
            where = pl.ds(pl.multiple_of(t * 32, 32), 32)
            put(where, *exact(jnp.concatenate(stack_heads(query[0, where, :]), axis=0)), 32)

        put_decode(*exact(jnp.concatenate(stack_heads(dquery[0]), axis=0)))


def prior(meta, owner, query, dquery, mine, theirs, before, first, n):
    def at(i, ids, offs, lens, owner):
        return (first + i, 0, 0)

    def decode_at(i, ids, offs, lens, owner):
        return (owner[ids[3] * LOCAL + first + i], 0, 0)

    shapes = [
        ((LOCAL, FINAL_LENGTH, HEADS * HEAD_SIZE), BF16),
        ((LOCAL, FINAL_LENGTH, HEAD_SIZE), F32),
        ((LOCAL, DROWS, HEADS * HEAD_SIZE), BF16),
        ((LOCAL, DROWS, HEAD_SIZE), F32),
    ]
    return call(
        functools.partial(prior_kernel, first=first),
        (*meta, owner),
        (query, dquery, mine, theirs, *before),
        [jax.ShapeDtypeStruct(*s) for s in shapes],
        [
            pltpu.VMEM((2, CONTEXT_LENGTH, PAIR), BF16),
            pltpu.VMEM((CONTEXT_LENGTH, PAIR), BF16),
            pltpu.VMEM((8, HEAD_SIZE), F32),
            pltpu.VMEM((8, HEAD_SIZE), F32),
            pltpu.SemaphoreType.DMA((2, 2)),
        ],
        grid=(n,),
        specs=[
            pl.BlockSpec((1, FINAL_LENGTH, HEADS * HEAD_SIZE), at),
            pl.BlockSpec((1, DROWS, HEADS * HEAD_SIZE), decode_at),
            ANY,
            ANY,
        ]
        + [ANY] * len(before),
        out_specs=[pl.BlockSpec((1,) + s[1:], at) for s, _ in shapes],
        aliases={8 + i: i for i in range(len(before))},
        flops=n * 3 * 10**9,
        moved=n * 2 * 10**6,
    )


def assemble(ids, pieces, fbuf, sem, q, act):
    for i, core in enumerate((ids[2], 1 - ids[2])):
        target = fbuf.at[pl.ds(pl.multiple_of(core * q, G), q)]
        c = pltpu.make_async_copy(pieces[i], target, sem.at[i])
        c.start() if act == "start" else c.wait()


def load_fresh(ids, pieces, fbuf, sem, q):
    assemble(ids, pieces, fbuf, sem, q, "start")
    fbuf[2 * q :, :] = jnp.zeros((FINAL_LENGTH, PAIR), BF16)
    assemble(ids, pieces, fbuf, sem, q, "wait")


def fresh_kernel(ids, offs, lens, own, other, query, prior_out, prior_stat, out, fbuf, vbuf, *refs, q):
    *bounds, sem = refs
    p = pl.program_id(0)

    @pl.when(p == 0)
    def _():
        load_fresh(ids, (own, other), fbuf, sem, q)
        vbuf[:, HEAD_SIZE:] = jnp.ones((FINAL_LENGTH, HEAD_SIZE), BF16)

    starts, _, _ = plan(ids, offs, lens)
    start = jnp.int32(0)
    for i in range(1, LOCAL):
        start = jnp.where(p == i, starts[i], start)
    at = ids[3] * LOCAL + p
    count = lens[at] - offs[at]
    where_keys = pl.ds(pl.multiple_of(start * G, G), FINAL_LENGTH)
    vbuf[:, :HEAD_SIZE] = fbuf[where_keys, HEAD_SIZE:]
    n = HEADS * TILE
    least, most = bounds
    least[...] = jnp.full(least.shape, 1.0, F32)
    most[...] = jnp.full(most.shape, 1.0, F32)

    for t in range(FINAL_LENGTH // TILE):
        where = slice(t * TILE, (t + 1) * TILE)

        @pl.when(count <= t * TILE)
        def _(where=where):
            out[0, where, :] = jnp.zeros((TILE, HEADS * HEAD_SIZE), BF16)

        @pl.when(count > t * TILE)
        def _(where=where, t=t):
            seen = (t + 1) * TILE
            keys = pl.ds(pl.multiple_of(start * G, G), seen)
            row = lax.broadcasted_iota(jnp.int32, (TILE, seen), 0) + t * TILE
            allowed = (lax.broadcasted_iota(jnp.int32, (TILE, seen), 1) <= row).astype(F32)
            scores = scores_of(jnp.concatenate(stack_heads(query[0, where, :]), axis=0), fbuf[keys, :HEAD_SIZE])
            weights = jnp.concatenate(
                [
                    (jnp.exp2(scores[h * TILE : (h + 1) * TILE]) * allowed).astype(BF16)
                    for h in range(HEADS)
                ],
                axis=0,
            )
            mixed = jnp.dot(weights, vbuf[:seen, :], preferred_element_type=F32)
            keep = lax.broadcasted_iota(jnp.int32, (TILE, HEAD_SIZE), 0) + t * TILE < count
            before = jnp.exp2(prior_stat[0, where, :])
            low, high = least[...], most[...]
            for h in range(HEADS):
                lanes = slice(h * HEAD_SIZE, (h + 1) * HEAD_SIZE)
                stack = slice(h * TILE, (h + 1) * TILE)
                share = before[:, h : h + 1]
                total = mixed[stack, HEAD_SIZE:] + share
                low, high = jnp.minimum(low, smallest(total)), jnp.maximum(high, largest(total))
                old = prior_out[0, where, lanes].astype(F32)
                value = (mixed[stack, :HEAD_SIZE] + old * share) * (1.0 / total)
                out[0, where, lanes] = jnp.where(keep, value, 0.0).astype(BF16)
            least[...], most[...] = low, high

    fine = jnp.logical_and(jnp.min(least[...]) >= LOW, jnp.max(most[...]) <= HIGH)

    @pl.when(jnp.logical_not(fine))
    def _():
        some = 32
        keys = pl.ds(pl.multiple_of(start * G, G), FINAL_LENGTH)
        n = HEADS * some

        @pl.loop(0, FINAL_LENGTH // some)
        def _(t):
            where = pl.ds(pl.multiple_of(t * some, some), some)
            position = lax.bitwise_and(lax.broadcasted_iota(jnp.int32, (n, FINAL_LENGTH), 0), some - 1)
            ahead = lax.broadcasted_iota(jnp.int32, (n, FINAL_LENGTH), 1) - position
            scores = scores_of(jnp.concatenate(stack_heads(query[0, where, :]), axis=0), fbuf[keys, :HEAD_SIZE])
            scores = jnp.where(ahead <= t * some, scores, NEG)
            before = gather_column(prior_stat[0, where, :])
            top = jnp.maximum(jnp.max(scores, axis=1, keepdims=True), before)
            weights = jnp.exp2(scores - top).astype(BF16)
            share = jnp.exp2(before - top)
            mixed = jnp.dot(weights, vbuf[...], preferred_element_type=F32)
            total = mixed[:, HEAD_SIZE:] + share
            keep = lax.broadcasted_iota(jnp.int32, (some, HEAD_SIZE), 0) + t * some < count
            for h in range(HEADS):
                lanes = slice(h * HEAD_SIZE, (h + 1) * HEAD_SIZE)
                stack = slice(h * some, (h + 1) * some)
                old = prior_out[0, where, lanes].astype(F32)
                value = (mixed[stack, :HEAD_SIZE] + old * share[stack]) / total[stack]
                out[0, where, lanes] = jnp.where(keep, value, 0.0).astype(BF16)


def fresh(meta, pieces, query, prior_out, prior_stat, q):
    def at(p, ids, offs, lens):
        return (p, 0, 0)

    wide = pl.BlockSpec((1, FINAL_LENGTH, HEADS * HEAD_SIZE), at)
    return call(
        functools.partial(fresh_kernel, q=q),
        meta,
        (*pieces, query, prior_out, prior_stat),
        jax.ShapeDtypeStruct((LOCAL, FINAL_LENGTH, HEADS * HEAD_SIZE), BF16),
        [
            pltpu.VMEM((2 * q + FINAL_LENGTH, PAIR), BF16),
            pltpu.VMEM((FINAL_LENGTH, PAIR), BF16),
            pltpu.VMEM((8, HEAD_SIZE), F32),
            pltpu.VMEM((8, HEAD_SIZE), F32),
            pltpu.SemaphoreType.DMA((2,)),
        ],
        grid=(LOCAL,),
        specs=[ANY, ANY, wide, wide, pl.BlockSpec((1, FINAL_LENGTH, HEAD_SIZE), at)],
        out_specs=wide,
        flops=4 * 10**9,
        moved=10**7,
    )


def decode_kernel(ids, offs, lens, owner, own, other, query, recent, prior_out, prior_stat, out, fbuf, sem, *, q):
    load_fresh(ids, (own, other), fbuf, sem, q)
    starts, _, _ = plan(ids, offs, lens)
    n = HEADS * DROWS
    step = lax.bitwise_and(lax.broadcasted_iota(jnp.int32, (n, DROWS), 0), DROWS - 1)
    later = lax.broadcasted_iota(jnp.int32, (n, DROWS), 1) > step
    column = lax.broadcasted_iota(jnp.int32, (n, FINAL_LENGTH), 1)
    for p in range(LOCAL):
        i = ids[3] * LOCAL + p
        slot = owner[i]
        keys = pl.ds(pl.multiple_of(starts[p] * G, G), FINAL_LENGTH)
        tile = jnp.concatenate(stack_heads(query[slot]), axis=0)
        block = scores_of(tile, fbuf[keys, :HEAD_SIZE])
        block = jnp.where(column < lens[i] - offs[i], block, NEG)
        near = scores_of(tile, recent[slot, :, :HEAD_SIZE])
        near = jnp.where(later, NEG, near)
        before = gather_column(prior_stat[p])
        top = jnp.maximum(jnp.max(block, axis=1, keepdims=True), jnp.max(near, axis=1, keepdims=True))
        top = jnp.maximum(top, before)
        block_weights = jnp.exp2(block - top)
        near_weights = jnp.exp2(near - top)
        share = jnp.exp2(before - top)
        total = (
            jnp.sum(block_weights, axis=1, keepdims=True)
            + jnp.sum(near_weights, axis=1, keepdims=True)
            + share
        )
        mixed = jnp.dot(block_weights.astype(BF16), fbuf[keys, HEAD_SIZE:], preferred_element_type=F32)
        mixed = mixed + jnp.dot(
            near_weights.astype(BF16), recent[slot, :, HEAD_SIZE:], preferred_element_type=F32
        )
        for h in range(HEADS):
            lanes = slice(h * HEAD_SIZE, (h + 1) * HEAD_SIZE)
            stack = slice(h * DROWS, (h + 1) * DROWS)
            value = (mixed[stack] + prior_out[p, :, lanes].astype(F32) * share[stack]) / total[stack]
            out[slot, :, lanes] = value[:STEPS].astype(BF16)


def decode(meta, owner, pieces, query, recent, prior_out, prior_stat, q):
    return call(
        functools.partial(decode_kernel, q=q),
        (*meta, owner),
        (*pieces, query, recent, prior_out, prior_stat),
        jax.ShapeDtypeStruct((LOCAL, STEPS, HEADS * HEAD_SIZE), BF16),
        [pltpu.VMEM((2 * q + FINAL_LENGTH, PAIR), BF16), pltpu.SemaphoreType.DMA((2,))],
        specs=[ANY] * 2 + [VMEM] * 4,
        out_specs=VMEM,
        flops=10**8,
        moved=2 * 10**6,
    )


def exchange(value):
    return lax.all_to_all(value, "grp", split_axis=0, concat_axis=0, tiled=True)


def per_device(
    hidden_rows,
    key_value_weight,
    prefill_query,
    earlier_cache,
    stretch_offset,
    prompt_length,
    decode_owner,
    decode_query,
    decode_kv,
):
    lane = lax.axis_index("tp")
    group = lax.axis_index("grp")
    ids = jnp.stack([lane // 4, lane // 2 % 2, lane % 2, group]).astype(jnp.int32)
    meta = (ids, stretch_offset, prompt_length)
    cap = LOCAL * FINAL_LENGTH
    q = cap // 2
    hid = hidden_rows.reshape(LOCAL * FINAL_LENGTH, -1)
    cache = earlier_cache.reshape(LOCAL, PART, PAIR)

    other_half = lax.ppermute(send_half(meta, hid, key_value_weight, q), "tp", SIBLING)
    other_cache = lax.ppermute(cache, "tp", SIBLING)
    recent = lax.dynamic_slice_in_dim(decode_kv, (lane // 2) * PAIR, PAIR, 2)
    asked = exchange(jnp.concatenate([decode_query, recent], axis=2))
    asked = jnp.pad(asked, ((0, 0), (0, DROWS - STEPS), (0, 0)))
    dquery = asked[..., : HEADS * HEAD_SIZE]
    recent = asked[..., HEADS * HEAD_SIZE :]
    turn = rope_rows(meta, jnp.asarray(rope_table()), q)

    local, *sent = keep_half(meta, hid, key_value_weight, other_half, q)
    arrived = [lax.ppermute(v, "tp", way) for v, way in zip(sent, FIRST)]
    kept, *sent = middle(ids, local, arrived, q)
    arrived = [lax.ppermute(v, "tp", way) for v, way in zip(sent, SECOND)]
    new = finish(meta, kept, arrived, turn, q)
    pieces = (new, lax.ppermute(new, "tp", SIBLING))

    before = ()
    for i in range(0, LOCAL, 2):
        before = prior(meta, decode_owner, prefill_query, dquery, cache, other_cache, before, i, 2)
    prior_out, prior_stat, prior_dout, prior_dstat = before
    answer = decode(meta, decode_owner, pieces, dquery, recent, prior_dout, prior_dstat, q)
    decode_out = exchange(answer)
    prefill_out = fresh(meta, pieces, prefill_query, prior_out, prior_stat, q)
    return (prefill_out, decode_out)


def solution(mesh):
    in_specs = (
        P("grp", None, "tp"),
        P("tp", None),
        P("grp", None, "tp"),
        P("grp", "tp", None, None),
        P(),
        P(),
        P(),
        P("grp", None, "tp"),
        P("grp", None, None),
    )
    out_specs = (P("grp", None, "tp"), P("grp", None, "tp"))
    return jax.shard_map(
        per_device, mesh=mesh, in_specs=in_specs, out_specs=out_specs, check_vma=False
    )
```

```python
import functools
import math

import jax
import jax.numpy as jnp
import numpy as np
from jax import lax
from jax.experimental import pallas as pl
from jax.experimental.pallas import tpu as pltpu
from jax.sharding import PartitionSpec as P

HEAD_SIZE = 128
PAIR = 2 * HEAD_SIZE
LOCAL = 8
FINAL_LENGTH = 256
CONTEXT_LENGTH = 1024
PART = 512
STEPS = 4
HEADS = 8
ROPE_BASE = 500000.0
G = 16
DROWS = 16
TILE = 128
SCALE2 = HEAD_SIZE**-0.5 * math.log2(math.e)
NEG = -1e30
F32 = jnp.float32
BF16 = jnp.bfloat16
ANY = pl.BlockSpec(memory_space=pl.ANY)
VMEM = pl.BlockSpec(memory_space=pltpu.VMEM)
HBM = pl.BlockSpec(memory_space=pltpu.HBM)
ROOM = pltpu.CompilerParams(vmem_limit_bytes=22 * 2**20)
CAPS = (1280, 1408, 1536, 1792, 2048)
LOW, HIGH = 2.0**-100, 2.0**100


def pairs(*moves):
    out = []
    for x in range(4):
        for z in range(2):
            for core in range(2):
                if moves[core] is None:
                    continue
                dx, dz, dc = moves[core]
                out.append((x * 4 + z * 2 + core, (x + dx) % 4 * 4 + (z + dz) % 2 * 2 + (core + dc) % 2))
    return out


SIBLING = pairs((0, 0, 1), (0, 0, 1))
FIRST = [pairs((1, 0, 0), (0, 1, 0)), pairs((2, 0, 0), None), pairs((3, 0, 0), (0, 1, 0))]
SECOND = [pairs((0, 1, 0), (1, 0, 0)), pairs(None, (2, 0, 0)), pairs(None, (3, 0, 0))]


def rope_table():
    half = HEAD_SIZE // 2
    freq = ROPE_BASE ** (np.arange(half, dtype=np.float64) * (-2.0 / HEAD_SIZE))
    angle = np.arange(CONTEXT_LENGTH + FINAL_LENGTH, dtype=np.float64)[:, None] * freq
    cosine, sine = np.cos(angle), np.sin(angle)
    return np.concatenate([cosine, cosine, -sine, sine], axis=1).astype(np.float32)


def plan(ids, offs, lens):
    starts, counts, at = [], [], jnp.int32(0)
    for p in range(LOCAL):
        i = ids[3] * LOCAL + p
        count = lax.shift_right_logical(lens[i] - offs[i] + (G - 1), 4)
        starts.append(at)
        counts.append(count)
        at = at + count
    return starts, counts, at


def ragged(starts, counts, first_block, blocks, copy):
    for p in range(LOCAL):
        low = jnp.maximum(starts[p], first_block)
        high = jnp.minimum(starts[p] + counts[p], first_block + blocks)
        n = jnp.maximum(high - low, 0)
        for bit in range(4, -1, -1):
            done = lax.shift_left(lax.shift_right_logical(n, bit + 1), bit + 1)

            @pl.when(lax.bitwise_and(n, 1 << bit) != 0)
            def _(p=p, bit=bit, low=low, done=done):
                copy(p, bit, low + done - starts[p], low + done - first_block, 1 << bit)


def rows(block, count):
    return pl.ds(pl.multiple_of(block * G, G), count * G)


def project(ids, offs, lens, hid, w, hbuf, wbuf, hsem, wsem, first_block, blocks):
    starts, counts, total = plan(ids, offs, lens)

    def hidden_copy(p, bit, source, target, count):
        return pltpu.make_async_copy(
            hid.at[rows(p * (FINAL_LENGTH // G) + source, count)],
            hbuf.at[rows(target, count)],
            hsem.at[p, bit],
        )

    def weight_copy(d):
        first = lax.rem(ids[0] + d, 4) * (2 * PAIR)
        return pltpu.make_async_copy(
            w.at[:, pl.ds(pl.multiple_of(first, 2 * PAIR), 2 * PAIR)], wbuf.at[d], wsem.at[d]
        )

    weight_copy(0).start()
    ragged(starts, counts, first_block, blocks, lambda *a: hidden_copy(*a).start())
    for d in range(1, 4):
        weight_copy(d).start()

    @pl.loop(jnp.clip(total - first_block, 0, blocks), blocks)
    def _(b):
        hbuf[rows(b, 1), :] = jnp.zeros((G, hbuf.shape[1]), BF16)

    ragged(starts, counts, first_block, blocks, lambda *a: hidden_copy(*a).wait())

    def product(d, e, where):
        if e == 0 and where.start == 0:
            weight_copy(d).wait()
        columns = pl.ds(pl.multiple_of(lax.rem(ids[1] + e, 2) * PAIR, PAIR), PAIR)
        return jnp.dot(hbuf[where, :], wbuf[d, :, columns], preferred_element_type=F32)

    return product


def row_tiles(q):
    n = next(n for n in (256, 224, 192, 176, 160, 128, 64) if q % n == 0)
    return [slice(r, r + n) for r in range(0, q, n)]


def send_kernel(ids, offs, lens, hid, w, out, hbuf, wbuf, obuf, hsem, wsem, osem, *, q):
    product = project(ids, offs, lens, hid, w, hbuf, wbuf, hsem, wsem, (1 - ids[2]) * (q // G), q // G)
    for j in range(8):
        for where in row_tiles(q):
            obuf[j, where, :] = product(j // 2, j % 2, where).astype(BF16)
        pltpu.make_async_copy(obuf.at[j], out.at[j], osem.at[j]).start()
    for j in range(8):
        pltpu.make_async_copy(obuf.at[j], out.at[j], osem.at[j]).wait()


def keep_kernel(ids, offs, lens, hid, w, other, local, s1, s2, s3, hbuf, wbuf, rbuf, obuf, hsem, wsem, rsem, osem, *, q):
    core = ids[2]
    product = project(ids, offs, lens, hid, w, hbuf, wbuf, hsem, wsem, core * (q // G), q // G)
    for j in range(8):
        pltpu.make_async_copy(other.at[j], rbuf.at[j], rsem.at[j]).start()

    def leave(j, verb):
        d, e = j // 2, j % 2
        along = (local, s1, s2, s3)[d].at[e]
        across = local.at[d] if e == 0 else (s1 if d < 2 else s3).at[d % 2]
        for c, target in enumerate((along, across)):

            @pl.when(core == c)
            def _(target=target):
                copy = pltpu.make_async_copy(obuf.at[j], target, osem.at[j])
                copy.start() if verb == "start" else copy.wait()

    for j in range(8):
        for where in row_tiles(q):
            value = product(j // 2, j % 2, where)
            if where.start == 0:
                pltpu.make_async_copy(other.at[j], rbuf.at[j], rsem.at[j]).wait()
            obuf[j, where, :] = (value + rbuf[j, where, :].astype(F32)).astype(BF16)
        leave(j, "start")
    for j in range(8):
        leave(j, "wait")


def call(kernel, prefetched, operands, out_shape, scratch=(), specs=None, out_specs=None, grid=(), flops=0, moved=0, aliases=None):
    n = len(prefetched)
    return pl.pallas_call(
        kernel,
        out_shape=out_shape,
        grid_spec=pltpu.PrefetchScalarGridSpec(
            num_scalar_prefetch=n,
            grid=grid,
            in_specs=specs if specs is not None else [ANY] * len(operands),
            out_specs=out_specs if out_specs is not None else jax.tree.map(lambda _: ANY, out_shape),
            scratch_shapes=list(scratch),
        ),
        compiler_params=ROOM,
        input_output_aliases=aliases or {},
        cost_estimate=pl.CostEstimate(flops=flops, bytes_accessed=moved, transcendentals=0),
    )(*prefetched, *operands)


def half_scratch(q):
    return [pltpu.VMEM((q, 1024), BF16), pltpu.VMEM((4, 1024, 2 * PAIR), BF16)]


def half_semaphores():
    return [pltpu.SemaphoreType.DMA((LOCAL, 5)), pltpu.SemaphoreType.DMA((4,))]


def send_half(meta, hid, w, q):
    return call(
        functools.partial(send_kernel, q=q),
        meta,
        (hid, w),
        jax.ShapeDtypeStruct((8, q, PAIR), BF16),
        half_scratch(q)
        + [pltpu.VMEM((8, q, PAIR), BF16)]
        + half_semaphores()
        + [pltpu.SemaphoreType.DMA((8,))],
        specs=[HBM, HBM],
        flops=2 * q * 1024 * 2048,
        moved=2 * (q * 1024 + 1024 * 2048 + q * 2048),
    )


def keep_half(meta, hid, w, other, q):
    return call(
        functools.partial(keep_kernel, q=q),
        meta,
        (hid, w, other),
        [jax.ShapeDtypeStruct((n, q, PAIR), BF16) for n in (4, 2, 2, 2)],
        half_scratch(q)
        + [pltpu.VMEM((8, q, PAIR), BF16)] * 2
        + half_semaphores()
        + [pltpu.SemaphoreType.DMA((8,))] * 2,
        specs=[HBM, HBM, ANY],
        flops=2 * q * 1024 * 2048,
        moved=2 * (q * 1024 + 1024 * 2048 + 2 * q * 2048),
    )


def middle_kernel(ids, local, r1, r2, r3, kept, s1, s2, s3):
    @pl.when(ids[2] == 0)
    def _():
        for e, out in ((0, kept), (1, s1)):
            total = (local[e].astype(F32) + r1[e].astype(F32)) + (r2[e].astype(F32) + r3[e].astype(F32))
            out[...] = total.astype(out.dtype)

    @pl.when(ids[2] == 1)
    def _():
        for d, out in enumerate((kept, s1, s2, s3)):
            arrived = (r1 if d < 2 else r3)[d % 2]
            out[...] = (local[d].astype(F32) + arrived.astype(F32)).astype(out.dtype)


def middle(ids, local, arrived, q):
    n = 2

    def three(i, ids):
        return (0, i, 0)

    def two(i, ids):
        return (i, 0)

    return call(
        middle_kernel,
        (ids,),
        (local, *arrived),
        [jax.ShapeDtypeStruct((q, PAIR), t) for t in (F32, BF16, BF16, BF16)],
        grid=(n,),
        specs=[pl.BlockSpec((a.shape[0], q // n, PAIR), three) for a in (local, *arrived)],
        out_specs=[pl.BlockSpec((q // n, PAIR), two)] * 4,
        moved=2 * PAIR * q * 15,
        flops=PAIR * q * 8,
    )


def rope_rows_kernel(ids, offs, lens, table, out, sem, *, q):
    starts, counts, _ = plan(ids, offs, lens)
    for verb in ("start", "wait"):

        def copy(p, bit, source, target, count, verb=verb):
            base = lax.shift_right_logical(offs[ids[3] * LOCAL + p], 4)
            c = pltpu.make_async_copy(
                table.at[rows(base + source, count)], out.at[rows(target, count)], sem.at[p, bit]
            )
            c.start() if verb == "start" else c.wait()

        ragged(starts, counts, ids[2] * (q // G), q // G, copy)


def rope_rows(meta, table, q):
    return call(
        functools.partial(rope_rows_kernel, q=q),
        meta,
        (table,),
        jax.ShapeDtypeStruct((q, PAIR), F32),
        [pltpu.SemaphoreType.DMA((LOCAL, 5))],
        specs=[HBM],
        moved=q * PAIR * 8,
    )


def finish_kernel(ids, offs, lens, kept, r1, r2, r3, turn, out, *, q):
    _, _, total = plan(ids, offs, lens)
    valid = (total - ids[2] * (q // G)) * G

    def put(value):
        row = lax.broadcasted_iota(jnp.int32, (q, HEAD_SIZE), 0)
        key = value[:, :HEAD_SIZE]
        key = key * turn[:, :HEAD_SIZE] + pltpu.roll(key, HEAD_SIZE // 2, 1) * turn[:, HEAD_SIZE:]
        out[:, :HEAD_SIZE] = jnp.where(row < valid, key, 0.0).astype(BF16)
        out[:, HEAD_SIZE:] = value[:, HEAD_SIZE:].astype(BF16)

    @pl.when(ids[2] == 0)
    def _():
        put(kept[...] + r1[...].astype(F32))

    @pl.when(ids[2] == 1)
    def _():
        put((kept[...] + r1[...].astype(F32)) + (r2[...].astype(F32) + r3[...].astype(F32)))


def finish(meta, kept, arrived, turn, q):
    return call(
        functools.partial(finish_kernel, q=q),
        meta,
        (kept, *arrived, turn),
        jax.ShapeDtypeStruct((q, PAIR), BF16),
        specs=[VMEM] * 5,
        out_specs=VMEM,
        moved=q * PAIR * 16,
        flops=q * PAIR * 4,
    )


def stack_heads(tile):
    return [tile[:, h * HEAD_SIZE : (h + 1) * HEAD_SIZE] for h in range(HEADS)]


def scores_of(query, keys):
    return lax.dot_general(query, keys, (((1,), (1,)), ((), ())), preferred_element_type=F32) * SCALE2


def spread(column, n):
    lane = lax.broadcasted_iota(jnp.int32, (n, HEAD_SIZE), 1)
    out = jnp.zeros((n, HEAD_SIZE), F32)
    for h in range(HEADS):
        out = jnp.where(lane == h, column[h * n : (h + 1) * n], out)
    return out


def smallest(value):
    return jnp.min(value.reshape(-1, 8, HEAD_SIZE), axis=0)


def largest(value):
    return jnp.max(value.reshape(-1, 8, HEAD_SIZE), axis=0)


def gather_column(stats):
    return jnp.concatenate([stats[:, h : h + 1] for h in range(HEADS)], axis=0)


def prior_kernel(ids, offs, lens, owner, query, dquery, mine, theirs, *refs, first):
    out, stat, dout, dstat, kbuf, vbuf, *bounds, sem = refs[-9:]
    step = pl.program_id(0)
    steps = pl.num_programs(0)

    def copies(i):
        slot = lax.rem(i, 2)
        core = ids[2]
        return (
            pltpu.make_async_copy(
                mine.at[first + i],
                kbuf.at[slot, pl.ds(pl.multiple_of(core * PART, PART), PART)],
                sem.at[slot, 0],
            ),
            pltpu.make_async_copy(
                theirs.at[first + i],
                kbuf.at[slot, pl.ds(pl.multiple_of((1 - core) * PART, PART), PART)],
                sem.at[slot, 1],
            ),
        )

    @pl.when(step == 0)
    def _():
        for c in copies(step):
            c.start()
        vbuf[:, HEAD_SIZE:] = jnp.ones((CONTEXT_LENGTH, HEAD_SIZE), BF16)

    @pl.when(step + 1 < steps)
    def _():
        for c in copies(step + 1):
            c.start()

    for c in copies(step):
        c.wait()

    slot = lax.rem(step, 2)
    at = ids[3] * LOCAL + first + step
    offset, length = offs[at], lens[at]
    tiles = lax.div(length - offset + (TILE - 1), TILE)
    vbuf[:, :HEAD_SIZE] = kbuf[slot, :, HEAD_SIZE:]

    least, most = bounds
    least[...] = jnp.full(least.shape, 1.0, F32)
    most[...] = jnp.full(most.shape, 1.0, F32)

    def put(where, value, stats, n):
        for h in range(HEADS):
            out[0, where, h * HEAD_SIZE : (h + 1) * HEAD_SIZE] = value[h * n : (h + 1) * n]
        stat[0, where, :] = spread(stats, n)

    def put_decode(value, stats):
        for h in range(HEADS):
            dout[0, :, h * HEAD_SIZE : (h + 1) * HEAD_SIZE] = value[h * DROWS : (h + 1) * DROWS]
        dstat[0] = spread(stats, DROWS)

    for blocks in range(1, 5):

        @pl.when(offset == blocks * 256)
        def _(keys=blocks * 256):
            @pl.loop(0, tiles)
            def _(t):
                where = pl.ds(pl.multiple_of(t * TILE, TILE), TILE)
                tile = jnp.concatenate(stack_heads(query[0, where, :]) + stack_heads(dquery[0]), axis=0)
                weights = jnp.exp2(scores_of(tile, kbuf[slot, :keys, :HEAD_SIZE])).astype(BF16)
                mixed = jnp.dot(weights, vbuf[:keys, :], preferred_element_type=F32)
                total = mixed[:, HEAD_SIZE:]
                least[...] = jnp.minimum(least[...], smallest(total))
                most[...] = jnp.maximum(most[...], largest(total))
                value = (mixed[:, :HEAD_SIZE] * (1.0 / total)).astype(BF16)
                stats = jnp.log2(total)
                n = HEADS * TILE
                put(where, value[:n], stats[:n], TILE)
                put_decode(value[n:], stats[n:])

    fine = jnp.logical_and(jnp.min(least[...]) >= LOW, jnp.max(most[...]) <= HIGH)

    @pl.when(jnp.logical_not(fine))
    def _():
        def exact(tile):
            def block(b, carry):
                top, mixed = carry
                keys = pl.ds(pl.multiple_of(b * 256, 256), 256)
                scores = scores_of(tile, kbuf[slot, keys, :HEAD_SIZE])
                now = jnp.maximum(jnp.max(scores, axis=1, keepdims=True), top)
                weights = jnp.exp2(scores - now).astype(BF16)
                more = jnp.dot(weights, vbuf[keys, :], preferred_element_type=F32)
                return now, mixed * jnp.exp2(top - now) + more

            n = tile.shape[0]
            first = (jnp.full((n, 1), NEG, F32), jnp.zeros((n, PAIR), F32))
            top, mixed = lax.fori_loop(0, lax.shift_right_logical(offset, 8), block, first)
            total = mixed[:, HEAD_SIZE:]
            return (mixed[:, :HEAD_SIZE] / total).astype(BF16), top + jnp.log2(total)

        @pl.loop(0, FINAL_LENGTH // 32)
        def _(t):
            where = pl.ds(pl.multiple_of(t * 32, 32), 32)
            put(where, *exact(jnp.concatenate(stack_heads(query[0, where, :]), axis=0)), 32)

        put_decode(*exact(jnp.concatenate(stack_heads(dquery[0]), axis=0)))


def prior(meta, owner, query, dquery, mine, theirs, before, first, n):
    def at(i, ids, offs, lens, owner):
        return (first + i, 0, 0)

    def decode_at(i, ids, offs, lens, owner):
        return (owner[ids[3] * LOCAL + first + i], 0, 0)

    shapes = [
        ((LOCAL, FINAL_LENGTH, HEADS * HEAD_SIZE), BF16),
        ((LOCAL, FINAL_LENGTH, HEAD_SIZE), F32),
        ((LOCAL, DROWS, HEADS * HEAD_SIZE), BF16),
        ((LOCAL, DROWS, HEAD_SIZE), F32),
    ]
    return call(
        functools.partial(prior_kernel, first=first),
        (*meta, owner),
        (query, dquery, mine, theirs, *before),
        [jax.ShapeDtypeStruct(*s) for s in shapes],
        [
            pltpu.VMEM((2, CONTEXT_LENGTH, PAIR), BF16),
            pltpu.VMEM((CONTEXT_LENGTH, PAIR), BF16),
            pltpu.VMEM((8, HEAD_SIZE), F32),
            pltpu.VMEM((8, HEAD_SIZE), F32),
            pltpu.SemaphoreType.DMA((2, 2)),
        ],
        grid=(n,),
        specs=[
            pl.BlockSpec((1, FINAL_LENGTH, HEADS * HEAD_SIZE), at),
            pl.BlockSpec((1, DROWS, HEADS * HEAD_SIZE), decode_at),
            HBM,
            HBM,
        ]
        + [ANY] * len(before),
        out_specs=[pl.BlockSpec((1,) + s[1:], at) for s, _ in shapes],
        aliases={8 + i: i for i in range(len(before))},
        flops=n * 3 * 10**9,
        moved=n * 2 * 10**6,
    )


def assemble(ids, pieces, fbuf, sem, q, act):
    for i, core in enumerate((ids[2], 1 - ids[2])):
        target = fbuf.at[pl.ds(pl.multiple_of(core * q, G), q)]
        c = pltpu.make_async_copy(pieces[i], target, sem.at[i])
        c.start() if act == "start" else c.wait()


def load_fresh(ids, pieces, fbuf, sem, q):
    assemble(ids, pieces, fbuf, sem, q, "start")
    fbuf[2 * q :, :] = jnp.zeros((FINAL_LENGTH, PAIR), BF16)
    assemble(ids, pieces, fbuf, sem, q, "wait")


def fresh_kernel(ids, offs, lens, own, other, query, prior_out, prior_stat, out, fbuf, vbuf, *refs, q):
    *bounds, sem = refs
    p = pl.program_id(0)

    @pl.when(p == 0)
    def _():
        load_fresh(ids, (own, other), fbuf, sem, q)
        vbuf[:, HEAD_SIZE:] = jnp.ones((FINAL_LENGTH, HEAD_SIZE), BF16)

    starts, _, _ = plan(ids, offs, lens)
    start = jnp.int32(0)
    for i in range(1, LOCAL):
        start = jnp.where(p == i, starts[i], start)
    at = ids[3] * LOCAL + p
    count = lens[at] - offs[at]
    where_keys = pl.ds(pl.multiple_of(start * G, G), FINAL_LENGTH)
    vbuf[:, :HEAD_SIZE] = fbuf[where_keys, HEAD_SIZE:]
    n = HEADS * TILE
    least, most = bounds
    least[...] = jnp.full(least.shape, 1.0, F32)
    most[...] = jnp.full(most.shape, 1.0, F32)

    for t in range(FINAL_LENGTH // TILE):
        where = slice(t * TILE, (t + 1) * TILE)

        @pl.when(count <= t * TILE)
        def _(where=where):
            out[0, where, :] = jnp.zeros((TILE, HEADS * HEAD_SIZE), BF16)

        @pl.when(count > t * TILE)
        def _(where=where, t=t):
            seen = (t + 1) * TILE
            keys = pl.ds(pl.multiple_of(start * G, G), seen)
            row = lax.broadcasted_iota(jnp.int32, (TILE, seen), 0) + t * TILE
            allowed = (lax.broadcasted_iota(jnp.int32, (TILE, seen), 1) <= row).astype(F32)
            scores = scores_of(jnp.concatenate(stack_heads(query[0, where, :]), axis=0), fbuf[keys, :HEAD_SIZE])
            weights = jnp.concatenate(
                [
                    (jnp.exp2(scores[h * TILE : (h + 1) * TILE]) * allowed).astype(BF16)
                    for h in range(HEADS)
                ],
                axis=0,
            )
            mixed = jnp.dot(weights, vbuf[:seen, :], preferred_element_type=F32)
            keep = lax.broadcasted_iota(jnp.int32, (TILE, HEAD_SIZE), 0) + t * TILE < count
            before = jnp.exp2(prior_stat[0, where, :])
            low, high = least[...], most[...]
            for h in range(HEADS):
                lanes = slice(h * HEAD_SIZE, (h + 1) * HEAD_SIZE)
                stack = slice(h * TILE, (h + 1) * TILE)
                share = before[:, h : h + 1]
                total = mixed[stack, HEAD_SIZE:] + share
                low, high = jnp.minimum(low, smallest(total)), jnp.maximum(high, largest(total))
                old = prior_out[0, where, lanes].astype(F32)
                value = (mixed[stack, :HEAD_SIZE] + old * share) * (1.0 / total)
                out[0, where, lanes] = jnp.where(keep, value, 0.0).astype(BF16)
            least[...], most[...] = low, high

    fine = jnp.logical_and(jnp.min(least[...]) >= LOW, jnp.max(most[...]) <= HIGH)

    @pl.when(jnp.logical_not(fine))
    def _():
        some = 32
        keys = pl.ds(pl.multiple_of(start * G, G), FINAL_LENGTH)
        n = HEADS * some

        @pl.loop(0, FINAL_LENGTH // some)
        def _(t):
            where = pl.ds(pl.multiple_of(t * some, some), some)
            position = lax.bitwise_and(lax.broadcasted_iota(jnp.int32, (n, FINAL_LENGTH), 0), some - 1)
            ahead = lax.broadcasted_iota(jnp.int32, (n, FINAL_LENGTH), 1) - position
            scores = scores_of(jnp.concatenate(stack_heads(query[0, where, :]), axis=0), fbuf[keys, :HEAD_SIZE])
            scores = jnp.where(ahead <= t * some, scores, NEG)
            before = gather_column(prior_stat[0, where, :])
            top = jnp.maximum(jnp.max(scores, axis=1, keepdims=True), before)
            weights = jnp.exp2(scores - top).astype(BF16)
            share = jnp.exp2(before - top)
            mixed = jnp.dot(weights, vbuf[...], preferred_element_type=F32)
            total = mixed[:, HEAD_SIZE:] + share
            keep = lax.broadcasted_iota(jnp.int32, (some, HEAD_SIZE), 0) + t * some < count
            for h in range(HEADS):
                lanes = slice(h * HEAD_SIZE, (h + 1) * HEAD_SIZE)
                stack = slice(h * some, (h + 1) * some)
                old = prior_out[0, where, lanes].astype(F32)
                value = (mixed[stack, :HEAD_SIZE] + old * share[stack]) / total[stack]
                out[0, where, lanes] = jnp.where(keep, value, 0.0).astype(BF16)


def fresh(meta, pieces, query, prior_out, prior_stat, q):
    def at(p, ids, offs, lens):
        return (p, 0, 0)

    wide = pl.BlockSpec((1, FINAL_LENGTH, HEADS * HEAD_SIZE), at)
    return call(
        functools.partial(fresh_kernel, q=q),
        meta,
        (*pieces, query, prior_out, prior_stat),
        jax.ShapeDtypeStruct((LOCAL, FINAL_LENGTH, HEADS * HEAD_SIZE), BF16),
        [
            pltpu.VMEM((2 * q + FINAL_LENGTH, PAIR), BF16),
            pltpu.VMEM((FINAL_LENGTH, PAIR), BF16),
            pltpu.VMEM((8, HEAD_SIZE), F32),
            pltpu.VMEM((8, HEAD_SIZE), F32),
            pltpu.SemaphoreType.DMA((2,)),
        ],
        grid=(LOCAL,),
        specs=[ANY, ANY, wide, wide, pl.BlockSpec((1, FINAL_LENGTH, HEAD_SIZE), at)],
        out_specs=wide,
        flops=4 * 10**9,
        moved=10**7,
    )


def decode_kernel(ids, offs, lens, owner, own, other, query, recent, prior_out, prior_stat, out, fbuf, sem, *, q):
    load_fresh(ids, (own, other), fbuf, sem, q)
    starts, _, _ = plan(ids, offs, lens)
    n = HEADS * DROWS
    step = lax.bitwise_and(lax.broadcasted_iota(jnp.int32, (n, DROWS), 0), DROWS - 1)
    later = lax.broadcasted_iota(jnp.int32, (n, DROWS), 1) > step
    column = lax.broadcasted_iota(jnp.int32, (n, FINAL_LENGTH), 1)
    for p in range(LOCAL):
        i = ids[3] * LOCAL + p
        slot = owner[i]
        keys = pl.ds(pl.multiple_of(starts[p] * G, G), FINAL_LENGTH)
        tile = jnp.concatenate(stack_heads(query[slot]), axis=0)
        block = scores_of(tile, fbuf[keys, :HEAD_SIZE])
        block = jnp.where(column < lens[i] - offs[i], block, NEG)
        near = scores_of(tile, recent[slot, :, :HEAD_SIZE])
        near = jnp.where(later, NEG, near)
        before = gather_column(prior_stat[p])
        top = jnp.maximum(jnp.max(block, axis=1, keepdims=True), jnp.max(near, axis=1, keepdims=True))
        top = jnp.maximum(top, before)
        block_weights = jnp.exp2(block - top)
        near_weights = jnp.exp2(near - top)
        share = jnp.exp2(before - top)
        total = (
            jnp.sum(block_weights, axis=1, keepdims=True)
            + jnp.sum(near_weights, axis=1, keepdims=True)
            + share
        )
        mixed = jnp.dot(block_weights.astype(BF16), fbuf[keys, HEAD_SIZE:], preferred_element_type=F32)
        mixed = mixed + jnp.dot(
            near_weights.astype(BF16), recent[slot, :, HEAD_SIZE:], preferred_element_type=F32
        )
        for h in range(HEADS):
            lanes = slice(h * HEAD_SIZE, (h + 1) * HEAD_SIZE)
            stack = slice(h * DROWS, (h + 1) * DROWS)
            value = (mixed[stack] + prior_out[p, :, lanes].astype(F32) * share[stack]) / total[stack]
            out[slot, :, lanes] = value[:STEPS].astype(BF16)


def decode(meta, owner, pieces, query, recent, prior_out, prior_stat, q):
    return call(
        functools.partial(decode_kernel, q=q),
        (*meta, owner),
        (*pieces, query, recent, prior_out, prior_stat),
        jax.ShapeDtypeStruct((LOCAL, STEPS, HEADS * HEAD_SIZE), BF16),
        [pltpu.VMEM((2 * q + FINAL_LENGTH, PAIR), BF16), pltpu.SemaphoreType.DMA((2,))],
        specs=[ANY] * 2 + [VMEM] * 4,
        out_specs=VMEM,
        flops=10**8,
        moved=2 * 10**6,
    )


def exchange(value):
    return lax.all_to_all(value, "grp", split_axis=0, concat_axis=0, tiled=True)


def attention_layer(
    cap,
    ids,
    hid,
    key_value_weight,
    prefill_query,
    cache,
    stretch_offset,
    prompt_length,
    decode_owner,
    decode_query,
    recent,
):
    meta = (ids, stretch_offset, prompt_length)
    q = cap // 2
    other_half = lax.ppermute(send_half(meta, hid, key_value_weight, q), "tp", SIBLING)
    other_cache = lax.ppermute(cache, "tp", SIBLING)
    asked = exchange(jnp.concatenate([decode_query, recent], axis=2))
    turn = rope_rows(meta, jnp.asarray(rope_table()), q)

    local, *sent = keep_half(meta, hid, key_value_weight, other_half, q)
    arrived = [lax.ppermute(v, "tp", way) for v, way in zip(sent, FIRST)]
    asked, _ = lax.optimization_barrier((asked, local))
    asked = jnp.pad(asked, ((0, 0), (0, DROWS - STEPS), (0, 0)))
    dquery = asked[..., : HEADS * HEAD_SIZE]
    recent = asked[..., HEADS * HEAD_SIZE :]
    kept, *sent = middle(ids, local, arrived, q)
    arrived = [lax.ppermute(v, "tp", way) for v, way in zip(sent, SECOND)]
    new = finish(meta, kept, arrived, turn, q)
    pieces = (new, lax.ppermute(new, "tp", SIBLING))

    before = ()
    for i in range(0, LOCAL, 2):
        before = prior(meta, decode_owner, prefill_query, dquery, cache, other_cache, before, i, 2)
    prior_out, prior_stat, prior_dout, prior_dstat = before
    answer = decode(meta, decode_owner, pieces, dquery, recent, prior_dout, prior_dstat, q)
    decode_out = exchange(answer)
    prefill_out = fresh(meta, pieces, prefill_query, prior_out, prior_stat, q)
    return (prefill_out, decode_out)


def per_device(
    hidden_rows,
    key_value_weight,
    prefill_query,
    earlier_cache,
    stretch_offset,
    prompt_length,
    decode_owner,
    decode_query,
    decode_kv,
):
    lane = lax.axis_index("tp")
    group = lax.axis_index("grp")
    ids = jnp.stack([lane // 4, lane // 2 % 2, lane % 2, group]).astype(jnp.int32)
    recent = lax.dynamic_slice_in_dim(decode_kv, (lane // 2) * PAIR, PAIR, 2)
    blocks = lax.shift_right_logical(prompt_length - stretch_offset + (G - 1), 4)
    most = jnp.max(jnp.sum(blocks.reshape(-1, LOCAL), axis=1)) * G
    branch = sum((most > cap).astype(jnp.int32) for cap in CAPS[:-1])
    return lax.switch(
        branch,
        [functools.partial(attention_layer, cap) for cap in CAPS],
        ids,
        hidden_rows.reshape(LOCAL * FINAL_LENGTH, -1),
        key_value_weight,
        prefill_query,
        earlier_cache.reshape(LOCAL, PART, PAIR),
        stretch_offset,
        prompt_length,
        decode_owner,
        decode_query,
        recent,
    )


def solution(mesh):
    in_specs = (
        P("grp", None, "tp"),
        P("tp", None),
        P("grp", None, "tp"),
        P("grp", "tp", None, None),
        P(),
        P(),
        P(),
        P("grp", None, "tp"),
        P("grp", None, None),
    )
    out_specs = (P("grp", None, "tp"), P("grp", None, "tp"))
    return jax.shard_map(
        per_device, mesh=mesh, in_specs=in_specs, out_specs=out_specs, check_vma=False
    )
```

```python
import functools
import math

import jax
import jax.numpy as jnp
import numpy as np
from jax import lax
from jax.experimental import pallas as pl
from jax.experimental.pallas import tpu as pltpu
from jax.sharding import PartitionSpec as P

HEAD_SIZE = 128
PAIR = 2 * HEAD_SIZE
LOCAL = 8
FINAL_LENGTH = 256
CONTEXT_LENGTH = 1024
PART = 512
STEPS = 4
HEADS = 8
ROPE_BASE = 500000.0
G = 16
DROWS = 16
TILE = 128
SCALE2 = HEAD_SIZE**-0.5 * math.log2(math.e)
NEG = -1e30
F32 = jnp.float32
BF16 = jnp.bfloat16
ANY = pl.BlockSpec(memory_space=pl.ANY)
VMEM = pl.BlockSpec(memory_space=pltpu.VMEM)
HBM = pl.BlockSpec(memory_space=pltpu.HBM)
SMALL = 22
ROOM = 1664
LOW, HIGH = 2.0**-100, 2.0**100


def pairs(*moves):
    out = []
    for x in range(4):
        for z in range(2):
            for core in range(2):
                if moves[core] is None:
                    continue
                dx, dz, dc = moves[core]
                out.append((x * 4 + z * 2 + core, (x + dx) % 4 * 4 + (z + dz) % 2 * 2 + (core + dc) % 2))
    return out


SIBLING = pairs((0, 0, 1), (0, 0, 1))
FIRST = [pairs((1, 0, 0), (0, 1, 0)), pairs((2, 0, 0), None), pairs((3, 0, 0), (0, 1, 0))]
SECOND = [pairs((0, 1, 0), (1, 0, 0)), pairs(None, (2, 0, 0)), pairs(None, (3, 0, 0))]
ORDER = (0, 2, 1)


def rope_table():
    half = HEAD_SIZE // 2
    freq = ROPE_BASE ** (np.arange(half, dtype=np.float64) * (-2.0 / HEAD_SIZE))
    angle = np.arange(CONTEXT_LENGTH + FINAL_LENGTH, dtype=np.float64)[:, None] * freq
    cosine, sine = np.cos(angle), np.sin(angle)
    return np.concatenate([cosine, cosine, -sine, sine], axis=1).astype(np.float32)


def plan(ids, offs, lens):
    starts, counts, at = [], [], jnp.int32(0)
    for p in range(LOCAL):
        i = ids[3] * LOCAL + p
        count = lax.shift_right_logical(lens[i] - offs[i] + (G - 1), 4)
        starts.append(at)
        counts.append(count)
        at = at + count
    return starts, counts, at


def ragged(starts, counts, first_block, blocks, copy):
    for p in range(LOCAL):
        low = jnp.maximum(starts[p], first_block)
        high = jnp.minimum(starts[p] + counts[p], first_block + blocks)
        n = jnp.maximum(high - low, 0)
        for bit in range(4, -1, -1):
            done = lax.shift_left(lax.shift_right_logical(n, bit + 1), bit + 1)

            @pl.when(lax.bitwise_and(n, 1 << bit) != 0)
            def _(p=p, bit=bit, low=low, done=done):
                copy(p, bit, low + done - starts[p], low + done - first_block, 1 << bit)


def rows(block, count):
    return pl.ds(pl.multiple_of(block * G, G), count * G)


def project(ids, offs, lens, hid, w, hbuf, wbuf, hsem, wsem, first_block, blocks):
    starts, counts, total = plan(ids, offs, lens)

    def hidden_copy(p, bit, source, target, count):
        return pltpu.make_async_copy(
            hid.at[rows(p * (FINAL_LENGTH // G) + source, count)],
            hbuf.at[rows(target, count)],
            hsem.at[p, bit],
        )

    def weight_copy(d):
        first = lax.rem(ids[0] + d, 4) * (2 * PAIR)
        return pltpu.make_async_copy(
            w.at[:, pl.ds(pl.multiple_of(first, 2 * PAIR), 2 * PAIR)], wbuf.at[d], wsem.at[d]
        )

    weight_copy(0).start()
    ragged(starts, counts, first_block, blocks, lambda *a: hidden_copy(*a).start())
    for d in range(1, 4):
        weight_copy(d).start()

    @pl.loop(jnp.clip(total - first_block, 0, blocks), blocks)
    def _(b):
        hbuf[rows(b, 1), :] = jnp.zeros((G, hbuf.shape[1]), BF16)

    ragged(starts, counts, first_block, blocks, lambda *a: hidden_copy(*a).wait())

    def product(d, e, where):
        if e == 0 and where.start == 0:
            weight_copy(d).wait()
        columns = pl.ds(pl.multiple_of(lax.rem(ids[1] + e, 2) * PAIR, PAIR), PAIR)
        return jnp.dot(hbuf[where, :], wbuf[d, :, columns], preferred_element_type=F32)

    return product


def row_tiles(q):
    n = next(n for n in (256, 224, 208, 192, 176, 160, 128, 64) if q % n == 0)
    return [slice(r, r + n) for r in range(0, q, n)]


def send_kernel(ids, offs, lens, hid, w, out, hbuf, wbuf, obuf, hsem, wsem, osem, *, base, q):
    first = base // G + (1 - ids[2]) * (q // G)
    product = project(ids, offs, lens, hid, w, hbuf, wbuf, hsem, wsem, first, q // G)
    for j in range(8):
        for where in row_tiles(q):
            obuf[j, where, :] = product(j // 2, j % 2, where).astype(BF16)
        pltpu.make_async_copy(obuf.at[j], out.at[j], osem.at[j]).start()
    for j in range(8):
        pltpu.make_async_copy(obuf.at[j], out.at[j], osem.at[j]).wait()


def keep_kernel(ids, offs, lens, hid, w, other, local, s1, s2, s3, hbuf, wbuf, rbuf, obuf, hsem, wsem, rsem, osem, *, base, q):
    core = ids[2]
    product = project(ids, offs, lens, hid, w, hbuf, wbuf, hsem, wsem, base // G + core * (q // G), q // G)
    for j in range(8):
        pltpu.make_async_copy(other.at[j], rbuf.at[j], rsem.at[j]).start()

    def leave(j, verb):
        d, e = j // 2, j % 2
        along = (local, s1, s2, s3)[d].at[e]
        across = local.at[d] if e == 0 else (s1 if d < 2 else s3).at[d % 2]
        for c, target in enumerate((along, across)):

            @pl.when(core == c)
            def _(target=target):
                copy = pltpu.make_async_copy(obuf.at[j], target, osem.at[j])
                copy.start() if verb == "start" else copy.wait()

    for j in range(8):
        for where in row_tiles(q):
            value = product(j // 2, j % 2, where)
            if where.start == 0:
                pltpu.make_async_copy(other.at[j], rbuf.at[j], rsem.at[j]).wait()
            obuf[j, where, :] = (value + rbuf[j, where, :].astype(F32)).astype(BF16)
        leave(j, "start")
    for j in range(8):
        leave(j, "wait")


def call(kernel, prefetched, operands, out_shape, scratch=(), specs=None, out_specs=None, grid=(), flops=0, moved=0, aliases=None, vmem=SMALL):
    n = len(prefetched)
    return pl.pallas_call(
        kernel,
        out_shape=out_shape,
        grid_spec=pltpu.PrefetchScalarGridSpec(
            num_scalar_prefetch=n,
            grid=grid,
            in_specs=specs if specs is not None else [ANY] * len(operands),
            out_specs=out_specs if out_specs is not None else jax.tree.map(lambda _: ANY, out_shape),
            scratch_shapes=list(scratch),
        ),
        compiler_params=pltpu.CompilerParams(vmem_limit_bytes=vmem * 2**20),
        input_output_aliases=aliases or {},
        cost_estimate=pl.CostEstimate(flops=flops, bytes_accessed=moved, transcendentals=0),
    )(*prefetched, *operands)


def half_scratch(q):
    return [pltpu.VMEM((q, 1024), BF16), pltpu.VMEM((4, 1024, 2 * PAIR), BF16)]


def half_semaphores():
    return [pltpu.SemaphoreType.DMA((LOCAL, 5)), pltpu.SemaphoreType.DMA((4,))]


def send_half(meta, hid, w, base, q):
    return call(
        functools.partial(send_kernel, base=base, q=q),
        meta,
        (hid, w),
        jax.ShapeDtypeStruct((8, q, PAIR), BF16),
        half_scratch(q)
        + [pltpu.VMEM((8, q, PAIR), BF16)]
        + half_semaphores()
        + [pltpu.SemaphoreType.DMA((8,))],
        specs=[HBM, HBM],
        flops=2 * q * 1024 * 2048,
        moved=2 * (q * 1024 + 1024 * 2048 + q * 2048),
    )


def keep_half(meta, hid, w, other, base, q):
    return call(
        functools.partial(keep_kernel, base=base, q=q),
        meta,
        (hid, w, other),
        [jax.ShapeDtypeStruct((n, q, PAIR), BF16) for n in (4, 2, 2, 2)],
        half_scratch(q)
        + [pltpu.VMEM((8, q, PAIR), BF16)] * 2
        + half_semaphores()
        + [pltpu.SemaphoreType.DMA((8,))] * 2,
        specs=[HBM, HBM, ANY],
        flops=2 * q * 1024 * 2048,
        moved=2 * (q * 1024 + 1024 * 2048 + 2 * q * 2048),
    )


def middle_kernel(ids, local, r1, r2, r3, kept, s1, s2, s3):
    @pl.when(ids[2] == 0)
    def _():
        for e, out in ((0, kept), (1, s1)):
            total = (local[e].astype(F32) + r1[e].astype(F32)) + (r2[e].astype(F32) + r3[e].astype(F32))
            out[...] = total.astype(out.dtype)

    @pl.when(ids[2] == 1)
    def _():
        for d, out in enumerate((kept, s1, s2, s3)):
            arrived = (r1 if d < 2 else r3)[d % 2]
            out[...] = (local[d].astype(F32) + arrived.astype(F32)).astype(out.dtype)


def middle(ids, local, arrived, q):
    n = 2

    def three(i, ids):
        return (0, i, 0)

    def two(i, ids):
        return (i, 0)

    return call(
        middle_kernel,
        (ids,),
        (local, *arrived),
        [jax.ShapeDtypeStruct((q, PAIR), t) for t in (F32, BF16, BF16, BF16)],
        grid=(n,),
        specs=[pl.BlockSpec((a.shape[0], q // n, PAIR), three) for a in (local, *arrived)],
        out_specs=[pl.BlockSpec((q // n, PAIR), two)] * 4,
        moved=2 * PAIR * q * 15,
        flops=PAIR * q * 8,
    )


def rope_rows_kernel(ids, offs, lens, table, out, sem, *, base, q):
    starts, counts, _ = plan(ids, offs, lens)
    for verb in ("start", "wait"):

        def copy(p, bit, source, target, count, verb=verb):
            position = lax.shift_right_logical(offs[ids[3] * LOCAL + p], 4)
            c = pltpu.make_async_copy(
                table.at[rows(position + source, count)], out.at[rows(target, count)], sem.at[p, bit]
            )
            c.start() if verb == "start" else c.wait()

        ragged(starts, counts, base // G + ids[2] * (q // G), q // G, copy)


def rope_rows(meta, table, base, q):
    return call(
        functools.partial(rope_rows_kernel, base=base, q=q),
        meta,
        (table,),
        jax.ShapeDtypeStruct((q, PAIR), F32),
        [pltpu.SemaphoreType.DMA((LOCAL, 5))],
        specs=[HBM],
        moved=q * PAIR * 8,
    )


def finish_kernel(ids, offs, lens, kept, r1, r2, r3, turn, out, *, base, q):
    _, _, total = plan(ids, offs, lens)
    valid = (total - base // G - ids[2] * (q // G)) * G

    def put(value):
        row = lax.broadcasted_iota(jnp.int32, (q, HEAD_SIZE), 0)
        key = value[:, :HEAD_SIZE]
        key = key * turn[:, :HEAD_SIZE] + pltpu.roll(key, HEAD_SIZE // 2, 1) * turn[:, HEAD_SIZE:]
        out[:, :HEAD_SIZE] = jnp.where(row < valid, key, 0.0).astype(BF16)
        out[:, HEAD_SIZE:] = value[:, HEAD_SIZE:].astype(BF16)

    @pl.when(ids[2] == 0)
    def _():
        put(kept[...] + r1[...].astype(F32))

    @pl.when(ids[2] == 1)
    def _():
        put((kept[...] + r1[...].astype(F32)) + (r2[...].astype(F32) + r3[...].astype(F32)))


def finish(meta, kept, arrived, turn, base, q):
    return call(
        functools.partial(finish_kernel, base=base, q=q),
        meta,
        (kept, *arrived, turn),
        jax.ShapeDtypeStruct((q, PAIR), BF16),
        specs=[VMEM] * 5,
        out_specs=VMEM,
        moved=q * PAIR * 16,
        flops=q * PAIR * 4,
    )


def stack_heads(tile):
    return [tile[:, h * HEAD_SIZE : (h + 1) * HEAD_SIZE] for h in range(HEADS)]


def scores_of(query, keys):
    return lax.dot_general(query, keys, (((1,), (1,)), ((), ())), preferred_element_type=F32) * SCALE2


def spread(column, n):
    lane = lax.broadcasted_iota(jnp.int32, (n, HEAD_SIZE), 1)
    out = jnp.zeros((n, HEAD_SIZE), F32)
    for h in range(HEADS):
        out = jnp.where(lane == h, column[h * n : (h + 1) * n], out)
    return out


def smallest(value):
    return jnp.min(value.reshape(-1, 8, HEAD_SIZE), axis=0)


def largest(value):
    return jnp.max(value.reshape(-1, 8, HEAD_SIZE), axis=0)


def gather_column(stats):
    return jnp.concatenate([stats[:, h : h + 1] for h in range(HEADS)], axis=0)


def prior_kernel(ids, offs, lens, owner, query, dquery, mine, theirs, *refs, first):
    out, stat, dout, dstat, kbuf, vbuf, *bounds, sem = refs[-9:]
    step = pl.program_id(0)
    steps = pl.num_programs(0)

    def copies(i):
        slot = lax.rem(i, 2)
        core = ids[2]
        return (
            pltpu.make_async_copy(
                mine.at[first + i],
                kbuf.at[slot, pl.ds(pl.multiple_of(core * PART, PART), PART)],
                sem.at[slot, 0],
            ),
            pltpu.make_async_copy(
                theirs.at[first + i],
                kbuf.at[slot, pl.ds(pl.multiple_of((1 - core) * PART, PART), PART)],
                sem.at[slot, 1],
            ),
        )

    @pl.when(step == 0)
    def _():
        for c in copies(step):
            c.start()
        vbuf[:, HEAD_SIZE:] = jnp.ones((CONTEXT_LENGTH, HEAD_SIZE), BF16)

    @pl.when(step + 1 < steps)
    def _():
        for c in copies(step + 1):
            c.start()

    for c in copies(step):
        c.wait()

    slot = lax.rem(step, 2)
    at = ids[3] * LOCAL + first + step
    offset, length = offs[at], lens[at]
    tiles = lax.div(length - offset + (TILE - 1), TILE)
    vbuf[:, :HEAD_SIZE] = kbuf[slot, :, HEAD_SIZE:]

    least, most = bounds
    least[...] = jnp.full(least.shape, 1.0, F32)
    most[...] = jnp.full(most.shape, 1.0, F32)

    def put(where, value, stats, n):
        for h in range(HEADS):
            out[0, where, h * HEAD_SIZE : (h + 1) * HEAD_SIZE] = value[h * n : (h + 1) * n]
        stat[0, where, :] = spread(stats, n)

    def put_decode(value, stats):
        for h in range(HEADS):
            dout[0, :, h * HEAD_SIZE : (h + 1) * HEAD_SIZE] = value[h * DROWS : (h + 1) * DROWS]
        dstat[0] = spread(stats, DROWS)

    for blocks in range(1, 5):

        @pl.when(offset == blocks * 256)
        def _(keys=blocks * 256):
            @pl.loop(0, tiles)
            def _(t):
                where = pl.ds(pl.multiple_of(t * TILE, TILE), TILE)
                tile = jnp.concatenate(stack_heads(query[0, where, :]) + stack_heads(dquery[0]), axis=0)
                weights = jnp.exp2(scores_of(tile, kbuf[slot, :keys, :HEAD_SIZE])).astype(BF16)
                mixed = jnp.dot(weights, vbuf[:keys, :], preferred_element_type=F32)
                total = mixed[:, HEAD_SIZE:]
                least[...] = jnp.minimum(least[...], smallest(total))
                most[...] = jnp.maximum(most[...], largest(total))
                value = (mixed[:, :HEAD_SIZE] * (1.0 / total)).astype(BF16)
                stats = jnp.log2(total)
                n = HEADS * TILE
                put(where, value[:n], stats[:n], TILE)
                put_decode(value[n:], stats[n:])

    fine = jnp.logical_and(jnp.min(least[...]) >= LOW, jnp.max(most[...]) <= HIGH)

    @pl.when(jnp.logical_not(fine))
    def _():
        def exact(tile):
            def block(b, carry):
                top, mixed = carry
                keys = pl.ds(pl.multiple_of(b * 256, 256), 256)
                scores = scores_of(tile, kbuf[slot, keys, :HEAD_SIZE])
                now = jnp.maximum(jnp.max(scores, axis=1, keepdims=True), top)
                weights = jnp.exp2(scores - now).astype(BF16)
                more = jnp.dot(weights, vbuf[keys, :], preferred_element_type=F32)
                return now, mixed * jnp.exp2(top - now) + more

            n = tile.shape[0]
            first = (jnp.full((n, 1), NEG, F32), jnp.zeros((n, PAIR), F32))
            top, mixed = lax.fori_loop(0, lax.shift_right_logical(offset, 8), block, first)
            total = mixed[:, HEAD_SIZE:]
            return (mixed[:, :HEAD_SIZE] / total).astype(BF16), top + jnp.log2(total)

        @pl.loop(0, FINAL_LENGTH // 32)
        def _(t):
            where = pl.ds(pl.multiple_of(t * 32, 32), 32)
            put(where, *exact(jnp.concatenate(stack_heads(query[0, where, :]), axis=0)), 32)

        put_decode(*exact(jnp.concatenate(stack_heads(dquery[0]), axis=0)))


def prior(meta, owner, query, dquery, mine, theirs, before, first, n):
    def at(i, ids, offs, lens, owner):
        return (first + i, 0, 0)

    def decode_at(i, ids, offs, lens, owner):
        return (owner[ids[3] * LOCAL + first + i], 0, 0)

    shapes = [
        ((LOCAL, FINAL_LENGTH, HEADS * HEAD_SIZE), BF16),
        ((LOCAL, FINAL_LENGTH, HEAD_SIZE), F32),
        ((LOCAL, DROWS, HEADS * HEAD_SIZE), BF16),
        ((LOCAL, DROWS, HEAD_SIZE), F32),
    ]
    return call(
        functools.partial(prior_kernel, first=first),
        (*meta, owner),
        (query, dquery, mine, theirs, *before),
        [pltpu.HBM(*s) for s in shapes[:2]] + [jax.ShapeDtypeStruct(*s) for s in shapes[2:]],
        [
            pltpu.VMEM((2, CONTEXT_LENGTH, PAIR), BF16),
            pltpu.VMEM((CONTEXT_LENGTH, PAIR), BF16),
            pltpu.VMEM((8, HEAD_SIZE), F32),
            pltpu.VMEM((8, HEAD_SIZE), F32),
            pltpu.SemaphoreType.DMA((2, 2)),
        ],
        grid=(n,),
        specs=[
            pl.BlockSpec((1, FINAL_LENGTH, HEADS * HEAD_SIZE), at),
            pl.BlockSpec((1, DROWS, HEADS * HEAD_SIZE), decode_at),
            HBM,
            HBM,
        ]
        + [ANY] * len(before),
        out_specs=[pl.BlockSpec((1,) + s[1:], at) for s, _ in shapes],
        aliases={8 + i: i for i in range(len(before))},
        flops=n * 3 * 10**9,
        moved=n * 2 * 10**6,
    )


def load_fresh(ids, pieces, fbuf, sem):
    copies, base = [], 0
    for c in range(2):
        q = pieces[2 * c].shape[0]
        for i, core in enumerate((ids[2], 1 - ids[2])):
            target = fbuf.at[pl.ds(pl.multiple_of(base + core * q, G), q)]
            copies.append(pltpu.make_async_copy(pieces[2 * c + i], target, sem.at[2 * c + i]))
        base += 2 * q
    for c in copies:
        c.start()
    fbuf[base:, :] = jnp.zeros((FINAL_LENGTH, PAIR), BF16)
    for c in copies:
        c.wait()


def fresh_kernel(ids, offs, lens, *refs):
    pieces = refs[:4]
    query, prior_out, prior_stat, out, fbuf, vbuf, *bounds, sem = refs[4:]
    p = pl.program_id(0)

    @pl.when(p == 0)
    def _():
        load_fresh(ids, pieces, fbuf, sem)
        vbuf[:, HEAD_SIZE:] = jnp.ones((FINAL_LENGTH, HEAD_SIZE), BF16)

    starts, _, _ = plan(ids, offs, lens)
    start = jnp.int32(0)
    for i in range(1, LOCAL):
        start = jnp.where(p == i, starts[i], start)
    at = ids[3] * LOCAL + p
    count = lens[at] - offs[at]
    where_keys = pl.ds(pl.multiple_of(start * G, G), FINAL_LENGTH)
    vbuf[:, :HEAD_SIZE] = fbuf[where_keys, HEAD_SIZE:]
    n = HEADS * TILE
    least, most = bounds
    least[...] = jnp.full(least.shape, 1.0, F32)
    most[...] = jnp.full(most.shape, 1.0, F32)

    for t in range(FINAL_LENGTH // TILE):
        where = slice(t * TILE, (t + 1) * TILE)

        @pl.when(count <= t * TILE)
        def _(where=where):
            out[0, where, :] = jnp.zeros((TILE, HEADS * HEAD_SIZE), BF16)

        @pl.when(count > t * TILE)
        def _(where=where, t=t):
            seen = (t + 1) * TILE
            keys = pl.ds(pl.multiple_of(start * G, G), seen)
            row = lax.broadcasted_iota(jnp.int32, (TILE, seen), 0) + t * TILE
            allowed = (lax.broadcasted_iota(jnp.int32, (TILE, seen), 1) <= row).astype(F32)
            scores = scores_of(jnp.concatenate(stack_heads(query[0, where, :]), axis=0), fbuf[keys, :HEAD_SIZE])
            weights = jnp.concatenate(
                [
                    (jnp.exp2(scores[h * TILE : (h + 1) * TILE]) * allowed).astype(BF16)
                    for h in range(HEADS)
                ],
                axis=0,
            )
            mixed = jnp.dot(weights, vbuf[:seen, :], preferred_element_type=F32)
            keep = lax.broadcasted_iota(jnp.int32, (TILE, HEAD_SIZE), 0) + t * TILE < count
            before = jnp.exp2(prior_stat[0, where, :])
            low, high = least[...], most[...]
            for h in range(HEADS):
                lanes = slice(h * HEAD_SIZE, (h + 1) * HEAD_SIZE)
                stack = slice(h * TILE, (h + 1) * TILE)
                share = before[:, h : h + 1]
                total = mixed[stack, HEAD_SIZE:] + share
                low, high = jnp.minimum(low, smallest(total)), jnp.maximum(high, largest(total))
                old = prior_out[0, where, lanes].astype(F32)
                value = (mixed[stack, :HEAD_SIZE] + old * share) * (1.0 / total)
                out[0, where, lanes] = jnp.where(keep, value, 0.0).astype(BF16)
            least[...], most[...] = low, high

    fine = jnp.logical_and(jnp.min(least[...]) >= LOW, jnp.max(most[...]) <= HIGH)

    @pl.when(jnp.logical_not(fine))
    def _():
        some = 32
        keys = pl.ds(pl.multiple_of(start * G, G), FINAL_LENGTH)
        n = HEADS * some

        @pl.loop(0, FINAL_LENGTH // some)
        def _(t):
            where = pl.ds(pl.multiple_of(t * some, some), some)
            position = lax.bitwise_and(lax.broadcasted_iota(jnp.int32, (n, FINAL_LENGTH), 0), some - 1)
            ahead = lax.broadcasted_iota(jnp.int32, (n, FINAL_LENGTH), 1) - position
            scores = scores_of(jnp.concatenate(stack_heads(query[0, where, :]), axis=0), fbuf[keys, :HEAD_SIZE])
            scores = jnp.where(ahead <= t * some, scores, NEG)
            before = gather_column(prior_stat[0, where, :])
            top = jnp.maximum(jnp.max(scores, axis=1, keepdims=True), before)
            weights = jnp.exp2(scores - top).astype(BF16)
            share = jnp.exp2(before - top)
            mixed = jnp.dot(weights, vbuf[...], preferred_element_type=F32)
            total = mixed[:, HEAD_SIZE:] + share
            keep = lax.broadcasted_iota(jnp.int32, (some, HEAD_SIZE), 0) + t * some < count
            for h in range(HEADS):
                lanes = slice(h * HEAD_SIZE, (h + 1) * HEAD_SIZE)
                stack = slice(h * some, (h + 1) * some)
                old = prior_out[0, where, lanes].astype(F32)
                value = (mixed[stack, :HEAD_SIZE] + old * share[stack]) / total[stack]
                out[0, where, lanes] = jnp.where(keep, value, 0.0).astype(BF16)


def fresh(meta, pieces, query, prior_out, prior_stat):
    def at(p, ids, offs, lens):
        return (p, 0, 0)

    wide = pl.BlockSpec((1, FINAL_LENGTH, HEADS * HEAD_SIZE), at)
    return call(
        fresh_kernel,
        meta,
        (*pieces, query, prior_out, prior_stat),
        jax.ShapeDtypeStruct((LOCAL, FINAL_LENGTH, HEADS * HEAD_SIZE), BF16),
        [
            pltpu.VMEM(((LOCAL + 1) * FINAL_LENGTH, PAIR), BF16),
            pltpu.VMEM((FINAL_LENGTH, PAIR), BF16),
            pltpu.VMEM((8, HEAD_SIZE), F32),
            pltpu.VMEM((8, HEAD_SIZE), F32),
            pltpu.SemaphoreType.DMA((4,)),
        ],
        grid=(LOCAL,),
        specs=[ANY] * 4 + [wide, wide, pl.BlockSpec((1, FINAL_LENGTH, HEAD_SIZE), at)],
        out_specs=wide,
        flops=4 * 10**9,
        moved=10**7,
    )


def decode_kernel(ids, offs, lens, owner, *refs):
    pieces = refs[:4]
    query, recent, prior_out, prior_stat, out, fbuf, sem = refs[4:]
    load_fresh(ids, pieces, fbuf, sem)
    starts, _, _ = plan(ids, offs, lens)
    n = HEADS * DROWS
    step = lax.bitwise_and(lax.broadcasted_iota(jnp.int32, (n, DROWS), 0), DROWS - 1)
    later = lax.broadcasted_iota(jnp.int32, (n, DROWS), 1) > step
    column = lax.broadcasted_iota(jnp.int32, (n, FINAL_LENGTH), 1)
    for p in range(LOCAL):
        i = ids[3] * LOCAL + p
        slot = owner[i]
        keys = pl.ds(pl.multiple_of(starts[p] * G, G), FINAL_LENGTH)
        tile = jnp.concatenate(stack_heads(query[slot]), axis=0)
        block = scores_of(tile, fbuf[keys, :HEAD_SIZE])
        block = jnp.where(column < lens[i] - offs[i], block, NEG)
        near = scores_of(tile, recent[slot, :, :HEAD_SIZE])
        near = jnp.where(later, NEG, near)
        before = gather_column(prior_stat[p])
        top = jnp.maximum(jnp.max(block, axis=1, keepdims=True), jnp.max(near, axis=1, keepdims=True))
        top = jnp.maximum(top, before)
        block_weights = jnp.exp2(block - top)
        near_weights = jnp.exp2(near - top)
        share = jnp.exp2(before - top)
        total = (
            jnp.sum(block_weights, axis=1, keepdims=True)
            + jnp.sum(near_weights, axis=1, keepdims=True)
            + share
        )
        mixed = jnp.dot(block_weights.astype(BF16), fbuf[keys, HEAD_SIZE:], preferred_element_type=F32)
        mixed = mixed + jnp.dot(
            near_weights.astype(BF16), recent[slot, :, HEAD_SIZE:], preferred_element_type=F32
        )
        for h in range(HEADS):
            lanes = slice(h * HEAD_SIZE, (h + 1) * HEAD_SIZE)
            stack = slice(h * DROWS, (h + 1) * DROWS)
            value = (mixed[stack] + prior_out[p, :, lanes].astype(F32) * share[stack]) / total[stack]
            out[slot, :, lanes] = value[:STEPS].astype(BF16)


def decode(meta, owner, pieces, query, recent, prior_out, prior_stat):
    return call(
        decode_kernel,
        (*meta, owner),
        (*pieces, query, recent, prior_out, prior_stat),
        jax.ShapeDtypeStruct((LOCAL, STEPS, HEADS * HEAD_SIZE), BF16),
        [pltpu.VMEM(((LOCAL + 1) * FINAL_LENGTH, PAIR), BF16), pltpu.SemaphoreType.DMA((4,))],
        specs=[ANY] * 4 + [VMEM] * 4,
        out_specs=VMEM,
        flops=10**8,
        moved=2 * 10**6,
    )


def exchange(value):
    return lax.all_to_all(value, "grp", split_axis=0, concat_axis=0, tiled=True)


def permute(value, way):
    return lax.ppermute(value, "tp", way)


def after(value, *others):
    return lax.optimization_barrier((value, *others))[0]


def spread_sums(sent, ways):
    arrived = [None] * 3
    for i in ORDER:
        arrived[i] = permute(sent[i], ways[i])
    return arrived


def rest_of_keys(meta, hid, weight, table, base, q):
    other_half = permute(send_half(meta, hid, weight, base, q), SIBLING)
    local, *sent = keep_half(meta, hid, weight, other_half, base, q)
    kept, *sent = middle(meta[0], local, spread_sums(sent, FIRST), q)
    new = finish(meta, kept, spread_sums(sent, SECOND), rope_rows(meta, table, base, q), base, q)
    return new, permute(new, SIBLING)


def per_device(
    hidden_rows,
    key_value_weight,
    prefill_query,
    earlier_cache,
    stretch_offset,
    prompt_length,
    decode_owner,
    decode_query,
    decode_kv,
):
    lane = lax.axis_index("tp")
    group = lax.axis_index("grp")
    ids = jnp.stack([lane // 4, lane // 2 % 2, lane % 2, group]).astype(jnp.int32)
    meta = (ids, stretch_offset, prompt_length)
    table = jnp.asarray(rope_table())
    hid = hidden_rows.reshape(LOCAL * FINAL_LENGTH, -1)
    cache = earlier_cache.reshape(LOCAL, PART, PAIR)
    hid, key_value_weight, prefill_query = (
        pltpu.with_memory_space_constraint(a, pltpu.HBM) for a in (hid, key_value_weight, prefill_query)
    )
    q = ROOM // 2

    other_half = permute(send_half(meta, hid, key_value_weight, 0, q), SIBLING)
    other_cache = permute(cache, SIBLING)
    recent = lax.dynamic_slice_in_dim(decode_kv, (lane // 2) * PAIR, PAIR, 2)
    asked = exchange(jnp.concatenate([decode_query, recent], axis=2))

    local, *sent = keep_half(meta, hid, key_value_weight, other_half, 0, q)
    arrived = spread_sums(sent, FIRST)

    asked = jnp.pad(after(asked, local), ((0, 0), (0, DROWS - STEPS), (0, 0)))
    dquery = asked[..., : HEADS * HEAD_SIZE]
    recent = asked[..., HEADS * HEAD_SIZE :]
    turn = rope_rows(meta, after(table, local), 0, q)
    before = prior(meta, decode_owner, prefill_query, dquery, cache, other_cache, (), 0, 3)
    blocks = lax.shift_right_logical(after(prompt_length, before[3]) - stretch_offset + (G - 1), 4)
    most = jnp.max(jnp.sum(blocks.reshape(-1, LOCAL), axis=1)) * G
    more = LOCAL * FINAL_LENGTH - ROOM
    rest = lax.cond(
        most > ROOM,
        lambda *a: rest_of_keys(a[:3], *a[3:], ROOM, more // 2),
        lambda *a: (jnp.zeros((more // 2, PAIR), BF16),) * 2,
        *meta,
        hid,
        key_value_weight,
        table,
    )
    before = prior(meta, decode_owner, prefill_query, dquery, cache, other_cache, before, 3, 3)

    kept, *sent = middle(ids, after(local, rest[0]), arrived, q)
    arrived = spread_sums(sent, SECOND)
    before = prior(meta, decode_owner, prefill_query, dquery, cache, other_cache, before, 6, 2)
    prior_out, prior_stat = (pltpu.with_memory_space_constraint(a, pltpu.HBM) for a in before[:2])
    prior_dout, prior_dstat = before[2:]
    new = finish(meta, after(kept, prior_dstat), arrived, turn, 0, q)
    pieces = (new, permute(new, SIBLING), *rest)

    answer = decode(meta, decode_owner, pieces, dquery, recent, prior_dout, prior_dstat)
    decode_out = exchange(answer)
    prefill_out = fresh(meta, pieces, prefill_query, prior_out, prior_stat)
    return (prefill_out, decode_out)


def solution(mesh):
    in_specs = (
        P("grp", None, "tp"),
        P("tp", None),
        P("grp", None, "tp"),
        P("grp", "tp", None, None),
        P(),
        P(),
        P(),
        P("grp", None, "tp"),
        P("grp", None, None),
    )
    out_specs = (P("grp", None, "tp"), P("grp", None, "tp"))
    return jax.shard_map(
        per_device, mesh=mesh, in_specs=in_specs, out_specs=out_specs, check_vma=False
    )
```

```python
import functools
import math

import jax
import jax.numpy as jnp
import numpy as np
from jax import lax
from jax.experimental import pallas as pl
from jax.experimental.pallas import tpu as pltpu
from jax.sharding import PartitionSpec as P

HEAD_SIZE = 128
PAIR = 2 * HEAD_SIZE
LOCAL = 8
FINAL_LENGTH = 256
CONTEXT_LENGTH = 1024
PART = 512
STEPS = 4
HEADS = 8
ROPE_BASE = 500000.0
G = 16
DROWS = 16
TILE = 128
SCALE2 = HEAD_SIZE**-0.5 * math.log2(math.e)
NEG = -1e30
F32 = jnp.float32
BF16 = jnp.bfloat16
ANY = pl.BlockSpec(memory_space=pl.ANY)
VMEM = pl.BlockSpec(memory_space=pltpu.VMEM)
HBM = pl.BlockSpec(memory_space=pltpu.HBM)
SMALL = 26
ROOM = 1664
LOW, HIGH = 2.0**-100, 2.0**100


def pairs(*moves):
    out = []
    for x in range(4):
        for z in range(2):
            for core in range(2):
                if moves[core] is None:
                    continue
                dx, dz, dc = moves[core]
                out.append((x * 4 + z * 2 + core, (x + dx) % 4 * 4 + (z + dz) % 2 * 2 + (core + dc) % 2))
    return out


SIBLING = pairs((0, 0, 1), (0, 0, 1))
FIRST = [pairs((1, 0, 0), (0, 1, 0)), pairs((2, 0, 0), None), pairs((3, 0, 0), (0, 1, 0))]
SECOND = [pairs((0, 1, 0), (1, 0, 0)), pairs(None, (2, 0, 0)), pairs(None, (3, 0, 0))]
ORDER = (0, 2, 1)


def rope_table():
    half = HEAD_SIZE // 2
    freq = ROPE_BASE ** (np.arange(half, dtype=np.float64) * (-2.0 / HEAD_SIZE))
    angle = np.arange(CONTEXT_LENGTH + FINAL_LENGTH, dtype=np.float64)[:, None] * freq
    cosine, sine = np.cos(angle), np.sin(angle)
    return np.concatenate([cosine, cosine, -sine, sine], axis=1).astype(np.float32)


def plan(ids, offs, lens):
    starts, counts, at = [], [], jnp.int32(0)
    for p in range(LOCAL):
        i = ids[3] * LOCAL + p
        count = lax.shift_right_logical(lens[i] - offs[i] + (G - 1), 4)
        starts.append(at)
        counts.append(count)
        at = at + count
    return starts, counts, at


def ragged(starts, counts, first_block, blocks, copy):
    for p in range(LOCAL):
        low = jnp.maximum(starts[p], first_block)
        high = jnp.minimum(starts[p] + counts[p], first_block + blocks)
        n = jnp.maximum(high - low, 0)
        for bit in range(4, -1, -1):
            done = lax.shift_left(lax.shift_right_logical(n, bit + 1), bit + 1)

            @pl.when(lax.bitwise_and(n, 1 << bit) != 0)
            def _(p=p, bit=bit, low=low, done=done):
                copy(p, bit, low + done - starts[p], low + done - first_block, 1 << bit)


def rows(block, count):
    return pl.ds(pl.multiple_of(block * G, G), count * G)


def project(ids, offs, lens, hid, w, hbuf, wbuf, hsem, wsem, first_block, blocks):
    starts, counts, total = plan(ids, offs, lens)

    def hidden_copy(p, bit, source, target, count):
        return pltpu.make_async_copy(
            hid.at[rows(p * (FINAL_LENGTH // G) + source, count)],
            hbuf.at[rows(target, count)],
            hsem.at[p, bit],
        )

    def weight_copy(d):
        first = lax.rem(ids[0] + d, 4) * (2 * PAIR)
        return pltpu.make_async_copy(
            w.at[:, pl.ds(pl.multiple_of(first, 2 * PAIR), 2 * PAIR)], wbuf.at[d], wsem.at[d]
        )

    weight_copy(0).start()
    ragged(starts, counts, first_block, blocks, lambda *a: hidden_copy(*a).start())
    for d in range(1, 4):
        weight_copy(d).start()

    @pl.loop(jnp.clip(total - first_block, 0, blocks), blocks)
    def _(b):
        hbuf[rows(b, 1), :] = jnp.zeros((G, hbuf.shape[1]), BF16)

    ragged(starts, counts, first_block, blocks, lambda *a: hidden_copy(*a).wait())

    def product(d, e, where):
        if e == 0 and where.start == 0:
            weight_copy(d).wait()
        columns = pl.ds(pl.multiple_of(lax.rem(ids[1] + e, 2) * PAIR, PAIR), PAIR)
        return jnp.dot(hbuf[where, :], wbuf[d, :, columns], preferred_element_type=F32)

    return product


def row_tiles(q):
    n = next(n for n in (256, 224, 208, 192, 176, 160, 128, 64) if q % n == 0)
    return [slice(r, r + n) for r in range(0, q, n)]


def send_kernel(ids, offs, lens, hid, w, out, hbuf, wbuf, obuf, hsem, wsem, osem, *, base, q):
    first = base // G + (1 - ids[2]) * (q // G)
    product = project(ids, offs, lens, hid, w, hbuf, wbuf, hsem, wsem, first, q // G)
    for j in range(8):
        for where in row_tiles(q):
            obuf[j, where, :] = product(j // 2, j % 2, where).astype(BF16)
        pltpu.make_async_copy(obuf.at[j], out.at[j], osem.at[j]).start()
    for j in range(8):
        pltpu.make_async_copy(obuf.at[j], out.at[j], osem.at[j]).wait()


def keep_kernel(ids, offs, lens, hid, w, other, local, s1, s2, s3, hbuf, wbuf, rbuf, obuf, hsem, wsem, rsem, osem, *, base, q):
    core = ids[2]
    product = project(ids, offs, lens, hid, w, hbuf, wbuf, hsem, wsem, base // G + core * (q // G), q // G)
    for j in range(8):
        pltpu.make_async_copy(other.at[j], rbuf.at[j], rsem.at[j]).start()

    def leave(j, verb):
        d, e = j // 2, j % 2
        along = (local, s1, s2, s3)[d].at[e]
        across = local.at[d] if e == 0 else (s1 if d < 2 else s3).at[d % 2]
        for c, target in enumerate((along, across)):

            @pl.when(core == c)
            def _(target=target):
                copy = pltpu.make_async_copy(obuf.at[j], target, osem.at[j])
                copy.start() if verb == "start" else copy.wait()

    for j in range(8):
        for where in row_tiles(q):
            value = product(j // 2, j % 2, where)
            if where.start == 0:
                pltpu.make_async_copy(other.at[j], rbuf.at[j], rsem.at[j]).wait()
            obuf[j, where, :] = (value + rbuf[j, where, :].astype(F32)).astype(BF16)
        leave(j, "start")
    for j in range(8):
        leave(j, "wait")


def call(kernel, prefetched, operands, out_shape, scratch=(), specs=None, out_specs=None, grid=(), flops=0, moved=0, aliases=None, vmem=SMALL):
    n = len(prefetched)
    return pl.pallas_call(
        kernel,
        out_shape=out_shape,
        grid_spec=pltpu.PrefetchScalarGridSpec(
            num_scalar_prefetch=n,
            grid=grid,
            in_specs=specs if specs is not None else [ANY] * len(operands),
            out_specs=out_specs if out_specs is not None else jax.tree.map(lambda _: ANY, out_shape),
            scratch_shapes=list(scratch),
        ),
        compiler_params=pltpu.CompilerParams(vmem_limit_bytes=vmem * 2**20),
        input_output_aliases=aliases or {},
        cost_estimate=pl.CostEstimate(flops=flops, bytes_accessed=moved, transcendentals=0),
    )(*prefetched, *operands)


def half_scratch(q):
    return [pltpu.VMEM((q, 1024), BF16), pltpu.VMEM((4, 1024, 2 * PAIR), BF16)]


def half_semaphores():
    return [pltpu.SemaphoreType.DMA((LOCAL, 5)), pltpu.SemaphoreType.DMA((4,))]


def send_half(meta, hid, w, base, q):
    return call(
        functools.partial(send_kernel, base=base, q=q),
        meta,
        (hid, w),
        jax.ShapeDtypeStruct((8, q, PAIR), BF16),
        half_scratch(q)
        + [pltpu.VMEM((8, q, PAIR), BF16)]
        + half_semaphores()
        + [pltpu.SemaphoreType.DMA((8,))],
        specs=[HBM, HBM],
        flops=2 * q * 1024 * 2048,
        moved=2 * (q * 1024 + 1024 * 2048 + q * 2048),
    )


def keep_half(meta, hid, w, other, base, q):
    return call(
        functools.partial(keep_kernel, base=base, q=q),
        meta,
        (hid, w, other),
        [pltpu.HBM((n, q, PAIR), BF16) for n in (4, 2, 2, 2)],
        half_scratch(q)
        + [pltpu.VMEM((8, q, PAIR), BF16)] * 2
        + half_semaphores()
        + [pltpu.SemaphoreType.DMA((8,))] * 2,
        specs=[HBM, HBM, ANY],
        flops=2 * q * 1024 * 2048,
        moved=2 * (q * 1024 + 1024 * 2048 + 2 * q * 2048),
    )


def middle_kernel(ids, local, r1, r2, r3, kept, s1, s2, s3):
    @pl.when(ids[2] == 0)
    def _():
        for e, out in ((0, kept), (1, s1)):
            total = (local[e].astype(F32) + r1[e].astype(F32)) + (r2[e].astype(F32) + r3[e].astype(F32))
            out[...] = total.astype(out.dtype)

    @pl.when(ids[2] == 1)
    def _():
        for d, out in enumerate((kept, s1, s2, s3)):
            arrived = (r1 if d < 2 else r3)[d % 2]
            out[...] = (local[d].astype(F32) + arrived.astype(F32)).astype(out.dtype)


def middle(ids, local, arrived, q):
    n = 2

    def three(i, ids):
        return (0, i, 0)

    def two(i, ids):
        return (i, 0)

    return call(
        middle_kernel,
        (ids,),
        (local, *arrived),
        [jax.ShapeDtypeStruct((q, PAIR), t) for t in (F32, BF16, BF16, BF16)],
        grid=(n,),
        specs=[pl.BlockSpec((a.shape[0], q // n, PAIR), three) for a in (local, *arrived)],
        out_specs=[pl.BlockSpec((q // n, PAIR), two)] * 4,
        moved=2 * PAIR * q * 15,
        flops=PAIR * q * 8,
    )


def rope_rows_kernel(ids, offs, lens, table, out, sem, *, base, q):
    starts, counts, _ = plan(ids, offs, lens)
    for verb in ("start", "wait"):

        def copy(p, bit, source, target, count, verb=verb):
            position = lax.shift_right_logical(offs[ids[3] * LOCAL + p], 4)
            c = pltpu.make_async_copy(
                table.at[rows(position + source, count)], out.at[rows(target, count)], sem.at[p, bit]
            )
            c.start() if verb == "start" else c.wait()

        ragged(starts, counts, base // G + ids[2] * (q // G), q // G, copy)


def rope_rows(meta, table, base, q):
    return call(
        functools.partial(rope_rows_kernel, base=base, q=q),
        meta,
        (table,),
        jax.ShapeDtypeStruct((q, PAIR), F32),
        [pltpu.SemaphoreType.DMA((LOCAL, 5))],
        specs=[HBM],
        moved=q * PAIR * 8,
    )


def finish_kernel(ids, offs, lens, kept, r1, r2, r3, turn, out, *, base, q):
    _, _, total = plan(ids, offs, lens)
    valid = (total - base // G - ids[2] * (q // G)) * G

    def put(value):
        row = lax.broadcasted_iota(jnp.int32, (q, HEAD_SIZE), 0)
        key = value[:, :HEAD_SIZE]
        key = key * turn[:, :HEAD_SIZE] + pltpu.roll(key, HEAD_SIZE // 2, 1) * turn[:, HEAD_SIZE:]
        out[:, :HEAD_SIZE] = jnp.where(row < valid, key, 0.0).astype(BF16)
        out[:, HEAD_SIZE:] = value[:, HEAD_SIZE:].astype(BF16)

    @pl.when(ids[2] == 0)
    def _():
        put(kept[...] + r1[...].astype(F32))

    @pl.when(ids[2] == 1)
    def _():
        put((kept[...] + r1[...].astype(F32)) + (r2[...].astype(F32) + r3[...].astype(F32)))


def finish(meta, kept, arrived, turn, base, q):
    return call(
        functools.partial(finish_kernel, base=base, q=q),
        meta,
        (kept, *arrived, turn),
        jax.ShapeDtypeStruct((q, PAIR), BF16),
        specs=[VMEM] * 5,
        out_specs=VMEM,
        moved=q * PAIR * 16,
        flops=q * PAIR * 4,
    )


def stack_heads(tile):
    return [tile[:, h * HEAD_SIZE : (h + 1) * HEAD_SIZE] for h in range(HEADS)]


def scores_of(query, keys):
    return lax.dot_general(query, keys, (((1,), (1,)), ((), ())), preferred_element_type=F32) * SCALE2


def spread(column, n):
    lane = lax.broadcasted_iota(jnp.int32, (n, HEAD_SIZE), 1)
    out = jnp.zeros((n, HEAD_SIZE), F32)
    for h in range(HEADS):
        out = jnp.where(lane == h, column[h * n : (h + 1) * n], out)
    return out


def smallest(value):
    return jnp.min(value.reshape(-1, 8, HEAD_SIZE), axis=0)


def largest(value):
    return jnp.max(value.reshape(-1, 8, HEAD_SIZE), axis=0)


def gather_column(stats):
    return jnp.concatenate([stats[:, h : h + 1] for h in range(HEADS)], axis=0)


def tile_rows(t):
    return slice(t * TILE, (t + 1) * TILE)


def when_tile(count, t):
    return pl.when(count > t * TILE)


TILES = FINAL_LENGTH // TILE


def prior_kernel(ids, offs, lens, owner, dquery, query, mine, theirs, *refs, first, n):
    (*outs, qbuf, kbuf, vbuf, obuf, sbuf, dobuf, dsbuf, least, most, qsem, ksem, osem, dsem) = refs
    out, stat, dout, dstat = outs[-4:]
    core = ids[2]

    def place(i):
        at = ids[3] * LOCAL + first + i
        return offs[at], lens[at] - offs[at], owner[at]

    def query_copy(i, t):
        return pltpu.make_async_copy(query.at[first + i, tile_rows(t)], qbuf.at[i, tile_rows(t)], qsem.at[i, t])

    def key_copy(i, part):
        here = core if part == 0 else 1 - core
        target = kbuf.at[i, pl.ds(pl.multiple_of(here * PART, PART), PART)]
        return pltpu.make_async_copy((mine, theirs)[part].at[first + i], target, ksem.at[i, part])

    def when_part(offset, part):
        here = core if part == 0 else 1 - core
        return pl.when(jnp.logical_or(here == 0, offset > PART))

    def out_copies(i, t):
        return (
            pltpu.make_async_copy(obuf.at[i, tile_rows(t)], out.at[first + i, tile_rows(t)], osem.at[i, t, 0]),
            pltpu.make_async_copy(sbuf.at[i, tile_rows(t)], stat.at[first + i, tile_rows(t)], osem.at[i, t, 1]),
        )

    def decode_copies(i):
        return (
            pltpu.make_async_copy(dobuf.at[i], dout.at[first + i], dsem.at[i, 0]),
            pltpu.make_async_copy(dsbuf.at[i], dstat.at[first + i], dsem.at[i, 1]),
        )

    for i in range(n):
        offset, count, _ = place(i)
        for part in range(2):
            when_part(offset, part)(lambda i=i, part=part: key_copy(i, part).start())
        for t in range(TILES):
            when_tile(count, t)(lambda i=i, t=t: query_copy(i, t).start())
    vbuf[:, HEAD_SIZE:] = jnp.ones((CONTEXT_LENGTH, HEAD_SIZE), BF16)

    @pl.loop(0, n)
    def _(i):
        offset, count, slot = place(i)
        for part in range(2):
            when_part(offset, part)(lambda part=part: key_copy(i, part).wait())
        for t in range(TILES):
            when_tile(count, t)(lambda t=t: query_copy(i, t).wait())
        least[...] = jnp.full(least.shape, 1.0, F32)
        most[...] = jnp.full(most.shape, 1.0, F32)

        def put(where, value, stats, rows_of_head):
            for h in range(HEADS):
                lanes = slice(h * HEAD_SIZE, (h + 1) * HEAD_SIZE)
                obuf[i, where, lanes] = value[h * rows_of_head : (h + 1) * rows_of_head]
            sbuf[i, where, :] = spread(stats, rows_of_head)

        def put_decode(value, stats):
            for h in range(HEADS):
                dobuf[i, :, h * HEAD_SIZE : (h + 1) * HEAD_SIZE] = value[h * DROWS : (h + 1) * DROWS]
            dsbuf[i] = spread(stats, DROWS)

        for blocks in range(1, 5):

            @pl.when(offset == blocks * 256)
            def _(keys=blocks * 256):
                vbuf[:keys, :HEAD_SIZE] = kbuf[i, :keys, HEAD_SIZE:]
                for t in range(TILES):

                    @when_tile(count, t)
                    def _(t=t):
                        tile = stack_heads(qbuf[i, tile_rows(t), :])
                        if t == 0:
                            tile = tile + stack_heads(dquery[slot])
                        tile = jnp.concatenate(tile, axis=0)
                        weights = jnp.exp2(scores_of(tile, kbuf[i, :keys, :HEAD_SIZE])).astype(BF16)
                        mixed = jnp.dot(weights, vbuf[:keys, :], preferred_element_type=F32)
                        total = mixed[:, HEAD_SIZE:]
                        least[...] = jnp.minimum(least[...], smallest(total))
                        most[...] = jnp.maximum(most[...], largest(total))
                        value = (mixed[:, :HEAD_SIZE] * (1.0 / total)).astype(BF16)
                        stats = jnp.log2(total)
                        m = HEADS * TILE
                        put(tile_rows(t), value[:m], stats[:m], TILE)
                        if t == 0:
                            put_decode(value[m:], stats[m:])

        fine = jnp.logical_and(jnp.min(least[...]) >= LOW, jnp.max(most[...]) <= HIGH)

        @pl.when(jnp.logical_not(fine))
        def _():
            def exact(tile):
                def block(b, carry):
                    top, mixed = carry
                    keys = pl.ds(pl.multiple_of(b * 256, 256), 256)
                    scores = scores_of(tile, kbuf[i, keys, :HEAD_SIZE])
                    now = jnp.maximum(jnp.max(scores, axis=1, keepdims=True), top)
                    weights = jnp.exp2(scores - now).astype(BF16)
                    more = jnp.dot(weights, vbuf[keys, :], preferred_element_type=F32)
                    return now, mixed * jnp.exp2(top - now) + more

                m = tile.shape[0]
                start = (jnp.full((m, 1), NEG, F32), jnp.zeros((m, PAIR), F32))
                top, mixed = lax.fori_loop(0, lax.shift_right_logical(offset, 8), block, start)
                total = mixed[:, HEAD_SIZE:]
                return (mixed[:, :HEAD_SIZE] / total).astype(BF16), top + jnp.log2(total)

            @pl.loop(0, lax.shift_right_logical(count + 31, 5))
            def _(t):
                where = pl.ds(pl.multiple_of(t * 32, 32), 32)
                put(where, *exact(jnp.concatenate(stack_heads(qbuf[i, where, :]), axis=0)), 32)

            put_decode(*exact(jnp.concatenate(stack_heads(dquery[slot]), axis=0)))

        for t in range(TILES):
            when_tile(count, t)(lambda t=t: [c.start() for c in out_copies(i, t)] and None)
        for c in decode_copies(i):
            c.start()

    for i in range(n):
        _, count, _ = place(i)
        for t in range(TILES):
            when_tile(count, t)(lambda i=i, t=t: [c.wait() for c in out_copies(i, t)] and None)
        for c in decode_copies(i):
            c.wait()


def prior(meta, owner, query, dquery, mine, theirs, before, first, n):
    wide, narrow = (FINAL_LENGTH, HEADS * HEAD_SIZE), (FINAL_LENGTH, HEAD_SIZE)
    dwide, dnarrow = (DROWS, HEADS * HEAD_SIZE), (DROWS, HEAD_SIZE)
    shapes = [(wide, BF16), (narrow, F32), (dwide, BF16), (dnarrow, F32)]
    return call(
        functools.partial(prior_kernel, first=first, n=n),
        (*meta, owner),
        (dquery, query, mine, theirs, *before),
        [pltpu.HBM((LOCAL, *s), t) for s, t in shapes],
        [
            pltpu.VMEM((n, *wide), BF16),
            pltpu.VMEM((n, CONTEXT_LENGTH, PAIR), BF16),
            pltpu.VMEM((CONTEXT_LENGTH, PAIR), BF16),
            pltpu.VMEM((n, *wide), BF16),
            pltpu.VMEM((n, *narrow), F32),
            pltpu.VMEM((n, *dwide), BF16),
            pltpu.VMEM((n, *dnarrow), F32),
            pltpu.VMEM((8, HEAD_SIZE), F32),
            pltpu.VMEM((8, HEAD_SIZE), F32),
            pltpu.SemaphoreType.DMA((n, TILES)),
            pltpu.SemaphoreType.DMA((n, 2)),
            pltpu.SemaphoreType.DMA((n, TILES, 2)),
            pltpu.SemaphoreType.DMA((n, 2)),
        ],
        specs=[VMEM] + [ANY] * (3 + len(before)),
        aliases={8 + i: i for i in range(len(before))},
        flops=n * 3 * 10**9,
        moved=n * 2 * 10**6,
    )


def load_fresh(ids, pieces, fbuf, sem):
    copies, base = [], 0
    for c in range(2):
        q = pieces[2 * c].shape[0]
        for i, core in enumerate((ids[2], 1 - ids[2])):
            target = fbuf.at[pl.ds(pl.multiple_of(base + core * q, G), q)]
            copies.append(pltpu.make_async_copy(pieces[2 * c + i], target, sem.at[2 * c + i]))
        base += 2 * q
    for c in copies:
        c.start()
    fbuf[base:, :] = jnp.zeros((FINAL_LENGTH, PAIR), BF16)
    for c in copies:
        c.wait()


def fresh_kernel(ids, offs, lens, *refs):
    pieces = refs[:4]
    query, prior_out, prior_stat, out, fbuf, vbuf, qbuf, pbuf, sbuf, obuf, least, most, sem, isem, osem = refs[4:]

    def count_of(p):
        at = ids[3] * LOCAL + p
        return lens[at] - offs[at]

    def in_copies(p, t):
        pairs_of = ((query, qbuf), (prior_out, pbuf), (prior_stat, sbuf))
        return [
            pltpu.make_async_copy(ref.at[p, tile_rows(t)], buf.at[p, tile_rows(t)], isem.at[p, t, i])
            for i, (ref, buf) in enumerate(pairs_of)
        ]

    def out_copy(p):
        return pltpu.make_async_copy(obuf.at[p], out.at[p], osem.at[p])

    for p in range(LOCAL):
        for t in range(TILES):
            when_tile(count_of(p), t)(lambda p=p, t=t: [c.start() for c in in_copies(p, t)] and None)
    load_fresh(ids, pieces, fbuf, sem)
    vbuf[:, HEAD_SIZE:] = jnp.ones((FINAL_LENGTH, HEAD_SIZE), BF16)

    def prompt(p, start):
        count = count_of(p)
        first_key = pl.multiple_of(start * G, G)
        vbuf[:, :HEAD_SIZE] = fbuf[pl.ds(first_key, FINAL_LENGTH), HEAD_SIZE:]
        least[...] = jnp.full(least.shape, 1.0, F32)
        most[...] = jnp.full(most.shape, 1.0, F32)

        for t in range(TILES):
            where = tile_rows(t)

            @pl.when(count <= t * TILE)
            def _(where=where):
                obuf[p, where, :] = jnp.zeros((TILE, HEADS * HEAD_SIZE), BF16)

            @when_tile(count, t)
            def _(where=where, t=t):
                for c in in_copies(p, t):
                    c.wait()
                seen = (t + 1) * TILE
                row = lax.broadcasted_iota(jnp.int32, (TILE, seen), 0) + t * TILE
                allowed = (lax.broadcasted_iota(jnp.int32, (TILE, seen), 1) <= row).astype(F32)
                tile = jnp.concatenate(stack_heads(qbuf[p, where, :]), axis=0)
                scores = scores_of(tile, fbuf[pl.ds(first_key, seen), :HEAD_SIZE])
                weights = jnp.concatenate(
                    [
                        (jnp.exp2(scores[h * TILE : (h + 1) * TILE]) * allowed).astype(BF16)
                        for h in range(HEADS)
                    ],
                    axis=0,
                )
                mixed = jnp.dot(weights, vbuf[:seen, :], preferred_element_type=F32)
                keep = lax.broadcasted_iota(jnp.int32, (TILE, HEAD_SIZE), 0) + t * TILE < count
                before = jnp.exp2(sbuf[p, where, :])
                low, high = least[...], most[...]
                for h in range(HEADS):
                    lanes = slice(h * HEAD_SIZE, (h + 1) * HEAD_SIZE)
                    stack = slice(h * TILE, (h + 1) * TILE)
                    share = before[:, h : h + 1]
                    total = mixed[stack, HEAD_SIZE:] + share
                    low, high = jnp.minimum(low, smallest(total)), jnp.maximum(high, largest(total))
                    old = pbuf[p, where, lanes].astype(F32)
                    value = (mixed[stack, :HEAD_SIZE] + old * share) * (1.0 / total)
                    obuf[p, where, lanes] = jnp.where(keep, value, 0.0).astype(BF16)
                least[...], most[...] = low, high

        fine = jnp.logical_and(jnp.min(least[...]) >= LOW, jnp.max(most[...]) <= HIGH)

        @pl.when(jnp.logical_not(fine))
        def _():
            some = 32
            n = HEADS * some

            @pl.loop(0, lax.shift_right_logical(count + (some - 1), 5))
            def _(t):
                where = pl.ds(pl.multiple_of(t * some, some), some)
                position = lax.bitwise_and(lax.broadcasted_iota(jnp.int32, (n, FINAL_LENGTH), 0), some - 1)
                ahead = lax.broadcasted_iota(jnp.int32, (n, FINAL_LENGTH), 1) - position
                tile = jnp.concatenate(stack_heads(qbuf[p, where, :]), axis=0)
                scores = scores_of(tile, fbuf[pl.ds(first_key, FINAL_LENGTH), :HEAD_SIZE])
                scores = jnp.where(ahead <= t * some, scores, NEG)
                before = gather_column(sbuf[p, where, :])
                top = jnp.maximum(jnp.max(scores, axis=1, keepdims=True), before)
                weights = jnp.exp2(scores - top).astype(BF16)
                share = jnp.exp2(before - top)
                mixed = jnp.dot(weights, vbuf[...], preferred_element_type=F32)
                total = mixed[:, HEAD_SIZE:] + share
                keep = lax.broadcasted_iota(jnp.int32, (some, HEAD_SIZE), 0) + t * some < count
                for h in range(HEADS):
                    lanes = slice(h * HEAD_SIZE, (h + 1) * HEAD_SIZE)
                    stack = slice(h * some, (h + 1) * some)
                    old = pbuf[p, where, lanes].astype(F32)
                    value = (mixed[stack, :HEAD_SIZE] + old * share[stack]) / total[stack]
                    obuf[p, where, lanes] = jnp.where(keep, value, 0.0).astype(BF16)

        out_copy(p).start()
        return start + lax.shift_right_logical(count + (G - 1), 4)

    lax.fori_loop(0, LOCAL, prompt, jnp.int32(0))
    for p in range(LOCAL):
        out_copy(p).wait()


def fresh(meta, pieces, query, prior_out, prior_stat):
    wide, narrow = (LOCAL, FINAL_LENGTH, HEADS * HEAD_SIZE), (LOCAL, FINAL_LENGTH, HEAD_SIZE)
    return call(
        fresh_kernel,
        meta,
        (*pieces, query, prior_out, prior_stat),
        pltpu.HBM(wide, BF16),
        [
            pltpu.VMEM(((LOCAL + 1) * FINAL_LENGTH, PAIR), BF16),
            pltpu.VMEM((FINAL_LENGTH, PAIR), BF16),
            pltpu.VMEM(wide, BF16),
            pltpu.VMEM(wide, BF16),
            pltpu.VMEM(narrow, F32),
            pltpu.VMEM(wide, BF16),
            pltpu.VMEM((8, HEAD_SIZE), F32),
            pltpu.VMEM((8, HEAD_SIZE), F32),
            pltpu.SemaphoreType.DMA((4,)),
            pltpu.SemaphoreType.DMA((LOCAL, TILES, 3)),
            pltpu.SemaphoreType.DMA((LOCAL,)),
        ],
        flops=4 * 10**9,
        moved=10**7,
        vmem=40,
    )


def decode_kernel(ids, offs, lens, owner, *refs):
    pieces = refs[:4]
    query, recent, prior_out, prior_stat, out, fbuf, sem = refs[4:]
    load_fresh(ids, pieces, fbuf, sem)
    starts, _, _ = plan(ids, offs, lens)
    n = HEADS * DROWS
    step = lax.bitwise_and(lax.broadcasted_iota(jnp.int32, (n, DROWS), 0), DROWS - 1)
    later = lax.broadcasted_iota(jnp.int32, (n, DROWS), 1) > step
    column = lax.broadcasted_iota(jnp.int32, (n, FINAL_LENGTH), 1)
    for p in range(LOCAL):
        i = ids[3] * LOCAL + p
        slot = owner[i]
        keys = pl.ds(pl.multiple_of(starts[p] * G, G), FINAL_LENGTH)
        tile = jnp.concatenate(stack_heads(query[slot]), axis=0)
        block = scores_of(tile, fbuf[keys, :HEAD_SIZE])
        block = jnp.where(column < lens[i] - offs[i], block, NEG)
        near = scores_of(tile, recent[slot, :, :HEAD_SIZE])
        near = jnp.where(later, NEG, near)
        before = gather_column(prior_stat[p])
        top = jnp.maximum(jnp.max(block, axis=1, keepdims=True), jnp.max(near, axis=1, keepdims=True))
        top = jnp.maximum(top, before)
        block_weights = jnp.exp2(block - top)
        near_weights = jnp.exp2(near - top)
        share = jnp.exp2(before - top)
        total = (
            jnp.sum(block_weights, axis=1, keepdims=True)
            + jnp.sum(near_weights, axis=1, keepdims=True)
            + share
        )
        mixed = jnp.dot(block_weights.astype(BF16), fbuf[keys, HEAD_SIZE:], preferred_element_type=F32)
        mixed = mixed + jnp.dot(
            near_weights.astype(BF16), recent[slot, :, HEAD_SIZE:], preferred_element_type=F32
        )
        for h in range(HEADS):
            lanes = slice(h * HEAD_SIZE, (h + 1) * HEAD_SIZE)
            stack = slice(h * DROWS, (h + 1) * DROWS)
            value = (mixed[stack] + prior_out[p, :, lanes].astype(F32) * share[stack]) / total[stack]
            out[slot, :, lanes] = value[:STEPS].astype(BF16)


def decode(meta, owner, pieces, query, recent, prior_out, prior_stat):
    return call(
        decode_kernel,
        (*meta, owner),
        (*pieces, query, recent, prior_out, prior_stat),
        jax.ShapeDtypeStruct((LOCAL, STEPS, HEADS * HEAD_SIZE), BF16),
        [pltpu.VMEM(((LOCAL + 1) * FINAL_LENGTH, PAIR), BF16), pltpu.SemaphoreType.DMA((4,))],
        specs=[ANY] * 4 + [VMEM] * 4,
        out_specs=VMEM,
        flops=10**8,
        moved=2 * 10**6,
    )


def exchange(value):
    return lax.all_to_all(value, "grp", split_axis=0, concat_axis=0, tiled=True)


def permute(value, way):
    return lax.ppermute(value, "tp", way)


def after(value, *others):
    return lax.optimization_barrier((value, *others))[0]


def spread_sums(sent, ways):
    arrived = [None] * 3
    for i in ORDER:
        arrived[i] = permute(sent[i], ways[i])
    return arrived


def rest_of_keys(meta, hid, weight, table, base, q):
    other_half = permute(send_half(meta, hid, weight, base, q), SIBLING)
    local, *sent = keep_half(meta, hid, weight, other_half, base, q)
    kept, *sent = middle(meta[0], local, spread_sums(sent, FIRST), q)
    new = finish(meta, kept, spread_sums(sent, SECOND), rope_rows(meta, table, base, q), base, q)
    return new, permute(new, SIBLING)


def per_device(
    hidden_rows,
    key_value_weight,
    prefill_query,
    earlier_cache,
    stretch_offset,
    prompt_length,
    decode_owner,
    decode_query,
    decode_kv,
):
    lane = lax.axis_index("tp")
    group = lax.axis_index("grp")
    ids = jnp.stack([lane // 4, lane // 2 % 2, lane % 2, group]).astype(jnp.int32)
    meta = (ids, stretch_offset, prompt_length)
    table = jnp.asarray(rope_table())
    hid = hidden_rows.reshape(LOCAL * FINAL_LENGTH, -1)
    cache = earlier_cache.reshape(LOCAL, PART, PAIR)
    hid, key_value_weight, prefill_query = (
        pltpu.with_memory_space_constraint(a, pltpu.HBM) for a in (hid, key_value_weight, prefill_query)
    )
    q = ROOM // 2

    sent_half = send_half(meta, hid, key_value_weight, 0, q)
    other_half = permute(sent_half, SIBLING)
    other_cache = permute(cache, SIBLING)
    recent = lax.dynamic_slice_in_dim(decode_kv, (lane // 2) * PAIR, PAIR, 2)
    asked = exchange(jnp.concatenate([decode_query, recent], axis=2))

    blocks = lax.shift_right_logical(after(prompt_length, sent_half) - stretch_offset + (G - 1), 4)
    most = jnp.max(jnp.sum(blocks.reshape(-1, LOCAL), axis=1)) * G
    more = LOCAL * FINAL_LENGTH - ROOM
    rest = lax.cond(
        most > ROOM,
        lambda *a: rest_of_keys(a[:3], *a[3:], ROOM, more // 2),
        lambda *a: (jnp.zeros((more // 2, PAIR), BF16),) * 2,
        *meta,
        hid,
        key_value_weight,
        table,
    )

    local, *sent = keep_half(meta, hid, key_value_weight, after(other_half, rest[0]), 0, q)
    arrived = spread_sums(sent, FIRST)

    asked = jnp.pad(after(asked, local), ((0, 0), (0, DROWS - STEPS), (0, 0)))
    dquery = asked[..., : HEADS * HEAD_SIZE]
    recent = asked[..., HEADS * HEAD_SIZE :]
    turn = rope_rows(meta, after(table, local), 0, q)
    before = prior(meta, decode_owner, prefill_query, dquery, cache, other_cache, (), 0, 3)
    before = prior(meta, decode_owner, prefill_query, dquery, cache, other_cache, before, 3, 3)

    kept, *sent = middle(ids, local, arrived, q)
    arrived = spread_sums(sent, SECOND)
    before = prior(meta, decode_owner, prefill_query, dquery, cache, other_cache, before, 6, 2)
    prior_out, prior_stat = (pltpu.with_memory_space_constraint(a, pltpu.HBM) for a in before[:2])
    prior_dout, prior_dstat = before[2:]
    new = finish(meta, after(kept, prior_dstat), arrived, turn, 0, q)
    pieces = (new, permute(new, SIBLING), *rest)

    answer = decode(meta, decode_owner, pieces, dquery, recent, prior_dout, prior_dstat)
    decode_out = exchange(answer)
    prefill_out = fresh(meta, pieces, prefill_query, prior_out, prior_stat)
    return (prefill_out, decode_out)


def solution(mesh):
    in_specs = (
        P("grp", None, "tp"),
        P("tp", None),
        P("grp", None, "tp"),
        P("grp", "tp", None, None),
        P(),
        P(),
        P(),
        P("grp", None, "tp"),
        P("grp", None, None),
    )
    out_specs = (P("grp", None, "tp"), P("grp", None, "tp"))
    return jax.shard_map(
        per_device, mesh=mesh, in_specs=in_specs, out_specs=out_specs, check_vma=False
    )
```

```python
import functools
import math

import jax
import jax.numpy as jnp
import numpy as np
from jax import lax
from jax.experimental import pallas as pl
from jax.experimental.pallas import tpu as pltpu
from jax.sharding import PartitionSpec as P

HEAD_SIZE = 128
PAIR = 2 * HEAD_SIZE
LOCAL = 8
FINAL_LENGTH = 256
CONTEXT_LENGTH = 1024
PART = 512
STEPS = 4
HEADS = 8
ROPE_BASE = 500000.0
G = 16
DROWS = 16
TILE = 128
SCALE2 = HEAD_SIZE**-0.5 * math.log2(math.e)
NEG = -1e30
F32 = jnp.float32
BF16 = jnp.bfloat16
ANY = pl.BlockSpec(memory_space=pl.ANY)
VMEM = pl.BlockSpec(memory_space=pltpu.VMEM)
HBM = pl.BlockSpec(memory_space=pltpu.HBM)
SMALL, LARGE = 26, 60
ROOM = 1664
LOW, HIGH = 2.0**-100, 2.0**100


def pairs(*moves):
    out = []
    for x in range(4):
        for z in range(2):
            for core in range(2):
                if moves[core] is None:
                    continue
                dx, dz, dc = moves[core]
                out.append((x * 4 + z * 2 + core, (x + dx) % 4 * 4 + (z + dz) % 2 * 2 + (core + dc) % 2))
    return out


SIBLING = pairs((0, 0, 1), (0, 0, 1))
FIRST = [pairs((1, 0, 0), (0, 1, 0)), pairs((2, 0, 0), None), pairs((3, 0, 0), (0, 1, 0))]
SECOND = [pairs((0, 1, 0), (1, 0, 0)), pairs(None, (2, 0, 0)), pairs(None, (3, 0, 0))]
ORDER = (0, 2, 1)


def rope_table():
    half = HEAD_SIZE // 2
    freq = ROPE_BASE ** (np.arange(half, dtype=np.float64) * (-2.0 / HEAD_SIZE))
    angle = np.arange(CONTEXT_LENGTH + FINAL_LENGTH, dtype=np.float64)[:, None] * freq
    cosine, sine = np.cos(angle), np.sin(angle)
    return np.concatenate([cosine, cosine, -sine, sine], axis=1).astype(np.float32)


def plan(ids, offs, lens):
    starts, counts, at = [], [], jnp.int32(0)
    for p in range(LOCAL):
        i = ids[3] * LOCAL + p
        count = lax.shift_right_logical(lens[i] - offs[i] + (G - 1), 4)
        starts.append(at)
        counts.append(count)
        at = at + count
    return starts, counts, at


def ragged(starts, counts, first_block, blocks, copy):
    for p in range(LOCAL):
        low = jnp.maximum(starts[p], first_block)
        high = jnp.minimum(starts[p] + counts[p], first_block + blocks)
        n = jnp.maximum(high - low, 0)
        for bit in range(4, -1, -1):
            done = lax.shift_left(lax.shift_right_logical(n, bit + 1), bit + 1)

            @pl.when(lax.bitwise_and(n, 1 << bit) != 0)
            def _(p=p, bit=bit, low=low, done=done):
                copy(p, bit, low + done - starts[p], low + done - first_block, 1 << bit)


def rows(block, count):
    return pl.ds(pl.multiple_of(block * G, G), count * G)


def project(ids, offs, lens, hid, w, hbuf, wbuf, hsem, wsem, first_block, blocks, ahead):
    starts, counts, total = plan(ids, offs, lens)

    def hidden_copy(p, bit, source, target, count):
        return pltpu.make_async_copy(
            hid.at[rows(p * (FINAL_LENGTH // G) + source, count)],
            hbuf.at[rows(target, count)],
            hsem.at[p, bit],
        )

    def weight_copy(d):
        first = lax.rem(ids[0] + d, 4) * (2 * PAIR)
        return pltpu.make_async_copy(
            w.at[:, pl.ds(pl.multiple_of(first, 2 * PAIR), 2 * PAIR)], wbuf.at[d], wsem.at[d]
        )

    weight_copy(0).start()
    ragged(starts, counts, first_block, blocks, lambda *a: hidden_copy(*a).start())

    @pl.loop(jnp.clip(total - first_block, 0, blocks), blocks)
    def _(b):
        hbuf[rows(b, 1), :] = jnp.zeros((G, hbuf.shape[1]), BF16)

    ahead(0)
    ragged(starts, counts, first_block, blocks, lambda *a: hidden_copy(*a).wait())

    def product(d, e, where):
        if e == 0 and where.start == 0:
            weight_copy(d).wait()
            if d < 3:
                weight_copy(d + 1).start()
                ahead(d + 1)
        columns = pl.ds(pl.multiple_of(lax.rem(ids[1] + e, 2) * PAIR, PAIR), PAIR)
        return jnp.dot(hbuf[where, :], wbuf[d, :, columns], preferred_element_type=F32)

    return product


def row_tiles(q):
    n = next(n for n in (256, 224, 208, 192, 176, 160, 128, 64) if q % n == 0)
    return [slice(r, r + n) for r in range(0, q, n)]


def send_kernel(ids, offs, lens, hid, w, out, more, hbuf, wbuf, obuf, hsem, wsem, osem, *, base, q):
    def count_rows(_):
        def group(g, most):
            total = jnp.int32(0)
            for p in range(LOCAL):
                i = g * LOCAL + p
                total = total + lax.shift_right_logical(lens[i] - offs[i] + (G - 1), 4)
            return jnp.maximum(most, total)

        if _ == 0:
            most = lax.fori_loop(0, lens.shape[0] // LOCAL, group, jnp.int32(0))
            more[0] = (most * G > ROOM).astype(jnp.int32)

    first = base // G + (1 - ids[2]) * (q // G)
    product = project(ids, offs, lens, hid, w, hbuf, wbuf, hsem, wsem, first, q // G, count_rows)
    for j in range(8):
        for where in row_tiles(q):
            obuf[j, where, :] = product(j // 2, j % 2, where).astype(BF16)
        pltpu.make_async_copy(obuf.at[j], out.at[j], osem.at[j]).start()
    for j in range(8):
        pltpu.make_async_copy(obuf.at[j], out.at[j], osem.at[j]).wait()


def keep_kernel(ids, offs, lens, hid, w, other, local, s1, s2, s3, hbuf, wbuf, rbuf, obuf, hsem, wsem, rsem, osem, *, base, q):
    core = ids[2]

    def other_copy(j):
        return pltpu.make_async_copy(other.at[j], rbuf.at[j], rsem.at[j])

    def load_other(d):
        for e in range(2):
            other_copy(2 * d + e).start()

    first = base // G + core * (q // G)
    product = project(ids, offs, lens, hid, w, hbuf, wbuf, hsem, wsem, first, q // G, load_other)

    def leave(j, verb):
        d, e = j // 2, j % 2
        along = (local, s1, s2, s3)[d].at[e]
        across = local.at[d] if e == 0 else (s1 if d < 2 else s3).at[d % 2]
        for c, target in enumerate((along, across)):

            @pl.when(core == c)
            def _(target=target):
                copy = pltpu.make_async_copy(obuf.at[j], target, osem.at[j])
                copy.start() if verb == "start" else copy.wait()

    for j in range(8):
        for where in row_tiles(q):
            value = product(j // 2, j % 2, where)
            if where.start == 0:
                other_copy(j).wait()
            obuf[j, where, :] = (value + rbuf[j, where, :].astype(F32)).astype(BF16)
        leave(j, "start")
    for j in range(8):
        leave(j, "wait")


def call(kernel, prefetched, operands, out_shape, scratch=(), specs=None, out_specs=None, grid=(), flops=0, moved=0, aliases=None, vmem=SMALL):
    n = len(prefetched)
    return pl.pallas_call(
        kernel,
        out_shape=out_shape,
        grid_spec=pltpu.PrefetchScalarGridSpec(
            num_scalar_prefetch=n,
            grid=grid,
            in_specs=specs if specs is not None else [ANY] * len(operands),
            out_specs=out_specs if out_specs is not None else jax.tree.map(lambda _: ANY, out_shape),
            scratch_shapes=list(scratch),
        ),
        compiler_params=pltpu.CompilerParams(vmem_limit_bytes=vmem * 2**20),
        input_output_aliases=aliases or {},
        cost_estimate=pl.CostEstimate(flops=flops, bytes_accessed=moved, transcendentals=0),
    )(*prefetched, *operands)


def half_scratch(q):
    return [pltpu.VMEM((q, 1024), BF16), pltpu.VMEM((4, 1024, 2 * PAIR), BF16)]


def half_semaphores():
    return [pltpu.SemaphoreType.DMA((LOCAL, 5)), pltpu.SemaphoreType.DMA((4,))]


def send_half(meta, hid, w, base, q):
    return call(
        functools.partial(send_kernel, base=base, q=q),
        meta,
        (hid, w),
        [pltpu.HBM((8, q, PAIR), BF16), jax.ShapeDtypeStruct((1,), jnp.int32)],
        half_scratch(q)
        + [pltpu.VMEM((8, q, PAIR), BF16)]
        + half_semaphores()
        + [pltpu.SemaphoreType.DMA((8,))],
        specs=[HBM, HBM],
        out_specs=[ANY, pl.BlockSpec(memory_space=pltpu.SMEM)],
        flops=2 * q * 1024 * 2048,
        moved=2 * (q * 1024 + 1024 * 2048 + q * 2048),
        vmem=LARGE,
    )


def keep_half(meta, hid, w, other, base, q):
    return call(
        functools.partial(keep_kernel, base=base, q=q),
        meta,
        (hid, w, other),
        [pltpu.HBM((n, q, PAIR), BF16) for n in (4, 2, 2, 2)],
        half_scratch(q)
        + [pltpu.VMEM((8, q, PAIR), BF16)] * 2
        + half_semaphores()
        + [pltpu.SemaphoreType.DMA((8,))] * 2,
        specs=[HBM, HBM, ANY],
        flops=2 * q * 1024 * 2048,
        moved=2 * (q * 1024 + 1024 * 2048 + 2 * q * 2048),
        vmem=LARGE,
    )


def middle_kernel(ids, local, r1, r2, r3, kept, s1, s2, s3):
    @pl.when(ids[2] == 0)
    def _():
        for e, out in ((0, kept), (1, s1)):
            total = (local[e].astype(F32) + r1[e].astype(F32)) + (r2[e].astype(F32) + r3[e].astype(F32))
            out[...] = total.astype(out.dtype)

    @pl.when(ids[2] == 1)
    def _():
        for d, out in enumerate((kept, s1, s2, s3)):
            arrived = (r1 if d < 2 else r3)[d % 2]
            out[...] = (local[d].astype(F32) + arrived.astype(F32)).astype(out.dtype)


def middle(ids, local, arrived, q):
    n = 2

    def three(i, ids):
        return (0, i, 0)

    def two(i, ids):
        return (i, 0)

    return call(
        middle_kernel,
        (ids,),
        (local, *arrived),
        [jax.ShapeDtypeStruct((q, PAIR), t) for t in (F32, BF16, BF16, BF16)],
        grid=(n,),
        specs=[pl.BlockSpec((a.shape[0], q // n, PAIR), three) for a in (local, *arrived)],
        out_specs=[pl.BlockSpec((q // n, PAIR), two)] * 4,
        moved=2 * PAIR * q * 15,
        flops=PAIR * q * 8,
    )


def rope_rows_kernel(ids, offs, lens, table, out, sem, *, base, q):
    starts, counts, _ = plan(ids, offs, lens)
    for verb in ("start", "wait"):

        def copy(p, bit, source, target, count, verb=verb):
            position = lax.shift_right_logical(offs[ids[3] * LOCAL + p], 4)
            c = pltpu.make_async_copy(
                table.at[rows(position + source, count)], out.at[rows(target, count)], sem.at[p, bit]
            )
            c.start() if verb == "start" else c.wait()

        ragged(starts, counts, base // G + ids[2] * (q // G), q // G, copy)


def rope_rows(meta, table, base, q):
    return call(
        functools.partial(rope_rows_kernel, base=base, q=q),
        meta,
        (table,),
        jax.ShapeDtypeStruct((q, PAIR), F32),
        [pltpu.SemaphoreType.DMA((LOCAL, 5))],
        specs=[HBM],
        moved=q * PAIR * 8,
    )


def finish_kernel(ids, offs, lens, kept, r1, r2, r3, turn, out, *, base, q):
    _, _, total = plan(ids, offs, lens)
    valid = (total - base // G - ids[2] * (q // G)) * G

    def put(value):
        row = lax.broadcasted_iota(jnp.int32, (q, HEAD_SIZE), 0)
        key = value[:, :HEAD_SIZE]
        key = key * turn[:, :HEAD_SIZE] + pltpu.roll(key, HEAD_SIZE // 2, 1) * turn[:, HEAD_SIZE:]
        out[:, :HEAD_SIZE] = jnp.where(row < valid, key, 0.0).astype(BF16)
        out[:, HEAD_SIZE:] = value[:, HEAD_SIZE:].astype(BF16)

    @pl.when(ids[2] == 0)
    def _():
        put(kept[...] + r1[...].astype(F32))

    @pl.when(ids[2] == 1)
    def _():
        put((kept[...] + r1[...].astype(F32)) + (r2[...].astype(F32) + r3[...].astype(F32)))


def finish(meta, kept, arrived, turn, base, q):
    return call(
        functools.partial(finish_kernel, base=base, q=q),
        meta,
        (kept, *arrived, turn),
        jax.ShapeDtypeStruct((q, PAIR), BF16),
        specs=[VMEM] * 5,
        out_specs=VMEM,
        moved=q * PAIR * 16,
        flops=q * PAIR * 4,
    )


def stack_heads(tile):
    return [tile[:, h * HEAD_SIZE : (h + 1) * HEAD_SIZE] for h in range(HEADS)]


def scores_of(query, keys):
    return lax.dot_general(query, keys, (((1,), (1,)), ((), ())), preferred_element_type=F32) * SCALE2


def spread(column, n):
    lane = lax.broadcasted_iota(jnp.int32, (n, HEAD_SIZE), 1)
    out = jnp.zeros((n, HEAD_SIZE), F32)
    for h in range(HEADS):
        out = jnp.where(lane == h, column[h * n : (h + 1) * n], out)
    return out


def smallest(value):
    return jnp.min(value.reshape(-1, 8, HEAD_SIZE), axis=0)


def largest(value):
    return jnp.max(value.reshape(-1, 8, HEAD_SIZE), axis=0)


def gather_column(stats):
    return jnp.concatenate([stats[:, h : h + 1] for h in range(HEADS)], axis=0)


def tile_rows(t):
    return slice(t * TILE, (t + 1) * TILE)


def when_tile(count, t):
    return pl.when(count > t * TILE)


TILES = FINAL_LENGTH // TILE


def prior_kernel(ids, offs, lens, owner, asked, query, mine, theirs, *refs, first, n, q):
    (*outs, qbuf, kbuf, vbuf, obuf, sbuf, dpad, dobuf, dsbuf, least, most, qsem, ksem, osem, dsem, tsem) = refs
    if q:
        table, *outs, turn = outs
    out, stat, dout, dstat = outs[-4:]
    core = ids[2]

    def place(i):
        at = ids[3] * LOCAL + first + i
        return offs[at], lens[at] - offs[at], owner[at]

    def query_copy(i, t):
        return pltpu.make_async_copy(query.at[first + i, tile_rows(t)], qbuf.at[i, tile_rows(t)], qsem.at[i, t])

    def key_copy(i, part):
        here = core if part == 0 else 1 - core
        target = kbuf.at[i, pl.ds(pl.multiple_of(here * PART, PART), PART)]
        return pltpu.make_async_copy((mine, theirs)[part].at[first + i], target, ksem.at[i, part])

    def when_part(offset, part):
        here = core if part == 0 else 1 - core
        return pl.when(jnp.logical_or(here == 0, offset > PART))

    def out_copies(i, t):
        return (
            pltpu.make_async_copy(obuf.at[i, tile_rows(t)], out.at[first + i, tile_rows(t)], osem.at[i, t, 0]),
            pltpu.make_async_copy(sbuf.at[i, tile_rows(t)], stat.at[first + i, tile_rows(t)], osem.at[i, t, 1]),
        )

    def decode_copies(i):
        return (
            pltpu.make_async_copy(dobuf.at[i], dout.at[first + i], dsem.at[i, 0]),
            pltpu.make_async_copy(dsbuf.at[i], dstat.at[first + i], dsem.at[i, 1]),
        )

    def load(i):
        offset, count, _ = place(i)
        for part in range(2):
            when_part(offset, part)(lambda: key_copy(i, part).start())
        for t in range(TILES):
            when_tile(count, t)(lambda: query_copy(i, t).start())

    def turn_copies(verb):
        starts, counts, _ = plan(ids, offs, lens)

        def copy(p, bit, source, target, count):
            position = lax.shift_right_logical(offs[ids[3] * LOCAL + p], 4)
            c = pltpu.make_async_copy(
                table.at[rows(position + source, count)], turn.at[rows(target, count)], tsem.at[p, bit]
            )
            c.start() if verb == "start" else c.wait()

        ragged(starts, counts, core * (q // G), q // G, copy)

    load(0)
    vbuf[:, HEAD_SIZE:] = jnp.ones((CONTEXT_LENGTH, HEAD_SIZE), BF16)
    dpad[...] = jnp.zeros(dpad.shape, BF16)
    load(1)
    if q:
        turn_copies("start")

    @pl.loop(0, n)
    def _(i):
        offset, count, slot = place(i)
        pl.when(i + 2 < n)(lambda: load(i + 2))
        for part in range(2):
            when_part(offset, part)(lambda part=part: key_copy(i, part).wait())
        for t in range(TILES):
            when_tile(count, t)(lambda t=t: query_copy(i, t).wait())
        dpad[:STEPS, :] = asked[slot, :, : HEADS * HEAD_SIZE]
        least[...] = jnp.full(least.shape, 1.0, F32)
        most[...] = jnp.full(most.shape, 1.0, F32)

        def put(where, value, stats, rows_of_head):
            for h in range(HEADS):
                lanes = slice(h * HEAD_SIZE, (h + 1) * HEAD_SIZE)
                obuf[i, where, lanes] = value[h * rows_of_head : (h + 1) * rows_of_head]
            sbuf[i, where, :] = spread(stats, rows_of_head)

        def put_decode(value, stats):
            for h in range(HEADS):
                dobuf[i, :, h * HEAD_SIZE : (h + 1) * HEAD_SIZE] = value[h * DROWS : (h + 1) * DROWS]
            dsbuf[i] = spread(stats, DROWS)

        for blocks in range(1, 5):

            @pl.when(offset == blocks * 256)
            def _(keys=blocks * 256):
                vbuf[:keys, :HEAD_SIZE] = kbuf[i, :keys, HEAD_SIZE:]
                for t in range(TILES):

                    @when_tile(count, t)
                    def _(t=t):
                        tile = stack_heads(qbuf[i, tile_rows(t), :])
                        if t == 0:
                            tile = tile + stack_heads(dpad[...])
                        tile = jnp.concatenate(tile, axis=0)
                        weights = jnp.exp2(scores_of(tile, kbuf[i, :keys, :HEAD_SIZE])).astype(BF16)
                        mixed = jnp.dot(weights, vbuf[:keys, :], preferred_element_type=F32)
                        total = mixed[:, HEAD_SIZE:]
                        least[...] = jnp.minimum(least[...], smallest(total))
                        most[...] = jnp.maximum(most[...], largest(total))
                        value = (mixed[:, :HEAD_SIZE] * (1.0 / total)).astype(BF16)
                        stats = jnp.log2(total)
                        m = HEADS * TILE
                        put(tile_rows(t), value[:m], stats[:m], TILE)
                        if t == 0:
                            put_decode(value[m:], stats[m:])

        fine = jnp.logical_and(jnp.min(least[...]) >= LOW, jnp.max(most[...]) <= HIGH)

        @pl.when(jnp.logical_not(fine))
        def _():
            def exact(tile):
                def block(b, carry):
                    top, mixed = carry
                    keys = pl.ds(pl.multiple_of(b * 256, 256), 256)
                    scores = scores_of(tile, kbuf[i, keys, :HEAD_SIZE])
                    now = jnp.maximum(jnp.max(scores, axis=1, keepdims=True), top)
                    weights = jnp.exp2(scores - now).astype(BF16)
                    more = jnp.dot(weights, vbuf[keys, :], preferred_element_type=F32)
                    return now, mixed * jnp.exp2(top - now) + more

                m = tile.shape[0]
                start = (jnp.full((m, 1), NEG, F32), jnp.zeros((m, PAIR), F32))
                top, mixed = lax.fori_loop(0, lax.shift_right_logical(offset, 8), block, start)
                total = mixed[:, HEAD_SIZE:]
                return (mixed[:, :HEAD_SIZE] / total).astype(BF16), top + jnp.log2(total)

            @pl.loop(0, lax.shift_right_logical(count + 31, 5))
            def _(t):
                where = pl.ds(pl.multiple_of(t * 32, 32), 32)
                put(where, *exact(jnp.concatenate(stack_heads(qbuf[i, where, :]), axis=0)), 32)

            put_decode(*exact(jnp.concatenate(stack_heads(dpad[...]), axis=0)))

        for t in range(TILES):
            when_tile(count, t)(lambda t=t: [c.start() for c in out_copies(i, t)] and None)
        for c in decode_copies(i):
            c.start()

    for i in range(n):
        _, count, _ = place(i)
        for t in range(TILES):
            when_tile(count, t)(lambda i=i, t=t: [c.wait() for c in out_copies(i, t)] and None)
        for c in decode_copies(i):
            c.wait()
    if q:
        turn_copies("wait")


def prior(meta, owner, query, asked, mine, theirs, first, n, before=(), table=None, q=0):
    wide, narrow = (FINAL_LENGTH, HEADS * HEAD_SIZE), (FINAL_LENGTH, HEAD_SIZE)
    dwide, dnarrow = (DROWS, HEADS * HEAD_SIZE), (DROWS, HEAD_SIZE)
    shapes = [(wide, BF16), (narrow, F32), (dwide, BF16), (dnarrow, F32)]
    return call(
        functools.partial(prior_kernel, first=first, n=n, q=q),
        (*meta, owner),
        (asked, query, mine, theirs, *before, *([table] if q else [])),
        [pltpu.HBM((LOCAL, *s), t) for s, t in shapes] + ([jax.ShapeDtypeStruct((q, PAIR), F32)] if q else []),
        [
            pltpu.VMEM((n, *wide), BF16),
            pltpu.VMEM((n, CONTEXT_LENGTH, PAIR), BF16),
            pltpu.VMEM((CONTEXT_LENGTH, PAIR), BF16),
            pltpu.VMEM((n, *wide), BF16),
            pltpu.VMEM((n, *narrow), F32),
            pltpu.VMEM(dwide, BF16),
            pltpu.VMEM((n, *dwide), BF16),
            pltpu.VMEM((n, *dnarrow), F32),
            pltpu.VMEM((8, HEAD_SIZE), F32),
            pltpu.VMEM((8, HEAD_SIZE), F32),
            pltpu.SemaphoreType.DMA((n, TILES)),
            pltpu.SemaphoreType.DMA((n, 2)),
            pltpu.SemaphoreType.DMA((n, TILES, 2)),
            pltpu.SemaphoreType.DMA((n, 2)),
            pltpu.SemaphoreType.DMA((LOCAL, 5)),
        ],
        specs=[VMEM] + [ANY] * (3 + len(before) + (q > 0)),
        aliases={8 + i: i for i in range(len(before))},
        flops=n * 3 * 10**9,
        moved=n * 2 * 10**6,
    )


def load_fresh(ids, own, other, rest, fbuf, sem):
    copies, base = [], 0
    for c, pieces in enumerate(((own, other), (rest.at[0], rest.at[1]))):
        q = pieces[0].shape[0]
        for i, core in enumerate((ids[2], 1 - ids[2])):
            target = fbuf.at[pl.ds(pl.multiple_of(base + core * q, G), q)]
            copies.append(pltpu.make_async_copy(pieces[i], target, sem.at[2 * c + i]))
        base += 2 * q
    for c in copies:
        c.start()
    fbuf[base:, :] = jnp.zeros((FINAL_LENGTH, PAIR), BF16)
    return copies


def fresh_kernel(ids, offs, lens, *refs):
    pieces = refs[:3]
    query, prior_out, prior_stat, out, fbuf, vbuf, qbuf, pbuf, sbuf, obuf, least, most, sem, isem, osem = refs[3:]

    def count_of(p):
        at = ids[3] * LOCAL + p
        return lens[at] - offs[at]

    def in_copies(p, t):
        pairs_of = ((query, qbuf), (prior_out, pbuf), (prior_stat, sbuf))
        return [
            pltpu.make_async_copy(ref.at[p, tile_rows(t)], buf.at[p, tile_rows(t)], isem.at[p, t, i])
            for i, (ref, buf) in enumerate(pairs_of)
        ]

    def out_copy(p):
        return pltpu.make_async_copy(obuf.at[p], out.at[p], osem.at[p])

    def load(p):
        for t in range(TILES):
            when_tile(count_of(p), t)(lambda: [c.start() for c in in_copies(p, t)] and None)

    load(0)
    copies = load_fresh(ids, *pieces, fbuf, sem)
    vbuf[:, HEAD_SIZE:] = jnp.ones((FINAL_LENGTH, HEAD_SIZE), BF16)
    load(1)
    for c in copies:
        c.wait()

    def prompt(p, start):
        count = count_of(p)
        pl.when(p + 2 < LOCAL)(lambda: load(p + 2))
        first_key = pl.multiple_of(start * G, G)
        vbuf[:, :HEAD_SIZE] = fbuf[pl.ds(first_key, FINAL_LENGTH), HEAD_SIZE:]
        least[...] = jnp.full(least.shape, 1.0, F32)
        most[...] = jnp.full(most.shape, 1.0, F32)

        for t in range(TILES):
            where = tile_rows(t)

            @pl.when(count <= t * TILE)
            def _(where=where):
                obuf[p, where, :] = jnp.zeros((TILE, HEADS * HEAD_SIZE), BF16)

            @when_tile(count, t)
            def _(where=where, t=t):
                for c in in_copies(p, t):
                    c.wait()
                seen = (t + 1) * TILE
                row = lax.broadcasted_iota(jnp.int32, (TILE, seen), 0) + t * TILE
                allowed = lax.broadcasted_iota(jnp.int32, (TILE, seen), 1) <= row
                tile = jnp.concatenate(stack_heads(qbuf[p, where, :]), axis=0)
                scores = scores_of(tile, fbuf[pl.ds(first_key, seen), :HEAD_SIZE])
                weights = jnp.concatenate(
                    [
                        jnp.where(allowed, jnp.exp2(scores[h * TILE : (h + 1) * TILE]), 0.0).astype(BF16)
                        for h in range(HEADS)
                    ],
                    axis=0,
                )
                mixed = jnp.dot(weights, vbuf[:seen, :], preferred_element_type=F32)
                keep = lax.broadcasted_iota(jnp.int32, (TILE, HEAD_SIZE), 0) + t * TILE < count
                before = jnp.exp2(sbuf[p, where, :])
                low, high = least[...], most[...]
                for h in range(HEADS):
                    lanes = slice(h * HEAD_SIZE, (h + 1) * HEAD_SIZE)
                    stack = slice(h * TILE, (h + 1) * TILE)
                    share = before[:, h : h + 1]
                    total = mixed[stack, HEAD_SIZE:] + share
                    low, high = jnp.minimum(low, smallest(total)), jnp.maximum(high, largest(total))
                    old = pbuf[p, where, lanes].astype(F32)
                    value = (mixed[stack, :HEAD_SIZE] + old * share) * (1.0 / total)
                    obuf[p, where, lanes] = jnp.where(keep, value, 0.0).astype(BF16)
                least[...], most[...] = low, high

        fine = jnp.logical_and(jnp.min(least[...]) >= LOW, jnp.max(most[...]) <= HIGH)

        @pl.when(jnp.logical_not(fine))
        def _():
            some = 32
            n = HEADS * some

            @pl.loop(0, lax.shift_right_logical(count + (some - 1), 5))
            def _(t):
                where = pl.ds(pl.multiple_of(t * some, some), some)
                position = lax.bitwise_and(lax.broadcasted_iota(jnp.int32, (n, FINAL_LENGTH), 0), some - 1)
                ahead = lax.broadcasted_iota(jnp.int32, (n, FINAL_LENGTH), 1) - position
                tile = jnp.concatenate(stack_heads(qbuf[p, where, :]), axis=0)
                scores = scores_of(tile, fbuf[pl.ds(first_key, FINAL_LENGTH), :HEAD_SIZE])
                scores = jnp.where(ahead <= t * some, scores, NEG)
                before = gather_column(sbuf[p, where, :])
                top = jnp.maximum(jnp.max(scores, axis=1, keepdims=True), before)
                weights = jnp.exp2(scores - top).astype(BF16)
                share = jnp.exp2(before - top)
                mixed = jnp.dot(weights, vbuf[...], preferred_element_type=F32)
                total = mixed[:, HEAD_SIZE:] + share
                keep = lax.broadcasted_iota(jnp.int32, (some, HEAD_SIZE), 0) + t * some < count
                for h in range(HEADS):
                    lanes = slice(h * HEAD_SIZE, (h + 1) * HEAD_SIZE)
                    stack = slice(h * some, (h + 1) * some)
                    old = pbuf[p, where, lanes].astype(F32)
                    value = (mixed[stack, :HEAD_SIZE] + old * share[stack]) / total[stack]
                    obuf[p, where, lanes] = jnp.where(keep, value, 0.0).astype(BF16)

        out_copy(p).start()
        return start + lax.shift_right_logical(count + (G - 1), 4)

    lax.fori_loop(0, LOCAL, prompt, jnp.int32(0))
    for p in range(LOCAL):
        out_copy(p).wait()


def fresh(meta, pieces, query, prior_out, prior_stat):
    wide, narrow = (LOCAL, FINAL_LENGTH, HEADS * HEAD_SIZE), (LOCAL, FINAL_LENGTH, HEAD_SIZE)
    return call(
        fresh_kernel,
        meta,
        (*pieces, query, prior_out, prior_stat),
        pltpu.HBM(wide, BF16),
        [
            pltpu.VMEM(((LOCAL + 1) * FINAL_LENGTH, PAIR), BF16),
            pltpu.VMEM((FINAL_LENGTH, PAIR), BF16),
            pltpu.VMEM(wide, BF16),
            pltpu.VMEM(wide, BF16),
            pltpu.VMEM(narrow, F32),
            pltpu.VMEM(wide, BF16),
            pltpu.VMEM((8, HEAD_SIZE), F32),
            pltpu.VMEM((8, HEAD_SIZE), F32),
            pltpu.SemaphoreType.DMA((4,)),
            pltpu.SemaphoreType.DMA((LOCAL, TILES, 3)),
            pltpu.SemaphoreType.DMA((LOCAL,)),
        ],
        flops=4 * 10**9,
        moved=10**7,
        vmem=40,
    )


def decode_kernel(ids, offs, lens, owner, *refs):
    pieces = refs[:3]
    asked, prior_out, prior_stat, out, fbuf, dpad, sem = refs[3:]
    copies = load_fresh(ids, *pieces, fbuf, sem)
    dpad[...] = jnp.zeros(dpad.shape, BF16)
    for slot in range(LOCAL):
        dpad[slot, :STEPS, :] = asked[slot]
    for c in copies:
        c.wait()
    starts, _, _ = plan(ids, offs, lens)
    n = HEADS * DROWS
    step = lax.bitwise_and(lax.broadcasted_iota(jnp.int32, (n, DROWS), 0), DROWS - 1)
    reached = lax.broadcasted_iota(jnp.int32, (n, DROWS), 1) <= step
    column = lax.broadcasted_iota(jnp.int32, (n, FINAL_LENGTH), 1)
    ones = jnp.ones((FINAL_LENGTH, HEAD_SIZE), BF16)

    def product(left, right):
        return jnp.dot(left, right, preferred_element_type=F32)

    def scores(p, start):
        i = ids[3] * LOCAL + p
        slot = owner[i]
        keys = pl.ds(pl.multiple_of(start * G, G), FINAL_LENGTH)
        tile = jnp.concatenate(stack_heads(dpad[slot, :, : HEADS * HEAD_SIZE]), axis=0)
        recent = dpad[slot, :, HEADS * HEAD_SIZE :]
        block, near = scores_of(tile, fbuf[keys, :HEAD_SIZE]), scores_of(tile, recent[:, :HEAD_SIZE])
        allowed = column < lens[i] - offs[i]
        return slot, allowed, block, near, fbuf[keys, HEAD_SIZE:], recent[:, HEAD_SIZE:]

    def put(p, slot, mixed, total, share):
        for h in range(HEADS):
            lanes = slice(h * HEAD_SIZE, (h + 1) * HEAD_SIZE)
            stack = slice(h * DROWS, (h + 1) * DROWS)
            value = (mixed[stack] + prior_out[p, :, lanes].astype(F32) * share[stack]) / total[stack]
            out[slot, :, lanes] = value[:STEPS].astype(BF16)

    low = high = jnp.ones((8, HEAD_SIZE), F32)
    for p in range(LOCAL):
        slot, allowed, block, near, values, near_values = scores(p, starts[p])
        block = jnp.where(allowed, jnp.exp2(block), 0.0).astype(BF16)
        near = jnp.where(reached, jnp.exp2(near), 0.0).astype(BF16)
        share = gather_column(jnp.exp2(prior_stat[p]))
        total = product(block, ones) + product(near, ones[:DROWS]) + share
        low, high = jnp.minimum(low, smallest(total)), jnp.maximum(high, largest(total))
        put(p, slot, product(block, values) + product(near, near_values), total, share)

    fine = jnp.logical_and(jnp.min(low) >= LOW, jnp.max(high) <= HIGH)

    @pl.when(jnp.logical_not(fine))
    def _():
        for p in range(LOCAL):
            slot, allowed, block, near, values, near_values = scores(p, starts[p])
            block, near = jnp.where(allowed, block, NEG), jnp.where(reached, near, NEG)
            before = gather_column(prior_stat[p])
            top = jnp.maximum(jnp.max(block, axis=1, keepdims=True), jnp.max(near, axis=1, keepdims=True))
            top = jnp.maximum(top, before)
            block, near, share = jnp.exp2(block - top), jnp.exp2(near - top), jnp.exp2(before - top)
            total = jnp.sum(block, axis=1, keepdims=True) + jnp.sum(near, axis=1, keepdims=True) + share
            put(p, slot, product(block.astype(BF16), values) + product(near.astype(BF16), near_values), total, share)


def decode(meta, owner, pieces, asked, prior_out, prior_stat):
    return call(
        decode_kernel,
        (*meta, owner),
        (*pieces, asked, prior_out, prior_stat),
        jax.ShapeDtypeStruct((LOCAL, STEPS, HEADS * HEAD_SIZE), BF16),
        [
            pltpu.VMEM(((LOCAL + 1) * FINAL_LENGTH, PAIR), BF16),
            pltpu.VMEM((LOCAL, DROWS, HEADS * HEAD_SIZE + PAIR), BF16),
            pltpu.SemaphoreType.DMA((4,)),
        ],
        specs=[ANY] * 3 + [VMEM] * 3,
        out_specs=VMEM,
        flops=10**8,
        moved=2 * 10**6,
    )


def exchange(value):
    return lax.all_to_all(value, "grp", split_axis=0, concat_axis=0, tiled=True)


def permute(value, way):
    return lax.ppermute(value, "tp", way)


def after(value, *others):
    return lax.optimization_barrier((value, *others))[0]


def spread_sums(sent, ways):
    arrived = [None] * 3
    for i in ORDER:
        arrived[i] = permute(sent[i], ways[i])
    return arrived


def in_hbm(value):
    return pltpu.with_memory_space_constraint(value, pltpu.HBM)


def rest_of_keys(meta, hid, weight, table, base, q):
    half, _ = send_half(meta, hid, weight, base, q)
    local, *sent = keep_half(meta, hid, weight, permute(half, SIBLING), base, q)
    kept, *sent = middle(meta[0], local, spread_sums(sent, FIRST), q)
    new = finish(meta, kept, spread_sums(sent, SECOND), rope_rows(meta, table, base, q), base, q)
    return jnp.stack([new, permute(new, SIBLING)])


def per_device(
    hidden_rows,
    key_value_weight,
    prefill_query,
    earlier_cache,
    stretch_offset,
    prompt_length,
    decode_owner,
    decode_query,
    decode_kv,
):
    lane = lax.axis_index("tp")
    group = lax.axis_index("grp")
    ids = jnp.stack([lane // 4, lane // 2 % 2, lane % 2, group]).astype(jnp.int32)
    meta = (ids, stretch_offset, prompt_length)
    table = jnp.asarray(rope_table())
    hid = hidden_rows.reshape(LOCAL * FINAL_LENGTH, -1)
    cache = earlier_cache.reshape(LOCAL, PART, PAIR)
    hid, key_value_weight, prefill_query = (in_hbm(a) for a in (hid, key_value_weight, prefill_query))
    q = ROOM // 2

    half, more = send_half(meta, hid, key_value_weight, 0, q)
    other_half = permute(half, SIBLING)
    other_cache = permute(cache, SIBLING)
    recent = lax.dynamic_slice_in_dim(decode_kv, (lane // 2) * PAIR, PAIR, 2)
    asked = exchange(jnp.concatenate([decode_query, recent], axis=2))
    beyond = LOCAL * FINAL_LENGTH - ROOM
    rest = lax.cond(
        more[0] > 0,
        lambda *a: rest_of_keys(a[:3], *a[3:], ROOM, beyond // 2),
        lambda *a: jnp.zeros((2, beyond // 2, PAIR), BF16),
        *meta,
        hid,
        key_value_weight,
        table,
    )

    local, *sent = keep_half(meta, hid, key_value_weight, after(other_half, rest), 0, q)
    arrived = spread_sums(sent, FIRST)

    asked = after(asked, local)
    common = (meta, decode_owner, prefill_query, asked, cache, other_cache)
    *before, turn = prior(*common, 0, 6, table=after(table, local), q=q)
    kept, *sent = middle(ids, local, arrived, q)
    arrived = spread_sums(sent, SECOND)
    prior_out, prior_stat, prior_dout, prior_dstat = (in_hbm(a) for a in prior(*common, 6, 2, before=before))
    new = finish(meta, after(kept, prior_dstat), arrived, turn, 0, q)
    pieces = (new, permute(new, SIBLING), rest)

    answer = decode(meta, decode_owner, pieces, asked, prior_dout, prior_dstat)
    decode_out = exchange(answer)
    prefill_out = fresh(meta, pieces, prefill_query, prior_out, prior_stat)
    return (prefill_out, decode_out)


def solution(mesh):
    in_specs = (
        P("grp", None, "tp"),
        P("tp", None),
        P("grp", None, "tp"),
        P("grp", "tp", None, None),
        P(),
        P(),
        P(),
        P("grp", None, "tp"),
        P("grp", None, None),
    )
    out_specs = (P("grp", None, "tp"), P("grp", None, "tp"))
    return jax.shard_map(
        per_device, mesh=mesh, in_specs=in_specs, out_specs=out_specs, check_vma=False
    )
```

```python
import functools
import math

import jax
import jax.numpy as jnp
import numpy as np
from jax import lax
from jax.experimental import pallas as pl
from jax.experimental.pallas import tpu as pltpu
from jax.sharding import PartitionSpec as P

HEAD_SIZE = 128
PAIR = 2 * HEAD_SIZE
LOCAL = 8
FINAL_LENGTH = 256
CONTEXT_LENGTH = 1024
PART = 512
STEPS = 4
HEADS = 8
ROPE_BASE = 500000.0
G = 16
DROWS = 16
TILE = 128
SCALE2 = HEAD_SIZE**-0.5 * math.log2(math.e)
NEG = -1e30
F32 = jnp.float32
BF16 = jnp.bfloat16
ANY = pl.BlockSpec(memory_space=pl.ANY)
VMEM = pl.BlockSpec(memory_space=pltpu.VMEM)
HBM = pl.BlockSpec(memory_space=pltpu.HBM)
SMALL, LARGE = 26, 60
ROOM = 1664
LOW, HIGH = 2.0**-100, 2.0**100


def pairs(*moves):
    out = []
    for x in range(4):
        for z in range(2):
            for core in range(2):
                if moves[core] is None:
                    continue
                dx, dz, dc = moves[core]
                out.append((x * 4 + z * 2 + core, (x + dx) % 4 * 4 + (z + dz) % 2 * 2 + (core + dc) % 2))
    return out


SIBLING = pairs((0, 0, 1), (0, 0, 1))
FIRST = [pairs((1, 0, 0), (0, 1, 0)), pairs((2, 0, 0), None), pairs((3, 0, 0), (0, 1, 0))]
SECOND = [pairs((0, 1, 0), (1, 0, 0)), pairs(None, (2, 0, 0)), pairs(None, (3, 0, 0))]
ORDER = (0, 2, 1)


def rope_table():
    half = HEAD_SIZE // 2
    freq = ROPE_BASE ** (np.arange(half, dtype=np.float64) * (-2.0 / HEAD_SIZE))
    angle = np.arange(CONTEXT_LENGTH + FINAL_LENGTH, dtype=np.float64)[:, None] * freq
    cosine, sine = np.cos(angle), np.sin(angle)
    return np.concatenate([cosine, cosine, -sine, sine], axis=1).astype(np.float32)


def plan(ids, offs, lens):
    starts, counts, at = [], [], jnp.int32(0)
    for p in range(LOCAL):
        i = ids[3] * LOCAL + p
        count = lax.shift_right_logical(lens[i] - offs[i] + (G - 1), 4)
        starts.append(at)
        counts.append(count)
        at = at + count
    return starts, counts, at


def ragged(starts, counts, first_block, blocks, copy):
    for p in range(LOCAL):
        low = jnp.maximum(starts[p], first_block)
        high = jnp.minimum(starts[p] + counts[p], first_block + blocks)
        n = jnp.maximum(high - low, 0)
        for bit in range(4, -1, -1):
            done = lax.shift_left(lax.shift_right_logical(n, bit + 1), bit + 1)

            @pl.when(lax.bitwise_and(n, 1 << bit) != 0)
            def _(p=p, bit=bit, low=low, done=done):
                copy(p, bit, low + done - starts[p], low + done - first_block, 1 << bit)


def rows(block, count):
    return pl.ds(pl.multiple_of(block * G, G), count * G)


def project(ids, offs, lens, hid, w, hbuf, wbuf, hsem, wsem, first_block, blocks, ahead):
    starts, counts, total = plan(ids, offs, lens)

    def hidden_copy(p, bit, source, target, count):
        return pltpu.make_async_copy(
            hid.at[rows(p * (FINAL_LENGTH // G) + source, count)],
            hbuf.at[rows(target, count)],
            hsem.at[p, bit],
        )

    def weight_copy(d):
        first = lax.rem(ids[0] + d, 4) * (2 * PAIR)
        return pltpu.make_async_copy(
            w.at[:, pl.ds(pl.multiple_of(first, 2 * PAIR), 2 * PAIR)], wbuf.at[d], wsem.at[d]
        )

    weight_copy(0).start()
    ragged(starts, counts, first_block, blocks, lambda *a: hidden_copy(*a).start())

    @pl.loop(jnp.clip(total - first_block, 0, blocks), blocks)
    def _(b):
        hbuf[rows(b, 1), :] = jnp.zeros((G, hbuf.shape[1]), BF16)

    for d in range(1, 4):
        weight_copy(d).start()
    ahead()
    ragged(starts, counts, first_block, blocks, lambda *a: hidden_copy(*a).wait())

    def product(d, e, where):
        if e == 0 and where.start == 0:
            weight_copy(d).wait()
        columns = pl.ds(pl.multiple_of(lax.rem(ids[1] + e, 2) * PAIR, PAIR), PAIR)
        return jnp.dot(hbuf[where, :], wbuf[d, :, columns], preferred_element_type=F32)

    return product


def row_tiles(q):
    n = next(n for n in (256, 224, 208, 192, 176, 160, 128, 64) if q % n == 0)
    return [slice(r, r + n) for r in range(0, q, n)]


def send_kernel(ids, offs, lens, hid, w, out, more, hbuf, wbuf, obuf, hsem, wsem, osem, *, base, q):
    def count_rows():
        def group(g, most):
            total = jnp.int32(0)
            for p in range(LOCAL):
                i = g * LOCAL + p
                total = total + lax.shift_right_logical(lens[i] - offs[i] + (G - 1), 4)
            return jnp.maximum(most, total)

        most = lax.fori_loop(0, lens.shape[0] // LOCAL, group, jnp.int32(0))
        more[0] = (most * G > ROOM).astype(jnp.int32)

    first = base // G + (1 - ids[2]) * (q // G)
    product = project(ids, offs, lens, hid, w, hbuf, wbuf, hsem, wsem, first, q // G, count_rows)
    for j in range(8):
        for where in row_tiles(q):
            obuf[j, where, :] = product(j // 2, j % 2, where).astype(BF16)
        pltpu.make_async_copy(obuf.at[j], out.at[j], osem.at[j]).start()
    for j in range(8):
        pltpu.make_async_copy(obuf.at[j], out.at[j], osem.at[j]).wait()


def keep_kernel(ids, offs, lens, hid, w, other, local, s1, s2, s3, hbuf, wbuf, rbuf, obuf, hsem, wsem, rsem, osem, *, base, q):
    core = ids[2]

    def other_copy(j):
        return pltpu.make_async_copy(other.at[j], rbuf.at[j], rsem.at[j])

    def load_other():
        for j in range(8):
            other_copy(j).start()

    first = base // G + core * (q // G)
    product = project(ids, offs, lens, hid, w, hbuf, wbuf, hsem, wsem, first, q // G, load_other)

    def leave(j, verb):
        d, e = j // 2, j % 2
        along = (local, s1, s2, s3)[d].at[e]
        across = local.at[d] if e == 0 else (s1 if d < 2 else s3).at[d % 2]
        for c, target in enumerate((along, across)):

            @pl.when(core == c)
            def _(target=target):
                copy = pltpu.make_async_copy(obuf.at[j], target, osem.at[j])
                copy.start() if verb == "start" else copy.wait()

    for j in range(8):
        for where in row_tiles(q):
            value = product(j // 2, j % 2, where)
            if where.start == 0:
                other_copy(j).wait()
            obuf[j, where, :] = (value + rbuf[j, where, :].astype(F32)).astype(BF16)
        leave(j, "start")
    for j in range(8):
        leave(j, "wait")


def call(kernel, prefetched, operands, out_shape, scratch=(), specs=None, out_specs=None, grid=(), flops=0, moved=0, aliases=None, vmem=SMALL):
    n = len(prefetched)
    return pl.pallas_call(
        kernel,
        out_shape=out_shape,
        grid_spec=pltpu.PrefetchScalarGridSpec(
            num_scalar_prefetch=n,
            grid=grid,
            in_specs=specs if specs is not None else [ANY] * len(operands),
            out_specs=out_specs if out_specs is not None else jax.tree.map(lambda _: ANY, out_shape),
            scratch_shapes=list(scratch),
        ),
        compiler_params=pltpu.CompilerParams(vmem_limit_bytes=vmem * 2**20),
        input_output_aliases=aliases or {},
        cost_estimate=pl.CostEstimate(flops=flops, bytes_accessed=moved, transcendentals=0),
    )(*prefetched, *operands)


def half_scratch(q):
    return [pltpu.VMEM((q, 1024), BF16), pltpu.VMEM((4, 1024, 2 * PAIR), BF16)]


def half_semaphores():
    return [pltpu.SemaphoreType.DMA((LOCAL, 5)), pltpu.SemaphoreType.DMA((4,))]


def send_half(meta, hid, w, base, q):
    return call(
        functools.partial(send_kernel, base=base, q=q),
        meta,
        (hid, w),
        [pltpu.HBM((8, q, PAIR), BF16), jax.ShapeDtypeStruct((1,), jnp.int32)],
        half_scratch(q)
        + [pltpu.VMEM((8, q, PAIR), BF16)]
        + half_semaphores()
        + [pltpu.SemaphoreType.DMA((8,))],
        specs=[HBM, HBM],
        out_specs=[ANY, pl.BlockSpec(memory_space=pltpu.SMEM)],
        flops=2 * q * 1024 * 2048,
        moved=2 * (q * 1024 + 1024 * 2048 + q * 2048),
        vmem=LARGE,
    )


def keep_half(meta, hid, w, other, base, q):
    return call(
        functools.partial(keep_kernel, base=base, q=q),
        meta,
        (hid, w, other),
        [pltpu.HBM((n, q, PAIR), BF16) for n in (4, 2, 2, 2)],
        half_scratch(q)
        + [pltpu.VMEM((8, q, PAIR), BF16)] * 2
        + half_semaphores()
        + [pltpu.SemaphoreType.DMA((8,))] * 2,
        specs=[HBM, HBM, ANY],
        flops=2 * q * 1024 * 2048,
        moved=2 * (q * 1024 + 1024 * 2048 + 2 * q * 2048),
        vmem=LARGE,
    )


def middle_kernel(ids, local, r1, r2, r3, kept, s1, s2, s3):
    @pl.when(ids[2] == 0)
    def _():
        for e, out in ((0, kept), (1, s1)):
            total = (local[e].astype(F32) + r1[e].astype(F32)) + (r2[e].astype(F32) + r3[e].astype(F32))
            out[...] = total.astype(out.dtype)

    @pl.when(ids[2] == 1)
    def _():
        for d, out in enumerate((kept, s1, s2, s3)):
            arrived = (r1 if d < 2 else r3)[d % 2]
            out[...] = (local[d].astype(F32) + arrived.astype(F32)).astype(out.dtype)


def middle(ids, local, arrived, q):
    n = 2

    def three(i, ids):
        return (0, i, 0)

    def two(i, ids):
        return (i, 0)

    return call(
        middle_kernel,
        (ids,),
        (local, *arrived),
        [jax.ShapeDtypeStruct((q, PAIR), t) for t in (F32, BF16, BF16, BF16)],
        grid=(n,),
        specs=[pl.BlockSpec((a.shape[0], q // n, PAIR), three) for a in (local, *arrived)],
        out_specs=[pl.BlockSpec((q // n, PAIR), two)] * 4,
        moved=2 * PAIR * q * 15,
        flops=PAIR * q * 8,
    )


def rope_rows_kernel(ids, offs, lens, table, out, sem, *, base, q):
    starts, counts, _ = plan(ids, offs, lens)
    for verb in ("start", "wait"):

        def copy(p, bit, source, target, count, verb=verb):
            position = lax.shift_right_logical(offs[ids[3] * LOCAL + p], 4)
            c = pltpu.make_async_copy(
                table.at[rows(position + source, count)], out.at[rows(target, count)], sem.at[p, bit]
            )
            c.start() if verb == "start" else c.wait()

        ragged(starts, counts, base // G + ids[2] * (q // G), q // G, copy)


def rope_rows(meta, table, base, q):
    return call(
        functools.partial(rope_rows_kernel, base=base, q=q),
        meta,
        (table,),
        jax.ShapeDtypeStruct((q, PAIR), F32),
        [pltpu.SemaphoreType.DMA((LOCAL, 5))],
        specs=[HBM],
        moved=q * PAIR * 8,
    )


def finish_kernel(ids, offs, lens, kept, r1, r2, r3, turn, out, *, base, q):
    _, _, total = plan(ids, offs, lens)
    valid = (total - base // G - ids[2] * (q // G)) * G

    def put(value):
        row = lax.broadcasted_iota(jnp.int32, (q, HEAD_SIZE), 0)
        key = value[:, :HEAD_SIZE]
        key = key * turn[:, :HEAD_SIZE] + pltpu.roll(key, HEAD_SIZE // 2, 1) * turn[:, HEAD_SIZE:]
        out[:, :HEAD_SIZE] = jnp.where(row < valid, key, 0.0).astype(BF16)
        out[:, HEAD_SIZE:] = value[:, HEAD_SIZE:].astype(BF16)

    @pl.when(ids[2] == 0)
    def _():
        put(kept[...] + r1[...].astype(F32))

    @pl.when(ids[2] == 1)
    def _():
        put((kept[...] + r1[...].astype(F32)) + (r2[...].astype(F32) + r3[...].astype(F32)))


def finish(meta, kept, arrived, turn, base, q):
    return call(
        functools.partial(finish_kernel, base=base, q=q),
        meta,
        (kept, *arrived, turn),
        jax.ShapeDtypeStruct((q, PAIR), BF16),
        specs=[VMEM] * 5,
        out_specs=VMEM,
        moved=q * PAIR * 16,
        flops=q * PAIR * 4,
    )


def stack_heads(tile):
    return [tile[:, h * HEAD_SIZE : (h + 1) * HEAD_SIZE] for h in range(HEADS)]


def scores_of(query, keys):
    return lax.dot_general(query, keys, (((1,), (1,)), ((), ())), preferred_element_type=F32) * SCALE2


def spread(column, n):
    lane = lax.broadcasted_iota(jnp.int32, (n, HEAD_SIZE), 1)
    out = jnp.zeros((n, HEAD_SIZE), F32)
    for h in range(HEADS):
        out = jnp.where(lane == h, column[h * n : (h + 1) * n], out)
    return out


def smallest(value):
    return jnp.min(value.reshape(-1, 8, HEAD_SIZE), axis=0)


def largest(value):
    return jnp.max(value.reshape(-1, 8, HEAD_SIZE), axis=0)


def gather_column(stats):
    return jnp.concatenate([stats[:, h : h + 1] for h in range(HEADS)], axis=0)


def tile_rows(t):
    return slice(t * TILE, (t + 1) * TILE)


def when_tile(count, t):
    return pl.when(count > t * TILE)


TILES = FINAL_LENGTH // TILE


def prior_kernel(ids, offs, lens, owner, asked, query, mine, theirs, *refs, first, n, q):
    (*outs, qbuf, kbuf, vbuf, obuf, sbuf, dpad, dobuf, dsbuf, least, most, qsem, ksem, osem, dsem, tsem) = refs
    if q:
        table, *outs, turn = outs
    out, stat, dout, dstat = outs[-4:]
    core = ids[2]

    def place(i):
        at = ids[3] * LOCAL + first + i
        return offs[at], lens[at] - offs[at], owner[at]

    def query_copy(i, t):
        return pltpu.make_async_copy(query.at[first + i, tile_rows(t)], qbuf.at[i, tile_rows(t)], qsem.at[i, t])

    def key_copy(i, part):
        here = core if part == 0 else 1 - core
        target = kbuf.at[i, pl.ds(pl.multiple_of(here * PART, PART), PART)]
        return pltpu.make_async_copy((mine, theirs)[part].at[first + i], target, ksem.at[i, part])

    def when_part(offset, part):
        here = core if part == 0 else 1 - core
        return pl.when(jnp.logical_or(here == 0, offset > PART))

    def out_copies(i, t):
        return (
            pltpu.make_async_copy(obuf.at[i, tile_rows(t)], out.at[first + i, tile_rows(t)], osem.at[i, t, 0]),
            pltpu.make_async_copy(sbuf.at[i, tile_rows(t)], stat.at[first + i, tile_rows(t)], osem.at[i, t, 1]),
        )

    def decode_copies(i):
        return (
            pltpu.make_async_copy(dobuf.at[i], dout.at[first + i], dsem.at[i, 0]),
            pltpu.make_async_copy(dsbuf.at[i], dstat.at[first + i], dsem.at[i, 1]),
        )

    def load(i):
        offset, count, _ = place(i)
        for part in range(2):
            when_part(offset, part)(lambda: key_copy(i, part).start())
        for t in range(TILES):
            when_tile(count, t)(lambda: query_copy(i, t).start())

    def turn_copies(verb):
        starts, counts, _ = plan(ids, offs, lens)

        def copy(p, bit, source, target, count):
            position = lax.shift_right_logical(offs[ids[3] * LOCAL + p], 4)
            c = pltpu.make_async_copy(
                table.at[rows(position + source, count)], turn.at[rows(target, count)], tsem.at[p, bit]
            )
            c.start() if verb == "start" else c.wait()

        ragged(starts, counts, core * (q // G), q // G, copy)

    load(0)
    vbuf[:, HEAD_SIZE:] = jnp.ones((CONTEXT_LENGTH, HEAD_SIZE), BF16)
    dpad[...] = jnp.zeros(dpad.shape, BF16)
    load(1)
    if q:
        turn_copies("start")

    @pl.loop(0, n)
    def _(i):
        offset, count, slot = place(i)
        pl.when(i + 2 < n)(lambda: load(i + 2))
        for part in range(2):
            when_part(offset, part)(lambda part=part: key_copy(i, part).wait())
        for t in range(TILES):
            when_tile(count, t)(lambda t=t: query_copy(i, t).wait())
        dpad[:STEPS, :] = asked[slot, :, : HEADS * HEAD_SIZE]
        least[...] = jnp.full(least.shape, 1.0, F32)
        most[...] = jnp.full(most.shape, 1.0, F32)

        def put(where, value, stats, rows_of_head):
            for h in range(HEADS):
                lanes = slice(h * HEAD_SIZE, (h + 1) * HEAD_SIZE)
                obuf[i, where, lanes] = value[h * rows_of_head : (h + 1) * rows_of_head]
            sbuf[i, where, :] = spread(stats, rows_of_head)

        def put_decode(value, stats):
            for h in range(HEADS):
                dobuf[i, :, h * HEAD_SIZE : (h + 1) * HEAD_SIZE] = value[h * DROWS : (h + 1) * DROWS]
            dsbuf[i] = spread(stats, DROWS)

        for blocks in range(1, 5):

            @pl.when(offset == blocks * 256)
            def _(keys=blocks * 256):
                vbuf[:keys, :HEAD_SIZE] = kbuf[i, :keys, HEAD_SIZE:]
                for t in range(TILES):

                    @when_tile(count, t)
                    def _(t=t):
                        tile = stack_heads(qbuf[i, tile_rows(t), :])
                        if t == 0:
                            tile = tile + stack_heads(dpad[...])
                        tile = jnp.concatenate(tile, axis=0)
                        weights = jnp.exp2(scores_of(tile, kbuf[i, :keys, :HEAD_SIZE])).astype(BF16)
                        mixed = jnp.dot(weights, vbuf[:keys, :], preferred_element_type=F32)
                        total = mixed[:, HEAD_SIZE:]
                        least[...] = jnp.minimum(least[...], smallest(total))
                        most[...] = jnp.maximum(most[...], largest(total))
                        value = (mixed[:, :HEAD_SIZE] * (1.0 / total)).astype(BF16)
                        stats = jnp.log2(total)
                        m = HEADS * TILE
                        put(tile_rows(t), value[:m], stats[:m], TILE)
                        if t == 0:
                            put_decode(value[m:], stats[m:])

        fine = jnp.logical_and(jnp.min(least[...]) >= LOW, jnp.max(most[...]) <= HIGH)

        @pl.when(jnp.logical_not(fine))
        def _():
            def exact(tile):
                def block(b, carry):
                    top, mixed = carry
                    keys = pl.ds(pl.multiple_of(b * 256, 256), 256)
                    scores = scores_of(tile, kbuf[i, keys, :HEAD_SIZE])
                    now = jnp.maximum(jnp.max(scores, axis=1, keepdims=True), top)
                    weights = jnp.exp2(scores - now).astype(BF16)
                    more = jnp.dot(weights, vbuf[keys, :], preferred_element_type=F32)
                    return now, mixed * jnp.exp2(top - now) + more

                m = tile.shape[0]
                start = (jnp.full((m, 1), NEG, F32), jnp.zeros((m, PAIR), F32))
                top, mixed = lax.fori_loop(0, lax.shift_right_logical(offset, 8), block, start)
                total = mixed[:, HEAD_SIZE:]
                return (mixed[:, :HEAD_SIZE] / total).astype(BF16), top + jnp.log2(total)

            @pl.loop(0, lax.shift_right_logical(count + 31, 5))
            def _(t):
                where = pl.ds(pl.multiple_of(t * 32, 32), 32)
                put(where, *exact(jnp.concatenate(stack_heads(qbuf[i, where, :]), axis=0)), 32)

            put_decode(*exact(jnp.concatenate(stack_heads(dpad[...]), axis=0)))

        for t in range(TILES):
            when_tile(count, t)(lambda t=t: [c.start() for c in out_copies(i, t)] and None)
        for c in decode_copies(i):
            c.start()

    for i in range(n):
        _, count, _ = place(i)
        for t in range(TILES):
            when_tile(count, t)(lambda i=i, t=t: [c.wait() for c in out_copies(i, t)] and None)
        for c in decode_copies(i):
            c.wait()
    if q:
        turn_copies("wait")


def prior(meta, owner, query, asked, mine, theirs, first, n, before=(), table=None, q=0):
    wide, narrow = (FINAL_LENGTH, HEADS * HEAD_SIZE), (FINAL_LENGTH, HEAD_SIZE)
    dwide, dnarrow = (DROWS, HEADS * HEAD_SIZE), (DROWS, HEAD_SIZE)
    shapes = [(wide, BF16), (narrow, F32), (dwide, BF16), (dnarrow, F32)]
    return call(
        functools.partial(prior_kernel, first=first, n=n, q=q),
        (*meta, owner),
        (asked, query, mine, theirs, *before, *([table] if q else [])),
        [pltpu.HBM((LOCAL, *s), t) for s, t in shapes] + ([jax.ShapeDtypeStruct((q, PAIR), F32)] if q else []),
        [
            pltpu.VMEM((n, *wide), BF16),
            pltpu.VMEM((n, CONTEXT_LENGTH, PAIR), BF16),
            pltpu.VMEM((CONTEXT_LENGTH, PAIR), BF16),
            pltpu.VMEM((n, *wide), BF16),
            pltpu.VMEM((n, *narrow), F32),
            pltpu.VMEM(dwide, BF16),
            pltpu.VMEM((n, *dwide), BF16),
            pltpu.VMEM((n, *dnarrow), F32),
            pltpu.VMEM((8, HEAD_SIZE), F32),
            pltpu.VMEM((8, HEAD_SIZE), F32),
            pltpu.SemaphoreType.DMA((n, TILES)),
            pltpu.SemaphoreType.DMA((n, 2)),
            pltpu.SemaphoreType.DMA((n, TILES, 2)),
            pltpu.SemaphoreType.DMA((n, 2)),
            pltpu.SemaphoreType.DMA((LOCAL, 5)),
        ],
        specs=[VMEM] + [ANY] * (3 + len(before) + (q > 0)),
        aliases={8 + i: i for i in range(len(before))},
        flops=n * 3 * 10**9,
        moved=n * 2 * 10**6,
    )


def load_fresh(ids, own, other, rest, fbuf, sem):
    copies, base = [], 0
    for c, pieces in enumerate(((own, other), (rest.at[0], rest.at[1]))):
        q = pieces[0].shape[0]
        for i, core in enumerate((ids[2], 1 - ids[2])):
            target = fbuf.at[pl.ds(pl.multiple_of(base + core * q, G), q)]
            copies.append(pltpu.make_async_copy(pieces[i], target, sem.at[2 * c + i]))
        base += 2 * q
    for c in copies:
        c.start()
    fbuf[base:, :] = jnp.zeros((FINAL_LENGTH, PAIR), BF16)
    return copies


def fresh_kernel(ids, offs, lens, *refs):
    pieces = refs[:3]
    query, prior_out, prior_stat, out, fbuf, vbuf, qbuf, pbuf, sbuf, obuf, least, most, sem, isem, osem = refs[3:]

    def count_of(p):
        at = ids[3] * LOCAL + p
        return lens[at] - offs[at]

    def in_copies(p, t):
        pairs_of = ((query, qbuf), (prior_out, pbuf), (prior_stat, sbuf))
        return [
            pltpu.make_async_copy(ref.at[p, tile_rows(t)], buf.at[p, tile_rows(t)], isem.at[p, t, i])
            for i, (ref, buf) in enumerate(pairs_of)
        ]

    def out_copy(p):
        return pltpu.make_async_copy(obuf.at[p], out.at[p], osem.at[p])

    def load(p):
        for t in range(TILES):
            when_tile(count_of(p), t)(lambda: [c.start() for c in in_copies(p, t)] and None)

    load(0)
    copies = load_fresh(ids, *pieces, fbuf, sem)
    vbuf[:, HEAD_SIZE:] = jnp.ones((FINAL_LENGTH, HEAD_SIZE), BF16)
    load(1)
    for c in copies:
        c.wait()

    def prompt(p, start):
        count = count_of(p)
        pl.when(p + 2 < LOCAL)(lambda: load(p + 2))
        first_key = pl.multiple_of(start * G, G)
        vbuf[:, :HEAD_SIZE] = fbuf[pl.ds(first_key, FINAL_LENGTH), HEAD_SIZE:]
        least[...] = jnp.full(least.shape, 1.0, F32)
        most[...] = jnp.full(most.shape, 1.0, F32)

        for t in range(TILES):
            where = tile_rows(t)

            @pl.when(count <= t * TILE)
            def _(where=where):
                obuf[p, where, :] = jnp.zeros((TILE, HEADS * HEAD_SIZE), BF16)

            @when_tile(count, t)
            def _(where=where, t=t):
                for c in in_copies(p, t):
                    c.wait()
                seen = (t + 1) * TILE
                row = lax.broadcasted_iota(jnp.int32, (TILE, seen), 0) + t * TILE
                allowed = lax.broadcasted_iota(jnp.int32, (TILE, seen), 1) <= row
                tile = jnp.concatenate(stack_heads(qbuf[p, where, :]), axis=0)
                scores = scores_of(tile, fbuf[pl.ds(first_key, seen), :HEAD_SIZE])
                weights = jnp.concatenate(
                    [
                        jnp.where(allowed, jnp.exp2(scores[h * TILE : (h + 1) * TILE]), 0.0).astype(BF16)
                        for h in range(HEADS)
                    ],
                    axis=0,
                )
                mixed = jnp.dot(weights, vbuf[:seen, :], preferred_element_type=F32)
                keep = lax.broadcasted_iota(jnp.int32, (TILE, HEAD_SIZE), 0) + t * TILE < count
                before = jnp.exp2(sbuf[p, where, :])
                low, high = least[...], most[...]
                for h in range(HEADS):
                    lanes = slice(h * HEAD_SIZE, (h + 1) * HEAD_SIZE)
                    stack = slice(h * TILE, (h + 1) * TILE)
                    share = before[:, h : h + 1]
                    total = mixed[stack, HEAD_SIZE:] + share
                    low, high = jnp.minimum(low, smallest(total)), jnp.maximum(high, largest(total))
                    old = pbuf[p, where, lanes].astype(F32)
                    value = (mixed[stack, :HEAD_SIZE] + old * share) * (1.0 / total)
                    obuf[p, where, lanes] = jnp.where(keep, value, 0.0).astype(BF16)
                least[...], most[...] = low, high

        fine = jnp.logical_and(jnp.min(least[...]) >= LOW, jnp.max(most[...]) <= HIGH)

        @pl.when(jnp.logical_not(fine))
        def _():
            some = 32
            n = HEADS * some

            @pl.loop(0, lax.shift_right_logical(count + (some - 1), 5))
            def _(t):
                where = pl.ds(pl.multiple_of(t * some, some), some)
                position = lax.bitwise_and(lax.broadcasted_iota(jnp.int32, (n, FINAL_LENGTH), 0), some - 1)
                ahead = lax.broadcasted_iota(jnp.int32, (n, FINAL_LENGTH), 1) - position
                tile = jnp.concatenate(stack_heads(qbuf[p, where, :]), axis=0)
                scores = scores_of(tile, fbuf[pl.ds(first_key, FINAL_LENGTH), :HEAD_SIZE])
                scores = jnp.where(ahead <= t * some, scores, NEG)
                before = gather_column(sbuf[p, where, :])
                top = jnp.maximum(jnp.max(scores, axis=1, keepdims=True), before)
                weights = jnp.exp2(scores - top).astype(BF16)
                share = jnp.exp2(before - top)
                mixed = jnp.dot(weights, vbuf[...], preferred_element_type=F32)
                total = mixed[:, HEAD_SIZE:] + share
                keep = lax.broadcasted_iota(jnp.int32, (some, HEAD_SIZE), 0) + t * some < count
                for h in range(HEADS):
                    lanes = slice(h * HEAD_SIZE, (h + 1) * HEAD_SIZE)
                    stack = slice(h * some, (h + 1) * some)
                    old = pbuf[p, where, lanes].astype(F32)
                    value = (mixed[stack, :HEAD_SIZE] + old * share[stack]) / total[stack]
                    obuf[p, where, lanes] = jnp.where(keep, value, 0.0).astype(BF16)

        out_copy(p).start()
        return start + lax.shift_right_logical(count + (G - 1), 4)

    lax.fori_loop(0, LOCAL, prompt, jnp.int32(0))
    for p in range(LOCAL):
        out_copy(p).wait()


def fresh(meta, pieces, query, prior_out, prior_stat):
    wide, narrow = (LOCAL, FINAL_LENGTH, HEADS * HEAD_SIZE), (LOCAL, FINAL_LENGTH, HEAD_SIZE)
    return call(
        fresh_kernel,
        meta,
        (*pieces, query, prior_out, prior_stat),
        pltpu.HBM(wide, BF16),
        [
            pltpu.VMEM(((LOCAL + 1) * FINAL_LENGTH, PAIR), BF16),
            pltpu.VMEM((FINAL_LENGTH, PAIR), BF16),
            pltpu.VMEM(wide, BF16),
            pltpu.VMEM(wide, BF16),
            pltpu.VMEM(narrow, F32),
            pltpu.VMEM(wide, BF16),
            pltpu.VMEM((8, HEAD_SIZE), F32),
            pltpu.VMEM((8, HEAD_SIZE), F32),
            pltpu.SemaphoreType.DMA((4,)),
            pltpu.SemaphoreType.DMA((LOCAL, TILES, 3)),
            pltpu.SemaphoreType.DMA((LOCAL,)),
        ],
        flops=4 * 10**9,
        moved=10**7,
        vmem=40,
    )


def decode_kernel(ids, offs, lens, owner, *refs):
    pieces = refs[:3]
    asked, prior_out, prior_stat, out, fbuf, dpad, sem = refs[3:]
    copies = load_fresh(ids, *pieces, fbuf, sem)
    dpad[...] = jnp.zeros(dpad.shape, BF16)
    for slot in range(LOCAL):
        dpad[slot, :STEPS, :] = asked[slot]
    for c in copies:
        c.wait()
    starts, _, _ = plan(ids, offs, lens)
    n = HEADS * DROWS
    step = lax.bitwise_and(lax.broadcasted_iota(jnp.int32, (n, DROWS), 0), DROWS - 1)
    reached = lax.broadcasted_iota(jnp.int32, (n, DROWS), 1) <= step
    column = lax.broadcasted_iota(jnp.int32, (n, FINAL_LENGTH), 1)
    ones = jnp.ones((FINAL_LENGTH, HEAD_SIZE), BF16)

    def product(left, right):
        return jnp.dot(left, right, preferred_element_type=F32)

    def scores(p, start):
        i = ids[3] * LOCAL + p
        slot = owner[i]
        keys = pl.ds(pl.multiple_of(start * G, G), FINAL_LENGTH)
        tile = jnp.concatenate(stack_heads(dpad[slot, :, : HEADS * HEAD_SIZE]), axis=0)
        recent = dpad[slot, :, HEADS * HEAD_SIZE :]
        block, near = scores_of(tile, fbuf[keys, :HEAD_SIZE]), scores_of(tile, recent[:, :HEAD_SIZE])
        allowed = column < lens[i] - offs[i]
        return slot, allowed, block, near, fbuf[keys, HEAD_SIZE:], recent[:, HEAD_SIZE:]

    def put(p, slot, mixed, total, share):
        for h in range(HEADS):
            lanes = slice(h * HEAD_SIZE, (h + 1) * HEAD_SIZE)
            stack = slice(h * DROWS, (h + 1) * DROWS)
            value = (mixed[stack] + prior_out[p, :, lanes].astype(F32) * share[stack]) / total[stack]
            out[slot, :, lanes] = value[:STEPS].astype(BF16)

    low = high = jnp.ones((8, HEAD_SIZE), F32)
    for p in range(LOCAL):
        slot, allowed, block, near, values, near_values = scores(p, starts[p])
        block = jnp.where(allowed, jnp.exp2(block), 0.0).astype(BF16)
        near = jnp.where(reached, jnp.exp2(near), 0.0).astype(BF16)
        share = gather_column(jnp.exp2(prior_stat[p]))
        total = product(block, ones) + product(near, ones[:DROWS]) + share
        low, high = jnp.minimum(low, smallest(total)), jnp.maximum(high, largest(total))
        put(p, slot, product(block, values) + product(near, near_values), total, share)

    fine = jnp.logical_and(jnp.min(low) >= LOW, jnp.max(high) <= HIGH)

    @pl.when(jnp.logical_not(fine))
    def _():
        for p in range(LOCAL):
            slot, allowed, block, near, values, near_values = scores(p, starts[p])
            block, near = jnp.where(allowed, block, NEG), jnp.where(reached, near, NEG)
            before = gather_column(prior_stat[p])
            top = jnp.maximum(jnp.max(block, axis=1, keepdims=True), jnp.max(near, axis=1, keepdims=True))
            top = jnp.maximum(top, before)
            block, near, share = jnp.exp2(block - top), jnp.exp2(near - top), jnp.exp2(before - top)
            total = jnp.sum(block, axis=1, keepdims=True) + jnp.sum(near, axis=1, keepdims=True) + share
            put(p, slot, product(block.astype(BF16), values) + product(near.astype(BF16), near_values), total, share)


def decode(meta, owner, pieces, asked, prior_out, prior_stat):
    return call(
        decode_kernel,
        (*meta, owner),
        (*pieces, asked, prior_out, prior_stat),
        jax.ShapeDtypeStruct((LOCAL, STEPS, HEADS * HEAD_SIZE), BF16),
        [
            pltpu.VMEM(((LOCAL + 1) * FINAL_LENGTH, PAIR), BF16),
            pltpu.VMEM((LOCAL, DROWS, HEADS * HEAD_SIZE + PAIR), BF16),
            pltpu.SemaphoreType.DMA((4,)),
        ],
        specs=[ANY] * 3 + [VMEM] * 3,
        out_specs=VMEM,
        flops=10**8,
        moved=2 * 10**6,
    )


def exchange(value):
    return lax.all_to_all(value, "grp", split_axis=0, concat_axis=0, tiled=True)


def permute(value, way):
    return lax.ppermute(value, "tp", way)


def after(value, *others):
    return lax.optimization_barrier((value, *others))[0]


def spread_sums(sent, ways):
    arrived = [None] * 3
    for i in ORDER:
        arrived[i] = permute(sent[i], ways[i])
    return arrived


def in_hbm(value):
    return pltpu.with_memory_space_constraint(value, pltpu.HBM)


def rest_of_keys(meta, hid, weight, table, base, q):
    half, _ = send_half(meta, hid, weight, base, q)
    local, *sent = keep_half(meta, hid, weight, permute(half, SIBLING), base, q)
    kept, *sent = middle(meta[0], local, spread_sums(sent, FIRST), q)
    new = finish(meta, kept, spread_sums(sent, SECOND), rope_rows(meta, table, base, q), base, q)
    return jnp.stack([new, permute(new, SIBLING)])


def per_device(
    hidden_rows,
    key_value_weight,
    prefill_query,
    earlier_cache,
    stretch_offset,
    prompt_length,
    decode_owner,
    decode_query,
    decode_kv,
):
    lane = lax.axis_index("tp")
    group = lax.axis_index("grp")
    ids = jnp.stack([lane // 4, lane // 2 % 2, lane % 2, group]).astype(jnp.int32)
    meta = (ids, stretch_offset, prompt_length)
    table = jnp.asarray(rope_table())
    hid = hidden_rows.reshape(LOCAL * FINAL_LENGTH, -1)
    cache = earlier_cache.reshape(LOCAL, PART, PAIR)
    hid, key_value_weight, prefill_query = (in_hbm(a) for a in (hid, key_value_weight, prefill_query))
    q = ROOM // 2

    half, more = send_half(meta, hid, key_value_weight, 0, q)
    other_half = permute(half, SIBLING)
    other_cache = permute(cache, SIBLING)
    recent = lax.dynamic_slice_in_dim(decode_kv, (lane // 2) * PAIR, PAIR, 2)
    asked = exchange(jnp.concatenate([decode_query, recent], axis=2))
    beyond = LOCAL * FINAL_LENGTH - ROOM
    rest = lax.cond(
        more[0] > 0,
        lambda *a: rest_of_keys(a[:3], *a[3:], ROOM, beyond // 2),
        lambda *a: jnp.zeros((2, beyond // 2, PAIR), BF16),
        *meta,
        hid,
        key_value_weight,
        table,
    )

    local, *sent = keep_half(meta, hid, key_value_weight, after(other_half, rest), 0, q)
    arrived = spread_sums(sent, FIRST)

    asked = after(asked, local)
    common = (meta, decode_owner, prefill_query, asked, cache, other_cache)
    *before, turn = prior(*common, 0, 6, table=after(table, local), q=q)
    kept, *sent = middle(ids, local, arrived, q)
    arrived = spread_sums(sent, SECOND)
    prior_out, prior_stat, prior_dout, prior_dstat = (in_hbm(a) for a in prior(*common, 6, 2, before=before))
    new = finish(meta, after(kept, prior_dstat), arrived, turn, 0, q)
    pieces = (new, permute(new, SIBLING), rest)

    answer = decode(meta, decode_owner, pieces, asked, prior_dout, prior_dstat)
    decode_out = exchange(answer)
    prefill_out = fresh(meta, pieces, prefill_query, prior_out, prior_stat)
    return (prefill_out, decode_out)


def solution(mesh):
    in_specs = (
        P("grp", None, "tp"),
        P("tp", None),
        P("grp", None, "tp"),
        P("grp", "tp", None, None),
        P(),
        P(),
        P(),
        P("grp", None, "tp"),
        P("grp", None, None),
    )
    out_specs = (P("grp", None, "tp"), P("grp", None, "tp"))
    return jax.shard_map(
        per_device, mesh=mesh, in_specs=in_specs, out_specs=out_specs, check_vma=False
    )
```

```python
import functools
import math

import jax
import jax.numpy as jnp
import numpy as np
from jax import lax
from jax.experimental import pallas as pl
from jax.experimental.pallas import tpu as pltpu
from jax.sharding import PartitionSpec as P

HEAD_SIZE = 128
PAIR = 2 * HEAD_SIZE
LOCAL = 8
FINAL_LENGTH = 256
CONTEXT_LENGTH = 1024
PART = 512
STEPS = 4
HEADS = 8
ROPE_BASE = 500000.0
G = 16
DROWS = 16
TILE = 128
SCALE2 = HEAD_SIZE**-0.5 * math.log2(math.e)
NEG = -1e30
F32 = jnp.float32
BF16 = jnp.bfloat16
ANY = pl.BlockSpec(memory_space=pl.ANY)
VMEM = pl.BlockSpec(memory_space=pltpu.VMEM)
HBM = pl.BlockSpec(memory_space=pltpu.HBM)
SMALL, LARGE = 26, 60
ROOM = 1664
LOW, HIGH = 2.0**-100, 2.0**100


def pairs(*moves):
    out = []
    for x in range(4):
        for z in range(2):
            for core in range(2):
                if moves[core] is None:
                    continue
                dx, dz, dc = moves[core]
                out.append((x * 4 + z * 2 + core, (x + dx) % 4 * 4 + (z + dz) % 2 * 2 + (core + dc) % 2))
    return out


SIBLING = pairs((0, 0, 1), (0, 0, 1))
FIRST = [pairs((1, 0, 0), (0, 1, 0)), pairs((2, 0, 0), None), pairs((3, 0, 0), (0, 1, 0))]
SECOND = [pairs((0, 1, 0), (1, 0, 0)), pairs(None, (2, 0, 0)), pairs(None, (3, 0, 0))]
ORDER = (0, 2, 1)


def rope_table():
    half = HEAD_SIZE // 2
    freq = ROPE_BASE ** (np.arange(half, dtype=np.float64) * (-2.0 / HEAD_SIZE))
    angle = np.arange(CONTEXT_LENGTH + FINAL_LENGTH, dtype=np.float64)[:, None] * freq
    cosine, sine = np.cos(angle), np.sin(angle)
    return np.concatenate([cosine, cosine, -sine, sine], axis=1).astype(np.float32)


def plan(ids, offs, lens):
    starts, counts, at = [], [], jnp.int32(0)
    for p in range(LOCAL):
        i = ids[3] * LOCAL + p
        count = lax.shift_right_logical(lens[i] - offs[i] + (G - 1), 4)
        starts.append(at)
        counts.append(count)
        at = at + count
    return starts, counts, at


def ragged(starts, counts, first_block, blocks, copy):
    for p in range(LOCAL):
        low = jnp.maximum(starts[p], first_block)
        high = jnp.minimum(starts[p] + counts[p], first_block + blocks)
        n = jnp.maximum(high - low, 0)
        for bit in range(4, -1, -1):
            done = lax.shift_left(lax.shift_right_logical(n, bit + 1), bit + 1)

            @pl.when(lax.bitwise_and(n, 1 << bit) != 0)
            def _(p=p, bit=bit, low=low, done=done):
                copy(p, bit, low + done - starts[p], low + done - first_block, 1 << bit)


def rows(block, count):
    return pl.ds(pl.multiple_of(block * G, G), count * G)


def project(ids, offs, lens, hid, w, hbuf, wbuf, hsem, wsem, first_block, blocks, ahead):
    starts, counts, total = plan(ids, offs, lens)

    def hidden_copy(p, bit, source, target, count):
        return pltpu.make_async_copy(
            hid.at[rows(p * (FINAL_LENGTH // G) + source, count)],
            hbuf.at[rows(target, count)],
            hsem.at[p, bit],
        )

    def weight_copy(d):
        first = lax.rem(ids[0] + d, 4) * (2 * PAIR)
        return pltpu.make_async_copy(
            w.at[:, pl.ds(pl.multiple_of(first, 2 * PAIR), 2 * PAIR)], wbuf.at[d], wsem.at[d]
        )

    weight_copy(0).start()
    ragged(starts, counts, first_block, blocks, lambda *a: hidden_copy(*a).start())

    @pl.loop(jnp.clip(total - first_block, 0, blocks), blocks)
    def _(b):
        hbuf[rows(b, 1), :] = jnp.zeros((G, hbuf.shape[1]), BF16)

    for d in range(1, 4):
        weight_copy(d).start()
    ragged(starts, counts, first_block, blocks, lambda *a: hidden_copy(*a).wait())
    ahead()

    def product(d, e, where):
        if e == 0 and where.start == 0:
            weight_copy(d).wait()
        columns = pl.ds(pl.multiple_of(lax.rem(ids[1] + e, 2) * PAIR, PAIR), PAIR)
        return jnp.dot(hbuf[where, :], wbuf[d, :, columns], preferred_element_type=F32)

    return product


def row_tiles(q):
    n = next(n for n in (256, 224, 208, 192, 176, 160, 128, 64) if q % n == 0)
    return [slice(r, r + n) for r in range(0, q, n)]


def send_kernel(ids, offs, lens, hid, w, out, more, hbuf, wbuf, obuf, hsem, wsem, osem, *, base, q):
    def count_rows():
        def group(g, most):
            total = jnp.int32(0)
            for p in range(LOCAL):
                i = g * LOCAL + p
                total = total + lax.shift_right_logical(lens[i] - offs[i] + (G - 1), 4)
            return jnp.maximum(most, total)

        most = lax.fori_loop(0, lens.shape[0] // LOCAL, group, jnp.int32(0))
        more[0] = (most * G > ROOM).astype(jnp.int32)

    first = base // G + (1 - ids[2]) * (q // G)
    product = project(ids, offs, lens, hid, w, hbuf, wbuf, hsem, wsem, first, q // G, count_rows)
    for j in range(8):
        for where in row_tiles(q):
            obuf[j, where, :] = product(j // 2, j % 2, where).astype(BF16)
        pltpu.make_async_copy(obuf.at[j], out.at[j], osem.at[j]).start()
    for j in range(8):
        pltpu.make_async_copy(obuf.at[j], out.at[j], osem.at[j]).wait()


def keep_kernel(ids, offs, lens, hid, w, other, local, s1, s2, s3, hbuf, wbuf, rbuf, obuf, hsem, wsem, rsem, osem, *, base, q):
    core = ids[2]

    def other_copy(j):
        return pltpu.make_async_copy(other.at[j], rbuf.at[j], rsem.at[j])

    def load_other():
        for j in range(8):
            other_copy(j).start()

    first = base // G + core * (q // G)
    product = project(ids, offs, lens, hid, w, hbuf, wbuf, hsem, wsem, first, q // G, load_other)

    def leave(j, verb):
        d, e = j // 2, j % 2
        along = (local, s1, s2, s3)[d].at[e]
        across = local.at[d] if e == 0 else (s1 if d < 2 else s3).at[d % 2]
        for c, target in enumerate((along, across)):

            @pl.when(core == c)
            def _(target=target):
                copy = pltpu.make_async_copy(obuf.at[j], target, osem.at[j])
                copy.start() if verb == "start" else copy.wait()

    for j in range(8):
        for where in row_tiles(q):
            value = product(j // 2, j % 2, where)
            if where.start == 0:
                other_copy(j).wait()
            obuf[j, where, :] = (value + rbuf[j, where, :].astype(F32)).astype(BF16)
        leave(j, "start")
    for j in range(8):
        leave(j, "wait")


def call(kernel, prefetched, operands, out_shape, scratch=(), specs=None, out_specs=None, grid=(), flops=0, moved=0, aliases=None, vmem=SMALL):
    n = len(prefetched)
    return pl.pallas_call(
        kernel,
        out_shape=out_shape,
        grid_spec=pltpu.PrefetchScalarGridSpec(
            num_scalar_prefetch=n,
            grid=grid,
            in_specs=specs if specs is not None else [ANY] * len(operands),
            out_specs=out_specs if out_specs is not None else jax.tree.map(lambda _: ANY, out_shape),
            scratch_shapes=list(scratch),
        ),
        compiler_params=pltpu.CompilerParams(vmem_limit_bytes=vmem * 2**20),
        input_output_aliases=aliases or {},
        cost_estimate=pl.CostEstimate(flops=flops, bytes_accessed=moved, transcendentals=0),
    )(*prefetched, *operands)


def half_scratch(q):
    return [pltpu.VMEM((q, 1024), BF16), pltpu.VMEM((4, 1024, 2 * PAIR), BF16)]


def half_semaphores():
    return [pltpu.SemaphoreType.DMA((LOCAL, 5)), pltpu.SemaphoreType.DMA((4,))]


def send_half(meta, hid, w, base, q):
    return call(
        functools.partial(send_kernel, base=base, q=q),
        meta,
        (hid, w),
        [pltpu.HBM((8, q, PAIR), BF16), jax.ShapeDtypeStruct((1,), jnp.int32)],
        half_scratch(q)
        + [pltpu.VMEM((8, q, PAIR), BF16)]
        + half_semaphores()
        + [pltpu.SemaphoreType.DMA((8,))],
        specs=[HBM, HBM],
        out_specs=[ANY, pl.BlockSpec(memory_space=pltpu.SMEM)],
        flops=2 * q * 1024 * 2048,
        moved=2 * (q * 1024 + 1024 * 2048 + q * 2048),
        vmem=LARGE,
    )


def keep_half(meta, hid, w, other, base, q):
    return call(
        functools.partial(keep_kernel, base=base, q=q),
        meta,
        (hid, w, other),
        [pltpu.HBM((n, q, PAIR), BF16) for n in (4, 2, 2, 2)],
        half_scratch(q)
        + [pltpu.VMEM((8, q, PAIR), BF16)] * 2
        + half_semaphores()
        + [pltpu.SemaphoreType.DMA((8,))] * 2,
        specs=[HBM, HBM, ANY],
        flops=2 * q * 1024 * 2048,
        moved=2 * (q * 1024 + 1024 * 2048 + 2 * q * 2048),
        vmem=LARGE,
    )


def middle_kernel(ids, local, r1, r2, r3, kept, s1, s2, s3):
    @pl.when(ids[2] == 0)
    def _():
        for e, out in ((0, kept), (1, s1)):
            total = (local[e].astype(F32) + r1[e].astype(F32)) + (r2[e].astype(F32) + r3[e].astype(F32))
            out[...] = total.astype(out.dtype)

    @pl.when(ids[2] == 1)
    def _():
        for d, out in enumerate((kept, s1, s2, s3)):
            arrived = (r1 if d < 2 else r3)[d % 2]
            out[...] = (local[d].astype(F32) + arrived.astype(F32)).astype(out.dtype)


def middle(ids, local, arrived, q):
    n = 2

    def three(i, ids):
        return (0, i, 0)

    def two(i, ids):
        return (i, 0)

    return call(
        middle_kernel,
        (ids,),
        (local, *arrived),
        [jax.ShapeDtypeStruct((q, PAIR), t) for t in (F32, BF16, BF16, BF16)],
        grid=(n,),
        specs=[pl.BlockSpec((a.shape[0], q // n, PAIR), three) for a in (local, *arrived)],
        out_specs=[pl.BlockSpec((q // n, PAIR), two)] * 4,
        moved=2 * PAIR * q * 15,
        flops=PAIR * q * 8,
    )


def rope_rows_kernel(ids, offs, lens, table, out, sem, *, base, q):
    starts, counts, _ = plan(ids, offs, lens)
    for verb in ("start", "wait"):

        def copy(p, bit, source, target, count, verb=verb):
            position = lax.shift_right_logical(offs[ids[3] * LOCAL + p], 4)
            c = pltpu.make_async_copy(
                table.at[rows(position + source, count)], out.at[rows(target, count)], sem.at[p, bit]
            )
            c.start() if verb == "start" else c.wait()

        ragged(starts, counts, base // G + ids[2] * (q // G), q // G, copy)


def rope_rows(meta, table, base, q):
    return call(
        functools.partial(rope_rows_kernel, base=base, q=q),
        meta,
        (table,),
        jax.ShapeDtypeStruct((q, PAIR), F32),
        [pltpu.SemaphoreType.DMA((LOCAL, 5))],
        specs=[HBM],
        moved=q * PAIR * 8,
    )


def finish_kernel(ids, offs, lens, kept, r1, r2, r3, turn, out, *, base, q):
    _, _, total = plan(ids, offs, lens)
    valid = (total - base // G - ids[2] * (q // G)) * G

    def put(value):
        row = lax.broadcasted_iota(jnp.int32, (q, HEAD_SIZE), 0)
        key = value[:, :HEAD_SIZE]
        key = key * turn[:, :HEAD_SIZE] + pltpu.roll(key, HEAD_SIZE // 2, 1) * turn[:, HEAD_SIZE:]
        out[:, :HEAD_SIZE] = jnp.where(row < valid, key, 0.0).astype(BF16)
        out[:, HEAD_SIZE:] = value[:, HEAD_SIZE:].astype(BF16)

    @pl.when(ids[2] == 0)
    def _():
        put(kept[...] + r1[...].astype(F32))

    @pl.when(ids[2] == 1)
    def _():
        put((kept[...] + r1[...].astype(F32)) + (r2[...].astype(F32) + r3[...].astype(F32)))


def finish(meta, kept, arrived, turn, base, q):
    return call(
        functools.partial(finish_kernel, base=base, q=q),
        meta,
        (kept, *arrived, turn),
        jax.ShapeDtypeStruct((q, PAIR), BF16),
        specs=[VMEM] * 5,
        out_specs=VMEM,
        moved=q * PAIR * 16,
        flops=q * PAIR * 4,
    )


def stack_heads(tile):
    return [tile[:, h * HEAD_SIZE : (h + 1) * HEAD_SIZE] for h in range(HEADS)]


def scores_of(query, keys):
    return lax.dot_general(query, keys, (((1,), (1,)), ((), ())), preferred_element_type=F32) * SCALE2


def spread(column, n):
    lane = lax.broadcasted_iota(jnp.int32, (n, HEAD_SIZE), 1)
    out = jnp.zeros((n, HEAD_SIZE), F32)
    for h in range(HEADS):
        out = jnp.where(lane == h, column[h * n : (h + 1) * n], out)
    return out


def smallest(value):
    return jnp.min(value.reshape(-1, 8, HEAD_SIZE), axis=0)


def largest(value):
    return jnp.max(value.reshape(-1, 8, HEAD_SIZE), axis=0)


def gather_column(stats):
    return jnp.concatenate([stats[:, h : h + 1] for h in range(HEADS)], axis=0)


def tile_rows(t):
    return slice(t * TILE, (t + 1) * TILE)


def when_tile(count, t):
    return pl.when(count > t * TILE)


TILES = FINAL_LENGTH // TILE


def prior_kernel(ids, offs, lens, owner, asked, query, mine, theirs, *refs, first, n, q):
    (*outs, qbuf, kbuf, vbuf, obuf, sbuf, dpad, dobuf, dsbuf, least, most, qsem, ksem, osem, dsem, tsem) = refs
    if q:
        table, *outs, turn = outs
    out, stat, dout, dstat = outs[-4:]
    core = ids[2]

    def place(i):
        at = ids[3] * LOCAL + first + i
        return offs[at], lens[at] - offs[at], owner[at]

    def query_copy(i, t):
        return pltpu.make_async_copy(query.at[first + i, tile_rows(t)], qbuf.at[i, tile_rows(t)], qsem.at[i, t])

    def key_copy(i, part):
        here = core if part == 0 else 1 - core
        target = kbuf.at[i, pl.ds(pl.multiple_of(here * PART, PART), PART)]
        return pltpu.make_async_copy((mine, theirs)[part].at[first + i], target, ksem.at[i, part])

    def when_part(offset, part):
        here = core if part == 0 else 1 - core
        return pl.when(jnp.logical_or(here == 0, offset > PART))

    def out_copies(i, t):
        return (
            pltpu.make_async_copy(obuf.at[i, tile_rows(t)], out.at[first + i, tile_rows(t)], osem.at[i, t, 0]),
            pltpu.make_async_copy(sbuf.at[i, tile_rows(t)], stat.at[first + i, tile_rows(t)], osem.at[i, t, 1]),
        )

    def decode_copies(i):
        return (
            pltpu.make_async_copy(dobuf.at[i], dout.at[first + i], dsem.at[i, 0]),
            pltpu.make_async_copy(dsbuf.at[i], dstat.at[first + i], dsem.at[i, 1]),
        )

    def load(i):
        offset, count, _ = place(i)
        for part in range(2):
            when_part(offset, part)(lambda: key_copy(i, part).start())
        for t in range(TILES):
            when_tile(count, t)(lambda: query_copy(i, t).start())

    def turn_copies(verb):
        starts, counts, _ = plan(ids, offs, lens)

        def copy(p, bit, source, target, count):
            position = lax.shift_right_logical(offs[ids[3] * LOCAL + p], 4)
            c = pltpu.make_async_copy(
                table.at[rows(position + source, count)], turn.at[rows(target, count)], tsem.at[p, bit]
            )
            c.start() if verb == "start" else c.wait()

        ragged(starts, counts, core * (q // G), q // G, copy)

    load(0)
    vbuf[:, HEAD_SIZE:] = jnp.ones((CONTEXT_LENGTH, HEAD_SIZE), BF16)
    dpad[...] = jnp.zeros(dpad.shape, BF16)
    load(1)
    if q:
        turn_copies("start")

    @pl.loop(0, n)
    def _(i):
        offset, count, slot = place(i)
        if n > 2:
            pl.when(i + 2 < n)(lambda: load(i + 2))
        for part in range(2):
            when_part(offset, part)(lambda part=part: key_copy(i, part).wait())
        for t in range(TILES):
            when_tile(count, t)(lambda t=t: query_copy(i, t).wait())
        dpad[:STEPS, :] = asked[slot, :, : HEADS * HEAD_SIZE]
        least[...] = jnp.full(least.shape, 1.0, F32)
        most[...] = jnp.full(most.shape, 1.0, F32)

        def put(where, value, stats, rows_of_head):
            for h in range(HEADS):
                lanes = slice(h * HEAD_SIZE, (h + 1) * HEAD_SIZE)
                obuf[i, where, lanes] = value[h * rows_of_head : (h + 1) * rows_of_head]
            sbuf[i, where, :] = spread(stats, rows_of_head)

        def put_decode(value, stats):
            for h in range(HEADS):
                dobuf[i, :, h * HEAD_SIZE : (h + 1) * HEAD_SIZE] = value[h * DROWS : (h + 1) * DROWS]
            dsbuf[i] = spread(stats, DROWS)

        for blocks in range(1, 5):

            @pl.when(offset == blocks * 256)
            def _(keys=blocks * 256):
                vbuf[:keys, :HEAD_SIZE] = kbuf[i, :keys, HEAD_SIZE:]
                for t in range(TILES):

                    @when_tile(count, t)
                    def _(t=t):
                        tile = stack_heads(qbuf[i, tile_rows(t), :])
                        if t == 0:
                            tile = tile + stack_heads(dpad[...])
                        tile = jnp.concatenate(tile, axis=0)
                        weights = jnp.exp2(scores_of(tile, kbuf[i, :keys, :HEAD_SIZE])).astype(BF16)
                        mixed = jnp.dot(weights, vbuf[:keys, :], preferred_element_type=F32)
                        total = mixed[:, HEAD_SIZE:]
                        least[...] = jnp.minimum(least[...], smallest(total))
                        most[...] = jnp.maximum(most[...], largest(total))
                        value = (mixed[:, :HEAD_SIZE] * (1.0 / total)).astype(BF16)
                        stats = jnp.log2(total)
                        m = HEADS * TILE
                        put(tile_rows(t), value[:m], stats[:m], TILE)
                        if t == 0:
                            put_decode(value[m:], stats[m:])

        fine = jnp.logical_and(jnp.min(least[...]) >= LOW, jnp.max(most[...]) <= HIGH)

        @pl.when(jnp.logical_not(fine))
        def _():
            def exact(tile):
                def block(b, carry):
                    top, mixed = carry
                    keys = pl.ds(pl.multiple_of(b * 256, 256), 256)
                    scores = scores_of(tile, kbuf[i, keys, :HEAD_SIZE])
                    now = jnp.maximum(jnp.max(scores, axis=1, keepdims=True), top)
                    weights = jnp.exp2(scores - now).astype(BF16)
                    more = jnp.dot(weights, vbuf[keys, :], preferred_element_type=F32)
                    return now, mixed * jnp.exp2(top - now) + more

                m = tile.shape[0]
                start = (jnp.full((m, 1), NEG, F32), jnp.zeros((m, PAIR), F32))
                top, mixed = lax.fori_loop(0, lax.shift_right_logical(offset, 8), block, start)
                total = mixed[:, HEAD_SIZE:]
                return (mixed[:, :HEAD_SIZE] / total).astype(BF16), top + jnp.log2(total)

            @pl.loop(0, lax.shift_right_logical(count + 31, 5))
            def _(t):
                where = pl.ds(pl.multiple_of(t * 32, 32), 32)
                put(where, *exact(jnp.concatenate(stack_heads(qbuf[i, where, :]), axis=0)), 32)

            put_decode(*exact(jnp.concatenate(stack_heads(dpad[...]), axis=0)))

        for t in range(TILES):
            when_tile(count, t)(lambda t=t: [c.start() for c in out_copies(i, t)] and None)
        for c in decode_copies(i):
            c.start()

    for i in range(n):
        _, count, _ = place(i)
        for t in range(TILES):
            when_tile(count, t)(lambda i=i, t=t: [c.wait() for c in out_copies(i, t)] and None)
        for c in decode_copies(i):
            c.wait()
    if q:
        turn_copies("wait")


def prior(meta, owner, query, asked, mine, theirs, first, n, before=(), table=None, q=0):
    wide, narrow = (FINAL_LENGTH, HEADS * HEAD_SIZE), (FINAL_LENGTH, HEAD_SIZE)
    dwide, dnarrow = (DROWS, HEADS * HEAD_SIZE), (DROWS, HEAD_SIZE)
    shapes = [(wide, BF16), (narrow, F32), (dwide, BF16), (dnarrow, F32)]
    return call(
        functools.partial(prior_kernel, first=first, n=n, q=q),
        (*meta, owner),
        (asked, query, mine, theirs, *before, *([table] if q else [])),
        [pltpu.HBM((LOCAL, *s), t) for s, t in shapes] + ([jax.ShapeDtypeStruct((q, PAIR), F32)] if q else []),
        [
            pltpu.VMEM((n, *wide), BF16),
            pltpu.VMEM((n, CONTEXT_LENGTH, PAIR), BF16),
            pltpu.VMEM((CONTEXT_LENGTH, PAIR), BF16),
            pltpu.VMEM((n, *wide), BF16),
            pltpu.VMEM((n, *narrow), F32),
            pltpu.VMEM(dwide, BF16),
            pltpu.VMEM((n, *dwide), BF16),
            pltpu.VMEM((n, *dnarrow), F32),
            pltpu.VMEM((8, HEAD_SIZE), F32),
            pltpu.VMEM((8, HEAD_SIZE), F32),
            pltpu.SemaphoreType.DMA((n, TILES)),
            pltpu.SemaphoreType.DMA((n, 2)),
            pltpu.SemaphoreType.DMA((n, TILES, 2)),
            pltpu.SemaphoreType.DMA((n, 2)),
            pltpu.SemaphoreType.DMA((LOCAL, 5)),
        ],
        specs=[VMEM] + [ANY] * (3 + len(before) + (q > 0)),
        aliases={8 + i: i for i in range(len(before))},
        flops=n * 3 * 10**9,
        moved=n * 2 * 10**6,
    )


def load_fresh(ids, own, other, rest, fbuf, sem):
    copies, base = [], 0
    for c, pieces in enumerate(((own, other), (rest.at[0], rest.at[1]))):
        q = pieces[0].shape[0]
        for i, core in enumerate((ids[2], 1 - ids[2])):
            target = fbuf.at[pl.ds(pl.multiple_of(base + core * q, G), q)]
            copies.append(pltpu.make_async_copy(pieces[i], target, sem.at[2 * c + i]))
        base += 2 * q
    for c in copies:
        c.start()
    fbuf[base:, :] = jnp.zeros((FINAL_LENGTH, PAIR), BF16)
    return copies


def fresh_kernel(ids, offs, lens, *refs):
    pieces = refs[:3]
    query, prior_out, prior_stat, out, fbuf, vbuf, qbuf, pbuf, sbuf, obuf, least, most, sem, isem, osem = refs[3:]

    def count_of(p):
        at = ids[3] * LOCAL + p
        return lens[at] - offs[at]

    def in_copies(p, t):
        pairs_of = ((query, qbuf), (prior_out, pbuf), (prior_stat, sbuf))
        return [
            pltpu.make_async_copy(ref.at[p, tile_rows(t)], buf.at[p, tile_rows(t)], isem.at[p, t, i])
            for i, (ref, buf) in enumerate(pairs_of)
        ]

    def out_copy(p):
        return pltpu.make_async_copy(obuf.at[p], out.at[p], osem.at[p])

    def load(p):
        for t in range(TILES):
            when_tile(count_of(p), t)(lambda: [c.start() for c in in_copies(p, t)] and None)

    load(0)
    copies = load_fresh(ids, *pieces, fbuf, sem)
    vbuf[:, HEAD_SIZE:] = jnp.ones((FINAL_LENGTH, HEAD_SIZE), BF16)
    load(1)
    for c in copies:
        c.wait()

    def prompt(p, start):
        count = count_of(p)
        pl.when(p + 2 < LOCAL)(lambda: load(p + 2))
        first_key = pl.multiple_of(start * G, G)
        vbuf[:, :HEAD_SIZE] = fbuf[pl.ds(first_key, FINAL_LENGTH), HEAD_SIZE:]
        least[...] = jnp.full(least.shape, 1.0, F32)
        most[...] = jnp.full(most.shape, 1.0, F32)

        for t in range(TILES):
            where = tile_rows(t)

            @pl.when(count <= t * TILE)
            def _(where=where):
                obuf[p, where, :] = jnp.zeros((TILE, HEADS * HEAD_SIZE), BF16)

            @when_tile(count, t)
            def _(where=where, t=t):
                for c in in_copies(p, t):
                    c.wait()
                seen = (t + 1) * TILE
                row = lax.broadcasted_iota(jnp.int32, (TILE, seen), 0) + t * TILE
                allowed = lax.broadcasted_iota(jnp.int32, (TILE, seen), 1) <= row
                tile = jnp.concatenate(stack_heads(qbuf[p, where, :]), axis=0)
                scores = scores_of(tile, fbuf[pl.ds(first_key, seen), :HEAD_SIZE])
                weights = jnp.concatenate(
                    [
                        jnp.where(allowed, jnp.exp2(scores[h * TILE : (h + 1) * TILE]), 0.0).astype(BF16)
                        for h in range(HEADS)
                    ],
                    axis=0,
                )
                mixed = jnp.dot(weights, vbuf[:seen, :], preferred_element_type=F32)
                keep = lax.broadcasted_iota(jnp.int32, (TILE, HEAD_SIZE), 0) + t * TILE < count
                before = jnp.exp2(sbuf[p, where, :])
                low, high = least[...], most[...]
                for h in range(HEADS):
                    lanes = slice(h * HEAD_SIZE, (h + 1) * HEAD_SIZE)
                    stack = slice(h * TILE, (h + 1) * TILE)
                    share = before[:, h : h + 1]
                    total = mixed[stack, HEAD_SIZE:] + share
                    low, high = jnp.minimum(low, smallest(total)), jnp.maximum(high, largest(total))
                    old = pbuf[p, where, lanes].astype(F32)
                    value = (mixed[stack, :HEAD_SIZE] + old * share) * (1.0 / total)
                    obuf[p, where, lanes] = jnp.where(keep, value, 0.0).astype(BF16)
                least[...], most[...] = low, high

        fine = jnp.logical_and(jnp.min(least[...]) >= LOW, jnp.max(most[...]) <= HIGH)

        @pl.when(jnp.logical_not(fine))
        def _():
            some = 32
            n = HEADS * some

            @pl.loop(0, lax.shift_right_logical(count + (some - 1), 5))
            def _(t):
                where = pl.ds(pl.multiple_of(t * some, some), some)
                position = lax.bitwise_and(lax.broadcasted_iota(jnp.int32, (n, FINAL_LENGTH), 0), some - 1)
                ahead = lax.broadcasted_iota(jnp.int32, (n, FINAL_LENGTH), 1) - position
                tile = jnp.concatenate(stack_heads(qbuf[p, where, :]), axis=0)
                scores = scores_of(tile, fbuf[pl.ds(first_key, FINAL_LENGTH), :HEAD_SIZE])
                scores = jnp.where(ahead <= t * some, scores, NEG)
                before = gather_column(sbuf[p, where, :])
                top = jnp.maximum(jnp.max(scores, axis=1, keepdims=True), before)
                weights = jnp.exp2(scores - top).astype(BF16)
                share = jnp.exp2(before - top)
                mixed = jnp.dot(weights, vbuf[...], preferred_element_type=F32)
                total = mixed[:, HEAD_SIZE:] + share
                keep = lax.broadcasted_iota(jnp.int32, (some, HEAD_SIZE), 0) + t * some < count
                for h in range(HEADS):
                    lanes = slice(h * HEAD_SIZE, (h + 1) * HEAD_SIZE)
                    stack = slice(h * some, (h + 1) * some)
                    old = pbuf[p, where, lanes].astype(F32)
                    value = (mixed[stack, :HEAD_SIZE] + old * share[stack]) / total[stack]
                    obuf[p, where, lanes] = jnp.where(keep, value, 0.0).astype(BF16)

        out_copy(p).start()
        return start + lax.shift_right_logical(count + (G - 1), 4)

    lax.fori_loop(0, LOCAL, prompt, jnp.int32(0))
    for p in range(LOCAL):
        out_copy(p).wait()


def fresh(meta, pieces, query, prior_out, prior_stat):
    wide, narrow = (LOCAL, FINAL_LENGTH, HEADS * HEAD_SIZE), (LOCAL, FINAL_LENGTH, HEAD_SIZE)
    return call(
        fresh_kernel,
        meta,
        (*pieces, query, prior_out, prior_stat),
        pltpu.HBM(wide, BF16),
        [
            pltpu.VMEM(((LOCAL + 1) * FINAL_LENGTH, PAIR), BF16),
            pltpu.VMEM((FINAL_LENGTH, PAIR), BF16),
            pltpu.VMEM(wide, BF16),
            pltpu.VMEM(wide, BF16),
            pltpu.VMEM(narrow, F32),
            pltpu.VMEM(wide, BF16),
            pltpu.VMEM((8, HEAD_SIZE), F32),
            pltpu.VMEM((8, HEAD_SIZE), F32),
            pltpu.SemaphoreType.DMA((4,)),
            pltpu.SemaphoreType.DMA((LOCAL, TILES, 3)),
            pltpu.SemaphoreType.DMA((LOCAL,)),
        ],
        flops=4 * 10**9,
        moved=10**7,
        vmem=40,
    )


def decode_kernel(ids, offs, lens, owner, *refs):
    pieces = refs[:3]
    asked, prior_out, prior_stat, out, fbuf, dpad, sem = refs[3:]
    copies = load_fresh(ids, *pieces, fbuf, sem)
    dpad[...] = jnp.zeros(dpad.shape, BF16)
    for slot in range(LOCAL):
        dpad[slot, :STEPS, :] = asked[slot]
    for c in copies:
        c.wait()
    starts, _, _ = plan(ids, offs, lens)
    n = HEADS * DROWS
    step = lax.bitwise_and(lax.broadcasted_iota(jnp.int32, (n, DROWS), 0), DROWS - 1)
    reached = lax.broadcasted_iota(jnp.int32, (n, DROWS), 1) <= step
    column = lax.broadcasted_iota(jnp.int32, (n, FINAL_LENGTH), 1)
    ones = jnp.ones((FINAL_LENGTH, HEAD_SIZE), BF16)

    def product(left, right):
        return jnp.dot(left, right, preferred_element_type=F32)

    def scores(p, start):
        i = ids[3] * LOCAL + p
        slot = owner[i]
        keys = pl.ds(pl.multiple_of(start * G, G), FINAL_LENGTH)
        tile = jnp.concatenate(stack_heads(dpad[slot, :, : HEADS * HEAD_SIZE]), axis=0)
        recent = dpad[slot, :, HEADS * HEAD_SIZE :]
        block, near = scores_of(tile, fbuf[keys, :HEAD_SIZE]), scores_of(tile, recent[:, :HEAD_SIZE])
        allowed = column < lens[i] - offs[i]
        return slot, allowed, block, near, fbuf[keys, HEAD_SIZE:], recent[:, HEAD_SIZE:]

    def put(p, slot, mixed, total, share):
        for h in range(HEADS):
            lanes = slice(h * HEAD_SIZE, (h + 1) * HEAD_SIZE)
            stack = slice(h * DROWS, (h + 1) * DROWS)
            value = (mixed[stack] + prior_out[p, :, lanes].astype(F32) * share[stack]) / total[stack]
            out[slot, :, lanes] = value[:STEPS].astype(BF16)

    low = high = jnp.ones((8, HEAD_SIZE), F32)
    for p in range(LOCAL):
        slot, allowed, block, near, values, near_values = scores(p, starts[p])
        block = jnp.where(allowed, jnp.exp2(block), 0.0).astype(BF16)
        near = jnp.where(reached, jnp.exp2(near), 0.0).astype(BF16)
        share = gather_column(jnp.exp2(prior_stat[p]))
        total = product(block, ones) + product(near, ones[:DROWS]) + share
        low, high = jnp.minimum(low, smallest(total)), jnp.maximum(high, largest(total))
        put(p, slot, product(block, values) + product(near, near_values), total, share)

    fine = jnp.logical_and(jnp.min(low) >= LOW, jnp.max(high) <= HIGH)

    @pl.when(jnp.logical_not(fine))
    def _():
        for p in range(LOCAL):
            slot, allowed, block, near, values, near_values = scores(p, starts[p])
            block, near = jnp.where(allowed, block, NEG), jnp.where(reached, near, NEG)
            before = gather_column(prior_stat[p])
            top = jnp.maximum(jnp.max(block, axis=1, keepdims=True), jnp.max(near, axis=1, keepdims=True))
            top = jnp.maximum(top, before)
            block, near, share = jnp.exp2(block - top), jnp.exp2(near - top), jnp.exp2(before - top)
            total = jnp.sum(block, axis=1, keepdims=True) + jnp.sum(near, axis=1, keepdims=True) + share
            put(p, slot, product(block.astype(BF16), values) + product(near.astype(BF16), near_values), total, share)


def decode(meta, owner, pieces, asked, prior_out, prior_stat):
    return call(
        decode_kernel,
        (*meta, owner),
        (*pieces, asked, prior_out, prior_stat),
        jax.ShapeDtypeStruct((LOCAL, STEPS, HEADS * HEAD_SIZE), BF16),
        [
            pltpu.VMEM(((LOCAL + 1) * FINAL_LENGTH, PAIR), BF16),
            pltpu.VMEM((LOCAL, DROWS, HEADS * HEAD_SIZE + PAIR), BF16),
            pltpu.SemaphoreType.DMA((4,)),
        ],
        specs=[ANY] * 3 + [VMEM] * 3,
        out_specs=VMEM,
        flops=10**8,
        moved=2 * 10**6,
    )


def exchange(value):
    return lax.all_to_all(value, "grp", split_axis=0, concat_axis=0, tiled=True)


def permute(value, way):
    return lax.ppermute(value, "tp", way)


def after(value, *others):
    return lax.optimization_barrier((value, *others))[0]


def spread_sums(sent, ways):
    arrived = [None] * 3
    for i in ORDER:
        arrived[i] = permute(sent[i], ways[i])
    return arrived


def in_hbm(value):
    return pltpu.with_memory_space_constraint(value, pltpu.HBM)


def rest_of_keys(meta, hid, weight, table, base, q):
    half, _ = send_half(meta, hid, weight, base, q)
    local, *sent = keep_half(meta, hid, weight, permute(half, SIBLING), base, q)
    kept, *sent = middle(meta[0], local, spread_sums(sent, FIRST), q)
    new = finish(meta, kept, spread_sums(sent, SECOND), rope_rows(meta, table, base, q), base, q)
    return jnp.stack([new, permute(new, SIBLING)])


def per_device(
    hidden_rows,
    key_value_weight,
    prefill_query,
    earlier_cache,
    stretch_offset,
    prompt_length,
    decode_owner,
    decode_query,
    decode_kv,
):
    lane = lax.axis_index("tp")
    group = lax.axis_index("grp")
    ids = jnp.stack([lane // 4, lane // 2 % 2, lane % 2, group]).astype(jnp.int32)
    meta = (ids, stretch_offset, prompt_length)
    table = jnp.asarray(rope_table())
    hid = hidden_rows.reshape(LOCAL * FINAL_LENGTH, -1)
    cache = in_hbm(earlier_cache.reshape(LOCAL, PART, PAIR))
    hid, key_value_weight, prefill_query = (in_hbm(a) for a in (hid, key_value_weight, prefill_query))
    q = ROOM // 2

    half, more = send_half(meta, hid, key_value_weight, 0, q)
    other_half = permute(half, SIBLING)
    other_cache = permute(cache, SIBLING)
    recent = lax.dynamic_slice_in_dim(decode_kv, (lane // 2) * PAIR, PAIR, 2)
    asked = exchange(jnp.concatenate([decode_query, recent], axis=2))
    beyond = LOCAL * FINAL_LENGTH - ROOM
    rest = lax.cond(
        more[0] > 0,
        lambda *a: rest_of_keys(a[:3], *a[3:], ROOM, beyond // 2),
        lambda *a: jnp.zeros((2, beyond // 2, PAIR), BF16),
        *meta,
        hid,
        key_value_weight,
        table,
    )

    local, *sent = keep_half(meta, hid, key_value_weight, after(other_half, rest), 0, q)
    arrived = spread_sums(sent, FIRST)

    asked = after(asked, local)
    common = (meta, decode_owner, prefill_query, asked, cache, other_cache)
    *before, turn = prior(*common, 0, 6, table=after(table, local), q=q)
    kept, *sent = middle(ids, after(local, turn), arrived, q)
    arrived = spread_sums(sent, SECOND)
    prior_out, prior_stat, prior_dout, prior_dstat = (in_hbm(a) for a in prior(*common, 6, 2, before=before))
    new = finish(meta, after(kept, prior_dstat), arrived, turn, 0, q)
    pieces = (new, permute(new, SIBLING), rest)

    answer = decode(meta, decode_owner, pieces, asked, prior_dout, prior_dstat)
    decode_out = exchange(answer)
    prefill_out = fresh(meta, pieces, prefill_query, prior_out, prior_stat)
    return (prefill_out, decode_out)


def solution(mesh):
    in_specs = (
        P("grp", None, "tp"),
        P("tp", None),
        P("grp", None, "tp"),
        P("grp", "tp", None, None),
        P(),
        P(),
        P(),
        P("grp", None, "tp"),
        P("grp", None, None),
    )
    out_specs = (P("grp", None, "tp"), P("grp", None, "tp"))
    return jax.shard_map(
        per_device, mesh=mesh, in_specs=in_specs, out_specs=out_specs, check_vma=False
    )
```

```python
import functools
import math

import jax
import jax.numpy as jnp
import numpy as np
from jax import lax
from jax.experimental import pallas as pl
from jax.experimental.pallas import tpu as pltpu
from jax.sharding import PartitionSpec as P

HEAD_SIZE = 128
PAIR = 2 * HEAD_SIZE
LOCAL = 8
FINAL_LENGTH = 256
CONTEXT_LENGTH = 1024
PART = 512
STEPS = 4
HEADS = 8
ROPE_BASE = 500000.0
G = 16
DROWS = 16
TILE = 128
SCALE2 = HEAD_SIZE**-0.5 * math.log2(math.e)
NEG = -1e30
F32 = jnp.float32
BF16 = jnp.bfloat16
ANY = pl.BlockSpec(memory_space=pl.ANY)
VMEM = pl.BlockSpec(memory_space=pltpu.VMEM)
HBM = pl.BlockSpec(memory_space=pltpu.HBM)
SMALL, LARGE = 26, 60
ROOM = 1792
LOW, HIGH = 2.0**-100, 2.0**100


def pairs(*moves):
    out = []
    for x in range(4):
        for z in range(2):
            for core in range(2):
                if moves[core] is None:
                    continue
                dx, dz, dc = moves[core]
                out.append((x * 4 + z * 2 + core, (x + dx) % 4 * 4 + (z + dz) % 2 * 2 + (core + dc) % 2))
    return out


SIBLING = pairs((0, 0, 1), (0, 0, 1))
FIRST = [pairs((1, 0, 0), (0, 1, 0)), pairs((2, 0, 0), None), pairs((3, 0, 0), (0, 1, 0))]
SECOND = [pairs((0, 1, 0), (1, 0, 0)), pairs(None, (2, 0, 0)), pairs(None, (3, 0, 0))]
ORDER = (0, 2, 1)


def rope_table():
    half = HEAD_SIZE // 2
    freq = ROPE_BASE ** (np.arange(half, dtype=np.float64) * (-2.0 / HEAD_SIZE))
    angle = np.arange(CONTEXT_LENGTH + FINAL_LENGTH, dtype=np.float64)[:, None] * freq
    cosine, sine = np.cos(angle), np.sin(angle)
    return np.concatenate([cosine, cosine, -sine, sine], axis=1).astype(np.float32)


def plan(ids, offs, lens):
    starts, counts, at = [], [], jnp.int32(0)
    for p in range(LOCAL):
        i = ids[3] * LOCAL + p
        count = lax.shift_right_logical(lens[i] - offs[i] + (G - 1), 4)
        starts.append(at)
        counts.append(count)
        at = at + count
    return starts, counts, at


def ragged(starts, counts, first_block, blocks, copy):
    for p in range(LOCAL):
        low = jnp.maximum(starts[p], first_block)
        high = jnp.minimum(starts[p] + counts[p], first_block + blocks)
        n = jnp.maximum(high - low, 0)
        for bit in range(4, -1, -1):
            done = lax.shift_left(lax.shift_right_logical(n, bit + 1), bit + 1)

            @pl.when(lax.bitwise_and(n, 1 << bit) != 0)
            def _(p=p, bit=bit, low=low, done=done):
                copy(p, bit, low + done - starts[p], low + done - first_block, 1 << bit)


def rows(block, count):
    return pl.ds(pl.multiple_of(block * G, G), count * G)


def project(ids, offs, lens, hid, w, hbuf, wbuf, hsem, wsem, first_block, blocks, ahead):
    starts, counts, total = plan(ids, offs, lens)

    def hidden_copy(p, bit, source, target, count):
        return pltpu.make_async_copy(
            hid.at[rows(p * (FINAL_LENGTH // G) + source, count)],
            hbuf.at[rows(target, count)],
            hsem.at[p, bit],
        )

    def weight_copy(d):
        first = lax.rem(ids[0] + d, 4) * (2 * PAIR)
        return pltpu.make_async_copy(
            w.at[:, pl.ds(pl.multiple_of(first, 2 * PAIR), 2 * PAIR)], wbuf.at[d], wsem.at[d]
        )

    weight_copy(0).start()
    ragged(starts, counts, first_block, blocks, lambda *a: hidden_copy(*a).start())

    @pl.loop(jnp.clip(total - first_block, 0, blocks), blocks)
    def _(b):
        hbuf[rows(b, 1), :] = jnp.zeros((G, hbuf.shape[1]), BF16)

    for d in range(1, 4):
        weight_copy(d).start()
    ragged(starts, counts, first_block, blocks, lambda *a: hidden_copy(*a).wait())
    ahead()

    def product(d, e, where):
        if e == 0 and where.start == 0:
            weight_copy(d).wait()
        columns = pl.ds(pl.multiple_of(lax.rem(ids[1] + e, 2) * PAIR, PAIR), PAIR)
        return jnp.dot(hbuf[where, :], wbuf[d, :, columns], preferred_element_type=F32)

    return product


def row_tiles(q):
    n = next(n for n in (256, 224, 208, 192, 176, 160, 128, 64) if q % n == 0)
    return [slice(r, r + n) for r in range(0, q, n)]


def send_kernel(ids, offs, lens, hid, w, out, more, hbuf, wbuf, obuf, hsem, wsem, osem, *, base, q):
    def count_rows():
        def group(g, most):
            total = jnp.int32(0)
            for p in range(LOCAL):
                i = g * LOCAL + p
                total = total + lax.shift_right_logical(lens[i] - offs[i] + (G - 1), 4)
            return jnp.maximum(most, total)

        most = lax.fori_loop(0, lens.shape[0] // LOCAL, group, jnp.int32(0))
        more[0] = (most * G > ROOM).astype(jnp.int32)

    first = base // G + (1 - ids[2]) * (q // G)
    product = project(ids, offs, lens, hid, w, hbuf, wbuf, hsem, wsem, first, q // G, count_rows)
    for j in range(8):
        for where in row_tiles(q):
            obuf[j, where, :] = product(j // 2, j % 2, where).astype(BF16)
        pltpu.make_async_copy(obuf.at[j], out.at[j], osem.at[j]).start()
    for j in range(8):
        pltpu.make_async_copy(obuf.at[j], out.at[j], osem.at[j]).wait()


def keep_kernel(ids, offs, lens, hid, w, other, local, s1, s2, s3, hbuf, wbuf, rbuf, obuf, hsem, wsem, rsem, osem, *, base, q):
    core = ids[2]

    def other_copy(j):
        return pltpu.make_async_copy(other.at[j], rbuf.at[j], rsem.at[j])

    def load_other():
        for j in range(8):
            other_copy(j).start()

    first = base // G + core * (q // G)
    product = project(ids, offs, lens, hid, w, hbuf, wbuf, hsem, wsem, first, q // G, load_other)

    def leave(j, verb):
        d, e = j // 2, j % 2
        along = (local, s1, s2, s3)[d].at[e]
        across = local.at[d] if e == 0 else (s1 if d < 2 else s3).at[d % 2]
        for c, target in enumerate((along, across)):

            @pl.when(core == c)
            def _(target=target):
                copy = pltpu.make_async_copy(obuf.at[j], target, osem.at[j])
                copy.start() if verb == "start" else copy.wait()

    for j in range(8):
        for where in row_tiles(q):
            value = product(j // 2, j % 2, where)
            if where.start == 0:
                other_copy(j).wait()
            obuf[j, where, :] = (value + rbuf[j, where, :].astype(F32)).astype(BF16)
        leave(j, "start")
    for j in range(8):
        leave(j, "wait")


def call(kernel, prefetched, operands, out_shape, scratch=(), specs=None, out_specs=None, grid=(), flops=0, moved=0, aliases=None, vmem=SMALL):
    n = len(prefetched)
    return pl.pallas_call(
        kernel,
        out_shape=out_shape,
        grid_spec=pltpu.PrefetchScalarGridSpec(
            num_scalar_prefetch=n,
            grid=grid,
            in_specs=specs if specs is not None else [ANY] * len(operands),
            out_specs=out_specs if out_specs is not None else jax.tree.map(lambda _: ANY, out_shape),
            scratch_shapes=list(scratch),
        ),
        compiler_params=pltpu.CompilerParams(vmem_limit_bytes=vmem * 2**20),
        input_output_aliases=aliases or {},
        cost_estimate=pl.CostEstimate(flops=flops, bytes_accessed=moved, transcendentals=0),
    )(*prefetched, *operands)


def half_scratch(q):
    return [pltpu.VMEM((q, 1024), BF16), pltpu.VMEM((4, 1024, 2 * PAIR), BF16)]


def half_semaphores():
    return [pltpu.SemaphoreType.DMA((LOCAL, 5)), pltpu.SemaphoreType.DMA((4,))]


def send_half(meta, hid, w, base, q):
    return call(
        functools.partial(send_kernel, base=base, q=q),
        meta,
        (hid, w),
        [pltpu.HBM((8, q, PAIR), BF16), jax.ShapeDtypeStruct((1,), jnp.int32)],
        half_scratch(q)
        + [pltpu.VMEM((8, q, PAIR), BF16)]
        + half_semaphores()
        + [pltpu.SemaphoreType.DMA((8,))],
        specs=[HBM, HBM],
        out_specs=[ANY, pl.BlockSpec(memory_space=pltpu.SMEM)],
        flops=2 * q * 1024 * 2048,
        moved=2 * (q * 1024 + 1024 * 2048 + q * 2048),
        vmem=LARGE,
    )


def keep_half(meta, hid, w, other, base, q):
    return call(
        functools.partial(keep_kernel, base=base, q=q),
        meta,
        (hid, w, other),
        [pltpu.HBM((n, q, PAIR), BF16) for n in (4, 2, 2, 2)],
        half_scratch(q)
        + [pltpu.VMEM((8, q, PAIR), BF16)] * 2
        + half_semaphores()
        + [pltpu.SemaphoreType.DMA((8,))] * 2,
        specs=[HBM, HBM, ANY],
        flops=2 * q * 1024 * 2048,
        moved=2 * (q * 1024 + 1024 * 2048 + 2 * q * 2048),
        vmem=LARGE,
    )


def middle_kernel(ids, local, r1, r2, r3, kept, s1, s2, s3):
    @pl.when(ids[2] == 0)
    def _():
        for e, out in ((0, kept), (1, s1)):
            total = (local[e].astype(F32) + r1[e].astype(F32)) + (r2[e].astype(F32) + r3[e].astype(F32))
            out[...] = total.astype(out.dtype)

    @pl.when(ids[2] == 1)
    def _():
        for d, out in enumerate((kept, s1, s2, s3)):
            arrived = (r1 if d < 2 else r3)[d % 2]
            out[...] = (local[d].astype(F32) + arrived.astype(F32)).astype(out.dtype)


def middle(ids, local, arrived, q):
    n = 2

    def three(i, ids):
        return (0, i, 0)

    def two(i, ids):
        return (i, 0)

    return call(
        middle_kernel,
        (ids,),
        (local, *arrived),
        [jax.ShapeDtypeStruct((q, PAIR), t) for t in (F32, BF16, BF16, BF16)],
        grid=(n,),
        specs=[pl.BlockSpec((a.shape[0], q // n, PAIR), three) for a in (local, *arrived)],
        out_specs=[pl.BlockSpec((q // n, PAIR), two)] * 4,
        moved=2 * PAIR * q * 15,
        flops=PAIR * q * 8,
    )


def rope_rows_kernel(ids, offs, lens, table, out, sem, *, base, q):
    starts, counts, _ = plan(ids, offs, lens)
    for verb in ("start", "wait"):

        def copy(p, bit, source, target, count, verb=verb):
            position = lax.shift_right_logical(offs[ids[3] * LOCAL + p], 4)
            c = pltpu.make_async_copy(
                table.at[rows(position + source, count)], out.at[rows(target, count)], sem.at[p, bit]
            )
            c.start() if verb == "start" else c.wait()

        ragged(starts, counts, base // G + ids[2] * (q // G), q // G, copy)


def rope_rows(meta, table, base, q):
    return call(
        functools.partial(rope_rows_kernel, base=base, q=q),
        meta,
        (table,),
        jax.ShapeDtypeStruct((q, PAIR), F32),
        [pltpu.SemaphoreType.DMA((LOCAL, 5))],
        specs=[HBM],
        moved=q * PAIR * 8,
    )


def finish_kernel(ids, offs, lens, kept, r1, r2, r3, turn, out, *, base, q):
    _, _, total = plan(ids, offs, lens)
    valid = (total - base // G - ids[2] * (q // G)) * G

    def put(value):
        row = lax.broadcasted_iota(jnp.int32, (q, HEAD_SIZE), 0)
        key = value[:, :HEAD_SIZE]
        key = key * turn[:, :HEAD_SIZE] + pltpu.roll(key, HEAD_SIZE // 2, 1) * turn[:, HEAD_SIZE:]
        out[:, :HEAD_SIZE] = jnp.where(row < valid, key, 0.0).astype(BF16)
        out[:, HEAD_SIZE:] = value[:, HEAD_SIZE:].astype(BF16)

    @pl.when(ids[2] == 0)
    def _():
        put(kept[...] + r1[...].astype(F32))

    @pl.when(ids[2] == 1)
    def _():
        put((kept[...] + r1[...].astype(F32)) + (r2[...].astype(F32) + r3[...].astype(F32)))


def finish(meta, kept, arrived, turn, base, q):
    return call(
        functools.partial(finish_kernel, base=base, q=q),
        meta,
        (kept, *arrived, turn),
        jax.ShapeDtypeStruct((q, PAIR), BF16),
        specs=[VMEM] * 5,
        out_specs=VMEM,
        moved=q * PAIR * 16,
        flops=q * PAIR * 4,
    )


def stack_heads(tile):
    return [tile[:, h * HEAD_SIZE : (h + 1) * HEAD_SIZE] for h in range(HEADS)]


def scores_of(query, keys):
    return lax.dot_general(query, keys, (((1,), (1,)), ((), ())), preferred_element_type=F32) * SCALE2


def spread(column, n):
    lane = lax.broadcasted_iota(jnp.int32, (n, HEAD_SIZE), 1)
    out = jnp.zeros((n, HEAD_SIZE), F32)
    for h in range(HEADS):
        out = jnp.where(lane == h, column[h * n : (h + 1) * n], out)
    return out


def smallest(value):
    return jnp.min(value.reshape(-1, 8, HEAD_SIZE), axis=0)


def largest(value):
    return jnp.max(value.reshape(-1, 8, HEAD_SIZE), axis=0)


def gather_column(stats):
    return jnp.concatenate([stats[:, h : h + 1] for h in range(HEADS)], axis=0)


def tile_rows(t):
    return slice(t * TILE, (t + 1) * TILE)


def when_tile(count, t):
    return pl.when(count > t * TILE)


TILES = FINAL_LENGTH // TILE


def prior_kernel(ids, offs, lens, owner, asked, query, mine, theirs, *refs, first, n, q):
    (*outs, qbuf, kbuf, vbuf, obuf, sbuf, dpad, dobuf, dsbuf, least, most, qsem, ksem, osem, dsem, tsem) = refs
    if q:
        table, *outs, turn = outs
    out, stat, dout, dstat = outs[-4:]
    core = ids[2]

    def place(i):
        at = ids[3] * LOCAL + first + i
        return offs[at], lens[at] - offs[at], owner[at]

    def query_copy(i, t):
        return pltpu.make_async_copy(query.at[first + i, tile_rows(t)], qbuf.at[i, tile_rows(t)], qsem.at[i, t])

    def key_copy(i, part):
        here = core if part == 0 else 1 - core
        target = kbuf.at[i, pl.ds(pl.multiple_of(here * PART, PART), PART)]
        return pltpu.make_async_copy((mine, theirs)[part].at[first + i], target, ksem.at[i, part])

    def when_part(offset, part):
        here = core if part == 0 else 1 - core
        return pl.when(jnp.logical_or(here == 0, offset > PART))

    def out_copies(i, t):
        return (
            pltpu.make_async_copy(obuf.at[i, tile_rows(t)], out.at[first + i, tile_rows(t)], osem.at[i, t, 0]),
            pltpu.make_async_copy(sbuf.at[i, tile_rows(t)], stat.at[first + i, tile_rows(t)], osem.at[i, t, 1]),
        )

    def decode_copies(i):
        return (
            pltpu.make_async_copy(dobuf.at[i], dout.at[first + i], dsem.at[i, 0]),
            pltpu.make_async_copy(dsbuf.at[i], dstat.at[first + i], dsem.at[i, 1]),
        )

    def load(i):
        offset, count, _ = place(i)
        for part in range(2):
            when_part(offset, part)(lambda: key_copy(i, part).start())
        for t in range(TILES):
            when_tile(count, t)(lambda: query_copy(i, t).start())

    def turn_copies(verb):
        starts, counts, _ = plan(ids, offs, lens)

        def copy(p, bit, source, target, count):
            position = lax.shift_right_logical(offs[ids[3] * LOCAL + p], 4)
            c = pltpu.make_async_copy(
                table.at[rows(position + source, count)], turn.at[rows(target, count)], tsem.at[p, bit]
            )
            c.start() if verb == "start" else c.wait()

        ragged(starts, counts, core * (q // G), q // G, copy)

    load(0)
    vbuf[:, HEAD_SIZE:] = jnp.ones((CONTEXT_LENGTH, HEAD_SIZE), BF16)
    dpad[...] = jnp.zeros(dpad.shape, BF16)
    load(1)
    if q:
        turn_copies("start")

    @pl.loop(0, n)
    def _(i):
        offset, count, slot = place(i)
        if n > 2:
            pl.when(i + 2 < n)(lambda: load(i + 2))
        for part in range(2):
            when_part(offset, part)(lambda part=part: key_copy(i, part).wait())
        for t in range(TILES):
            when_tile(count, t)(lambda t=t: query_copy(i, t).wait())
        dpad[:STEPS, :] = asked[slot, :, : HEADS * HEAD_SIZE]
        least[...] = jnp.full(least.shape, 1.0, F32)
        most[...] = jnp.full(most.shape, 1.0, F32)

        def put(where, value, stats, rows_of_head):
            for h in range(HEADS):
                lanes = slice(h * HEAD_SIZE, (h + 1) * HEAD_SIZE)
                obuf[i, where, lanes] = value[h * rows_of_head : (h + 1) * rows_of_head]
            sbuf[i, where, :] = spread(stats, rows_of_head)

        def put_decode(value, stats):
            for h in range(HEADS):
                dobuf[i, :, h * HEAD_SIZE : (h + 1) * HEAD_SIZE] = value[h * DROWS : (h + 1) * DROWS]
            dsbuf[i] = spread(stats, DROWS)

        for blocks in range(1, 5):

            @pl.when(offset == blocks * 256)
            def _(keys=blocks * 256):
                vbuf[:keys, :HEAD_SIZE] = kbuf[i, :keys, HEAD_SIZE:]
                for t in range(TILES):

                    @when_tile(count, t)
                    def _(t=t):
                        tile = stack_heads(qbuf[i, tile_rows(t), :])
                        if t == 0:
                            tile = tile + stack_heads(dpad[...])
                        tile = jnp.concatenate(tile, axis=0)
                        weights = jnp.exp2(scores_of(tile, kbuf[i, :keys, :HEAD_SIZE])).astype(BF16)
                        mixed = jnp.dot(weights, vbuf[:keys, :], preferred_element_type=F32)
                        total = mixed[:, HEAD_SIZE:]
                        least[...] = jnp.minimum(least[...], smallest(total))
                        most[...] = jnp.maximum(most[...], largest(total))
                        value = (mixed[:, :HEAD_SIZE] * (1.0 / total)).astype(BF16)
                        stats = jnp.log2(total)
                        m = HEADS * TILE
                        put(tile_rows(t), value[:m], stats[:m], TILE)
                        if t == 0:
                            put_decode(value[m:], stats[m:])

        fine = jnp.logical_and(jnp.min(least[...]) >= LOW, jnp.max(most[...]) <= HIGH)

        @pl.when(jnp.logical_not(fine))
        def _():
            def exact(tile):
                def block(b, carry):
                    top, mixed = carry
                    keys = pl.ds(pl.multiple_of(b * 256, 256), 256)
                    scores = scores_of(tile, kbuf[i, keys, :HEAD_SIZE])
                    now = jnp.maximum(jnp.max(scores, axis=1, keepdims=True), top)
                    weights = jnp.exp2(scores - now).astype(BF16)
                    more = jnp.dot(weights, vbuf[keys, :], preferred_element_type=F32)
                    return now, mixed * jnp.exp2(top - now) + more

                m = tile.shape[0]
                start = (jnp.full((m, 1), NEG, F32), jnp.zeros((m, PAIR), F32))
                top, mixed = lax.fori_loop(0, lax.shift_right_logical(offset, 8), block, start)
                total = mixed[:, HEAD_SIZE:]
                return (mixed[:, :HEAD_SIZE] / total).astype(BF16), top + jnp.log2(total)

            @pl.loop(0, lax.shift_right_logical(count + 31, 5))
            def _(t):
                where = pl.ds(pl.multiple_of(t * 32, 32), 32)
                put(where, *exact(jnp.concatenate(stack_heads(qbuf[i, where, :]), axis=0)), 32)

            put_decode(*exact(jnp.concatenate(stack_heads(dpad[...]), axis=0)))

        for t in range(TILES):
            when_tile(count, t)(lambda t=t: [c.start() for c in out_copies(i, t)] and None)
        for c in decode_copies(i):
            c.start()

    for i in range(n):
        _, count, _ = place(i)
        for t in range(TILES):
            when_tile(count, t)(lambda i=i, t=t: [c.wait() for c in out_copies(i, t)] and None)
        for c in decode_copies(i):
            c.wait()
    if q:
        turn_copies("wait")


def prior(meta, owner, query, asked, mine, theirs, first, n, before=(), table=None, q=0):
    wide, narrow = (FINAL_LENGTH, HEADS * HEAD_SIZE), (FINAL_LENGTH, HEAD_SIZE)
    dwide, dnarrow = (DROWS, HEADS * HEAD_SIZE), (DROWS, HEAD_SIZE)
    shapes = [(wide, BF16), (narrow, F32), (dwide, BF16), (dnarrow, F32)]
    return call(
        functools.partial(prior_kernel, first=first, n=n, q=q),
        (*meta, owner),
        (asked, query, mine, theirs, *before, *([table] if q else [])),
        [pltpu.HBM((LOCAL, *s), t) for s, t in shapes] + ([jax.ShapeDtypeStruct((q, PAIR), F32)] if q else []),
        [
            pltpu.VMEM((n, *wide), BF16),
            pltpu.VMEM((n, CONTEXT_LENGTH, PAIR), BF16),
            pltpu.VMEM((CONTEXT_LENGTH, PAIR), BF16),
            pltpu.VMEM((n, *wide), BF16),
            pltpu.VMEM((n, *narrow), F32),
            pltpu.VMEM(dwide, BF16),
            pltpu.VMEM((n, *dwide), BF16),
            pltpu.VMEM((n, *dnarrow), F32),
            pltpu.VMEM((8, HEAD_SIZE), F32),
            pltpu.VMEM((8, HEAD_SIZE), F32),
            pltpu.SemaphoreType.DMA((n, TILES)),
            pltpu.SemaphoreType.DMA((n, 2)),
            pltpu.SemaphoreType.DMA((n, TILES, 2)),
            pltpu.SemaphoreType.DMA((n, 2)),
            pltpu.SemaphoreType.DMA((LOCAL, 5)),
        ],
        specs=[VMEM] + [ANY] * (3 + len(before) + (q > 0)),
        aliases={8 + i: i for i in range(len(before))},
        flops=n * 3 * 10**9,
        moved=n * 2 * 10**6,
    )


def load_fresh(ids, own, other, rest, fbuf, sem):
    copies, base = [], 0
    for c, pieces in enumerate(((own, other), (rest.at[0], rest.at[1]))):
        q = pieces[0].shape[0]
        for i, core in enumerate((ids[2], 1 - ids[2])):
            target = fbuf.at[pl.ds(pl.multiple_of(base + core * q, G), q)]
            copies.append(pltpu.make_async_copy(pieces[i], target, sem.at[2 * c + i]))
        base += 2 * q
    for c in copies:
        c.start()
    fbuf[base:, :] = jnp.zeros((FINAL_LENGTH, PAIR), BF16)
    return copies


def fresh_kernel(ids, offs, lens, *refs):
    pieces = refs[:3]
    query, prior_out, prior_stat, out, fbuf, vbuf, qbuf, pbuf, sbuf, obuf, least, most, sem, isem, osem = refs[3:]

    def count_of(p):
        at = ids[3] * LOCAL + p
        return lens[at] - offs[at]

    def in_copies(p, t):
        pairs_of = ((query, qbuf), (prior_out, pbuf), (prior_stat, sbuf))
        return [
            pltpu.make_async_copy(ref.at[p, tile_rows(t)], buf.at[p, tile_rows(t)], isem.at[p, t, i])
            for i, (ref, buf) in enumerate(pairs_of)
        ]

    def out_copy(p):
        return pltpu.make_async_copy(obuf.at[p], out.at[p], osem.at[p])

    def load(p):
        for t in range(TILES):
            when_tile(count_of(p), t)(lambda: [c.start() for c in in_copies(p, t)] and None)

    load(0)
    copies = load_fresh(ids, *pieces, fbuf, sem)
    vbuf[:, HEAD_SIZE:] = jnp.ones((FINAL_LENGTH, HEAD_SIZE), BF16)
    load(1)
    for c in copies:
        c.wait()

    def prompt(p, start):
        count = count_of(p)
        pl.when(p + 2 < LOCAL)(lambda: load(p + 2))
        first_key = pl.multiple_of(start * G, G)
        vbuf[:, :HEAD_SIZE] = fbuf[pl.ds(first_key, FINAL_LENGTH), HEAD_SIZE:]
        least[...] = jnp.full(least.shape, 1.0, F32)
        most[...] = jnp.full(most.shape, 1.0, F32)

        for t in range(TILES):
            where = tile_rows(t)

            @pl.when(count <= t * TILE)
            def _(where=where):
                obuf[p, where, :] = jnp.zeros((TILE, HEADS * HEAD_SIZE), BF16)

            @when_tile(count, t)
            def _(where=where, t=t):
                for c in in_copies(p, t):
                    c.wait()
                seen = (t + 1) * TILE
                row = lax.broadcasted_iota(jnp.int32, (TILE, seen), 0) + t * TILE
                allowed = lax.broadcasted_iota(jnp.int32, (TILE, seen), 1) <= row
                tile = jnp.concatenate(stack_heads(qbuf[p, where, :]), axis=0)
                scores = scores_of(tile, fbuf[pl.ds(first_key, seen), :HEAD_SIZE])
                weights = jnp.concatenate(
                    [
                        jnp.where(allowed, jnp.exp2(scores[h * TILE : (h + 1) * TILE]), 0.0).astype(BF16)
                        for h in range(HEADS)
                    ],
                    axis=0,
                )
                mixed = jnp.dot(weights, vbuf[:seen, :], preferred_element_type=F32)
                keep = lax.broadcasted_iota(jnp.int32, (TILE, HEAD_SIZE), 0) + t * TILE < count
                before = jnp.exp2(sbuf[p, where, :])
                low, high = least[...], most[...]
                for h in range(HEADS):
                    lanes = slice(h * HEAD_SIZE, (h + 1) * HEAD_SIZE)
                    stack = slice(h * TILE, (h + 1) * TILE)
                    share = before[:, h : h + 1]
                    total = mixed[stack, HEAD_SIZE:] + share
                    low, high = jnp.minimum(low, smallest(total)), jnp.maximum(high, largest(total))
                    old = pbuf[p, where, lanes].astype(F32)
                    value = (mixed[stack, :HEAD_SIZE] + old * share) * (1.0 / total)
                    obuf[p, where, lanes] = jnp.where(keep, value, 0.0).astype(BF16)
                least[...], most[...] = low, high

        fine = jnp.logical_and(jnp.min(least[...]) >= LOW, jnp.max(most[...]) <= HIGH)

        @pl.when(jnp.logical_not(fine))
        def _():
            some = 32
            n = HEADS * some

            @pl.loop(0, lax.shift_right_logical(count + (some - 1), 5))
            def _(t):
                where = pl.ds(pl.multiple_of(t * some, some), some)
                position = lax.bitwise_and(lax.broadcasted_iota(jnp.int32, (n, FINAL_LENGTH), 0), some - 1)
                ahead = lax.broadcasted_iota(jnp.int32, (n, FINAL_LENGTH), 1) - position
                tile = jnp.concatenate(stack_heads(qbuf[p, where, :]), axis=0)
                scores = scores_of(tile, fbuf[pl.ds(first_key, FINAL_LENGTH), :HEAD_SIZE])
                scores = jnp.where(ahead <= t * some, scores, NEG)
                before = gather_column(sbuf[p, where, :])
                top = jnp.maximum(jnp.max(scores, axis=1, keepdims=True), before)
                weights = jnp.exp2(scores - top).astype(BF16)
                share = jnp.exp2(before - top)
                mixed = jnp.dot(weights, vbuf[...], preferred_element_type=F32)
                total = mixed[:, HEAD_SIZE:] + share
                keep = lax.broadcasted_iota(jnp.int32, (some, HEAD_SIZE), 0) + t * some < count
                for h in range(HEADS):
                    lanes = slice(h * HEAD_SIZE, (h + 1) * HEAD_SIZE)
                    stack = slice(h * some, (h + 1) * some)
                    old = pbuf[p, where, lanes].astype(F32)
                    value = (mixed[stack, :HEAD_SIZE] + old * share[stack]) / total[stack]
                    obuf[p, where, lanes] = jnp.where(keep, value, 0.0).astype(BF16)

        out_copy(p).start()
        return start + lax.shift_right_logical(count + (G - 1), 4)

    lax.fori_loop(0, LOCAL, prompt, jnp.int32(0))
    for p in range(LOCAL):
        out_copy(p).wait()


def fresh(meta, pieces, query, prior_out, prior_stat):
    wide, narrow = (LOCAL, FINAL_LENGTH, HEADS * HEAD_SIZE), (LOCAL, FINAL_LENGTH, HEAD_SIZE)
    return call(
        fresh_kernel,
        meta,
        (*pieces, query, prior_out, prior_stat),
        pltpu.HBM(wide, BF16),
        [
            pltpu.VMEM(((LOCAL + 1) * FINAL_LENGTH, PAIR), BF16),
            pltpu.VMEM((FINAL_LENGTH, PAIR), BF16),
            pltpu.VMEM(wide, BF16),
            pltpu.VMEM(wide, BF16),
            pltpu.VMEM(narrow, F32),
            pltpu.VMEM(wide, BF16),
            pltpu.VMEM((8, HEAD_SIZE), F32),
            pltpu.VMEM((8, HEAD_SIZE), F32),
            pltpu.SemaphoreType.DMA((4,)),
            pltpu.SemaphoreType.DMA((LOCAL, TILES, 3)),
            pltpu.SemaphoreType.DMA((LOCAL,)),
        ],
        flops=4 * 10**9,
        moved=10**7,
        vmem=40,
    )


def decode_kernel(ids, offs, lens, owner, *refs):
    pieces = refs[:3]
    asked, prior_out, prior_stat, out, fbuf, dpad, sem = refs[3:]
    copies = load_fresh(ids, *pieces, fbuf, sem)
    dpad[...] = jnp.zeros(dpad.shape, BF16)
    for slot in range(LOCAL):
        dpad[slot, :STEPS, :] = asked[slot]
    for c in copies:
        c.wait()
    starts, _, _ = plan(ids, offs, lens)
    n = HEADS * DROWS
    step = lax.bitwise_and(lax.broadcasted_iota(jnp.int32, (n, DROWS), 0), DROWS - 1)
    reached = lax.broadcasted_iota(jnp.int32, (n, DROWS), 1) <= step
    column = lax.broadcasted_iota(jnp.int32, (n, FINAL_LENGTH), 1)
    ones = jnp.ones((FINAL_LENGTH, HEAD_SIZE), BF16)

    def product(left, right):
        return jnp.dot(left, right, preferred_element_type=F32)

    def scores(p, start):
        i = ids[3] * LOCAL + p
        slot = owner[i]
        keys = pl.ds(pl.multiple_of(start * G, G), FINAL_LENGTH)
        tile = jnp.concatenate(stack_heads(dpad[slot, :, : HEADS * HEAD_SIZE]), axis=0)
        recent = dpad[slot, :, HEADS * HEAD_SIZE :]
        block, near = scores_of(tile, fbuf[keys, :HEAD_SIZE]), scores_of(tile, recent[:, :HEAD_SIZE])
        allowed = column < lens[i] - offs[i]
        return slot, allowed, block, near, fbuf[keys, HEAD_SIZE:], recent[:, HEAD_SIZE:]

    def put(p, slot, mixed, total, share):
        for h in range(HEADS):
            lanes = slice(h * HEAD_SIZE, (h + 1) * HEAD_SIZE)
            stack = slice(h * DROWS, (h + 1) * DROWS)
            value = (mixed[stack] + prior_out[p, :, lanes].astype(F32) * share[stack]) / total[stack]
            out[slot, :, lanes] = value[:STEPS].astype(BF16)

    low = high = jnp.ones((8, HEAD_SIZE), F32)
    for p in range(LOCAL):
        slot, allowed, block, near, values, near_values = scores(p, starts[p])
        block = jnp.where(allowed, jnp.exp2(block), 0.0).astype(BF16)
        near = jnp.where(reached, jnp.exp2(near), 0.0).astype(BF16)
        share = gather_column(jnp.exp2(prior_stat[p]))
        total = product(block, ones) + product(near, ones[:DROWS]) + share
        low, high = jnp.minimum(low, smallest(total)), jnp.maximum(high, largest(total))
        put(p, slot, product(block, values) + product(near, near_values), total, share)

    fine = jnp.logical_and(jnp.min(low) >= LOW, jnp.max(high) <= HIGH)

    @pl.when(jnp.logical_not(fine))
    def _():
        for p in range(LOCAL):
            slot, allowed, block, near, values, near_values = scores(p, starts[p])
            block, near = jnp.where(allowed, block, NEG), jnp.where(reached, near, NEG)
            before = gather_column(prior_stat[p])
            top = jnp.maximum(jnp.max(block, axis=1, keepdims=True), jnp.max(near, axis=1, keepdims=True))
            top = jnp.maximum(top, before)
            block, near, share = jnp.exp2(block - top), jnp.exp2(near - top), jnp.exp2(before - top)
            total = jnp.sum(block, axis=1, keepdims=True) + jnp.sum(near, axis=1, keepdims=True) + share
            put(p, slot, product(block.astype(BF16), values) + product(near.astype(BF16), near_values), total, share)


def decode(meta, owner, pieces, asked, prior_out, prior_stat):
    return call(
        decode_kernel,
        (*meta, owner),
        (*pieces, asked, prior_out, prior_stat),
        jax.ShapeDtypeStruct((LOCAL, STEPS, HEADS * HEAD_SIZE), BF16),
        [
            pltpu.VMEM(((LOCAL + 1) * FINAL_LENGTH, PAIR), BF16),
            pltpu.VMEM((LOCAL, DROWS, HEADS * HEAD_SIZE + PAIR), BF16),
            pltpu.SemaphoreType.DMA((4,)),
        ],
        specs=[ANY] * 3 + [VMEM] * 3,
        out_specs=VMEM,
        flops=10**8,
        moved=2 * 10**6,
    )


def exchange(value):
    return lax.all_to_all(value, "grp", split_axis=0, concat_axis=0, tiled=True)


def permute(value, way):
    return lax.ppermute(value, "tp", way)


def after(value, *others):
    return lax.optimization_barrier((value, *others))[0]


def spread_sums(sent, ways):
    arrived = [None] * 3
    for i in ORDER:
        arrived[i] = permute(sent[i], ways[i])
    return arrived


def in_hbm(value):
    return pltpu.with_memory_space_constraint(value, pltpu.HBM)


def rest_of_keys(meta, hid, weight, table, base, q):
    half, _ = send_half(meta, hid, weight, base, q)
    local, *sent = keep_half(meta, hid, weight, permute(half, SIBLING), base, q)
    kept, *sent = middle(meta[0], local, spread_sums(sent, FIRST), q)
    new = finish(meta, kept, spread_sums(sent, SECOND), rope_rows(meta, table, base, q), base, q)
    return jnp.stack([new, permute(new, SIBLING)])


def per_device(
    hidden_rows,
    key_value_weight,
    prefill_query,
    earlier_cache,
    stretch_offset,
    prompt_length,
    decode_owner,
    decode_query,
    decode_kv,
):
    lane = lax.axis_index("tp")
    group = lax.axis_index("grp")
    ids = jnp.stack([lane // 4, lane // 2 % 2, lane % 2, group]).astype(jnp.int32)
    meta = (ids, stretch_offset, prompt_length)
    table = jnp.asarray(rope_table())
    hid = hidden_rows.reshape(LOCAL * FINAL_LENGTH, -1)
    cache = in_hbm(earlier_cache.reshape(LOCAL, PART, PAIR))
    hid, key_value_weight, prefill_query = (in_hbm(a) for a in (hid, key_value_weight, prefill_query))
    q = ROOM // 2

    half, more = send_half(meta, hid, key_value_weight, 0, q)
    other_half = permute(half, SIBLING)
    other_cache = permute(cache, SIBLING)
    recent = lax.dynamic_slice_in_dim(decode_kv, (lane // 2) * PAIR, PAIR, 2)
    asked = exchange(jnp.concatenate([decode_query, recent], axis=2))
    beyond = LOCAL * FINAL_LENGTH - ROOM
    rest = lax.cond(
        more[0] > 0,
        lambda *a: rest_of_keys(a[:3], *a[3:], ROOM, beyond // 2),
        lambda *a: jnp.zeros((2, beyond // 2, PAIR), BF16),
        *meta,
        hid,
        key_value_weight,
        table,
    )

    local, *sent = keep_half(meta, hid, key_value_weight, after(other_half, rest, asked), 0, q)
    arrived = spread_sums(sent, FIRST)

    common = (meta, decode_owner, prefill_query, asked, cache, other_cache)
    *before, turn = prior(*common, 0, 6, table=after(table, local), q=q)
    kept, *sent = middle(ids, after(local, turn), arrived, q)
    arrived = spread_sums(sent, SECOND)
    prior_out, prior_stat, prior_dout, prior_dstat = (in_hbm(a) for a in prior(*common, 6, 2, before=before))
    new = finish(meta, after(kept, prior_dstat), arrived, turn, 0, q)
    pieces = (new, permute(new, SIBLING), rest)

    answer = decode(meta, decode_owner, pieces, asked, prior_dout, prior_dstat)
    decode_out = exchange(answer)
    prefill_out = fresh(meta, pieces, prefill_query, prior_out, prior_stat)
    return (prefill_out, decode_out)


def solution(mesh):
    in_specs = (
        P("grp", None, "tp"),
        P("tp", None),
        P("grp", None, "tp"),
        P("grp", "tp", None, None),
        P(),
        P(),
        P(),
        P("grp", None, "tp"),
        P("grp", None, None),
    )
    out_specs = (P("grp", None, "tp"), P("grp", None, "tp"))
    return jax.shard_map(
        per_device, mesh=mesh, in_specs=in_specs, out_specs=out_specs, check_vma=False
    )
```

```python
import functools
import math

import jax
import jax.numpy as jnp
import numpy as np
from jax import lax
from jax.experimental import pallas as pl
from jax.experimental.pallas import tpu as pltpu
from jax.sharding import PartitionSpec as P

HEAD_SIZE = 128
PAIR = 2 * HEAD_SIZE
LOCAL = 8
FINAL_LENGTH = 256
CONTEXT_LENGTH = 1024
PART = 512
STEPS = 4
HEADS = 8
ROPE_BASE = 500000.0
G = 16
DROWS = 16
TILE = 128
SCALE2 = HEAD_SIZE**-0.5 * math.log2(math.e)
NEG = -1e30
F32 = jnp.float32
BF16 = jnp.bfloat16
ANY = pl.BlockSpec(memory_space=pl.ANY)
VMEM = pl.BlockSpec(memory_space=pltpu.VMEM)
HBM = pl.BlockSpec(memory_space=pltpu.HBM)
SMALL, LARGE = 26, 60
ROOM = 1792
LOW, HIGH = 2.0**-100, 2.0**100


def pairs(*moves):
    out = []
    for x in range(4):
        for z in range(2):
            for core in range(2):
                if moves[core] is None:
                    continue
                dx, dz, dc = moves[core]
                out.append((x * 4 + z * 2 + core, (x + dx) % 4 * 4 + (z + dz) % 2 * 2 + (core + dc) % 2))
    return out


SIBLING = pairs((0, 0, 1), (0, 0, 1))
FIRST = [pairs((1, 0, 0), (0, 1, 0)), pairs((2, 0, 0), None), pairs((3, 0, 0), (0, 1, 0))]
SECOND = [pairs((0, 1, 0), (1, 0, 0)), pairs(None, (2, 0, 0)), pairs(None, (3, 0, 0))]
ORDER = (0, 2, 1)


def rope_table():
    half = HEAD_SIZE // 2
    freq = ROPE_BASE ** (np.arange(half, dtype=np.float64) * (-2.0 / HEAD_SIZE))
    angle = np.arange(CONTEXT_LENGTH + FINAL_LENGTH, dtype=np.float64)[:, None] * freq
    cosine, sine = np.cos(angle), np.sin(angle)
    return np.concatenate([cosine, cosine, -sine, sine], axis=1).astype(np.float32)


def plan(ids, offs, lens):
    starts, counts, at = [], [], jnp.int32(0)
    for p in range(LOCAL):
        i = ids[3] * LOCAL + p
        count = lax.shift_right_logical(lens[i] - offs[i] + (G - 1), 4)
        starts.append(at)
        counts.append(count)
        at = at + count
    return starts, counts, at


def ragged(starts, counts, first_block, blocks, copy):
    for p in range(LOCAL):
        low = jnp.maximum(starts[p], first_block)
        high = jnp.minimum(starts[p] + counts[p], first_block + blocks)
        n = jnp.maximum(high - low, 0)
        for bit in range(4, -1, -1):
            done = lax.shift_left(lax.shift_right_logical(n, bit + 1), bit + 1)

            @pl.when(lax.bitwise_and(n, 1 << bit) != 0)
            def _(p=p, bit=bit, low=low, done=done):
                copy(p, bit, low + done - starts[p], low + done - first_block, 1 << bit)


def rows(block, count):
    return pl.ds(pl.multiple_of(block * G, G), count * G)


def project(ids, offs, lens, hid, w, hbuf, wbuf, hsem, wsem, first_block, blocks, ahead):
    starts, counts, total = plan(ids, offs, lens)

    def hidden_copy(p, bit, source, target, count):
        return pltpu.make_async_copy(
            hid.at[rows(p * (FINAL_LENGTH // G) + source, count)],
            hbuf.at[rows(target, count)],
            hsem.at[p, bit],
        )

    def weight_copy(d):
        first = lax.rem(ids[0] + d, 4) * (2 * PAIR)
        return pltpu.make_async_copy(
            w.at[:, pl.ds(pl.multiple_of(first, 2 * PAIR), 2 * PAIR)], wbuf.at[d], wsem.at[d]
        )

    weight_copy(0).start()
    ragged(starts, counts, first_block, blocks, lambda *a: hidden_copy(*a).start())

    @pl.loop(jnp.clip(total - first_block, 0, blocks), blocks)
    def _(b):
        hbuf[rows(b, 1), :] = jnp.zeros((G, hbuf.shape[1]), BF16)

    for d in range(1, 4):
        weight_copy(d).start()
    ragged(starts, counts, first_block, blocks, lambda *a: hidden_copy(*a).wait())
    ahead()

    def product(d, e, where):
        if e == 0 and where.start == 0:
            weight_copy(d).wait()
        columns = pl.ds(pl.multiple_of(lax.rem(ids[1] + e, 2) * PAIR, PAIR), PAIR)
        return jnp.dot(hbuf[where, :], wbuf[d, :, columns], preferred_element_type=F32)

    return product


def row_tiles(q):
    n = next(n for n in (256, 224, 208, 192, 176, 160, 128, 64) if q % n == 0)
    return [slice(r, r + n) for r in range(0, q, n)]


def send_kernel(ids, offs, lens, hid, w, out, more, hbuf, wbuf, obuf, hsem, wsem, osem, *, base, q):
    def count_rows():
        def group(g, most):
            total = jnp.int32(0)
            for p in range(LOCAL):
                i = g * LOCAL + p
                total = total + lax.shift_right_logical(lens[i] - offs[i] + (G - 1), 4)
            return jnp.maximum(most, total)

        most = lax.fori_loop(0, lens.shape[0] // LOCAL, group, jnp.int32(0))
        more[0] = (most * G > ROOM).astype(jnp.int32)

    first = base // G + (1 - ids[2]) * (q // G)
    product = project(ids, offs, lens, hid, w, hbuf, wbuf, hsem, wsem, first, q // G, count_rows)
    for j in range(8):
        for where in row_tiles(q):
            obuf[j, where, :] = product(j // 2, j % 2, where).astype(BF16)
        pltpu.make_async_copy(obuf.at[j], out.at[j], osem.at[j]).start()
    for j in range(8):
        pltpu.make_async_copy(obuf.at[j], out.at[j], osem.at[j]).wait()


def keep_kernel(ids, offs, lens, hid, w, other, local, s1, s2, s3, hbuf, wbuf, rbuf, obuf, hsem, wsem, rsem, osem, *, base, q):
    core = ids[2]

    def other_copy(j):
        return pltpu.make_async_copy(other.at[j], rbuf.at[j], rsem.at[j])

    def load_other():
        for j in range(8):
            other_copy(j).start()

    first = base // G + core * (q // G)
    product = project(ids, offs, lens, hid, w, hbuf, wbuf, hsem, wsem, first, q // G, load_other)

    def leave(j, verb):
        d, e = j // 2, j % 2
        along = (local, s1, s2, s3)[d].at[e]
        across = local.at[d] if e == 0 else (s1 if d < 2 else s3).at[d % 2]
        for c, target in enumerate((along, across)):

            @pl.when(core == c)
            def _(target=target):
                copy = pltpu.make_async_copy(obuf.at[j], target, osem.at[j])
                copy.start() if verb == "start" else copy.wait()

    for j in range(8):
        for where in row_tiles(q):
            value = product(j // 2, j % 2, where)
            if where.start == 0:
                other_copy(j).wait()
            obuf[j, where, :] = (value + rbuf[j, where, :].astype(F32)).astype(BF16)
        leave(j, "start")
    for j in range(8):
        leave(j, "wait")


def call(kernel, prefetched, operands, out_shape, scratch=(), specs=None, out_specs=None, grid=(), flops=0, moved=0, aliases=None, vmem=SMALL):
    n = len(prefetched)
    return pl.pallas_call(
        kernel,
        out_shape=out_shape,
        grid_spec=pltpu.PrefetchScalarGridSpec(
            num_scalar_prefetch=n,
            grid=grid,
            in_specs=specs if specs is not None else [ANY] * len(operands),
            out_specs=out_specs if out_specs is not None else jax.tree.map(lambda _: ANY, out_shape),
            scratch_shapes=list(scratch),
        ),
        compiler_params=pltpu.CompilerParams(vmem_limit_bytes=vmem * 2**20),
        input_output_aliases=aliases or {},
        cost_estimate=pl.CostEstimate(flops=flops, bytes_accessed=moved, transcendentals=0),
    )(*prefetched, *operands)


def half_scratch(q):
    return [pltpu.VMEM((q, 1024), BF16), pltpu.VMEM((4, 1024, 2 * PAIR), BF16)]


def half_semaphores():
    return [pltpu.SemaphoreType.DMA((LOCAL, 5)), pltpu.SemaphoreType.DMA((4,))]


def send_half(meta, hid, w, base, q):
    return call(
        functools.partial(send_kernel, base=base, q=q),
        meta,
        (hid, w),
        [pltpu.HBM((8, q, PAIR), BF16), jax.ShapeDtypeStruct((1,), jnp.int32)],
        half_scratch(q)
        + [pltpu.VMEM((8, q, PAIR), BF16)]
        + half_semaphores()
        + [pltpu.SemaphoreType.DMA((8,))],
        specs=[HBM, HBM],
        out_specs=[ANY, pl.BlockSpec(memory_space=pltpu.SMEM)],
        flops=2 * q * 1024 * 2048,
        moved=2 * (q * 1024 + 1024 * 2048 + q * 2048),
        vmem=LARGE,
    )


def keep_half(meta, hid, w, other, base, q):
    return call(
        functools.partial(keep_kernel, base=base, q=q),
        meta,
        (hid, w, other),
        [pltpu.HBM((n, q, PAIR), BF16) for n in (4, 2, 2, 2)],
        half_scratch(q)
        + [pltpu.VMEM((8, q, PAIR), BF16)] * 2
        + half_semaphores()
        + [pltpu.SemaphoreType.DMA((8,))] * 2,
        specs=[HBM, HBM, ANY],
        flops=2 * q * 1024 * 2048,
        moved=2 * (q * 1024 + 1024 * 2048 + 2 * q * 2048),
        vmem=LARGE,
    )


def middle_kernel(ids, local, r1, r2, r3, kept, s1, s2, s3):
    @pl.when(ids[2] == 0)
    def _():
        for e, out in ((0, kept), (1, s1)):
            total = (local[e].astype(F32) + r1[e].astype(F32)) + (r2[e].astype(F32) + r3[e].astype(F32))
            out[...] = total.astype(out.dtype)

    @pl.when(ids[2] == 1)
    def _():
        for d, out in enumerate((kept, s1, s2, s3)):
            arrived = (r1 if d < 2 else r3)[d % 2]
            out[...] = (local[d].astype(F32) + arrived.astype(F32)).astype(out.dtype)


def middle(ids, local, arrived, q):
    n = 2

    def three(i, ids):
        return (0, i, 0)

    def two(i, ids):
        return (i, 0)

    return call(
        middle_kernel,
        (ids,),
        (local, *arrived),
        [jax.ShapeDtypeStruct((q, PAIR), t) for t in (F32, BF16, BF16, BF16)],
        grid=(n,),
        specs=[pl.BlockSpec((a.shape[0], q // n, PAIR), three) for a in (local, *arrived)],
        out_specs=[pl.BlockSpec((q // n, PAIR), two)] * 4,
        moved=2 * PAIR * q * 15,
        flops=PAIR * q * 8,
    )


def rope_rows_kernel(ids, offs, lens, table, out, sem, *, base, q):
    starts, counts, _ = plan(ids, offs, lens)
    for verb in ("start", "wait"):

        def copy(p, bit, source, target, count, verb=verb):
            position = lax.shift_right_logical(offs[ids[3] * LOCAL + p], 4)
            c = pltpu.make_async_copy(
                table.at[rows(position + source, count)], out.at[rows(target, count)], sem.at[p, bit]
            )
            c.start() if verb == "start" else c.wait()

        ragged(starts, counts, base // G + ids[2] * (q // G), q // G, copy)


def rope_rows(meta, table, base, q):
    return call(
        functools.partial(rope_rows_kernel, base=base, q=q),
        meta,
        (table,),
        jax.ShapeDtypeStruct((q, PAIR), F32),
        [pltpu.SemaphoreType.DMA((LOCAL, 5))],
        specs=[HBM],
        moved=q * PAIR * 8,
    )


def finish_kernel(ids, offs, lens, kept, r1, r2, r3, turn, out, *, base, q):
    _, _, total = plan(ids, offs, lens)
    valid = (total - base // G - ids[2] * (q // G)) * G

    def put(value):
        row = lax.broadcasted_iota(jnp.int32, (q, HEAD_SIZE), 0)
        key = value[:, :HEAD_SIZE]
        key = key * turn[:, :HEAD_SIZE] + pltpu.roll(key, HEAD_SIZE // 2, 1) * turn[:, HEAD_SIZE:]
        out[:, :HEAD_SIZE] = jnp.where(row < valid, key, 0.0).astype(BF16)
        out[:, HEAD_SIZE:] = value[:, HEAD_SIZE:].astype(BF16)

    @pl.when(ids[2] == 0)
    def _():
        put(kept[...] + r1[...].astype(F32))

    @pl.when(ids[2] == 1)
    def _():
        put((kept[...] + r1[...].astype(F32)) + (r2[...].astype(F32) + r3[...].astype(F32)))


def finish(meta, kept, arrived, turn, base, q):
    return call(
        functools.partial(finish_kernel, base=base, q=q),
        meta,
        (kept, *arrived, turn),
        jax.ShapeDtypeStruct((q, PAIR), BF16),
        specs=[VMEM] * 5,
        out_specs=VMEM,
        moved=q * PAIR * 16,
        flops=q * PAIR * 4,
    )


def stack_heads(tile):
    return [tile[:, h * HEAD_SIZE : (h + 1) * HEAD_SIZE] for h in range(HEADS)]


def scores_of(query, keys):
    return lax.dot_general(query, keys, (((1,), (1,)), ((), ())), preferred_element_type=F32) * SCALE2


def spread(column, n):
    lane = lax.broadcasted_iota(jnp.int32, (n, HEAD_SIZE), 1)
    out = jnp.zeros((n, HEAD_SIZE), F32)
    for h in range(HEADS):
        out = jnp.where(lane == h, column[h * n : (h + 1) * n], out)
    return out


def smallest(value):
    return jnp.min(value.reshape(-1, 8, HEAD_SIZE), axis=0)


def largest(value):
    return jnp.max(value.reshape(-1, 8, HEAD_SIZE), axis=0)


def gather_column(stats):
    return jnp.concatenate([stats[:, h : h + 1] for h in range(HEADS)], axis=0)


def tile_rows(t):
    return slice(t * TILE, (t + 1) * TILE)


def when_tile(count, t):
    return pl.when(count > t * TILE)


TILES = FINAL_LENGTH // TILE


def prior_kernel(ids, offs, lens, owner, asked, query, mine, theirs, *refs, first, n, q):
    (*outs, qbuf, kbuf, vbuf, obuf, sbuf, dpad, dobuf, dsbuf, least, most, qsem, ksem, osem, dsem, tsem) = refs
    if q:
        table, *outs, turn = outs
    out, stat, dout, dstat = outs[-4:]
    core = ids[2]

    def place(i):
        at = ids[3] * LOCAL + first + i
        return offs[at], lens[at] - offs[at], owner[at]

    def query_copy(i, t):
        return pltpu.make_async_copy(query.at[first + i, tile_rows(t)], qbuf.at[i, tile_rows(t)], qsem.at[i, t])

    def key_copy(i, part):
        here = core if part == 0 else 1 - core
        target = kbuf.at[i, pl.ds(pl.multiple_of(here * PART, PART), PART)]
        return pltpu.make_async_copy((mine, theirs)[part].at[first + i], target, ksem.at[i, part])

    def when_part(offset, part):
        here = core if part == 0 else 1 - core
        return pl.when(jnp.logical_or(here == 0, offset > PART))

    def out_copies(i, t):
        return (
            pltpu.make_async_copy(obuf.at[i, tile_rows(t)], out.at[first + i, tile_rows(t)], osem.at[i, t, 0]),
            pltpu.make_async_copy(sbuf.at[i, tile_rows(t)], stat.at[first + i, tile_rows(t)], osem.at[i, t, 1]),
        )

    def decode_copies(i):
        return (
            pltpu.make_async_copy(dobuf.at[i], dout.at[first + i], dsem.at[i, 0]),
            pltpu.make_async_copy(dsbuf.at[i], dstat.at[first + i], dsem.at[i, 1]),
        )

    def load(i):
        offset, count, _ = place(i)
        for part in range(2):
            when_part(offset, part)(lambda: key_copy(i, part).start())
        for t in range(TILES):
            when_tile(count, t)(lambda: query_copy(i, t).start())

    def turn_copies(verb):
        starts, counts, _ = plan(ids, offs, lens)

        def copy(p, bit, source, target, count):
            position = lax.shift_right_logical(offs[ids[3] * LOCAL + p], 4)
            c = pltpu.make_async_copy(
                table.at[rows(position + source, count)], turn.at[rows(target, count)], tsem.at[p, bit]
            )
            c.start() if verb == "start" else c.wait()

        ragged(starts, counts, core * (q // G), q // G, copy)

    load(0)
    vbuf[:, HEAD_SIZE:] = jnp.ones((CONTEXT_LENGTH, HEAD_SIZE), BF16)
    dpad[...] = jnp.zeros(dpad.shape, BF16)
    if n > 1:
        load(1)
    if q:
        turn_copies("start")

    @pl.loop(0, n)
    def _(i):
        offset, count, slot = place(i)
        if n > 2:
            pl.when(i + 2 < n)(lambda: load(i + 2))
        for part in range(2):
            when_part(offset, part)(lambda part=part: key_copy(i, part).wait())
        for t in range(TILES):
            when_tile(count, t)(lambda t=t: query_copy(i, t).wait())
        dpad[:STEPS, :] = asked[slot, :, : HEADS * HEAD_SIZE]
        least[...] = jnp.full(least.shape, 1.0, F32)
        most[...] = jnp.full(most.shape, 1.0, F32)

        def put(where, value, stats, rows_of_head):
            for h in range(HEADS):
                lanes = slice(h * HEAD_SIZE, (h + 1) * HEAD_SIZE)
                obuf[i, where, lanes] = value[h * rows_of_head : (h + 1) * rows_of_head]
            sbuf[i, where, :] = spread(stats, rows_of_head)

        def put_decode(value, stats):
            for h in range(HEADS):
                dobuf[i, :, h * HEAD_SIZE : (h + 1) * HEAD_SIZE] = value[h * DROWS : (h + 1) * DROWS]
            dsbuf[i] = spread(stats, DROWS)

        for blocks in range(1, 5):

            @pl.when(offset == blocks * 256)
            def _(keys=blocks * 256):
                vbuf[:keys, :HEAD_SIZE] = kbuf[i, :keys, HEAD_SIZE:]
                for t in range(TILES):

                    @when_tile(count, t)
                    def _(t=t):
                        tile = stack_heads(qbuf[i, tile_rows(t), :])
                        if t == 0:
                            tile = tile + stack_heads(dpad[...])
                        tile = jnp.concatenate(tile, axis=0)
                        weights = jnp.exp2(scores_of(tile, kbuf[i, :keys, :HEAD_SIZE])).astype(BF16)
                        mixed = jnp.dot(weights, vbuf[:keys, :], preferred_element_type=F32)
                        total = mixed[:, HEAD_SIZE:]
                        least[...] = jnp.minimum(least[...], smallest(total))
                        most[...] = jnp.maximum(most[...], largest(total))
                        value = (mixed[:, :HEAD_SIZE] * (1.0 / total)).astype(BF16)
                        stats = jnp.log2(total)
                        m = HEADS * TILE
                        put(tile_rows(t), value[:m], stats[:m], TILE)
                        if t == 0:
                            put_decode(value[m:], stats[m:])

        fine = jnp.logical_and(jnp.min(least[...]) >= LOW, jnp.max(most[...]) <= HIGH)

        @pl.when(jnp.logical_not(fine))
        def _():
            def exact(tile):
                def block(b, carry):
                    top, mixed = carry
                    keys = pl.ds(pl.multiple_of(b * 256, 256), 256)
                    scores = scores_of(tile, kbuf[i, keys, :HEAD_SIZE])
                    now = jnp.maximum(jnp.max(scores, axis=1, keepdims=True), top)
                    weights = jnp.exp2(scores - now).astype(BF16)
                    more = jnp.dot(weights, vbuf[keys, :], preferred_element_type=F32)
                    return now, mixed * jnp.exp2(top - now) + more

                m = tile.shape[0]
                start = (jnp.full((m, 1), NEG, F32), jnp.zeros((m, PAIR), F32))
                top, mixed = lax.fori_loop(0, lax.shift_right_logical(offset, 8), block, start)
                total = mixed[:, HEAD_SIZE:]
                return (mixed[:, :HEAD_SIZE] / total).astype(BF16), top + jnp.log2(total)

            @pl.loop(0, lax.shift_right_logical(count + 31, 5))
            def _(t):
                where = pl.ds(pl.multiple_of(t * 32, 32), 32)
                put(where, *exact(jnp.concatenate(stack_heads(qbuf[i, where, :]), axis=0)), 32)

            put_decode(*exact(jnp.concatenate(stack_heads(dpad[...]), axis=0)))

        for t in range(TILES):
            when_tile(count, t)(lambda t=t: [c.start() for c in out_copies(i, t)] and None)
        for c in decode_copies(i):
            c.start()

    for i in range(n):
        _, count, _ = place(i)
        for t in range(TILES):
            when_tile(count, t)(lambda i=i, t=t: [c.wait() for c in out_copies(i, t)] and None)
        for c in decode_copies(i):
            c.wait()
    if q:
        turn_copies("wait")


def prior(meta, owner, query, asked, mine, theirs, first, n, before=(), table=None, q=0):
    wide, narrow = (FINAL_LENGTH, HEADS * HEAD_SIZE), (FINAL_LENGTH, HEAD_SIZE)
    dwide, dnarrow = (DROWS, HEADS * HEAD_SIZE), (DROWS, HEAD_SIZE)
    shapes = [(wide, BF16), (narrow, F32), (dwide, BF16), (dnarrow, F32)]
    return call(
        functools.partial(prior_kernel, first=first, n=n, q=q),
        (*meta, owner),
        (asked, query, mine, theirs, *before, *([table] if q else [])),
        [pltpu.HBM((LOCAL, *s), t) for s, t in shapes] + ([jax.ShapeDtypeStruct((q, PAIR), F32)] if q else []),
        [
            pltpu.VMEM((n, *wide), BF16),
            pltpu.VMEM((n, CONTEXT_LENGTH, PAIR), BF16),
            pltpu.VMEM((CONTEXT_LENGTH, PAIR), BF16),
            pltpu.VMEM((n, *wide), BF16),
            pltpu.VMEM((n, *narrow), F32),
            pltpu.VMEM(dwide, BF16),
            pltpu.VMEM((n, *dwide), BF16),
            pltpu.VMEM((n, *dnarrow), F32),
            pltpu.VMEM((8, HEAD_SIZE), F32),
            pltpu.VMEM((8, HEAD_SIZE), F32),
            pltpu.SemaphoreType.DMA((n, TILES)),
            pltpu.SemaphoreType.DMA((n, 2)),
            pltpu.SemaphoreType.DMA((n, TILES, 2)),
            pltpu.SemaphoreType.DMA((n, 2)),
            pltpu.SemaphoreType.DMA((LOCAL, 5)),
        ],
        specs=[VMEM] + [ANY] * (3 + len(before) + (q > 0)),
        aliases={8 + i: i for i in range(len(before))},
        flops=n * 3 * 10**9,
        moved=n * 2 * 10**6,
    )


def load_fresh(ids, own, other, rest, fbuf, sem):
    copies, base = [], 0
    for c, pieces in enumerate(((own, other), (rest.at[0], rest.at[1]))):
        q = pieces[0].shape[0]
        for i, core in enumerate((ids[2], 1 - ids[2])):
            target = fbuf.at[pl.ds(pl.multiple_of(base + core * q, G), q)]
            copies.append(pltpu.make_async_copy(pieces[i], target, sem.at[2 * c + i]))
        base += 2 * q
    for c in copies:
        c.start()
    fbuf[base:, :] = jnp.zeros((FINAL_LENGTH, PAIR), BF16)
    return copies


def fresh_kernel(ids, offs, lens, *refs):
    pieces = refs[:3]
    query, prior_out, prior_stat, out, fbuf, vbuf, qbuf, pbuf, sbuf, obuf, least, most, sem, isem, osem = refs[3:]

    def count_of(p):
        at = ids[3] * LOCAL + p
        return lens[at] - offs[at]

    def in_copies(p, t):
        pairs_of = ((query, qbuf), (prior_out, pbuf), (prior_stat, sbuf))
        return [
            pltpu.make_async_copy(ref.at[p, tile_rows(t)], buf.at[p, tile_rows(t)], isem.at[p, t, i])
            for i, (ref, buf) in enumerate(pairs_of)
        ]

    def out_copy(p):
        return pltpu.make_async_copy(obuf.at[p], out.at[p], osem.at[p])

    def load(p):
        for t in range(TILES):
            when_tile(count_of(p), t)(lambda: [c.start() for c in in_copies(p, t)] and None)

    load(0)
    copies = load_fresh(ids, *pieces, fbuf, sem)
    vbuf[:, HEAD_SIZE:] = jnp.ones((FINAL_LENGTH, HEAD_SIZE), BF16)
    load(1)
    for c in copies:
        c.wait()

    def prompt(p, start):
        count = count_of(p)
        pl.when(p + 2 < LOCAL)(lambda: load(p + 2))
        first_key = pl.multiple_of(start * G, G)
        vbuf[:, :HEAD_SIZE] = fbuf[pl.ds(first_key, FINAL_LENGTH), HEAD_SIZE:]
        least[...] = jnp.full(least.shape, 1.0, F32)
        most[...] = jnp.full(most.shape, 1.0, F32)

        for t in range(TILES):
            where = tile_rows(t)

            @pl.when(count <= t * TILE)
            def _(where=where):
                obuf[p, where, :] = jnp.zeros((TILE, HEADS * HEAD_SIZE), BF16)

            @when_tile(count, t)
            def _(where=where, t=t):
                for c in in_copies(p, t):
                    c.wait()
                seen = (t + 1) * TILE
                row = lax.broadcasted_iota(jnp.int32, (TILE, seen), 0) + t * TILE
                allowed = lax.broadcasted_iota(jnp.int32, (TILE, seen), 1) <= row
                tile = jnp.concatenate(stack_heads(qbuf[p, where, :]), axis=0)
                scores = scores_of(tile, fbuf[pl.ds(first_key, seen), :HEAD_SIZE])
                weights = jnp.concatenate(
                    [
                        jnp.where(allowed, jnp.exp2(scores[h * TILE : (h + 1) * TILE]), 0.0).astype(BF16)
                        for h in range(HEADS)
                    ],
                    axis=0,
                )
                mixed = jnp.dot(weights, vbuf[:seen, :], preferred_element_type=F32)
                keep = lax.broadcasted_iota(jnp.int32, (TILE, HEAD_SIZE), 0) + t * TILE < count
                before = jnp.exp2(sbuf[p, where, :])
                low, high = least[...], most[...]
                for h in range(HEADS):
                    lanes = slice(h * HEAD_SIZE, (h + 1) * HEAD_SIZE)
                    stack = slice(h * TILE, (h + 1) * TILE)
                    share = before[:, h : h + 1]
                    total = mixed[stack, HEAD_SIZE:] + share
                    low, high = jnp.minimum(low, smallest(total)), jnp.maximum(high, largest(total))
                    old = pbuf[p, where, lanes].astype(F32)
                    value = (mixed[stack, :HEAD_SIZE] + old * share) * (1.0 / total)
                    obuf[p, where, lanes] = jnp.where(keep, value, 0.0).astype(BF16)
                least[...], most[...] = low, high

        fine = jnp.logical_and(jnp.min(least[...]) >= LOW, jnp.max(most[...]) <= HIGH)

        @pl.when(jnp.logical_not(fine))
        def _():
            some = 32
            n = HEADS * some

            @pl.loop(0, lax.shift_right_logical(count + (some - 1), 5))
            def _(t):
                where = pl.ds(pl.multiple_of(t * some, some), some)
                position = lax.bitwise_and(lax.broadcasted_iota(jnp.int32, (n, FINAL_LENGTH), 0), some - 1)
                ahead = lax.broadcasted_iota(jnp.int32, (n, FINAL_LENGTH), 1) - position
                tile = jnp.concatenate(stack_heads(qbuf[p, where, :]), axis=0)
                scores = scores_of(tile, fbuf[pl.ds(first_key, FINAL_LENGTH), :HEAD_SIZE])
                scores = jnp.where(ahead <= t * some, scores, NEG)
                before = gather_column(sbuf[p, where, :])
                top = jnp.maximum(jnp.max(scores, axis=1, keepdims=True), before)
                weights = jnp.exp2(scores - top).astype(BF16)
                share = jnp.exp2(before - top)
                mixed = jnp.dot(weights, vbuf[...], preferred_element_type=F32)
                total = mixed[:, HEAD_SIZE:] + share
                keep = lax.broadcasted_iota(jnp.int32, (some, HEAD_SIZE), 0) + t * some < count
                for h in range(HEADS):
                    lanes = slice(h * HEAD_SIZE, (h + 1) * HEAD_SIZE)
                    stack = slice(h * some, (h + 1) * some)
                    old = pbuf[p, where, lanes].astype(F32)
                    value = (mixed[stack, :HEAD_SIZE] + old * share[stack]) / total[stack]
                    obuf[p, where, lanes] = jnp.where(keep, value, 0.0).astype(BF16)

        out_copy(p).start()
        return start + lax.shift_right_logical(count + (G - 1), 4)

    lax.fori_loop(0, LOCAL, prompt, jnp.int32(0))
    for p in range(LOCAL):
        out_copy(p).wait()


def fresh(meta, pieces, query, prior_out, prior_stat):
    wide, narrow = (LOCAL, FINAL_LENGTH, HEADS * HEAD_SIZE), (LOCAL, FINAL_LENGTH, HEAD_SIZE)
    return call(
        fresh_kernel,
        meta,
        (*pieces, query, prior_out, prior_stat),
        pltpu.HBM(wide, BF16),
        [
            pltpu.VMEM(((LOCAL + 1) * FINAL_LENGTH, PAIR), BF16),
            pltpu.VMEM((FINAL_LENGTH, PAIR), BF16),
            pltpu.VMEM(wide, BF16),
            pltpu.VMEM(wide, BF16),
            pltpu.VMEM(narrow, F32),
            pltpu.VMEM(wide, BF16),
            pltpu.VMEM((8, HEAD_SIZE), F32),
            pltpu.VMEM((8, HEAD_SIZE), F32),
            pltpu.SemaphoreType.DMA((4,)),
            pltpu.SemaphoreType.DMA((LOCAL, TILES, 3)),
            pltpu.SemaphoreType.DMA((LOCAL,)),
        ],
        flops=4 * 10**9,
        moved=10**7,
        vmem=40,
    )


def decode_kernel(ids, offs, lens, owner, *refs):
    pieces = refs[:3]
    asked, prior_out, prior_stat, out, fbuf, dpad, sem = refs[3:]
    copies = load_fresh(ids, *pieces, fbuf, sem)
    dpad[...] = jnp.zeros(dpad.shape, BF16)
    for slot in range(LOCAL):
        dpad[slot, :STEPS, :] = asked[slot]
    for c in copies:
        c.wait()
    starts, _, _ = plan(ids, offs, lens)
    n = HEADS * DROWS
    step = lax.bitwise_and(lax.broadcasted_iota(jnp.int32, (n, DROWS), 0), DROWS - 1)
    reached = lax.broadcasted_iota(jnp.int32, (n, DROWS), 1) <= step
    column = lax.broadcasted_iota(jnp.int32, (n, FINAL_LENGTH), 1)
    ones = jnp.ones((FINAL_LENGTH, HEAD_SIZE), BF16)

    def product(left, right):
        return jnp.dot(left, right, preferred_element_type=F32)

    def scores(p, start):
        i = ids[3] * LOCAL + p
        slot = owner[i]
        keys = pl.ds(pl.multiple_of(start * G, G), FINAL_LENGTH)
        tile = jnp.concatenate(stack_heads(dpad[slot, :, : HEADS * HEAD_SIZE]), axis=0)
        recent = dpad[slot, :, HEADS * HEAD_SIZE :]
        block, near = scores_of(tile, fbuf[keys, :HEAD_SIZE]), scores_of(tile, recent[:, :HEAD_SIZE])
        allowed = column < lens[i] - offs[i]
        return slot, allowed, block, near, fbuf[keys, HEAD_SIZE:], recent[:, HEAD_SIZE:]

    def put(p, slot, mixed, total, share):
        for h in range(HEADS):
            lanes = slice(h * HEAD_SIZE, (h + 1) * HEAD_SIZE)
            stack = slice(h * DROWS, (h + 1) * DROWS)
            value = (mixed[stack] + prior_out[p, :, lanes].astype(F32) * share[stack]) / total[stack]
            out[slot, :, lanes] = value[:STEPS].astype(BF16)

    low = high = jnp.ones((8, HEAD_SIZE), F32)
    for p in range(LOCAL):
        slot, allowed, block, near, values, near_values = scores(p, starts[p])
        block = jnp.where(allowed, jnp.exp2(block), 0.0).astype(BF16)
        near = jnp.where(reached, jnp.exp2(near), 0.0).astype(BF16)
        share = gather_column(jnp.exp2(prior_stat[p]))
        total = product(block, ones) + product(near, ones[:DROWS]) + share
        low, high = jnp.minimum(low, smallest(total)), jnp.maximum(high, largest(total))
        put(p, slot, product(block, values) + product(near, near_values), total, share)

    fine = jnp.logical_and(jnp.min(low) >= LOW, jnp.max(high) <= HIGH)

    @pl.when(jnp.logical_not(fine))
    def _():
        for p in range(LOCAL):
            slot, allowed, block, near, values, near_values = scores(p, starts[p])
            block, near = jnp.where(allowed, block, NEG), jnp.where(reached, near, NEG)
            before = gather_column(prior_stat[p])
            top = jnp.maximum(jnp.max(block, axis=1, keepdims=True), jnp.max(near, axis=1, keepdims=True))
            top = jnp.maximum(top, before)
            block, near, share = jnp.exp2(block - top), jnp.exp2(near - top), jnp.exp2(before - top)
            total = jnp.sum(block, axis=1, keepdims=True) + jnp.sum(near, axis=1, keepdims=True) + share
            put(p, slot, product(block.astype(BF16), values) + product(near.astype(BF16), near_values), total, share)


def decode(meta, owner, pieces, asked, prior_out, prior_stat):
    return call(
        decode_kernel,
        (*meta, owner),
        (*pieces, asked, prior_out, prior_stat),
        jax.ShapeDtypeStruct((LOCAL, STEPS, HEADS * HEAD_SIZE), BF16),
        [
            pltpu.VMEM(((LOCAL + 1) * FINAL_LENGTH, PAIR), BF16),
            pltpu.VMEM((LOCAL, DROWS, HEADS * HEAD_SIZE + PAIR), BF16),
            pltpu.SemaphoreType.DMA((4,)),
        ],
        specs=[ANY] * 3 + [VMEM] * 3,
        out_specs=VMEM,
        flops=10**8,
        moved=2 * 10**6,
    )


def exchange(value):
    return lax.all_to_all(value, "grp", split_axis=0, concat_axis=0, tiled=True)


def permute(value, way):
    return lax.ppermute(value, "tp", way)


def after(value, *others):
    return lax.optimization_barrier((value, *others))[0]


def spread_sums(sent, ways):
    arrived = [None] * 3
    for i in ORDER:
        arrived[i] = permute(sent[i], ways[i])
    return arrived


def in_hbm(value):
    return pltpu.with_memory_space_constraint(value, pltpu.HBM)


def rest_of_keys(meta, hid, weight, table, base, q):
    half, _ = send_half(meta, hid, weight, base, q)
    local, *sent = keep_half(meta, hid, weight, permute(half, SIBLING), base, q)
    kept, *sent = middle(meta[0], local, spread_sums(sent, FIRST), q)
    new = finish(meta, kept, spread_sums(sent, SECOND), rope_rows(meta, table, base, q), base, q)
    return jnp.stack([new, permute(new, SIBLING)])


def per_device(
    hidden_rows,
    key_value_weight,
    prefill_query,
    earlier_cache,
    stretch_offset,
    prompt_length,
    decode_owner,
    decode_query,
    decode_kv,
):
    lane = lax.axis_index("tp")
    group = lax.axis_index("grp")
    ids = jnp.stack([lane // 4, lane // 2 % 2, lane % 2, group]).astype(jnp.int32)
    meta = (ids, stretch_offset, prompt_length)
    table = jnp.asarray(rope_table())
    hid = hidden_rows.reshape(LOCAL * FINAL_LENGTH, -1)
    cache = in_hbm(earlier_cache.reshape(LOCAL, PART, PAIR))
    hid, key_value_weight, prefill_query = (in_hbm(a) for a in (hid, key_value_weight, prefill_query))
    q = ROOM // 2

    half, more = send_half(meta, hid, key_value_weight, 0, q)
    other_half = permute(half, SIBLING)
    other_cache = permute(cache, SIBLING)
    recent = lax.dynamic_slice_in_dim(decode_kv, (lane // 2) * PAIR, PAIR, 2)
    asked = exchange(jnp.concatenate([decode_query, recent], axis=2))
    beyond = LOCAL * FINAL_LENGTH - ROOM
    rest = lax.cond(
        more[0] > 0,
        lambda *a: rest_of_keys(a[:3], *a[3:], ROOM, beyond // 2),
        lambda *a: jnp.zeros((2, beyond // 2, PAIR), BF16),
        *meta,
        hid,
        key_value_weight,
        table,
    )

    local, *sent = keep_half(meta, hid, key_value_weight, after(other_half, rest, asked), 0, q)
    arrived = spread_sums(sent, FIRST)

    common = (meta, decode_owner, prefill_query, asked, cache, other_cache)
    *before, turn = prior(*common, 0, 7, table=after(table, local), q=q)
    kept, *sent = middle(ids, after(local, turn), arrived, q)
    arrived = spread_sums(sent, SECOND)
    prior_out, prior_stat, prior_dout, prior_dstat = (in_hbm(a) for a in prior(*common, 7, 1, before=before))
    new = finish(meta, after(kept, prior_dstat), arrived, turn, 0, q)
    pieces = (new, permute(new, SIBLING), rest)

    answer = decode(meta, decode_owner, pieces, asked, prior_dout, prior_dstat)
    decode_out = exchange(answer)
    prefill_out = fresh(meta, pieces, prefill_query, prior_out, prior_stat)
    return (prefill_out, decode_out)


def solution(mesh):
    in_specs = (
        P("grp", None, "tp"),
        P("tp", None),
        P("grp", None, "tp"),
        P("grp", "tp", None, None),
        P(),
        P(),
        P(),
        P("grp", None, "tp"),
        P("grp", None, None),
    )
    out_specs = (P("grp", None, "tp"), P("grp", None, "tp"))
    return jax.shard_map(
        per_device, mesh=mesh, in_specs=in_specs, out_specs=out_specs, check_vma=False
    )
```

```python
import functools
import math

import jax
import jax.numpy as jnp
import numpy as np
from jax import lax
from jax.experimental import pallas as pl
from jax.experimental.pallas import tpu as pltpu
from jax.sharding import PartitionSpec as P

HEAD_SIZE = 128
PAIR = 2 * HEAD_SIZE
LOCAL = 8
FINAL_LENGTH = 256
CONTEXT_LENGTH = 1024
PART = 512
STEPS = 4
HEADS = 8
ROPE_BASE = 500000.0
G = 16
DROWS = 16
TILE = 128
SCALE2 = HEAD_SIZE**-0.5 * math.log2(math.e)
NEG = -1e30
F32 = jnp.float32
BF16 = jnp.bfloat16
ANY = pl.BlockSpec(memory_space=pl.ANY)
VMEM = pl.BlockSpec(memory_space=pltpu.VMEM)
HBM = pl.BlockSpec(memory_space=pltpu.HBM)
SMALL, LARGE = 26, 56
ROOM = 1792
LOW, HIGH = 2.0**-100, 2.0**100


def pairs(*moves):
    out = []
    for x in range(4):
        for z in range(2):
            for core in range(2):
                if moves[core] is None:
                    continue
                dx, dz, dc = moves[core]
                out.append((x * 4 + z * 2 + core, (x + dx) % 4 * 4 + (z + dz) % 2 * 2 + (core + dc) % 2))
    return out


SIBLING = pairs((0, 0, 1), (0, 0, 1))
FIRST = [pairs((1, 0, 0), (0, 1, 0)), pairs((2, 0, 0), None), pairs((3, 0, 0), (0, 1, 0))]
SECOND = [pairs((0, 1, 0), (1, 0, 0)), pairs(None, (2, 0, 0)), pairs(None, (3, 0, 0))]
ORDER = (0, 2, 1)


def rope_table():
    half = HEAD_SIZE // 2
    freq = ROPE_BASE ** (np.arange(half, dtype=np.float64) * (-2.0 / HEAD_SIZE))
    angle = np.arange(CONTEXT_LENGTH + FINAL_LENGTH, dtype=np.float64)[:, None] * freq
    cosine, sine = np.cos(angle), np.sin(angle)
    return np.concatenate([cosine, cosine, -sine, sine], axis=1).astype(np.float32)


def plan(ids, offs, lens):
    starts, counts, at = [], [], jnp.int32(0)
    for p in range(LOCAL):
        i = ids[3] * LOCAL + p
        count = lax.shift_right_logical(lens[i] - offs[i] + (G - 1), 4)
        starts.append(at)
        counts.append(count)
        at = at + count
    return starts, counts, at


def ragged(starts, counts, first_block, blocks, copy):
    for p in range(LOCAL):
        low = jnp.maximum(starts[p], first_block)
        high = jnp.minimum(starts[p] + counts[p], first_block + blocks)
        n = jnp.maximum(high - low, 0)
        for bit in range(4, -1, -1):
            done = lax.shift_left(lax.shift_right_logical(n, bit + 1), bit + 1)

            @pl.when(lax.bitwise_and(n, 1 << bit) != 0)
            def _(p=p, bit=bit, low=low, done=done):
                copy(p, bit, low + done - starts[p], low + done - first_block, 1 << bit)


def rows(block, count):
    return pl.ds(pl.multiple_of(block * G, G), count * G)


def project(ids, offs, lens, hid, w, hbuf, wbuf, hsem, wsem, first_block, blocks, ahead):
    starts, counts, total = plan(ids, offs, lens)

    def hidden_copy(p, bit, source, target, count):
        return pltpu.make_async_copy(
            hid.at[rows(p * (FINAL_LENGTH // G) + source, count)],
            hbuf.at[rows(target, count)],
            hsem.at[p, bit],
        )

    def weight_copy(d):
        first = lax.rem(ids[0] + d, 4) * (2 * PAIR)
        return pltpu.make_async_copy(
            w.at[:, pl.ds(pl.multiple_of(first, 2 * PAIR), 2 * PAIR)], wbuf.at[d], wsem.at[d]
        )

    weight_copy(0).start()
    ragged(starts, counts, first_block, blocks, lambda *a: hidden_copy(*a).start())

    @pl.loop(jnp.clip(total - first_block, 0, blocks), blocks)
    def _(b):
        hbuf[rows(b, 1), :] = jnp.zeros((G, hbuf.shape[1]), BF16)

    for d in range(1, 4):
        weight_copy(d).start()
    ragged(starts, counts, first_block, blocks, lambda *a: hidden_copy(*a).wait())
    ahead()

    def product(d, e, where):
        if e == 0 and where.start == 0:
            weight_copy(d).wait()
        columns = pl.ds(pl.multiple_of(lax.rem(ids[1] + e, 2) * PAIR, PAIR), PAIR)
        return jnp.dot(hbuf[where, :], wbuf[d, :, columns], preferred_element_type=F32)

    return product


def row_tiles(q):
    n = next(n for n in (256, 224, 208, 192, 176, 160, 128, 64) if q % n == 0)
    return [slice(r, r + n) for r in range(0, q, n)]


def send_kernel(ids, offs, lens, hid, w, out, more, hbuf, wbuf, obuf, hsem, wsem, osem, *, base, q):
    def count_rows():
        def group(g, most):
            total = jnp.int32(0)
            for p in range(LOCAL):
                i = g * LOCAL + p
                total = total + lax.shift_right_logical(lens[i] - offs[i] + (G - 1), 4)
            return jnp.maximum(most, total)

        most = lax.fori_loop(0, lens.shape[0] // LOCAL, group, jnp.int32(0))
        more[0] = (most * G > ROOM).astype(jnp.int32)

    first = base // G + (1 - ids[2]) * (q // G)
    product = project(ids, offs, lens, hid, w, hbuf, wbuf, hsem, wsem, first, q // G, count_rows)
    for j in range(8):
        for where in row_tiles(q):
            obuf[j, where, :] = product(j // 2, j % 2, where).astype(BF16)
        pltpu.make_async_copy(obuf.at[j], out.at[j], osem.at[j]).start()
    for j in range(8):
        pltpu.make_async_copy(obuf.at[j], out.at[j], osem.at[j]).wait()


def keep_kernel(ids, offs, lens, hid, w, other, local, s1, s2, s3, hbuf, wbuf, rbuf, obuf, hsem, wsem, rsem, osem, *, base, q):
    core = ids[2]

    def other_copy(j):
        return pltpu.make_async_copy(other.at[j], rbuf.at[j], rsem.at[j])

    def load_other():
        for j in range(8):
            other_copy(j).start()

    first = base // G + core * (q // G)
    product = project(ids, offs, lens, hid, w, hbuf, wbuf, hsem, wsem, first, q // G, load_other)

    def leave(j, verb):
        d, e = j // 2, j % 2
        along = (local, s1, s2, s3)[d].at[e]
        across = local.at[d] if e == 0 else (s1 if d < 2 else s3).at[d % 2]
        for c, target in enumerate((along, across)):

            @pl.when(core == c)
            def _(target=target):
                copy = pltpu.make_async_copy(obuf.at[j], target, osem.at[j])
                copy.start() if verb == "start" else copy.wait()

    for j in range(8):
        for where in row_tiles(q):
            value = product(j // 2, j % 2, where)
            if where.start == 0:
                other_copy(j).wait()
            obuf[j, where, :] = (value + rbuf[j, where, :].astype(F32)).astype(BF16)
        leave(j, "start")
    for j in range(8):
        leave(j, "wait")


def call(kernel, prefetched, operands, out_shape, scratch=(), specs=None, out_specs=None, grid=(), flops=0, moved=0, aliases=None, vmem=SMALL):
    n = len(prefetched)
    return pl.pallas_call(
        kernel,
        out_shape=out_shape,
        grid_spec=pltpu.PrefetchScalarGridSpec(
            num_scalar_prefetch=n,
            grid=grid,
            in_specs=specs if specs is not None else [ANY] * len(operands),
            out_specs=out_specs if out_specs is not None else jax.tree.map(lambda _: ANY, out_shape),
            scratch_shapes=list(scratch),
        ),
        compiler_params=pltpu.CompilerParams(vmem_limit_bytes=vmem * 2**20),
        input_output_aliases=aliases or {},
        cost_estimate=pl.CostEstimate(flops=flops, bytes_accessed=moved, transcendentals=0),
    )(*prefetched, *operands)


def half_scratch(q):
    return [pltpu.VMEM((q, 1024), BF16), pltpu.VMEM((4, 1024, 2 * PAIR), BF16)]


def half_semaphores():
    return [pltpu.SemaphoreType.DMA((LOCAL, 5)), pltpu.SemaphoreType.DMA((4,))]


def send_half(meta, hid, w, base, q):
    return call(
        functools.partial(send_kernel, base=base, q=q),
        meta,
        (hid, w),
        [pltpu.HBM((8, q, PAIR), BF16), jax.ShapeDtypeStruct((1,), jnp.int32)],
        half_scratch(q)
        + [pltpu.VMEM((8, q, PAIR), BF16)]
        + half_semaphores()
        + [pltpu.SemaphoreType.DMA((8,))],
        specs=[HBM, HBM],
        out_specs=[ANY, pl.BlockSpec(memory_space=pltpu.SMEM)],
        flops=2 * q * 1024 * 2048,
        moved=2 * (q * 1024 + 1024 * 2048 + q * 2048),
        vmem=LARGE,
    )


def keep_half(meta, hid, w, other, base, q):
    return call(
        functools.partial(keep_kernel, base=base, q=q),
        meta,
        (hid, w, other),
        [pltpu.HBM((n, q, PAIR), BF16) for n in (4, 2, 2, 2)],
        half_scratch(q)
        + [pltpu.VMEM((8, q, PAIR), BF16)] * 2
        + half_semaphores()
        + [pltpu.SemaphoreType.DMA((8,))] * 2,
        specs=[HBM, HBM, ANY],
        flops=2 * q * 1024 * 2048,
        moved=2 * (q * 1024 + 1024 * 2048 + 2 * q * 2048),
        vmem=LARGE,
    )


def middle_kernel(ids, local, r1, r2, r3, kept, s1, s2, s3):
    @pl.when(ids[2] == 0)
    def _():
        for e, out in ((0, kept), (1, s1)):
            total = (local[e].astype(F32) + r1[e].astype(F32)) + (r2[e].astype(F32) + r3[e].astype(F32))
            out[...] = total.astype(out.dtype)

    @pl.when(ids[2] == 1)
    def _():
        for d, out in enumerate((kept, s1, s2, s3)):
            arrived = (r1 if d < 2 else r3)[d % 2]
            out[...] = (local[d].astype(F32) + arrived.astype(F32)).astype(out.dtype)


def middle(ids, local, arrived, q):
    n = 2

    def three(i, ids):
        return (0, i, 0)

    def two(i, ids):
        return (i, 0)

    return call(
        middle_kernel,
        (ids,),
        (local, *arrived),
        [jax.ShapeDtypeStruct((q, PAIR), t) for t in (F32, BF16, BF16, BF16)],
        grid=(n,),
        specs=[pl.BlockSpec((a.shape[0], q // n, PAIR), three) for a in (local, *arrived)],
        out_specs=[pl.BlockSpec((q // n, PAIR), two)] * 4,
        moved=2 * PAIR * q * 15,
        flops=PAIR * q * 8,
    )


def rope_rows_kernel(ids, offs, lens, table, out, sem, *, base, q):
    starts, counts, _ = plan(ids, offs, lens)
    for verb in ("start", "wait"):

        def copy(p, bit, source, target, count, verb=verb):
            position = lax.shift_right_logical(offs[ids[3] * LOCAL + p], 4)
            c = pltpu.make_async_copy(
                table.at[rows(position + source, count)], out.at[rows(target, count)], sem.at[p, bit]
            )
            c.start() if verb == "start" else c.wait()

        ragged(starts, counts, base // G + ids[2] * (q // G), q // G, copy)


def rope_rows(meta, table, base, q):
    return call(
        functools.partial(rope_rows_kernel, base=base, q=q),
        meta,
        (table,),
        jax.ShapeDtypeStruct((q, PAIR), F32),
        [pltpu.SemaphoreType.DMA((LOCAL, 5))],
        specs=[HBM],
        moved=q * PAIR * 8,
    )


def finish_kernel(ids, offs, lens, kept, r1, r2, r3, turn, out, *, base, q):
    _, _, total = plan(ids, offs, lens)
    valid = (total - base // G - ids[2] * (q // G)) * G

    def put(value):
        row = lax.broadcasted_iota(jnp.int32, (q, HEAD_SIZE), 0)
        key = value[:, :HEAD_SIZE]
        key = key * turn[:, :HEAD_SIZE] + pltpu.roll(key, HEAD_SIZE // 2, 1) * turn[:, HEAD_SIZE:]
        out[:, :HEAD_SIZE] = jnp.where(row < valid, key, 0.0).astype(BF16)
        out[:, HEAD_SIZE:] = value[:, HEAD_SIZE:].astype(BF16)

    @pl.when(ids[2] == 0)
    def _():
        put(kept[...] + r1[...].astype(F32))

    @pl.when(ids[2] == 1)
    def _():
        put((kept[...] + r1[...].astype(F32)) + (r2[...].astype(F32) + r3[...].astype(F32)))


def finish(meta, kept, arrived, turn, base, q):
    return call(
        functools.partial(finish_kernel, base=base, q=q),
        meta,
        (kept, *arrived, turn),
        jax.ShapeDtypeStruct((q, PAIR), BF16),
        specs=[VMEM] * 5,
        out_specs=VMEM,
        moved=q * PAIR * 16,
        flops=q * PAIR * 4,
    )


def stack_heads(tile):
    return [tile[:, h * HEAD_SIZE : (h + 1) * HEAD_SIZE] for h in range(HEADS)]


def scores_of(query, keys):
    return lax.dot_general(query, keys, (((1,), (1,)), ((), ())), preferred_element_type=F32) * SCALE2


def spread(column, n):
    lane = lax.broadcasted_iota(jnp.int32, (n, HEAD_SIZE), 1)
    out = jnp.zeros((n, HEAD_SIZE), F32)
    for h in range(HEADS):
        out = jnp.where(lane == h, column[h * n : (h + 1) * n], out)
    return out


def smallest(value):
    return jnp.min(value.reshape(-1, 8, HEAD_SIZE), axis=0)


def largest(value):
    return jnp.max(value.reshape(-1, 8, HEAD_SIZE), axis=0)


def gather_column(stats):
    return jnp.concatenate([stats[:, h : h + 1] for h in range(HEADS)], axis=0)


def tile_rows(t):
    return slice(t * TILE, (t + 1) * TILE)


def when_tile(count, t):
    return pl.when(count > t * TILE)


TILES = FINAL_LENGTH // TILE


def prior_kernel(ids, offs, lens, owner, asked, query, mine, theirs, *refs, first, n, q):
    (*outs, qbuf, kbuf, vbuf, obuf, sbuf, dpad, dobuf, dsbuf, least, most, qsem, ksem, osem, dsem, tsem) = refs
    if q:
        table, *outs, turn = outs
    out, stat, dout, dstat = outs[-4:]
    core = ids[2]

    def place(i):
        at = ids[3] * LOCAL + first + i
        return offs[at], lens[at] - offs[at], owner[at]

    def query_copy(i, t):
        return pltpu.make_async_copy(query.at[first + i, tile_rows(t)], qbuf.at[i, tile_rows(t)], qsem.at[i, t])

    def key_copy(i, part):
        here = core if part == 0 else 1 - core
        target = kbuf.at[i, pl.ds(pl.multiple_of(here * PART, PART), PART)]
        return pltpu.make_async_copy((mine, theirs)[part].at[first + i], target, ksem.at[i, part])

    def when_part(offset, part):
        here = core if part == 0 else 1 - core
        return pl.when(jnp.logical_or(here == 0, offset > PART))

    def out_copies(i, t):
        return (
            pltpu.make_async_copy(obuf.at[i, tile_rows(t)], out.at[first + i, tile_rows(t)], osem.at[i, t, 0]),
            pltpu.make_async_copy(sbuf.at[i, tile_rows(t)], stat.at[first + i, tile_rows(t)], osem.at[i, t, 1]),
        )

    def decode_copies(i):
        return (
            pltpu.make_async_copy(dobuf.at[i], dout.at[first + i], dsem.at[i, 0]),
            pltpu.make_async_copy(dsbuf.at[i], dstat.at[first + i], dsem.at[i, 1]),
        )

    def load(i):
        offset, count, _ = place(i)
        for part in range(2):
            when_part(offset, part)(lambda: key_copy(i, part).start())
        for t in range(TILES):
            when_tile(count, t)(lambda: query_copy(i, t).start())

    def turn_copies(verb):
        starts, counts, _ = plan(ids, offs, lens)

        def copy(p, bit, source, target, count):
            position = lax.shift_right_logical(offs[ids[3] * LOCAL + p], 4)
            c = pltpu.make_async_copy(
                table.at[rows(position + source, count)], turn.at[rows(target, count)], tsem.at[p, bit]
            )
            c.start() if verb == "start" else c.wait()

        ragged(starts, counts, core * (q // G), q // G, copy)

    load(0)
    vbuf[:, HEAD_SIZE:] = jnp.ones((CONTEXT_LENGTH, HEAD_SIZE), BF16)
    dpad[...] = jnp.zeros(dpad.shape, BF16)
    if n > 1:
        load(1)
    if q:
        turn_copies("start")

    @pl.loop(0, n)
    def _(i):
        offset, count, slot = place(i)
        if n > 2:
            pl.when(i + 2 < n)(lambda: load(i + 2))
        for part in range(2):
            when_part(offset, part)(lambda part=part: key_copy(i, part).wait())
        for t in range(TILES):
            when_tile(count, t)(lambda t=t: query_copy(i, t).wait())
        dpad[:STEPS, :] = asked[slot, :, : HEADS * HEAD_SIZE]
        least[...] = jnp.full(least.shape, 1.0, F32)
        most[...] = jnp.full(most.shape, 1.0, F32)

        def put(where, value, stats, rows_of_head):
            for h in range(HEADS):
                lanes = slice(h * HEAD_SIZE, (h + 1) * HEAD_SIZE)
                obuf[i, where, lanes] = value[h * rows_of_head : (h + 1) * rows_of_head]
            sbuf[i, where, :] = spread(stats, rows_of_head)

        def put_decode(value, stats):
            for h in range(HEADS):
                dobuf[i, :, h * HEAD_SIZE : (h + 1) * HEAD_SIZE] = value[h * DROWS : (h + 1) * DROWS]
            dsbuf[i] = spread(stats, DROWS)

        for blocks in range(1, 5):

            @pl.when(offset == blocks * 256)
            def _(keys=blocks * 256):
                vbuf[:keys, :HEAD_SIZE] = kbuf[i, :keys, HEAD_SIZE:]
                for t in range(TILES):

                    @when_tile(count, t)
                    def _(t=t):
                        tile = stack_heads(qbuf[i, tile_rows(t), :])
                        if t == 0:
                            tile = tile + stack_heads(dpad[...])
                        tile = jnp.concatenate(tile, axis=0)
                        weights = jnp.exp2(scores_of(tile, kbuf[i, :keys, :HEAD_SIZE])).astype(BF16)
                        mixed = jnp.dot(weights, vbuf[:keys, :], preferred_element_type=F32)
                        total = mixed[:, HEAD_SIZE:]
                        least[...] = jnp.minimum(least[...], smallest(total))
                        most[...] = jnp.maximum(most[...], largest(total))
                        value = (mixed[:, :HEAD_SIZE] * (1.0 / total)).astype(BF16)
                        stats = jnp.log2(total)
                        m = HEADS * TILE
                        put(tile_rows(t), value[:m], stats[:m], TILE)
                        if t == 0:
                            put_decode(value[m:], stats[m:])

        fine = jnp.logical_and(jnp.min(least[...]) >= LOW, jnp.max(most[...]) <= HIGH)

        @pl.when(jnp.logical_not(fine))
        def _():
            def exact(tile):
                def block(b, carry):
                    top, mixed = carry
                    keys = pl.ds(pl.multiple_of(b * 256, 256), 256)
                    scores = scores_of(tile, kbuf[i, keys, :HEAD_SIZE])
                    now = jnp.maximum(jnp.max(scores, axis=1, keepdims=True), top)
                    weights = jnp.exp2(scores - now).astype(BF16)
                    more = jnp.dot(weights, vbuf[keys, :], preferred_element_type=F32)
                    return now, mixed * jnp.exp2(top - now) + more

                m = tile.shape[0]
                start = (jnp.full((m, 1), NEG, F32), jnp.zeros((m, PAIR), F32))
                top, mixed = lax.fori_loop(0, lax.shift_right_logical(offset, 8), block, start)
                total = mixed[:, HEAD_SIZE:]
                return (mixed[:, :HEAD_SIZE] / total).astype(BF16), top + jnp.log2(total)

            @pl.loop(0, lax.shift_right_logical(count + 31, 5))
            def _(t):
                where = pl.ds(pl.multiple_of(t * 32, 32), 32)
                put(where, *exact(jnp.concatenate(stack_heads(qbuf[i, where, :]), axis=0)), 32)

            put_decode(*exact(jnp.concatenate(stack_heads(dpad[...]), axis=0)))

        for t in range(TILES):
            when_tile(count, t)(lambda t=t: [c.start() for c in out_copies(i, t)] and None)
        for c in decode_copies(i):
            c.start()

    for i in range(n):
        _, count, _ = place(i)
        for t in range(TILES):
            when_tile(count, t)(lambda i=i, t=t: [c.wait() for c in out_copies(i, t)] and None)
        for c in decode_copies(i):
            c.wait()
    if q:
        turn_copies("wait")


def prior(meta, owner, query, asked, mine, theirs, first, n, before=(), table=None, q=0):
    wide, narrow = (FINAL_LENGTH, HEADS * HEAD_SIZE), (FINAL_LENGTH, HEAD_SIZE)
    dwide, dnarrow = (DROWS, HEADS * HEAD_SIZE), (DROWS, HEAD_SIZE)
    shapes = [(wide, BF16), (narrow, F32), (dwide, BF16), (dnarrow, F32)]
    return call(
        functools.partial(prior_kernel, first=first, n=n, q=q),
        (*meta, owner),
        (asked, query, mine, theirs, *before, *([table] if q else [])),
        [pltpu.HBM((LOCAL, *s), t) for s, t in shapes] + ([jax.ShapeDtypeStruct((q, PAIR), F32)] if q else []),
        [
            pltpu.VMEM((n, *wide), BF16),
            pltpu.VMEM((n, CONTEXT_LENGTH, PAIR), BF16),
            pltpu.VMEM((CONTEXT_LENGTH, PAIR), BF16),
            pltpu.VMEM((n, *wide), BF16),
            pltpu.VMEM((n, *narrow), F32),
            pltpu.VMEM(dwide, BF16),
            pltpu.VMEM((n, *dwide), BF16),
            pltpu.VMEM((n, *dnarrow), F32),
            pltpu.VMEM((8, HEAD_SIZE), F32),
            pltpu.VMEM((8, HEAD_SIZE), F32),
            pltpu.SemaphoreType.DMA((n, TILES)),
            pltpu.SemaphoreType.DMA((n, 2)),
            pltpu.SemaphoreType.DMA((n, TILES, 2)),
            pltpu.SemaphoreType.DMA((n, 2)),
            pltpu.SemaphoreType.DMA((LOCAL, 5)),
        ],
        specs=[VMEM] + [ANY] * (3 + len(before) + (q > 0)),
        aliases={8 + i: i for i in range(len(before))},
        flops=n * 3 * 10**9,
        moved=n * 2 * 10**6,
    )


def load_fresh(ids, own, other, rest, fbuf, sem):
    copies, base = [], 0
    for c, pieces in enumerate(((own, other), (rest.at[0], rest.at[1]))):
        q = pieces[0].shape[0]
        for i, core in enumerate((ids[2], 1 - ids[2])):
            target = fbuf.at[pl.ds(pl.multiple_of(base + core * q, G), q)]
            copies.append(pltpu.make_async_copy(pieces[i], target, sem.at[2 * c + i]))
        base += 2 * q
    for c in copies:
        c.start()
    fbuf[base:, :] = jnp.zeros((FINAL_LENGTH, PAIR), BF16)
    return copies


def fresh_kernel(ids, offs, lens, *refs):
    pieces = refs[:3]
    query, prior_out, prior_stat, out, fbuf, vbuf, qbuf, pbuf, sbuf, obuf, least, most, sem, isem, osem = refs[3:]

    def count_of(p):
        at = ids[3] * LOCAL + p
        return lens[at] - offs[at]

    def in_copies(p, t):
        pairs_of = ((query, qbuf), (prior_out, pbuf), (prior_stat, sbuf))
        return [
            pltpu.make_async_copy(ref.at[p, tile_rows(t)], buf.at[p, tile_rows(t)], isem.at[p, t, i])
            for i, (ref, buf) in enumerate(pairs_of)
        ]

    def out_copy(p):
        return pltpu.make_async_copy(obuf.at[p], out.at[p], osem.at[p])

    def load(p):
        for t in range(TILES):
            when_tile(count_of(p), t)(lambda: [c.start() for c in in_copies(p, t)] and None)

    load(0)
    copies = load_fresh(ids, *pieces, fbuf, sem)
    vbuf[:, HEAD_SIZE:] = jnp.ones((FINAL_LENGTH, HEAD_SIZE), BF16)
    load(1)
    for c in copies:
        c.wait()

    def prompt(p, start):
        count = count_of(p)
        pl.when(p + 2 < LOCAL)(lambda: load(p + 2))
        first_key = pl.multiple_of(start * G, G)
        vbuf[:, :HEAD_SIZE] = fbuf[pl.ds(first_key, FINAL_LENGTH), HEAD_SIZE:]
        least[...] = jnp.full(least.shape, 1.0, F32)
        most[...] = jnp.full(most.shape, 1.0, F32)

        for t in range(TILES):
            where = tile_rows(t)

            @pl.when(count <= t * TILE)
            def _(where=where):
                obuf[p, where, :] = jnp.zeros((TILE, HEADS * HEAD_SIZE), BF16)

            @when_tile(count, t)
            def _(where=where, t=t):
                for c in in_copies(p, t):
                    c.wait()
                seen = (t + 1) * TILE
                row = lax.broadcasted_iota(jnp.int32, (TILE, seen), 0) + t * TILE
                allowed = lax.broadcasted_iota(jnp.int32, (TILE, seen), 1) <= row
                tile = jnp.concatenate(stack_heads(qbuf[p, where, :]), axis=0)
                scores = scores_of(tile, fbuf[pl.ds(first_key, seen), :HEAD_SIZE])
                weights = jnp.concatenate(
                    [
                        jnp.where(allowed, jnp.exp2(scores[h * TILE : (h + 1) * TILE]), 0.0).astype(BF16)
                        for h in range(HEADS)
                    ],
                    axis=0,
                )
                mixed = jnp.dot(weights, vbuf[:seen, :], preferred_element_type=F32)
                keep = lax.broadcasted_iota(jnp.int32, (TILE, HEAD_SIZE), 0) + t * TILE < count
                before = jnp.exp2(sbuf[p, where, :])
                low, high = least[...], most[...]
                for h in range(HEADS):
                    lanes = slice(h * HEAD_SIZE, (h + 1) * HEAD_SIZE)
                    stack = slice(h * TILE, (h + 1) * TILE)
                    share = before[:, h : h + 1]
                    total = mixed[stack, HEAD_SIZE:] + share
                    low, high = jnp.minimum(low, smallest(total)), jnp.maximum(high, largest(total))
                    old = pbuf[p, where, lanes].astype(F32)
                    value = (mixed[stack, :HEAD_SIZE] + old * share) * (1.0 / total)
                    obuf[p, where, lanes] = jnp.where(keep, value, 0.0).astype(BF16)
                least[...], most[...] = low, high

        fine = jnp.logical_and(jnp.min(least[...]) >= LOW, jnp.max(most[...]) <= HIGH)

        @pl.when(jnp.logical_not(fine))
        def _():
            some = 32
            n = HEADS * some

            @pl.loop(0, lax.shift_right_logical(count + (some - 1), 5))
            def _(t):
                where = pl.ds(pl.multiple_of(t * some, some), some)
                position = lax.bitwise_and(lax.broadcasted_iota(jnp.int32, (n, FINAL_LENGTH), 0), some - 1)
                ahead = lax.broadcasted_iota(jnp.int32, (n, FINAL_LENGTH), 1) - position
                tile = jnp.concatenate(stack_heads(qbuf[p, where, :]), axis=0)
                scores = scores_of(tile, fbuf[pl.ds(first_key, FINAL_LENGTH), :HEAD_SIZE])
                scores = jnp.where(ahead <= t * some, scores, NEG)
                before = gather_column(sbuf[p, where, :])
                top = jnp.maximum(jnp.max(scores, axis=1, keepdims=True), before)
                weights = jnp.exp2(scores - top).astype(BF16)
                share = jnp.exp2(before - top)
                mixed = jnp.dot(weights, vbuf[...], preferred_element_type=F32)
                total = mixed[:, HEAD_SIZE:] + share
                keep = lax.broadcasted_iota(jnp.int32, (some, HEAD_SIZE), 0) + t * some < count
                for h in range(HEADS):
                    lanes = slice(h * HEAD_SIZE, (h + 1) * HEAD_SIZE)
                    stack = slice(h * some, (h + 1) * some)
                    old = pbuf[p, where, lanes].astype(F32)
                    value = (mixed[stack, :HEAD_SIZE] + old * share[stack]) / total[stack]
                    obuf[p, where, lanes] = jnp.where(keep, value, 0.0).astype(BF16)

        out_copy(p).start()
        return start + lax.shift_right_logical(count + (G - 1), 4)

    lax.fori_loop(0, LOCAL, prompt, jnp.int32(0))
    for p in range(LOCAL):
        out_copy(p).wait()


def fresh(meta, pieces, query, prior_out, prior_stat):
    wide, narrow = (LOCAL, FINAL_LENGTH, HEADS * HEAD_SIZE), (LOCAL, FINAL_LENGTH, HEAD_SIZE)
    return call(
        fresh_kernel,
        meta,
        (*pieces, query, prior_out, prior_stat),
        pltpu.HBM(wide, BF16),
        [
            pltpu.VMEM(((LOCAL + 1) * FINAL_LENGTH, PAIR), BF16),
            pltpu.VMEM((FINAL_LENGTH, PAIR), BF16),
            pltpu.VMEM(wide, BF16),
            pltpu.VMEM(wide, BF16),
            pltpu.VMEM(narrow, F32),
            pltpu.VMEM(wide, BF16),
            pltpu.VMEM((8, HEAD_SIZE), F32),
            pltpu.VMEM((8, HEAD_SIZE), F32),
            pltpu.SemaphoreType.DMA((4,)),
            pltpu.SemaphoreType.DMA((LOCAL, TILES, 3)),
            pltpu.SemaphoreType.DMA((LOCAL,)),
        ],
        flops=4 * 10**9,
        moved=10**7,
        vmem=40,
    )


def decode_kernel(ids, offs, lens, owner, *refs):
    pieces = refs[:3]
    asked, prior_out, prior_stat, out, fbuf, dpad, sem = refs[3:]
    copies = load_fresh(ids, *pieces, fbuf, sem)
    dpad[...] = jnp.zeros(dpad.shape, BF16)
    for slot in range(LOCAL):
        dpad[slot, :STEPS, :] = asked[slot]
    for c in copies:
        c.wait()
    starts, _, _ = plan(ids, offs, lens)
    n = HEADS * DROWS
    step = lax.bitwise_and(lax.broadcasted_iota(jnp.int32, (n, DROWS), 0), DROWS - 1)
    reached = lax.broadcasted_iota(jnp.int32, (n, DROWS), 1) <= step
    column = lax.broadcasted_iota(jnp.int32, (n, FINAL_LENGTH), 1)
    ones = jnp.ones((FINAL_LENGTH, HEAD_SIZE), BF16)

    def product(left, right):
        return jnp.dot(left, right, preferred_element_type=F32)

    def scores(p, start):
        i = ids[3] * LOCAL + p
        slot = owner[i]
        keys = pl.ds(pl.multiple_of(start * G, G), FINAL_LENGTH)
        tile = jnp.concatenate(stack_heads(dpad[slot, :, : HEADS * HEAD_SIZE]), axis=0)
        recent = dpad[slot, :, HEADS * HEAD_SIZE :]
        block, near = scores_of(tile, fbuf[keys, :HEAD_SIZE]), scores_of(tile, recent[:, :HEAD_SIZE])
        allowed = column < lens[i] - offs[i]
        return slot, allowed, block, near, fbuf[keys, HEAD_SIZE:], recent[:, HEAD_SIZE:]

    def put(p, slot, mixed, total, share):
        for h in range(HEADS):
            lanes = slice(h * HEAD_SIZE, (h + 1) * HEAD_SIZE)
            stack = slice(h * DROWS, (h + 1) * DROWS)
            value = (mixed[stack] + prior_out[p, :, lanes].astype(F32) * share[stack]) / total[stack]
            out[slot, :, lanes] = value[:STEPS].astype(BF16)

    low = high = jnp.ones((8, HEAD_SIZE), F32)
    for p in range(LOCAL):
        slot, allowed, block, near, values, near_values = scores(p, starts[p])
        block = jnp.where(allowed, jnp.exp2(block), 0.0).astype(BF16)
        near = jnp.where(reached, jnp.exp2(near), 0.0).astype(BF16)
        share = gather_column(jnp.exp2(prior_stat[p]))
        total = product(block, ones) + product(near, ones[:DROWS]) + share
        low, high = jnp.minimum(low, smallest(total)), jnp.maximum(high, largest(total))
        put(p, slot, product(block, values) + product(near, near_values), total, share)

    fine = jnp.logical_and(jnp.min(low) >= LOW, jnp.max(high) <= HIGH)

    @pl.when(jnp.logical_not(fine))
    def _():
        for p in range(LOCAL):
            slot, allowed, block, near, values, near_values = scores(p, starts[p])
            block, near = jnp.where(allowed, block, NEG), jnp.where(reached, near, NEG)
            before = gather_column(prior_stat[p])
            top = jnp.maximum(jnp.max(block, axis=1, keepdims=True), jnp.max(near, axis=1, keepdims=True))
            top = jnp.maximum(top, before)
            block, near, share = jnp.exp2(block - top), jnp.exp2(near - top), jnp.exp2(before - top)
            total = jnp.sum(block, axis=1, keepdims=True) + jnp.sum(near, axis=1, keepdims=True) + share
            put(p, slot, product(block.astype(BF16), values) + product(near.astype(BF16), near_values), total, share)


def decode(meta, owner, pieces, asked, prior_out, prior_stat):
    return call(
        decode_kernel,
        (*meta, owner),
        (*pieces, asked, prior_out, prior_stat),
        jax.ShapeDtypeStruct((LOCAL, STEPS, HEADS * HEAD_SIZE), BF16),
        [
            pltpu.VMEM(((LOCAL + 1) * FINAL_LENGTH, PAIR), BF16),
            pltpu.VMEM((LOCAL, DROWS, HEADS * HEAD_SIZE + PAIR), BF16),
            pltpu.SemaphoreType.DMA((4,)),
        ],
        specs=[ANY] * 3 + [VMEM] * 3,
        out_specs=VMEM,
        flops=10**8,
        moved=2 * 10**6,
    )


def exchange(value):
    return lax.all_to_all(value, "grp", split_axis=0, concat_axis=0, tiled=True)


def permute(value, way):
    return lax.ppermute(value, "tp", way)


def after(value, *others):
    return lax.optimization_barrier((value, *others))[0]


def spread_sums(sent, ways):
    arrived = [None] * 3
    for i in ORDER:
        arrived[i] = permute(sent[i], ways[i])
    return arrived


def in_hbm(value):
    return pltpu.with_memory_space_constraint(value, pltpu.HBM)


def rest_of_keys(meta, hid, weight, table, base, q):
    half, _ = send_half(meta, hid, weight, base, q)
    local, *sent = keep_half(meta, hid, weight, permute(half, SIBLING), base, q)
    kept, *sent = middle(meta[0], local, spread_sums(sent, FIRST), q)
    new = finish(meta, kept, spread_sums(sent, SECOND), rope_rows(meta, table, base, q), base, q)
    return jnp.stack([new, permute(new, SIBLING)])


def per_device(
    hidden_rows,
    key_value_weight,
    prefill_query,
    earlier_cache,
    stretch_offset,
    prompt_length,
    decode_owner,
    decode_query,
    decode_kv,
):
    lane = lax.axis_index("tp")
    group = lax.axis_index("grp")
    ids = jnp.stack([lane // 4, lane // 2 % 2, lane % 2, group]).astype(jnp.int32)
    meta = (ids, stretch_offset, prompt_length)
    table = jnp.asarray(rope_table())
    hid = hidden_rows.reshape(LOCAL * FINAL_LENGTH, -1)
    cache = in_hbm(earlier_cache.reshape(LOCAL, PART, PAIR))
    hid, key_value_weight, prefill_query = (in_hbm(a) for a in (hid, key_value_weight, prefill_query))
    q = ROOM // 2

    half, more = send_half(meta, hid, key_value_weight, 0, q)
    other_half = permute(half, SIBLING)
    other_cache = permute(cache, SIBLING)
    recent = lax.dynamic_slice_in_dim(decode_kv, (lane // 2) * PAIR, PAIR, 2)
    asked = exchange(jnp.concatenate([decode_query, recent], axis=2))
    beyond = LOCAL * FINAL_LENGTH - ROOM
    rest = lax.cond(
        more[0] > 0,
        lambda *a: rest_of_keys(a[:3], *a[3:], ROOM, beyond // 2),
        lambda *a: jnp.zeros((2, beyond // 2, PAIR), BF16),
        *meta,
        hid,
        key_value_weight,
        table,
    )

    local, *sent = keep_half(meta, hid, key_value_weight, after(other_half, rest, asked), 0, q)
    arrived = spread_sums(sent, FIRST)

    common = (meta, decode_owner, prefill_query, asked, cache, other_cache)
    *before, turn = prior(*common, 0, 7, table=after(table, local), q=q)
    kept, *sent = middle(ids, after(local, turn), arrived, q)
    arrived = spread_sums(sent, SECOND)
    prior_out, prior_stat, prior_dout, prior_dstat = (in_hbm(a) for a in prior(*common, 7, 1, before=before))
    new = finish(meta, after(kept, prior_dstat), arrived, turn, 0, q)
    pieces = (new, permute(new, SIBLING), rest)

    answer = decode(meta, decode_owner, pieces, asked, prior_dout, prior_dstat)
    decode_out = exchange(answer)
    prefill_out = fresh(meta, pieces, prefill_query, prior_out, prior_stat)
    return (prefill_out, decode_out)


def solution(mesh):
    in_specs = (
        P("grp", None, "tp"),
        P("tp", None),
        P("grp", None, "tp"),
        P("grp", "tp", None, None),
        P(),
        P(),
        P(),
        P("grp", None, "tp"),
        P("grp", None, None),
    )
    out_specs = (P("grp", None, "tp"), P("grp", None, "tp"))
    return jax.shard_map(
        per_device, mesh=mesh, in_specs=in_specs, out_specs=out_specs, check_vma=False
    )
```
